32 devices in a mesh: tiles: 8 (over z, y), probes: 4 (over x, core).
Axes of the slice: x: 2, y: 2, z: 4, core: 2. Of those that a mesh axis runs over, the one named last changes fastest.
Arguments:
- blocks: bfloat16 [512, 192, 192], P('tiles'), may hold values from -0.21875 to 0.21875
- connectivity: int32 [512, 64], P('tiles'), may hold values from 0 to 4607, as said below
- basal_map: int32 [512, 64], P('tiles'), may hold values from 0 to 383
- friction: float32 [512, 64, 3], P('tiles'), may hold values from 0.2 to 2
- elem_counts: int32 [8], P('tiles'), may hold values from 1 to 64, 384 in all
- obs_weight: float32 [32768, 3], P('tiles'), may hold values from 0.2 to 2
- sign_bits: int32 [2048, 32], P('tiles', 'probes'), may hold values from 0 to 1
- cluster_ids: int32 [2048], P('tiles'), may hold values from 0 to 7, never falling along the last dimension, each value on 1 to 512 neighbouring positions
Outputs:
- samples: float32 [2048, 32], P('tiles', 'probes')
- refined: float32 [2048, 32], P('tiles', 'probes')
- gram: float32 [8, 32, 32], P(None, 'probes')
The draws below stay inside these ranges and needn't reach their ends.
Inputs may be any that keep to these rules, and one draw needn't show every extreme that they name: `connectivity`: about one reference in eight names a node of the next tile. `elem_counts`: some tile has all 64 slots live. `cluster_ids`: never falling along the cells; each cluster holds 1 to 512 cells.
All inputs are finite; a program needn't handle non-finite values. No bound on the sum of `elem_counts` on one device may be relied on, other than what follows from the above.
Results may differ from the reference program's by a relative error of at most 0.004.
Values may be sent and summed in bfloat16 or wider, within the bound.
No kernel may reach another device: no remote copies, remote signals or barrier semaphores. Data moves between devices by JAX's collectives and lax.ppermute only.
A program may use at most 64 MiB of HBM per device.

```python
import math
import jax
import jax.numpy as jnp
import numpy as np
from jax import lax

NPE = 64
DOF = 192
PROBES = 32
E_DEV = 64
NODE = 4096
HALO = 512
POWER = 2
BC = 256
RIM = 64
TILES = 8
ELEMS = 512
NNODE = 32768
NBAS = 2048
NCL = 8
N_TILES = 8


def draw_connectivity(key, part):
    key_pick = jax.random.fold_in(key, 11)
    key_own = jax.random.fold_in(key, 12)
    key_next = jax.random.fold_in(key, 13)
    choose = jax.random.randint(key_pick, (ELEMS, NPE), 0, 8)
    own_nodes = jax.random.randint(key_own, (ELEMS, NPE), 0, NODE)
    next_nodes = NODE + jax.random.randint(key_next, (ELEMS, NPE), 0, HALO)
    result = jnp.where(choose == 0, next_nodes, own_nodes).astype(jnp.int32)
    result = result.at[0, 0].set(NODE + HALO - 1)
    result = result.at[0, 1].set(0)
    return result


def place_ends(array, stream_key, low, largest):
    spot = [jax.random.randint(jax.random.fold_in(stream_key, axis), (), 0, length) for axis, length in enumerate(array.shape)]
    main_axis = array.shape.index(max(array.shape))
    beside = spot[:main_axis] + [(spot[main_axis] + 1) % array.shape[main_axis]] + spot[main_axis + 1:]
    return array.at[tuple(spot)].set(low).at[tuple(beside)].set(largest)


def shard_levels(key, extent, pieces, least, largest):
    level, own = 1.0, jax.random.fold_in(key, 6)
    for axis_at, blocks in pieces:
        steps = jnp.exp(jax.random.uniform(jax.random.fold_in(own, axis_at), (blocks,), jnp.float32, least / len(pieces), largest / len(pieces)))
        level = level * jnp.repeat(steps, extent[axis_at] // blocks).reshape([-1 if axis == axis_at else 1 for axis in range(len(extent))])
    return level


def split_up(count, total, limit, skew):
    weights = [(1 << 20) // math.isqrt(rank ** skew) + 1 for rank in range(2, count + 1)]
    spare, given = total - limit - (count - 1), [1] * (count - 1)
    while spare > 0:
        candidates = [i for i in range(count - 1) if given[i] < limit]
        whole, left = sum([weights[i] for i in candidates]), spare
        for i in candidates:
            extra = min(limit - given[i], max(1, left * weights[i] // whole), spare)
            given[i] = given[i] + extra
            spare = spare - extra
    return np.array([limit] + given)


def ragged(stream_key, count, total, reach, lean):
    if count == 2:
        one = jax.random.randint(stream_key, (), max(1, total - reach), min(reach, total - 1) + 1)
        return jnp.stack([one, total - one])
    tallies = jnp.asarray(split_up(count, total, reach, lean), jnp.int32)
    couples = (count - 1) // 2
    source_of, sink = tallies[1:1 + 2 * couples:2], tallies[2:2 + 2 * couples:2]
    slack = jnp.minimum(source_of - 1, reach - sink)
    shifted = jax.random.randint(jax.random.fold_in(stream_key, 1), (couples,), 0, 1 << 20) % (slack + 1)
    tallies = tallies.at[1:1 + 2 * couples:2].set(source_of - shifted).at[2:2 + 2 * couples:2].set(sink + shifted)
    return tallies[jax.random.permutation(jax.random.fold_in(stream_key, 2), count)]


def centred(key, extent, scale, reach, pieces=(), kind=jnp.bfloat16):
    factor_of = shard_levels(key, extent, pieces, -0.22, 0.18) if pieces else 1.0
    entries = jax.random.normal(key, extent, jnp.float32) * scale * factor_of
    return jnp.minimum(jnp.maximum(entries, -reach), reach).astype(kind)


def setup_inputs(seed: int = 0) -> dict:
    seeds = jax.random.split(jax.random.key(seed), 9)
    return {
        "blocks": centred(seeds[0], (ELEMS, DOF, DOF), (DOF * 4) ** -0.5, 0.21875, ((0, 8),)),
        "connectivity": draw_connectivity(jax.random.fold_in(seeds[8], 71), 0),
        "basal_map": place_ends(jax.random.randint(seeds[2], (ELEMS, NPE), 0, BC + 2 * RIM), jax.random.fold_in(seeds[2], 1), 0, (BC + 2 * RIM) - 1).astype(jnp.int32),
        "friction": jnp.clip(jnp.exp(math.log(2.0) - 2.3025851 * jax.random.uniform(seeds[3], (ELEMS, NPE, 3), jnp.float32) ** shard_levels(seeds[3], (ELEMS, NPE, 3), ((0, 8),), -0.2, 0.2)), 0.2, 2.0),
        "elem_counts": ragged(seeds[4], TILES, 3 * E_DEV * N_TILES // 4, E_DEV, 2).astype(jnp.int32),
        "obs_weight": jnp.clip(jnp.exp(math.log(2.0) - 2.3025851 * jax.random.uniform(seeds[5], (NNODE, 3), jnp.float32) ** shard_levels(seeds[5], (NNODE, 3), ((0, 8),), -0.2, 0.2)), 0.2, 2.0),
        "sign_bits": place_ends(jax.random.randint(seeds[6], (NBAS, PROBES), 0, 2), jax.random.fold_in(seeds[6], 1), 0, 1).astype(jnp.int32),
        "cluster_ids": jnp.searchsorted(jnp.cumsum(ragged(seeds[7], NCL, NBAS, 2 * BC, 1)), jnp.arange(NBAS), side="right").astype(jnp.int32),
    }


def reference(blocks, connectivity, basal_map, friction, elem_counts, obs_weight, sign_bits, cluster_ids):
    slot_range = jnp.arange(ELEMS, dtype=jnp.int32)
    tile_of = (slot_range // E_DEV).astype(jnp.int32)
    slot_of = (slot_range % E_DEV).astype(jnp.int32)
    alive_slots = slot_of < elem_counts[tile_of]
    node_global = tile_of[:, None] * NODE + connectivity
    node_valid = node_global < NNODE
    node_clip = jnp.clip(node_global, 0, NNODE - 1)
    node_target = jnp.where(node_valid, node_global, NNODE).reshape(-1)
    cell_global = tile_of[:, None] * BC + basal_map - RIM
    cell_valid = (cell_global >= 0) & (cell_global < NBAS)
    cell_clip = jnp.clip(cell_global, 0, NBAS - 1)
    cell_target = jnp.where(cell_valid, cell_global, NBAS).reshape(-1)
    tiled_blocks = blocks.reshape(N_TILES, E_DEV, DOF, DOF)

    def products(vectors, form):

        def one_tile(operands):
            return jnp.einsum(form, operands[0].astype(jnp.float32), operands[1].astype(jnp.float32), precision=lax.Precision.HIGHEST)
        result = lax.map(one_tile, (tiled_blocks, vectors.reshape(N_TILES, E_DEV, DOF, PROBES)))
        return result.reshape(ELEMS, DOF, PROBES)

    def hessian(field):
        gathered = jnp.where(cell_valid[:, :, None], field[cell_clip], jnp.float32(0.0))
        inputs = (friction[:, :, :, None] * gathered[:, :, None, :]).astype(jnp.bfloat16).reshape(ELEMS, DOF, PROBES)
        forward = products(inputs, 'eij,ejp->eip')
        forward = jnp.where(alive_slots[:, None, None], forward, jnp.float32(0.0))
        assembled = jax.ops.segment_sum(forward.reshape(ELEMS * NPE, 3 * PROBES), node_target, num_segments=NNODE + 1)[:NNODE]
        weighted = (obs_weight[:, :, None] * assembled.reshape(NNODE, 3, PROBES)).astype(jnp.bfloat16)
        adjoint_in = jnp.where(node_valid[:, :, None, None], weighted[node_clip], jnp.zeros((), jnp.bfloat16))
        adjoint_out = products(adjoint_in.reshape(ELEMS, DOF, PROBES), 'eji,ejp->eip')
        partials = lax.optimization_barrier(jnp.sum(friction[:, :, :, None] * adjoint_out.reshape(ELEMS, NPE, 3, PROBES), axis=2))
        partials = jnp.where(alive_slots[:, None, None], partials, jnp.float32(0.0))
        return jax.ops.segment_sum(partials.reshape(ELEMS * NPE, PROBES), cell_target, num_segments=NBAS + 1)[:NBAS]
    parity = jnp.arange(PROBES, dtype=jnp.int32) % 2
    same_colour = (cluster_ids % 2)[:, None] == parity[None, :]
    probe_start = jnp.where(same_colour, (2 * sign_bits - 1).astype(jnp.float32), jnp.float32(0.0))
    samples = jnp.where(same_colour, jnp.float32(0.0), hessian(probe_start))
    current = samples
    for power_step in range(POWER):
        rms_scale = jnp.sqrt(lax.optimization_barrier(jnp.sum(current * current, axis=0)) / NBAS + 1e-06)
        applied = hessian(current / rms_scale)
        if power_step % 2 == 0:
            current = jnp.where(same_colour, applied, jnp.float32(0.0))
        else:
            current = jnp.where(same_colour, jnp.float32(0.0), applied)
    refined = current
    onehot = (cluster_ids[:, None] == jnp.arange(NCL, dtype=jnp.int32)[None, :]).astype(jnp.float32)
    outer = refined[:, :, None] * refined[:, None, :]
    gram = jnp.dot(onehot.T, outer.reshape(NBAS, PROBES * PROBES), precision=lax.Precision.HIGHEST).reshape(NCL, PROBES, PROBES)
    return (samples, refined, gram)
```

```python
import functools

import jax
import jax.numpy as jnp
from jax import lax
from jax.experimental import pallas as pl
from jax.experimental.pallas import tpu as pltpu
from jax.sharding import PartitionSpec as P

HALO = 512
POWER = 2
RIM = 64
LANES = 128
VMEM_BYTES = 48 * 1024 * 1024

F32 = jnp.float32
BF16 = jnp.bfloat16


def dot(a, b):
    return lax.dot_general(a, b, (((1,), (0,)), ((), ())), preferred_element_type=F32)


def dot_nt(a, b):
    return lax.dot_general(a, b, (((1,), (1,)), ((), ())), preferred_element_type=F32)


def split(x):
    hi = x.astype(BF16)
    return hi, (x - hi.astype(F32)).astype(BF16)


def from_behind(block, axis, distance):
    devices = range(lax.axis_size(axis))
    route = [(i - distance, i) for i in devices if i - distance in devices]
    return lax.ppermute(block, axis, route)


def rows_iota(shape):
    return lax.broadcasted_iota(jnp.int32, shape, 0)


def lanes_iota(shape):
    return lax.broadcasted_iota(jnp.int32, shape, 1)


def one_hot_columns(ids, depth):
    rows = rows_iota((depth, LANES))
    parts = [
        jnp.where(rows == ids[m : m + 1, :], F32(1), F32(0)).astype(BF16)
        for m in range(ids.shape[0])
    ]
    return jnp.concatenate(parts, axis=1)


def spread_matrix(node_slots, padded_order):
    shape = (2 * node_slots, 2 * padded_order)
    row = rows_iota(shape)
    start = (row // node_slots) * padded_order + 3 * (row % node_slots)
    gap = lanes_iota(shape) - start
    return jnp.where((gap >= 0) & (gap < 3), F32(1), F32(0)).astype(BF16)


def order_matrix(node_slots, padded_order):
    pair = 2 * node_slots
    shape = (2 * padded_order, 3 * pair)
    col = lanes_iota(shape)
    inner = col % pair
    source = (inner // node_slots) * padded_order + 3 * (inner % node_slots) + col // pair
    return jnp.where(rows_iota(shape) == source, F32(1), F32(0)).astype(BF16)


def same_colour(meta):
    ids = meta[8:, :]
    return (ids % 2) == (rows_iota(ids.shape) % 2)


def start_probes(meta):
    signs = (2 * meta[:8, :] - 1).astype(F32)
    return jnp.where(same_colour(meta), signs, F32(0))


def total_field(before, own, after):
    lane = lanes_iota((own.shape[0], LANES))
    first = own[:, :LANES] + jnp.where(lane < RIM, before[:, 2 * LANES :], F32(0))
    second = own[:, LANES : 2 * LANES] + jnp.where(lane >= RIM, after[:, 2 * LANES :], F32(0))
    return jnp.concatenate([first, second], axis=1)


def field_of(g_ref, t, tiles):
    zero = jnp.zeros(g_ref.shape[1:], F32)
    if isinstance(t, int):
        before = g_ref[t - 1] if t > 0 else zero
        after = g_ref[t + 1] if t < tiles - 1 else zero
    else:
        before = jnp.where(t > 0, g_ref[jnp.maximum(t - 1, 0)], zero)
        after = jnp.where(t < tiles - 1, g_ref[jnp.minimum(t + 1, tiles - 1)], zero)
    return total_field(before, g_ref[t], after)


def masked(field, meta, keep_same):
    same = same_colour(meta)
    return jnp.where(same if keep_same else ~same, field, F32(0))


def forward_kernel(first, keep_same, want_field, tiles, *refs):
    scalars, meta_ref, *refs = refs
    if not first:
        g_ref, *refs = refs
    conn_ref, cell_ref, fr_ref, blocks_hbm, *refs = refs
    nodes_ref, lead_ref, spill_ref, *refs = refs
    if want_field:
        field_ref, *refs = refs
    blocks, f_ref, v_ref, onehot_ref, sem = refs

    slots = blocks.shape[0]
    order = blocks.shape[1]
    node_slots = order // 3
    padded_order = f_ref.shape[1] // 2
    pairs = slots // 2

    load = pltpu.make_async_copy(blocks_hbm, blocks, sem)
    load.start()

    tile = scalars[0]
    count = scalars[1]

    if first:
        current = lambda t: start_probes(meta_ref[t])
        scale = F32(1)
    else:
        current = lambda t: masked(field_of(g_ref, t, tiles), meta_ref[t], keep_same)

        def add_squares(t, acc):
            part = current(t)
            part = part * part
            return acc + part[:, :LANES] + part[:, LANES:]

        squares = lax.fori_loop(0, tiles, add_squares, jnp.zeros((8, LANES), F32), unroll=tiles <= 8)
        squares = jnp.sum(squares, axis=1, keepdims=True)
        scale = jnp.sqrt(squares / (tiles * 2 * LANES) + F32(1e-06))

    own = current(tile)
    if want_field:
        field_ref[...] = own.T
    below = jnp.where(tile > 0, current(jnp.maximum(tile - 1, 0)), F32(0))
    above = jnp.where(tile < tiles - 1, current(jnp.minimum(tile + 1, tiles - 1)), F32(0))
    lane = lanes_iota((8, LANES))
    rims = jnp.where(lane < RIM, above[:, :LANES], below[:, LANES:])
    window = jnp.concatenate([own[:, :LANES], own[:, LANES:], rims], axis=0)
    if not first:
        window = window / jnp.concatenate([scale, scale, scale], axis=0)

    cells = cell_ref[...]
    hi, lo = split(window)
    picked = dot(jnp.concatenate([hi, lo], axis=0), one_hot_columns(cells % LANES, LANES))
    tops = []
    rests = []
    for m in range(pairs):
        part = picked[:, m * LANES : (m + 1) * LANES]
        which = cells[m : m + 1, :] // LANES
        for base, out in ((0, tops), (24, rests)):
            chosen = jnp.where(which == 0, part[base : base + 8], F32(0))
            for level in (1, 2):
                at = base + 8 * level
                chosen = jnp.where(which == level, part[at : at + 8], chosen)
            out.append(chosen)
    stacked = jnp.concatenate(tops + rests, axis=0).astype(BF16)
    spread = dot(stacked, spread_matrix(node_slots, padded_order))
    half = 8 * pairs
    spread = spread[:half] + spread[half:]

    conn = conn_ref[...]
    onehot_ref[...] = one_hot_columns(conn % HALO, HALO)
    f_ref[...] = jnp.zeros_like(f_ref)

    load.wait()
    for m in range(pairs):
        inputs = spread[8 * m : 8 * m + 8, :] * fr_ref[m : m + 1, :]
        for side in range(2):
            at = side * padded_order
            slot = 2 * m + side
            out = dot_nt(inputs[:, at : at + order].astype(BF16), blocks[slot])
            f_ref[8 * m : 8 * m + 8, at : at + order] = jnp.where(slot < count, out, F32(0))

    ordered = dot(f_ref[...].astype(BF16), order_matrix(node_slots, padded_order))
    levels = nodes_ref.shape[0] // 24
    for m in range(pairs):
        which = conn[m : m + 1, :] // HALO
        values = [
            ordered[8 * m : 8 * m + 8, c * LANES : (c + 1) * LANES] for c in range(3)
        ]
        rows = [
            jnp.where(which == level, values[c], F32(0)) for level in range(levels) for c in range(3)
        ]
        v_ref[:, m * LANES : (m + 1) * LANES] = jnp.concatenate(rows, axis=0).astype(BF16)
    nodes = dot_nt(v_ref[...], onehot_ref[...])
    nodes_ref[...] = nodes
    lead_ref[...] = nodes[:24]
    spill_ref[...] = nodes[24 * (levels - 1) :]


def adjoint_kernel(
    scalars,
    nodes_ref,
    lead_ref,
    rim_ref,
    weight_ref,
    conn_ref,
    cell_ref,
    fr_ref,
    blocks_hbm,
    out_ref,
    blocks,
    p_ref,
    a_ref,
    v_ref,
    sem,
):
    slots = blocks.shape[0]
    order = blocks.shape[1]
    node_slots = order // 3
    padded_order = p_ref.shape[1] // 2
    pairs = slots // 2
    levels = nodes_ref.shape[0] // 24
    load = pltpu.make_async_copy(blocks_hbm, blocks, sem)
    load.start()
    count = scalars[1]

    rows = []
    for level in range(levels):
        for c in range(3):
            at = 24 * level + 8 * c
            value = nodes_ref[at : at + 8, :]
            if level == 0:
                value = value + lead_ref[8 * c : 8 * c + 8, :]
            if level == levels - 1:
                value = value + rim_ref[8 * c : 8 * c + 8, :]
            rows.append(value * weight_ref[3 * level + c : 3 * level + c + 1, :])
    weighted = jnp.concatenate(rows, axis=0).astype(BF16)

    conn = conn_ref[...]
    step = 2
    for start in range(0, pairs, step):
        here = conn[start : start + step, :]
        found = dot(weighted, one_hot_columns(here % HALO, HALO))
        for i in range(step):
            m = start + i
            which = here[i : i + 1, :] // HALO
            part = found[:, i * LANES : (i + 1) * LANES]
            chosen = jnp.where(which == 0, part[:24], F32(0))
            for level in range(1, levels):
                chosen = jnp.where(which == level, part[24 * level : 24 * level + 24], chosen)
            for c in range(3):
                a_ref[8 * m : 8 * m + 8, c * LANES : (c + 1) * LANES] = chosen[8 * c : 8 * c + 8]
    natural = dot_nt(a_ref[...].astype(BF16), order_matrix(node_slots, padded_order))
    p_ref[...] = jnp.zeros_like(p_ref)

    load.wait()
    for m in range(pairs):
        for side in range(2):
            at = side * padded_order
            slot = 2 * m + side
            out = dot(natural[8 * m : 8 * m + 8, at : at + order].astype(BF16), blocks[slot])
            out = out * fr_ref[m : m + 1, at : at + order]
            p_ref[8 * m : 8 * m + 8, at : at + order] = jnp.where(slot < count, out, F32(0))

    hi, lo = split(p_ref[...])
    partial = dot_nt(jnp.concatenate([hi, lo], axis=0), spread_matrix(node_slots, padded_order))
    half = 8 * pairs
    partial = partial[:half] + partial[half:]
    cells = cell_ref[...]
    for m in range(pairs):
        which = cells[m : m + 1, :] // LANES
        value = partial[8 * m : 8 * m + 8, :]
        rows = jnp.concatenate([jnp.where(which == level, value, F32(0)) for level in range(3)], axis=0)
        hi = rows.astype(BF16).astype(F32)
        both = jnp.concatenate([hi, rows - hi], axis=0)
        v_ref[:, m * LANES : (m + 1) * LANES] = both.astype(BF16)
    basal = dot_nt(v_ref[...], one_hot_columns(cells % LANES, LANES))
    basal = basal[:24] + basal[24:]
    for level in range(3):
        out_ref[:, level * LANES : (level + 1) * LANES] = basal[8 * level : 8 * level + 8]


def gram_kernel(keep_same, tiles, groups, scalars, meta_ref, g_ref, field_ref, gram_ref):
    tile = scalars[0]
    group = scalars[2]
    clusters = gram_ref.shape[0]

    def field(t, p):
        zero = jnp.zeros(g_ref.shape[2:], F32)
        if isinstance(t, int):
            before = g_ref[t - 1, p] if t > 0 else zero
            after = g_ref[t + 1, p] if t < tiles - 1 else zero
        else:
            before = jnp.where(t > 0, g_ref[jnp.maximum(t - 1, 0), p], zero)
            after = jnp.where(t < tiles - 1, g_ref[jnp.minimum(t + 1, tiles - 1), p], zero)
        return masked(total_field(before, g_ref[t, p], after), meta_ref[t], keep_same)

    field_ref[...] = field(tile, group).T

    def add_tile(t, acc):
        ids = meta_ref[t][8:, :]
        mine = field(t, group)
        every = jnp.concatenate([field(t, p) for p in range(groups)], axis=0)
        left = jnp.concatenate(
            [jnp.where(ids == k, mine, F32(0)) for k in range(clusters)], axis=0
        )
        return acc + lax.dot_general(
            left,
            every,
            (((1,), (1,)), ((), ())),
            precision=lax.Precision.HIGHEST,
            preferred_element_type=F32,
        )

    acc = jnp.zeros((8 * clusters, 8 * groups), F32)
    acc = lax.fori_loop(0, tiles, add_tile, acc, unroll=tiles <= 8)
    gram_ref[...] = acc.reshape(gram_ref.shape)


def shards(
    blocks, connectivity, basal_map, friction, elem_counts, obs_weight, sign_bits, cluster_ids
):
    slots, order, _ = blocks.shape
    node_slots = connectivity.shape[1]
    node_count = obs_weight.shape[0]
    cell_count, group_size = sign_bits.shape
    tiles = lax.axis_size("tiles")
    groups = lax.axis_size("probes")
    pairs = slots * node_slots // LANES
    levels = node_count // HALO + 1
    padded_order = 2 * LANES
    window = cell_count + 2 * RIM

    meta = jnp.concatenate(
        [sign_bits.T, jnp.broadcast_to(cluster_ids[None, :], (8, cell_count))], axis=0
    )
    meta = lax.all_gather(meta, "tiles", axis=0)
    weight = obs_weight.reshape(node_count // HALO, HALO, 3).transpose(0, 2, 1)
    weight_next = from_behind(weight[0], "tiles", -1)
    weight = jnp.concatenate([weight.reshape(-1, HALO), weight_next], axis=0)
    conn = connectivity.reshape(pairs, LANES)
    cells = ((basal_map + (window - RIM)) % window).reshape(pairs, LANES)
    fr = jnp.pad(friction.reshape(slots, order), ((0, 0), (0, padded_order - order)))
    fr = fr.reshape(pairs, 2 * padded_order)
    scalars = jnp.stack(
        [lax.axis_index("tiles"), elem_counts[0], lax.axis_index("probes")]
    ).astype(jnp.int32)

    smem = pl.BlockSpec(memory_space=pltpu.SMEM)
    vmem = pl.BlockSpec(memory_space=pltpu.VMEM)
    anywhere = pl.BlockSpec(memory_space=pl.ANY)
    params = pltpu.CompilerParams(vmem_limit_bytes=VMEM_BYTES)

    def forward(gathered, keep_same, want_field):
        first = gathered is None
        out_shape = [
            jax.ShapeDtypeStruct((24 * levels, HALO), F32),
            jax.ShapeDtypeStruct((24, HALO), F32),
            jax.ShapeDtypeStruct((24, HALO), F32),
        ]
        if want_field:
            out_shape.append(jax.ShapeDtypeStruct((cell_count, group_size), F32))
        operands = [scalars, meta] + ([] if first else [gathered]) + [conn, cells, fr, blocks]
        return pl.pallas_call(
            functools.partial(forward_kernel, first, keep_same, want_field, tiles),
            out_shape=out_shape,
            in_specs=[smem] + [vmem] * (len(operands) - 2) + [anywhere],
            out_specs=[vmem] * len(out_shape),
            scratch_shapes=[
                pltpu.VMEM(blocks.shape, BF16),
                pltpu.VMEM((8 * pairs, 2 * padded_order), F32),
                pltpu.VMEM((24 * levels, pairs * LANES), BF16),
                pltpu.VMEM((HALO, pairs * LANES), BF16),
                pltpu.SemaphoreType.DMA,
            ],
            compiler_params=params,
            name="forward",
        )(*operands)

    def adjoint(nodes, lead, rim):
        return pl.pallas_call(
            adjoint_kernel,
            out_shape=jax.ShapeDtypeStruct((group_size, window), F32),
            in_specs=[smem] + [vmem] * 7 + [anywhere],
            out_specs=vmem,
            scratch_shapes=[
                pltpu.VMEM(blocks.shape, BF16),
                pltpu.VMEM((8 * pairs, 2 * padded_order), F32),
                pltpu.VMEM((8 * pairs, 3 * LANES), F32),
                pltpu.VMEM((48, pairs * LANES), BF16),
                pltpu.SemaphoreType.DMA,
            ],
            compiler_params=params,
            name="adjoint",
        )(scalars, nodes, lead, rim, weight, conn, cells, fr, blocks)

    gathered = None
    samples = None
    for step in range(POWER + 1):
        nodes, lead, spill, *field = forward(gathered, step % 2 == 0, step == 1)
        if field:
            samples = field[0]
        from_earlier = from_behind(spill, "tiles", 1)
        from_later = from_behind(lead, "tiles", -1)
        basal = adjoint(nodes, from_earlier, from_later)
        axes = "tiles" if step < POWER else ("tiles", "probes")
        gathered = lax.all_gather(basal, axes, axis=0)

    gathered = gathered.reshape(tiles, groups, group_size, window)
    refined, gram = pl.pallas_call(
        functools.partial(gram_kernel, POWER % 2 == 1, tiles, groups),
        out_shape=[
            jax.ShapeDtypeStruct((cell_count, group_size), F32),
            jax.ShapeDtypeStruct((tiles, group_size, groups * group_size), F32),
        ],
        in_specs=[smem, vmem, vmem],
        out_specs=[vmem, vmem],
        compiler_params=params,
        name="gram",
    )(scalars, meta, gathered)
    return (samples, refined, gram)


def solution(mesh):
    in_specs = (
        P("tiles", None, None),
        P("tiles", None),
        P("tiles", None),
        P("tiles", None, None),
        P("tiles"),
        P("tiles", None),
        P("tiles", "probes"),
        P("tiles"),
    )
    out_specs = (P("tiles", "probes"), P("tiles", "probes"), P(None, "probes", None))
    return jax.shard_map(shards, mesh=mesh, in_specs=in_specs, out_specs=out_specs, check_vma=False)
```

```python
import functools

import jax
import jax.numpy as jnp
from jax import lax
from jax.experimental import pallas as pl
from jax.experimental.pallas import tpu as pltpu
from jax.sharding import PartitionSpec as P

HALO = 512
POWER = 2
RIM = 64
LANES = 128
VMEM_BYTES = 48 * 1024 * 1024

F32 = jnp.float32
BF16 = jnp.bfloat16


def dot(a, b):
    return lax.dot_general(a, b, (((1,), (0,)), ((), ())), preferred_element_type=F32)


def dot_nt(a, b):
    return lax.dot_general(a, b, (((1,), (1,)), ((), ())), preferred_element_type=F32)


def split(x):
    hi = x.astype(BF16)
    return hi, (x - hi.astype(F32)).astype(BF16)


def from_behind(block, axis, distance):
    devices = range(lax.axis_size(axis))
    route = [(i - distance, i) for i in devices if i - distance in devices]
    return lax.ppermute(block, axis, route)


def rows_iota(shape):
    return lax.broadcasted_iota(jnp.int32, shape, 0)


def lanes_iota(shape):
    return lax.broadcasted_iota(jnp.int32, shape, 1)


def one_hot_columns(ids, depth):
    rows = rows_iota((depth, LANES))
    parts = [
        jnp.where(rows == ids[m : m + 1, :], F32(1), F32(0)).astype(BF16)
        for m in range(ids.shape[0])
    ]
    return jnp.concatenate(parts, axis=1)


def spread_matrix(node_slots, padded_order):
    shape = (2 * node_slots, 2 * padded_order)
    row = rows_iota(shape)
    start = (row // node_slots) * padded_order + 3 * (row % node_slots)
    gap = lanes_iota(shape) - start
    return jnp.where((gap >= 0) & (gap < 3), F32(1), F32(0)).astype(BF16)


def order_matrix(node_slots, padded_order):
    pair = 2 * node_slots
    shape = (2 * padded_order, 3 * pair)
    col = lanes_iota(shape)
    inner = col % pair
    source = (inner // node_slots) * padded_order + 3 * (inner % node_slots) + col // pair
    return jnp.where(rows_iota(shape) == source, F32(1), F32(0)).astype(BF16)


def same_colour(meta):
    ids = meta[8:, :]
    return (ids % 2) == (rows_iota(ids.shape) % 2)


def start_probes(meta):
    signs = (2 * meta[:8, :] - 1).astype(F32)
    return jnp.where(same_colour(meta), signs, F32(0))


def total_field(before, own, after):
    lane = lanes_iota((own.shape[0], LANES))
    first = own[:, :LANES] + jnp.where(lane < RIM, before[:, 2 * LANES :], F32(0))
    second = own[:, LANES : 2 * LANES] + jnp.where(lane >= RIM, after[:, 2 * LANES :], F32(0))
    return jnp.concatenate([first, second], axis=1)


def field_of(g_ref, t, tiles):
    zero = jnp.zeros(g_ref.shape[1:], F32)
    if isinstance(t, int):
        before = g_ref[t - 1] if t > 0 else zero
        after = g_ref[t + 1] if t < tiles - 1 else zero
    else:
        before = jnp.where(t > 0, g_ref[jnp.maximum(t - 1, 0)], zero)
        after = jnp.where(t < tiles - 1, g_ref[jnp.minimum(t + 1, tiles - 1)], zero)
    return total_field(before, g_ref[t], after)


def masked(field, meta, keep_same):
    same = same_colour(meta)
    return jnp.where(same if keep_same else ~same, field, F32(0))


def forward_kernel(first, keep_same, want_field, tiles, *refs):
    scalars, meta_ref, *refs = refs
    if not first:
        g_ref, *refs = refs
    conn_ref, cell_ref, fr_ref, blocks_hbm, *refs = refs
    nodes_ref, lead_ref, spill_ref, *refs = refs
    if want_field:
        field_ref, *refs = refs
    blocks, f_ref, v_ref, onehot_ref, sem = refs

    slots = blocks.shape[0]
    order = blocks.shape[1]
    node_slots = order // 3
    padded_order = f_ref.shape[1] // 2
    pairs = slots // 2

    load = pltpu.make_async_copy(blocks_hbm, blocks, sem)
    load.start()

    tile = scalars[0]
    count = scalars[1]

    if first:
        current = lambda t: start_probes(meta_ref[t])
        scale = F32(1)
    else:
        current = lambda t: masked(field_of(g_ref, t, tiles), meta_ref[t], keep_same)

        def add_squares(t, acc):
            part = current(t)
            part = part * part
            return acc + part[:, :LANES] + part[:, LANES:]

        squares = lax.fori_loop(0, tiles, add_squares, jnp.zeros((8, LANES), F32), unroll=tiles <= 8)
        squares = jnp.sum(squares, axis=1, keepdims=True)
        scale = jnp.sqrt(squares / (tiles * 2 * LANES) + F32(1e-06))

    own = current(tile)
    if want_field:
        field_ref[...] = own.T
    below = jnp.where(tile > 0, current(jnp.maximum(tile - 1, 0)), F32(0))
    above = jnp.where(tile < tiles - 1, current(jnp.minimum(tile + 1, tiles - 1)), F32(0))
    lane = lanes_iota((8, LANES))
    rims = jnp.where(lane < RIM, above[:, :LANES], below[:, LANES:])
    window = jnp.concatenate([own[:, :LANES], own[:, LANES:], rims], axis=0)
    if not first:
        window = window / jnp.concatenate([scale, scale, scale], axis=0)

    cells = cell_ref[...]
    hi, lo = split(window)
    picked = dot(jnp.concatenate([hi, lo], axis=0), one_hot_columns(cells % LANES, LANES))
    tops = []
    rests = []
    for m in range(pairs):
        part = picked[:, m * LANES : (m + 1) * LANES]
        which = cells[m : m + 1, :] // LANES
        for base, out in ((0, tops), (24, rests)):
            chosen = jnp.where(which == 0, part[base : base + 8], F32(0))
            for level in (1, 2):
                at = base + 8 * level
                chosen = jnp.where(which == level, part[at : at + 8], chosen)
            out.append(chosen)
    stacked = jnp.concatenate(tops + rests, axis=0).astype(BF16)
    spread = dot(stacked, spread_matrix(node_slots, padded_order))
    half = 8 * pairs
    spread = spread[:half] + spread[half:]

    conn = conn_ref[...]
    onehot_ref[...] = one_hot_columns(conn % HALO, HALO)
    f_ref[...] = jnp.zeros_like(f_ref)

    load.wait()
    for m in range(pairs):
        inputs = spread[8 * m : 8 * m + 8, :] * fr_ref[m : m + 1, :]
        for side in range(2):
            at = side * padded_order
            slot = 2 * m + side
            out = dot_nt(inputs[:, at : at + order].astype(BF16), blocks[slot])
            f_ref[8 * m : 8 * m + 8, at : at + order] = jnp.where(slot < count, out, F32(0))

    ordered = dot(f_ref[...].astype(BF16), order_matrix(node_slots, padded_order))
    levels = nodes_ref.shape[0] // 24
    for m in range(pairs):
        which = conn[m : m + 1, :] // HALO
        values = [
            ordered[8 * m : 8 * m + 8, c * LANES : (c + 1) * LANES] for c in range(3)
        ]
        rows = [
            jnp.where(which == level, values[c], F32(0)) for level in range(levels) for c in range(3)
        ]
        v_ref[:, m * LANES : (m + 1) * LANES] = jnp.concatenate(rows, axis=0).astype(BF16)
    nodes = dot_nt(v_ref[...], onehot_ref[...])
    nodes_ref[...] = nodes
    lead_ref[...] = nodes[:24]
    spill_ref[...] = nodes[24 * (levels - 1) :]


def adjoint_kernel(
    scalars,
    nodes_ref,
    lead_ref,
    rim_ref,
    weight_ref,
    conn_ref,
    cell_ref,
    fr_ref,
    blocks_hbm,
    out_ref,
    blocks,
    p_ref,
    a_ref,
    v_ref,
    sem,
):
    slots = blocks.shape[0]
    order = blocks.shape[1]
    node_slots = order // 3
    padded_order = p_ref.shape[1] // 2
    pairs = slots // 2
    levels = nodes_ref.shape[0] // 24
    load = pltpu.make_async_copy(blocks_hbm, blocks, sem)
    load.start()
    count = scalars[1]

    rows = []
    for level in range(levels):
        for c in range(3):
            at = 24 * level + 8 * c
            value = nodes_ref[at : at + 8, :]
            if level == 0:
                value = value + lead_ref[8 * c : 8 * c + 8, :]
            if level == levels - 1:
                value = value + rim_ref[8 * c : 8 * c + 8, :]
            rows.append(value * weight_ref[3 * level + c : 3 * level + c + 1, :])
    weighted = jnp.concatenate(rows, axis=0).astype(BF16)

    conn = conn_ref[...]
    step = 2
    for start in range(0, pairs, step):
        here = conn[start : start + step, :]
        found = dot(weighted, one_hot_columns(here % HALO, HALO))
        for i in range(step):
            m = start + i
            which = here[i : i + 1, :] // HALO
            part = found[:, i * LANES : (i + 1) * LANES]
            chosen = jnp.where(which == 0, part[:24], F32(0))
            for level in range(1, levels):
                chosen = jnp.where(which == level, part[24 * level : 24 * level + 24], chosen)
            for c in range(3):
                a_ref[8 * m : 8 * m + 8, c * LANES : (c + 1) * LANES] = chosen[8 * c : 8 * c + 8]
    natural = dot_nt(a_ref[...].astype(BF16), order_matrix(node_slots, padded_order))
    p_ref[...] = jnp.zeros_like(p_ref)

    load.wait()
    for m in range(pairs):
        for side in range(2):
            at = side * padded_order
            slot = 2 * m + side
            out = dot(natural[8 * m : 8 * m + 8, at : at + order].astype(BF16), blocks[slot])
            out = out * fr_ref[m : m + 1, at : at + order]
            p_ref[8 * m : 8 * m + 8, at : at + order] = jnp.where(slot < count, out, F32(0))

    hi, lo = split(p_ref[...])
    partial = dot_nt(jnp.concatenate([hi, lo], axis=0), spread_matrix(node_slots, padded_order))
    half = 8 * pairs
    partial = partial[:half] + partial[half:]
    cells = cell_ref[...]
    for m in range(pairs):
        which = cells[m : m + 1, :] // LANES
        value = partial[8 * m : 8 * m + 8, :]
        rows = jnp.concatenate([jnp.where(which == level, value, F32(0)) for level in range(3)], axis=0)
        hi = rows.astype(BF16).astype(F32)
        both = jnp.concatenate([hi, rows - hi], axis=0)
        v_ref[:, m * LANES : (m + 1) * LANES] = both.astype(BF16)
    basal = dot_nt(v_ref[...], one_hot_columns(cells % LANES, LANES))
    basal = basal[:24] + basal[24:]
    basal = jnp.concatenate([basal[:8], basal[8:16], basal[16:]], axis=1)
    for t in range(out_ref.shape[0]):
        out_ref[t] = basal


def gram_kernel(keep_same, tiles, groups, scalars, meta_ref, g_ref, field_ref, gram_ref):
    tile = scalars[0]
    group = scalars[2]
    clusters = gram_ref.shape[0]

    def field(t, p):
        zero = jnp.zeros(g_ref.shape[2:], F32)
        if isinstance(t, int):
            before = g_ref[t - 1, p] if t > 0 else zero
            after = g_ref[t + 1, p] if t < tiles - 1 else zero
        else:
            before = jnp.where(t > 0, g_ref[jnp.maximum(t - 1, 0), p], zero)
            after = jnp.where(t < tiles - 1, g_ref[jnp.minimum(t + 1, tiles - 1), p], zero)
        return masked(total_field(before, g_ref[t, p], after), meta_ref[t], keep_same)

    field_ref[...] = field(tile, group).T

    def add_tile(t, acc):
        ids = meta_ref[t][8:, :]
        mine = field(t, group)
        every = jnp.concatenate([field(t, p) for p in range(groups)], axis=0)
        left = jnp.concatenate(
            [jnp.where(ids == k, mine, F32(0)) for k in range(clusters)], axis=0
        )
        return acc + lax.dot_general(
            left,
            every,
            (((1,), (1,)), ((), ())),
            precision=lax.Precision.HIGHEST,
            preferred_element_type=F32,
        )

    acc = jnp.zeros((8 * clusters, 8 * groups), F32)
    acc = lax.fori_loop(0, tiles, add_tile, acc, unroll=tiles <= 8)
    gram_ref[...] = acc.reshape(gram_ref.shape)


def shards(
    blocks, connectivity, basal_map, friction, elem_counts, obs_weight, sign_bits, cluster_ids
):
    slots, order, _ = blocks.shape
    node_slots = connectivity.shape[1]
    node_count = obs_weight.shape[0]
    cell_count, group_size = sign_bits.shape
    tiles = lax.axis_size("tiles")
    groups = lax.axis_size("probes")
    pairs = slots * node_slots // LANES
    levels = node_count // HALO + 1
    padded_order = 2 * LANES
    window = cell_count + 2 * RIM

    meta = jnp.concatenate(
        [sign_bits.T, jnp.broadcast_to(cluster_ids[None, :], (8, cell_count))], axis=0
    )
    meta = lax.all_to_all(jnp.broadcast_to(meta, (tiles, *meta.shape)), "tiles", 0, 0)
    weight = obs_weight.reshape(node_count // HALO, HALO, 3).transpose(0, 2, 1)
    weight_next = from_behind(weight[0], "tiles", -1)
    weight = jnp.concatenate([weight.reshape(-1, HALO), weight_next], axis=0)
    conn = connectivity.reshape(pairs, LANES)
    cells = ((basal_map + (window - RIM)) % window).reshape(pairs, LANES)
    fr = jnp.pad(friction.reshape(slots, order), ((0, 0), (0, padded_order - order)))
    fr = fr.reshape(pairs, 2 * padded_order)
    scalars = jnp.stack(
        [lax.axis_index("tiles"), elem_counts[0], lax.axis_index("probes")]
    ).astype(jnp.int32)

    smem = pl.BlockSpec(memory_space=pltpu.SMEM)
    vmem = pl.BlockSpec(memory_space=pltpu.VMEM)
    anywhere = pl.BlockSpec(memory_space=pl.ANY)
    params = pltpu.CompilerParams(vmem_limit_bytes=VMEM_BYTES)

    def forward(gathered, keep_same, want_field):
        first = gathered is None
        out_shape = [
            jax.ShapeDtypeStruct((24 * levels, HALO), F32),
            jax.ShapeDtypeStruct((24, HALO), F32),
            jax.ShapeDtypeStruct((24, HALO), F32),
        ]
        if want_field:
            out_shape.append(jax.ShapeDtypeStruct((cell_count, group_size), F32))
        operands = [scalars, meta] + ([] if first else [gathered]) + [conn, cells, fr, blocks]
        return pl.pallas_call(
            functools.partial(forward_kernel, first, keep_same, want_field, tiles),
            out_shape=out_shape,
            in_specs=[smem] + [vmem] * (len(operands) - 2) + [anywhere],
            out_specs=[vmem] * len(out_shape),
            scratch_shapes=[
                pltpu.VMEM(blocks.shape, BF16),
                pltpu.VMEM((8 * pairs, 2 * padded_order), F32),
                pltpu.VMEM((24 * levels, pairs * LANES), BF16),
                pltpu.VMEM((HALO, pairs * LANES), BF16),
                pltpu.SemaphoreType.DMA,
            ],
            compiler_params=params,
            name="forward",
        )(*operands)

    def adjoint(nodes, lead, rim, copies):
        return pl.pallas_call(
            adjoint_kernel,
            out_shape=jax.ShapeDtypeStruct((copies, group_size, window), F32),
            in_specs=[smem] + [vmem] * 7 + [anywhere],
            out_specs=vmem,
            scratch_shapes=[
                pltpu.VMEM(blocks.shape, BF16),
                pltpu.VMEM((8 * pairs, 2 * padded_order), F32),
                pltpu.VMEM((8 * pairs, 3 * LANES), F32),
                pltpu.VMEM((48, pairs * LANES), BF16),
                pltpu.SemaphoreType.DMA,
            ],
            compiler_params=params,
            name="adjoint",
        )(scalars, nodes, lead, rim, weight, conn, cells, fr, blocks)

    gathered = None
    samples = None
    for step in range(POWER + 1):
        nodes, lead, spill, *field = forward(gathered, step % 2 == 0, step == 1)
        if field:
            samples = field[0]
        from_earlier = from_behind(spill, "tiles", 1)
        from_later = from_behind(lead, "tiles", -1)
        axes = "tiles" if step < POWER else ("tiles", "probes")
        basal = adjoint(nodes, from_earlier, from_later, lax.axis_size(axes))
        gathered = lax.all_to_all(basal, axes, 0, 0)

    gathered = gathered.reshape(tiles, groups, group_size, window)
    refined, gram = pl.pallas_call(
        functools.partial(gram_kernel, POWER % 2 == 1, tiles, groups),
        out_shape=[
            jax.ShapeDtypeStruct((cell_count, group_size), F32),
            jax.ShapeDtypeStruct((tiles, group_size, groups * group_size), F32),
        ],
        in_specs=[smem, vmem, vmem],
        out_specs=[vmem, vmem],
        compiler_params=params,
        name="gram",
    )(scalars, meta, gathered)
    return (samples, refined, gram)


def solution(mesh):
    in_specs = (
        P("tiles", None, None),
        P("tiles", None),
        P("tiles", None),
        P("tiles", None, None),
        P("tiles"),
        P("tiles", None),
        P("tiles", "probes"),
        P("tiles"),
    )
    out_specs = (P("tiles", "probes"), P("tiles", "probes"), P(None, "probes", None))
    return jax.shard_map(shards, mesh=mesh, in_specs=in_specs, out_specs=out_specs, check_vma=False)
```

```python
import functools

import jax
import jax.numpy as jnp
from jax import lax
from jax.experimental import pallas as pl
from jax.experimental.pallas import tpu as pltpu
from jax.sharding import PartitionSpec as P

HALO = 512
POWER = 2
RIM = 64
LANES = 128
VMEM_BYTES = 30 * 1024 * 1024

F32 = jnp.float32
BF16 = jnp.bfloat16


def dot(a, b):
    return lax.dot_general(a, b, (((1,), (0,)), ((), ())), preferred_element_type=F32)


def dot_nt(a, b):
    return lax.dot_general(a, b, (((1,), (1,)), ((), ())), preferred_element_type=F32)


def split(x):
    hi = x.astype(BF16)
    return hi, (x - hi.astype(F32)).astype(BF16)


def rows_iota(shape):
    return lax.broadcasted_iota(jnp.int32, shape, 0)


def lanes_iota(shape):
    return lax.broadcasted_iota(jnp.int32, shape, 1)


def spread_matrix(node_slots, padded_order):
    shape = (2 * node_slots, 2 * padded_order)
    row = rows_iota(shape)
    start = (row // node_slots) * padded_order + 3 * (row % node_slots)
    gap = lanes_iota(shape) - start
    return jnp.where((gap >= 0) & (gap < 3), F32(1), F32(0)).astype(BF16)


def order_matrix(node_slots, padded_order):
    pair = 2 * node_slots
    shape = (2 * padded_order, 3 * pair)
    col = lanes_iota(shape)
    inner = col % pair
    source = (inner // node_slots) * padded_order + 3 * (inner % node_slots) + col // pair
    return jnp.where(rows_iota(shape) == source, F32(1), F32(0)).astype(BF16)


def same_colour(meta):
    ids = meta[8:16, :].astype(jnp.int32)
    return (ids % 2) == (rows_iota(ids.shape) % 2)


def start_probes(meta):
    signs = 2 * meta[:8, :] - 1
    return jnp.where(same_colour(meta), signs, F32(0))


def total_field(before, own, after):
    lane = lanes_iota((own.shape[0], LANES))
    first = own[:, :LANES] + jnp.where(lane < RIM, before[:, 2 * LANES :], F32(0))
    second = own[:, LANES : 2 * LANES] + jnp.where(lane >= RIM, after[:, 2 * LANES :], F32(0))
    return jnp.concatenate([first, second], axis=1)


def field_of(g_ref, t, tiles):
    zero = jnp.zeros(g_ref.shape[1:], F32)
    if isinstance(t, int):
        before = g_ref[t - 1] if t > 0 else zero
        after = g_ref[t + 1] if t < tiles - 1 else zero
    else:
        before = jnp.where(t > 0, g_ref[jnp.maximum(t - 1, 0)], zero)
        after = jnp.where(t < tiles - 1, g_ref[jnp.minimum(t + 1, tiles - 1)], zero)
    return total_field(before, g_ref[t], after)


def masked(field, meta, keep_same):
    same = same_colour(meta)
    return jnp.where(same if keep_same else ~same, field, F32(0))


def announce_kernel(signs_ref, ids_ref, weight_hbm, out_ref, lead, sem):
    load = pltpu.make_async_copy(weight_hbm.at[pl.ds(0, HALO)], lead, sem)
    load.start()
    half = HALO // 2
    out_ref[0, :8, :] = signs_ref[...].astype(F32).T
    out_ref[0, 8:16, :] = jnp.broadcast_to(ids_ref[...].astype(F32), (8, half))
    load.wait()
    turned = lead[...].T
    out_ref[0, 16:24, :] = jnp.zeros((8, half), F32)
    out_ref[0, 16:19, :] = turned[:, :half]
    out_ref[0, 19:22, :] = turned[:, half:]
    block = out_ref[0]
    for t in range(1, out_ref.shape[0]):
        out_ref[t] = block


def setup_kernel(
    node_slots,
    padded_order,
    conn_in,
    cell_in,
    conn_ref,
    cell_ref,
    node_hot_ref,
    cell_hot_ref,
    spread_ref,
    order_ref,
):
    pairs = conn_ref.shape[0]
    window = 3 * LANES

    def paired(ref):
        return jnp.concatenate(
            [ref[pl.ds(0, pairs, stride=2), :], ref[pl.ds(1, pairs, stride=2), :]], axis=1
        )

    conn = paired(conn_in)
    cells = paired(cell_in)
    cells = jnp.where(cells < RIM, cells + (window - RIM), cells - RIM)
    conn_ref[...] = conn
    cell_ref[...] = cells
    rows = rows_iota((HALO, LANES))
    for m in range(pairs):
        at = pl.ds(m * LANES, LANES)
        hot = rows == conn[m : m + 1, :] % HALO
        node_hot_ref[:, at] = jnp.where(hot, F32(1), F32(0)).astype(BF16)
        hot = rows[:LANES] == cells[m : m + 1, :] % LANES
        cell_hot_ref[:, at] = jnp.where(hot, F32(1), F32(0)).astype(BF16)
    spread_ref[...] = spread_matrix(node_slots, padded_order)
    order_ref[...] = order_matrix(node_slots, padded_order)


def forward_kernel(first, keep_same, want_field, tiles, levels, *refs):
    scalars, meta_ref, *refs = refs
    if not first:
        g_ref, *refs = refs
    conn_ref, cell_ref, fr_ref, blocks, node_hot, cell_hot, spread_ref, order_ref, *refs = refs
    ordered_ref, a_ref, b_ref, *refs = refs
    if want_field:
        field_ref, *refs = refs
    f_ref, v_ref = refs

    order = blocks.shape[1]
    padded_order = f_ref.shape[1] // 2
    pairs = blocks.shape[0] // 2
    tile = scalars[0]
    count = scalars[1]

    if first:
        current = lambda t: start_probes(meta_ref[t])
    else:
        current = lambda t: masked(field_of(g_ref, t, tiles), meta_ref[t], keep_same)

    own = current(tile)
    if want_field:
        field_ref[...] = own.T
    below = jnp.where(tile > 0, current(jnp.maximum(tile - 1, 0)), F32(0))
    above = jnp.where(tile < tiles - 1, current(jnp.minimum(tile + 1, tiles - 1)), F32(0))
    lane = lanes_iota((8, LANES))
    rims = jnp.where(lane < RIM, above[:, :LANES], below[:, LANES:])
    window = jnp.concatenate([own[:, :LANES], own[:, LANES:], rims], axis=0)
    if not first:

        def add_squares(t, acc):
            part = current(t)
            part = part * part
            return acc + part[:, :LANES] + part[:, LANES:]

        squares = lax.fori_loop(0, tiles, add_squares, jnp.zeros((8, LANES), F32), unroll=tiles <= 8)
        squares = jnp.sum(squares, axis=1, keepdims=True)
        scale = jnp.sqrt(squares / (tiles * 2 * LANES) + F32(1e-06))
        window = window / jnp.concatenate([scale, scale, scale], axis=0)

    cells = cell_ref[...]
    hi, lo = split(window)
    picked = dot(jnp.concatenate([hi, lo], axis=0), cell_hot[...])
    tops = []
    rests = []
    for m in range(pairs):
        part = picked[:, m * LANES : (m + 1) * LANES]
        which = cells[m : m + 1, :] // LANES
        for base, out in ((0, tops), (24, rests)):
            chosen = jnp.where(which == 0, part[base : base + 8], F32(0))
            for level in (1, 2):
                at = base + 8 * level
                chosen = jnp.where(which == level, part[at : at + 8], chosen)
            out.append(chosen)
    stacked = jnp.concatenate(tops + rests, axis=0).astype(BF16)
    spread = dot(stacked, spread_ref[...])
    half = 8 * pairs
    spread = spread[:half] + spread[half:]

    f_ref[...] = jnp.zeros_like(f_ref)
    for m in range(pairs):
        inputs = spread[8 * m : 8 * m + 8, :] * fr_ref[m : m + 1, :]
        for side in range(2):
            at = side * padded_order
            slot = 2 * m + side
            out = dot_nt(inputs[:, at : at + order].astype(BF16), blocks[slot])
            out = jnp.where(slot < count, out, F32(0))
            hi = out.astype(BF16).astype(F32)
            f_ref[16 * m : 16 * m + 8, at : at + order] = hi
            f_ref[16 * m + 8 : 16 * m + 16, at : at + order] = out - hi

    ordered = dot(f_ref[...].astype(BF16), order_ref[...])
    ordered_ref[...] = ordered
    conn = conn_ref[...]
    for m in range(pairs):
        which = conn[m : m + 1, :] // HALO
        rows = [
            jnp.where(
                which == level,
                ordered[16 * m : 16 * m + 16, c * LANES : (c + 1) * LANES],
                F32(0),
            )
            for level in (0, levels - 1)
            for c in range(3)
        ]
        v_ref[:, m * LANES : (m + 1) * LANES] = jnp.concatenate(rows, axis=0).astype(BF16)
    rim = dot_nt(v_ref[...], node_hot[...])
    even = tile % 2 == 0
    for c in range(3):
        lead = rim[16 * c : 16 * c + 8] + rim[16 * c + 8 : 16 * c + 16]
        at = 48 + 16 * c
        spill = rim[at : at + 8] + rim[at + 8 : at + 16]
        a_ref[8 * c : 8 * c + 8, :] = jnp.where(even, spill, lead)
        b_ref[8 * c : 8 * c + 8, :] = jnp.where(even, lead, spill)


def inner_kernel(levels, ordered_ref, weight_ref, conn_ref, node_hot, picked_ref, v_ref):
    pairs = conn_ref.shape[0]
    conn = conn_ref[...]
    for m in range(pairs):
        which = conn[m : m + 1, :] // HALO
        rows = [
            jnp.where(
                which == level,
                ordered_ref[16 * m : 16 * m + 16, c * LANES : (c + 1) * LANES],
                F32(0),
            )
            for level in range(1, levels - 1)
            for c in range(3)
        ]
        v_ref[:, m * LANES : (m + 1) * LANES] = jnp.concatenate(rows, axis=0).astype(BF16)
    nodes = dot_nt(v_ref[...], node_hot[...])
    rows = []
    for i in range(3 * (levels - 2)):
        value = nodes[16 * i : 16 * i + 8] + nodes[16 * i + 8 : 16 * i + 16]
        rows.append(value * weight_ref[i + 3 : i + 4, :])
    weighted = jnp.concatenate(rows, axis=0).astype(BF16)
    step = 2
    for start in range(0, pairs, step):
        found = dot(weighted, node_hot[:, start * LANES : (start + step) * LANES])
        for i in range(step):
            m = start + i
            which = conn[m : m + 1, :] // HALO
            part = found[:, i * LANES : (i + 1) * LANES]
            chosen = jnp.zeros((24, LANES), F32)
            for level in range(1, levels - 1):
                at = 24 * (level - 1)
                chosen = jnp.where(which == level, part[at : at + 24], chosen)
            for c in range(3):
                picked_ref[8 * m : 8 * m + 8, c * LANES : (c + 1) * LANES] = chosen[8 * c : 8 * c + 8]


def adjoint_kernel(
    tiles,
    levels,
    scalars,
    meta_ref,
    own_a,
    own_b,
    new_a,
    new_b,
    inner_ref,
    weight_ref,
    conn_ref,
    cell_ref,
    fr_ref,
    blocks,
    node_hot,
    cell_hot,
    spread_ref,
    order_ref,
    out_ref,
    p_ref,
    n_ref,
    v_ref,
):
    order = blocks.shape[1]
    padded_order = p_ref.shape[1] // 2
    pairs = blocks.shape[0] // 2
    tile = scalars[0]
    count = scalars[1]

    even = tile % 2 == 0
    lead = jnp.where(even, own_b[...] + new_b[...], own_a[...] + new_a[...])
    spill = jnp.where(even, own_a[...] + new_a[...], own_b[...] + new_b[...])
    after = meta_ref[jnp.minimum(tile + 1, tiles - 1)]
    after = jnp.where(tile < tiles - 1, after, F32(0))
    rows = [lead[8 * c : 8 * c + 8] * weight_ref[c : c + 1, :] for c in range(3)]
    for c in range(3):
        weight = jnp.concatenate([after[16 + c : 17 + c, :], after[19 + c : 20 + c, :]], axis=1)
        rows.append(spill[8 * c : 8 * c + 8] * weight)
    weighted = jnp.concatenate(rows, axis=0).astype(BF16)

    conn = conn_ref[...]
    step = 2
    for start in range(0, pairs, step):
        found = dot(weighted, node_hot[:, start * LANES : (start + step) * LANES])
        for i in range(step):
            m = start + i
            which = conn[m : m + 1, :] // HALO
            part = found[:, i * LANES : (i + 1) * LANES]
            for c in range(3):
                value = inner_ref[8 * m : 8 * m + 8, c * LANES : (c + 1) * LANES]
                value = jnp.where(which == 0, part[8 * c : 8 * c + 8], value)
                value = jnp.where(which == levels - 1, part[24 + 8 * c : 32 + 8 * c], value)
                n_ref[8 * m : 8 * m + 8, c * LANES : (c + 1) * LANES] = value
    natural = dot_nt(n_ref[...].astype(BF16), order_ref[...])
    p_ref[...] = jnp.zeros_like(p_ref)
    for m in range(pairs):
        for side in range(2):
            at = side * padded_order
            slot = 2 * m + side
            out = dot(natural[8 * m : 8 * m + 8, at : at + order].astype(BF16), blocks[slot])
            out = out * fr_ref[m : m + 1, at : at + order]
            p_ref[8 * m : 8 * m + 8, at : at + order] = jnp.where(slot < count, out, F32(0))

    hi, lo = split(p_ref[...])
    partial = dot_nt(jnp.concatenate([hi, lo], axis=0), spread_ref[...])
    half = 8 * pairs
    partial = partial[:half] + partial[half:]
    cells = cell_ref[...]
    for m in range(pairs):
        which = cells[m : m + 1, :] // LANES
        value = partial[8 * m : 8 * m + 8, :]
        rows = jnp.concatenate([jnp.where(which == level, value, F32(0)) for level in range(3)], axis=0)
        hi = rows.astype(BF16).astype(F32)
        both = jnp.concatenate([hi, rows - hi], axis=0)
        v_ref[:, m * LANES : (m + 1) * LANES] = both.astype(BF16)
    basal = dot_nt(v_ref[...], cell_hot[...])
    basal = basal[:24] + basal[24:]
    basal = jnp.concatenate([basal[:8], basal[8:16], basal[16:]], axis=1)
    for t in range(out_ref.shape[0]):
        out_ref[t] = basal


def gram_kernel(keep_same, tiles, groups, scalars, meta_ref, g_ref, field_ref, gram_ref):
    tile = scalars[0]
    group = scalars[2]
    clusters = gram_ref.shape[0]

    def field(t, p):
        zero = jnp.zeros(g_ref.shape[2:], F32)
        if isinstance(t, int):
            before = g_ref[t - 1, p] if t > 0 else zero
            after = g_ref[t + 1, p] if t < tiles - 1 else zero
        else:
            before = jnp.where(t > 0, g_ref[jnp.maximum(t - 1, 0), p], zero)
            after = jnp.where(t < tiles - 1, g_ref[jnp.minimum(t + 1, tiles - 1), p], zero)
        return masked(total_field(before, g_ref[t, p], after), meta_ref[t], keep_same)

    field_ref[...] = field(tile, group).T

    def add_tile(t, acc):
        ids = meta_ref[t][8:16, :].astype(jnp.int32)
        mine = field(t, group)
        every = jnp.concatenate([field(t, p) for p in range(groups)], axis=0)
        left = jnp.concatenate(
            [jnp.where(ids == k, mine, F32(0)) for k in range(clusters)], axis=0
        )
        return acc + lax.dot_general(
            left,
            every,
            (((1,), (1,)), ((), ())),
            precision=lax.Precision.HIGHEST,
            preferred_element_type=F32,
        )

    acc = jnp.zeros((8 * clusters, 8 * groups), F32)
    acc = lax.fori_loop(0, tiles, add_tile, acc, unroll=tiles <= 8)
    gram_ref[...] = acc.reshape(gram_ref.shape)


def shards(
    blocks, connectivity, basal_map, friction, elem_counts, obs_weight, sign_bits, cluster_ids
):
    slots, order, _ = blocks.shape
    node_slots = connectivity.shape[1]
    node_count = obs_weight.shape[0]
    cell_count, group_size = sign_bits.shape
    tiles = lax.axis_size("tiles")
    groups = lax.axis_size("probes")
    pairs = slots * node_slots // LANES
    refs = pairs * LANES
    levels = node_count // HALO + 1
    padded_order = 2 * LANES
    window = cell_count + 2 * RIM

    smem = pl.BlockSpec(memory_space=pltpu.SMEM)
    vmem = pl.BlockSpec(memory_space=pltpu.VMEM)
    anywhere = pl.BlockSpec(memory_space=pl.ANY)
    params = pltpu.CompilerParams(vmem_limit_bytes=VMEM_BYTES)
    shaped = jax.ShapeDtypeStruct

    def call(kernel, name, out_shape, operands, in_specs=None, scratch=()):
        return pl.pallas_call(
            kernel,
            out_shape=out_shape,
            in_specs=in_specs or [vmem] * len(operands),
            out_specs=jax.tree.map(lambda _: vmem, out_shape),
            scratch_shapes=list(scratch),
            compiler_params=params,
            name=name,
        )(*operands)

    meta = call(
        announce_kernel,
        "announce",
        shaped((tiles, 24, cell_count), F32),
        [sign_bits, cluster_ids.reshape(1, cell_count), obs_weight],
        [vmem, vmem, anywhere],
        [pltpu.VMEM((HALO, 3), F32), pltpu.SemaphoreType.DMA],
    )
    meta = lax.all_to_all(meta, "tiles", 0, 0)
    conn, cells, node_hot, cell_hot, spread, order_map = call(
        functools.partial(setup_kernel, node_slots, padded_order),
        "setup",
        [
            shaped((pairs, LANES), jnp.int32),
            shaped((pairs, LANES), jnp.int32),
            shaped((HALO, refs), BF16),
            shaped((LANES, refs), BF16),
            shaped((LANES, 2 * padded_order), BF16),
            shaped((2 * padded_order, 3 * LANES), BF16),
        ],
        [connectivity, basal_map],
    )
    weight = obs_weight.reshape(node_count // HALO, HALO, 3).transpose(0, 2, 1).reshape(-1, HALO)
    fr = jnp.pad(friction.reshape(slots, order), ((0, 0), (0, padded_order - order)))
    fr = fr.reshape(pairs, 2 * padded_order)
    scalars = jnp.stack(
        [lax.axis_index("tiles"), elem_counts[0], lax.axis_index("probes")]
    ).astype(jnp.int32)
    shared = [conn, cells, fr, blocks, node_hot, cell_hot, spread, order_map]

    evens = range(0, tiles - 1, 2)
    odds = range(1, tiles - 1, 2)
    swap_a = [(i, i + 1) for i in evens] + [(i + 1, i) for i in evens]
    swap_b = [(i, i + 1) for i in odds] + [(i + 1, i) for i in odds]

    def forward(gathered, keep_same, want_field):
        first = gathered is None
        out_shape = [
            shaped((16 * pairs, 3 * LANES), F32),
            shaped((24, HALO), F32),
            shaped((24, HALO), F32),
        ]
        if want_field:
            out_shape.append(shaped((cell_count, group_size), F32))
        operands = [scalars, meta] + ([] if first else [gathered]) + shared
        return call(
            functools.partial(forward_kernel, first, keep_same, want_field, tiles, levels),
            "forward",
            out_shape,
            operands,
            [smem] + [vmem] * (len(operands) - 1),
            [pltpu.VMEM((16 * pairs, 2 * padded_order), F32), pltpu.VMEM((96, refs), BF16)],
        )

    gathered = None
    samples = None
    for step in range(POWER + 1):
        ordered, own_a, own_b, *field = forward(gathered, step % 2 == 0, step == 1)
        if field:
            samples = field[0]
        new_b = lax.ppermute(own_b, "tiles", swap_b)
        new_a = lax.ppermute(own_a, "tiles", swap_a)
        inner = call(
            functools.partial(inner_kernel, levels),
            "inner",
            shaped((8 * pairs, 3 * LANES), F32),
            [ordered, weight, conn, node_hot],
            scratch=[pltpu.VMEM((48 * (levels - 2), refs), BF16)],
        )
        axes = "tiles" if step < POWER else ("tiles", "probes")
        operands = [scalars, meta, own_a, own_b, new_a, new_b, inner, weight] + shared
        basal = call(
            functools.partial(adjoint_kernel, tiles, levels),
            "adjoint",
            shaped((lax.axis_size(axes), group_size, window), F32),
            operands,
            [smem] + [vmem] * (len(operands) - 1),
            [
                pltpu.VMEM((8 * pairs, 2 * padded_order), F32),
                pltpu.VMEM((8 * pairs, 3 * LANES), F32),
                pltpu.VMEM((48, refs), BF16),
            ],
        )
        gathered = lax.all_to_all(basal, axes, 0, 0)

    gathered = gathered.reshape(tiles, groups, group_size, window)
    refined, gram = call(
        functools.partial(gram_kernel, POWER % 2 == 1, tiles, groups),
        "gram",
        [
            shaped((cell_count, group_size), F32),
            shaped((tiles, group_size, groups * group_size), F32),
        ],
        [scalars, meta, gathered],
        [smem, vmem, vmem],
    )
    return (samples, refined, gram)


def solution(mesh):
    in_specs = (
        P("tiles", None, None),
        P("tiles", None),
        P("tiles", None),
        P("tiles", None, None),
        P("tiles"),
        P("tiles", None),
        P("tiles", "probes"),
        P("tiles"),
    )
    out_specs = (P("tiles", "probes"), P("tiles", "probes"), P(None, "probes", None))
    return jax.shard_map(shards, mesh=mesh, in_specs=in_specs, out_specs=out_specs, check_vma=False)
```

```python
import functools

import jax
import jax.numpy as jnp
from jax import lax
from jax.experimental import pallas as pl
from jax.experimental.pallas import tpu as pltpu
from jax.sharding import PartitionSpec as P

HALO = 512
POWER = 2
RIM = 64
LANES = 128
VMEM_BYTES = 16 * 1024 * 1024

F32 = jnp.float32
BF16 = jnp.bfloat16


def dot(a, b):
    return lax.dot_general(a, b, (((1,), (0,)), ((), ())), preferred_element_type=F32)


def dot_nt(a, b):
    return lax.dot_general(a, b, (((1,), (1,)), ((), ())), preferred_element_type=F32)


def split(x):
    hi = x.astype(BF16)
    return hi, (x - hi.astype(F32)).astype(BF16)


def rows_iota(shape):
    return lax.broadcasted_iota(jnp.int32, shape, 0)


def lanes_iota(shape):
    return lax.broadcasted_iota(jnp.int32, shape, 1)


def spread_matrix(node_slots, padded_order):
    shape = (2 * node_slots, 2 * padded_order)
    row = rows_iota(shape)
    start = (row // node_slots) * padded_order + 3 * (row % node_slots)
    gap = lanes_iota(shape) - start
    return jnp.where((gap >= 0) & (gap < 3), F32(1), F32(0)).astype(BF16)


def order_matrix(node_slots, padded_order):
    pair = 2 * node_slots
    shape = (2 * padded_order, 3 * pair)
    col = lanes_iota(shape)
    inner = col % pair
    source = (inner // node_slots) * padded_order + 3 * (inner % node_slots) + col // pair
    return jnp.where(rows_iota(shape) == source, F32(1), F32(0)).astype(BF16)


def same_colour(meta):
    ids = meta[8:16, :].astype(jnp.int32)
    return (ids % 2) == (rows_iota(ids.shape) % 2)


def start_probes(meta):
    signs = 2 * meta[:8, :] - 1
    return jnp.where(same_colour(meta), signs, F32(0))


def total_field(before, own, after):
    lane = lanes_iota((own.shape[0], LANES))
    first = own[:, :LANES] + jnp.where(lane < RIM, before[:, 2 * LANES :], F32(0))
    second = own[:, LANES : 2 * LANES] + jnp.where(lane >= RIM, after[:, 2 * LANES :], F32(0))
    return jnp.concatenate([first, second], axis=1)


def field_of(g_ref, t, tiles):
    zero = jnp.zeros(g_ref.shape[1:], F32)
    if isinstance(t, int):
        before = g_ref[t - 1] if t > 0 else zero
        after = g_ref[t + 1] if t < tiles - 1 else zero
    else:
        before = jnp.where(t > 0, g_ref[jnp.maximum(t - 1, 0)], zero)
        after = jnp.where(t < tiles - 1, g_ref[jnp.minimum(t + 1, tiles - 1)], zero)
    return total_field(before, g_ref[t], after)


def masked(field, meta, keep_same):
    same = same_colour(meta)
    return jnp.where(same if keep_same else ~same, field, F32(0))


def announce_kernel(signs_ref, ids_ref, weight_ref, out_ref):
    half = HALO // 2
    out_ref[0, :8, :] = signs_ref[...].astype(F32)
    out_ref[0, 8:16, :] = jnp.broadcast_to(ids_ref[...].astype(F32), (8, half))
    out_ref[0, 16:24, :] = jnp.zeros((8, half), F32)
    out_ref[0, 16:19, :] = weight_ref[:, :half]
    out_ref[0, 19:22, :] = weight_ref[:, half:HALO]
    block = out_ref[0]
    for t in range(1, out_ref.shape[0]):
        out_ref[t] = block


def setup_kernel(
    conn_in,
    cell_in,
    friction_ref,
    conn_ref,
    cell_ref,
    fr_ref,
    node_hot_ref,
    cell_hot_ref,
    spread_ref,
    order_ref,
):
    pairs = conn_ref.shape[0]
    slots, padded_order = fr_ref.shape
    node_slots = conn_in.shape[1]
    window = 3 * LANES

    def paired(ref):
        return jnp.concatenate(
            [ref[pl.ds(0, pairs, stride=2), :], ref[pl.ds(1, pairs, stride=2), :]], axis=1
        )

    conn = paired(conn_in)
    cells = paired(cell_in)
    cells = jnp.where(cells < RIM, cells + (window - RIM), cells - RIM)
    conn_ref[...] = conn
    cell_ref[...] = cells
    rows = rows_iota((HALO, LANES))
    for m in range(pairs):
        at = pl.ds(m * LANES, LANES)
        hot = rows == conn[m : m + 1, :] % HALO
        node_hot_ref[:, at] = jnp.where(hot, F32(1), F32(0)).astype(BF16)
        hot = rows[:LANES] == cells[m : m + 1, :] % LANES
        cell_hot_ref[:, at] = jnp.where(hot, F32(1), F32(0)).astype(BF16)
    spread_ref[...] = spread_matrix(node_slots, padded_order)
    order_ref[...] = order_matrix(node_slots, padded_order)

    shape = (node_slots, padded_order)
    total = jnp.zeros((slots, padded_order), F32)
    for c in range(3):
        place = lanes_iota(shape) == 3 * rows_iota(shape) + c
        place = jnp.where(place, F32(1), F32(0)).astype(BF16)
        rest = friction_ref[c]
        for _ in range(3):
            part = rest.astype(BF16)
            total = total + dot(part, place)
            rest = rest - part.astype(F32)
    fr_ref[...] = total


def forward_kernel(first, keep_same, want_field, tiles, levels, *refs):
    scalars, meta_ref, *refs = refs
    if not first:
        g_ref, *refs = refs
    conn_ref, cell_ref, fr_ref, blocks, node_hot, cell_hot, spread_ref, order_ref, *refs = refs
    ordered_ref, a_ref, b_ref, *refs = refs
    if want_field:
        field_ref, *refs = refs
    f_ref, v_ref = refs

    order = blocks.shape[1]
    padded_order = f_ref.shape[1] // 2
    pairs = blocks.shape[0] // 2
    tile = scalars[0]
    count = scalars[1]

    if first:
        current = lambda t: start_probes(meta_ref[t])
    else:
        current = lambda t: masked(field_of(g_ref, t, tiles), meta_ref[t], keep_same)

    own = current(tile)
    if want_field:
        field_ref[...] = own
    below = jnp.where(tile > 0, current(jnp.maximum(tile - 1, 0)), F32(0))
    above = jnp.where(tile < tiles - 1, current(jnp.minimum(tile + 1, tiles - 1)), F32(0))
    lane = lanes_iota((8, LANES))
    rims = jnp.where(lane < RIM, above[:, :LANES], below[:, LANES:])
    window = jnp.concatenate([own[:, :LANES], own[:, LANES:], rims], axis=0)
    if not first:

        def add_squares(t, acc):
            part = current(t)
            part = part * part
            return acc + part[:, :LANES] + part[:, LANES:]

        squares = lax.fori_loop(0, tiles, add_squares, jnp.zeros((8, LANES), F32), unroll=tiles <= 8)
        squares = jnp.sum(squares, axis=1, keepdims=True)
        scale = jnp.sqrt(squares / (tiles * 2 * LANES) + F32(1e-06))
        window = window / jnp.concatenate([scale, scale, scale], axis=0)

    cells = cell_ref[...]
    hi, lo = split(window)
    picked = dot(jnp.concatenate([hi, lo], axis=0), cell_hot[...])
    tops = []
    rests = []
    for m in range(pairs):
        part = picked[:, m * LANES : (m + 1) * LANES]
        which = cells[m : m + 1, :] // LANES
        for base, out in ((0, tops), (24, rests)):
            chosen = jnp.where(which == 0, part[base : base + 8], F32(0))
            for level in (1, 2):
                at = base + 8 * level
                chosen = jnp.where(which == level, part[at : at + 8], chosen)
            out.append(chosen)
    stacked = jnp.concatenate(tops + rests, axis=0).astype(BF16)
    spread = dot(stacked, spread_ref[...])
    half = 8 * pairs
    spread = spread[:half] + spread[half:]

    f_ref[...] = jnp.zeros_like(f_ref)
    for m in range(pairs):
        for side in range(2):
            at = side * padded_order
            slot = 2 * m + side
            inputs = spread[8 * m : 8 * m + 8, at : at + order] * fr_ref[slot : slot + 1, :order]
            out = dot_nt(inputs.astype(BF16), blocks[slot])
            out = jnp.where(slot < count, out, F32(0))
            hi = out.astype(BF16).astype(F32)
            f_ref[16 * m : 16 * m + 8, at : at + order] = hi
            f_ref[16 * m + 8 : 16 * m + 16, at : at + order] = out - hi

    ordered = dot(f_ref[...].astype(BF16), order_ref[...])
    ordered_ref[...] = ordered
    conn = conn_ref[...]
    for m in range(pairs):
        which = conn[m : m + 1, :] // HALO
        rows = [
            jnp.where(
                which == level,
                ordered[16 * m : 16 * m + 16, c * LANES : (c + 1) * LANES],
                F32(0),
            )
            for level in (0, levels - 1)
            for c in range(3)
        ]
        v_ref[:, m * LANES : (m + 1) * LANES] = jnp.concatenate(rows, axis=0).astype(BF16)
    rim = dot_nt(v_ref[...], node_hot[...])
    even = tile % 2 == 0
    for c in range(3):
        lead = rim[16 * c : 16 * c + 8] + rim[16 * c + 8 : 16 * c + 16]
        at = 48 + 16 * c
        spill = rim[at : at + 8] + rim[at + 8 : at + 16]
        a_ref[8 * c : 8 * c + 8, :] = jnp.where(even, spill, lead)
        b_ref[8 * c : 8 * c + 8, :] = jnp.where(even, lead, spill)


def inner_kernel(levels, ordered_ref, weight_ref, conn_ref, node_hot, picked_ref, v_ref):
    pairs = conn_ref.shape[0]
    conn = conn_ref[...]
    for m in range(pairs):
        which = conn[m : m + 1, :] // HALO
        rows = [
            jnp.where(
                which == level,
                ordered_ref[16 * m : 16 * m + 16, c * LANES : (c + 1) * LANES],
                F32(0),
            )
            for level in range(1, levels - 1)
            for c in range(3)
        ]
        v_ref[:, m * LANES : (m + 1) * LANES] = jnp.concatenate(rows, axis=0).astype(BF16)
    nodes = dot_nt(v_ref[...], node_hot[...])
    rows = []
    for i in range(3 * (levels - 2)):
        value = nodes[16 * i : 16 * i + 8] + nodes[16 * i + 8 : 16 * i + 16]
        at = (i // 3 + 1) * HALO
        rows.append(value * weight_ref[i % 3 : i % 3 + 1, at : at + HALO])
    weighted = jnp.concatenate(rows, axis=0).astype(BF16)
    step = 2
    for start in range(0, pairs, step):
        found = dot(weighted, node_hot[:, start * LANES : (start + step) * LANES])
        for i in range(step):
            m = start + i
            which = conn[m : m + 1, :] // HALO
            part = found[:, i * LANES : (i + 1) * LANES]
            chosen = jnp.zeros((24, LANES), F32)
            for level in range(1, levels - 1):
                at = 24 * (level - 1)
                chosen = jnp.where(which == level, part[at : at + 24], chosen)
            for c in range(3):
                picked_ref[8 * m : 8 * m + 8, c * LANES : (c + 1) * LANES] = chosen[8 * c : 8 * c + 8]


def adjoint_kernel(
    tiles,
    levels,
    scalars,
    meta_ref,
    own_a,
    own_b,
    new_a,
    new_b,
    inner_ref,
    weight_ref,
    conn_ref,
    cell_ref,
    fr_ref,
    blocks,
    node_hot,
    cell_hot,
    spread_ref,
    order_ref,
    out_ref,
    *refs,
):
    *own_ref, p_ref, n_ref, v_ref = refs
    order = blocks.shape[1]
    padded_order = p_ref.shape[1] // 2
    pairs = blocks.shape[0] // 2
    tile = scalars[0]
    count = scalars[1]

    even = tile % 2 == 0
    lead = jnp.where(even, own_b[...] + new_b[...], own_a[...] + new_a[...])
    spill = jnp.where(even, own_a[...] + new_a[...], own_b[...] + new_b[...])
    after = meta_ref[jnp.minimum(tile + 1, tiles - 1)]
    after = jnp.where(tile < tiles - 1, after, F32(0))
    rows = [lead[8 * c : 8 * c + 8] * weight_ref[c : c + 1, :HALO] for c in range(3)]
    for c in range(3):
        weight = jnp.concatenate([after[16 + c : 17 + c, :], after[19 + c : 20 + c, :]], axis=1)
        rows.append(spill[8 * c : 8 * c + 8] * weight)
    weighted = jnp.concatenate(rows, axis=0).astype(BF16)

    conn = conn_ref[...]
    step = 2
    for start in range(0, pairs, step):
        found = dot(weighted, node_hot[:, start * LANES : (start + step) * LANES])
        for i in range(step):
            m = start + i
            which = conn[m : m + 1, :] // HALO
            part = found[:, i * LANES : (i + 1) * LANES]
            for c in range(3):
                value = inner_ref[8 * m : 8 * m + 8, c * LANES : (c + 1) * LANES]
                value = jnp.where(which == 0, part[8 * c : 8 * c + 8], value)
                value = jnp.where(which == levels - 1, part[24 + 8 * c : 32 + 8 * c], value)
                n_ref[8 * m : 8 * m + 8, c * LANES : (c + 1) * LANES] = value
    natural = dot_nt(n_ref[...].astype(BF16), order_ref[...])
    p_ref[...] = jnp.zeros_like(p_ref)
    for m in range(pairs):
        for side in range(2):
            at = side * padded_order
            slot = 2 * m + side
            out = dot(natural[8 * m : 8 * m + 8, at : at + order].astype(BF16), blocks[slot])
            out = out * fr_ref[slot : slot + 1, :order]
            p_ref[8 * m : 8 * m + 8, at : at + order] = jnp.where(slot < count, out, F32(0))

    hi, lo = split(p_ref[...])
    partial = dot_nt(jnp.concatenate([hi, lo], axis=0), spread_ref[...])
    half = 8 * pairs
    partial = partial[:half] + partial[half:]
    cells = cell_ref[...]
    for m in range(pairs):
        which = cells[m : m + 1, :] // LANES
        value = partial[8 * m : 8 * m + 8, :]
        rows = jnp.concatenate([jnp.where(which == level, value, F32(0)) for level in range(3)], axis=0)
        hi = rows.astype(BF16).astype(F32)
        both = jnp.concatenate([hi, rows - hi], axis=0)
        v_ref[:, m * LANES : (m + 1) * LANES] = both.astype(BF16)
    basal = dot_nt(v_ref[...], cell_hot[...])
    basal = basal[:24] + basal[24:]
    basal = jnp.concatenate([basal[:8], basal[8:16], basal[16:]], axis=1)
    if own_ref:
        own_ref[0][...] = basal
    basal = basal.astype(out_ref.dtype)
    for t in range(out_ref.shape[0]):
        out_ref[t] = basal


def gram_kernel(keep_same, tiles, groups, scalars, meta_ref, g_ref, own_ref, field_ref, gram_ref):
    tile = scalars[0]
    group = scalars[2]
    clusters = gram_ref.shape[0]

    def field(t, p, own=None):
        zero = jnp.zeros(g_ref.shape[2:], F32)
        if isinstance(t, int):
            before = g_ref[t - 1, p].astype(F32) if t > 0 else zero
            after = g_ref[t + 1, p].astype(F32) if t < tiles - 1 else zero
        else:
            before = jnp.where(t > 0, g_ref[jnp.maximum(t - 1, 0), p].astype(F32), zero)
            after = g_ref[jnp.minimum(t + 1, tiles - 1), p].astype(F32)
            after = jnp.where(t < tiles - 1, after, zero)
        if own is None:
            own = g_ref[t, p].astype(F32)
        return masked(total_field(before, own, after), meta_ref[t], keep_same)

    field_ref[...] = field(tile, group, own_ref[...])

    def add_tile(t, acc):
        ids = meta_ref[t][8:16, :].astype(jnp.int32)
        mine = field(t, group)
        every = jnp.concatenate([field(t, p) for p in range(groups)], axis=0)
        left = jnp.concatenate(
            [jnp.where(ids == k, mine, F32(0)) for k in range(clusters)], axis=0
        )
        return acc + lax.dot_general(
            left,
            every,
            (((1,), (1,)), ((), ())),
            precision=lax.Precision.HIGHEST,
            preferred_element_type=F32,
        )

    acc = jnp.zeros((8 * clusters, 8 * groups), F32)
    acc = lax.fori_loop(0, tiles, add_tile, acc, unroll=tiles <= 8)
    gram_ref[...] = acc.reshape(gram_ref.shape)


def shards(
    blocks, connectivity, basal_map, friction, elem_counts, obs_weight, sign_bits, cluster_ids
):
    slots = blocks.shape[0]
    node_slots = connectivity.shape[1]
    node_count = obs_weight.shape[0]
    cell_count, group_size = sign_bits.shape
    tiles = lax.axis_size("tiles")
    groups = lax.axis_size("probes")
    pairs = slots * node_slots // LANES
    refs = pairs * LANES
    levels = node_count // HALO + 1
    padded_order = 2 * LANES
    window = cell_count + 2 * RIM

    smem = pl.BlockSpec(memory_space=pltpu.SMEM)
    vmem = pl.BlockSpec(memory_space=pltpu.VMEM)
    params = pltpu.CompilerParams(vmem_limit_bytes=VMEM_BYTES)
    shaped = jax.ShapeDtypeStruct

    def call(kernel, name, out_shape, operands, in_specs=None, scratch=()):
        return pl.pallas_call(
            kernel,
            out_shape=out_shape,
            in_specs=in_specs or [vmem] * len(operands),
            out_specs=jax.tree.map(lambda _: vmem, out_shape),
            scratch_shapes=list(scratch),
            compiler_params=params,
            name=name,
        )(*operands)

    weight = obs_weight.T
    meta = call(
        announce_kernel,
        "announce",
        shaped((tiles, 24, cell_count), F32),
        [sign_bits.T, cluster_ids.reshape(1, cell_count), weight],
    )
    meta = lax.all_to_all(meta, "tiles", 0, 0)
    conn, cells, fr, node_hot, cell_hot, spread, order_map = call(
        setup_kernel,
        "setup",
        [
            shaped((pairs, LANES), jnp.int32),
            shaped((pairs, LANES), jnp.int32),
            shaped((slots, padded_order), F32),
            shaped((HALO, refs), BF16),
            shaped((LANES, refs), BF16),
            shaped((LANES, 2 * padded_order), BF16),
            shaped((2 * padded_order, 3 * LANES), BF16),
        ],
        [connectivity, basal_map, friction.transpose(2, 0, 1)],
    )
    scalars = jnp.stack(
        [lax.axis_index("tiles"), elem_counts[0], lax.axis_index("probes")]
    ).astype(jnp.int32)
    shared = [conn, cells, fr, blocks, node_hot, cell_hot, spread, order_map]

    evens = range(0, tiles - 1, 2)
    odds = range(1, tiles - 1, 2)
    swap_a = [(i, i + 1) for i in evens] + [(i + 1, i) for i in evens]
    swap_b = [(i, i + 1) for i in odds] + [(i + 1, i) for i in odds]

    def forward(gathered, keep_same, want_field):
        first = gathered is None
        out_shape = [
            shaped((16 * pairs, 3 * LANES), F32),
            shaped((24, HALO), F32),
            shaped((24, HALO), F32),
        ]
        if want_field:
            out_shape.append(shaped((group_size, cell_count), F32))
        operands = [scalars, meta] + ([] if first else [gathered]) + shared
        return call(
            functools.partial(forward_kernel, first, keep_same, want_field, tiles, levels),
            "forward",
            out_shape,
            operands,
            [smem] + [vmem] * (len(operands) - 1),
            [pltpu.VMEM((16 * pairs, 2 * padded_order), F32), pltpu.VMEM((96, refs), BF16)],
        )

    gathered = None
    samples = None
    for step in range(POWER + 1):
        ordered, own_a, own_b, *field = forward(gathered, step % 2 == 0, step == 1)
        if field:
            samples = field[0].T
        new_b = lax.ppermute(own_b, "tiles", swap_b)
        new_a = lax.ppermute(own_a, "tiles", swap_a)
        inner = call(
            functools.partial(inner_kernel, levels),
            "inner",
            shaped((8 * pairs, 3 * LANES), F32),
            [ordered, weight, conn, node_hot],
            scratch=[pltpu.VMEM((48 * (levels - 2), refs), BF16)],
        )
        axes = "tiles" if step < POWER else ("tiles", "probes")
        operands = [scalars, meta, own_a, own_b, new_a, new_b, inner, weight] + shared
        last = step == POWER
        shape = (group_size, window)
        out_shape = [shaped((lax.axis_size(axes), *shape), BF16 if last else F32)]
        basal, *own = call(
            functools.partial(adjoint_kernel, tiles, levels),
            "adjoint",
            out_shape + [shaped(shape, F32)] * last,
            operands,
            [smem] + [vmem] * (len(operands) - 1),
            [
                pltpu.VMEM((8 * pairs, 2 * padded_order), F32),
                pltpu.VMEM((8 * pairs, 3 * LANES), F32),
                pltpu.VMEM((48, refs), BF16),
            ],
        )
        gathered = lax.all_to_all(basal, axes, 0, 0)

    gathered = gathered.reshape(tiles, groups, group_size, window)
    refined, gram = call(
        functools.partial(gram_kernel, POWER % 2 == 1, tiles, groups),
        "gram",
        [
            shaped((group_size, cell_count), F32),
            shaped((tiles, group_size, groups * group_size), F32),
        ],
        [scalars, meta, gathered, own[0]],
        [smem, vmem, vmem, vmem],
    )
    return (samples, refined.T, gram)


def solution(mesh):
    in_specs = (
        P("tiles", None, None),
        P("tiles", None),
        P("tiles", None),
        P("tiles", None, None),
        P("tiles"),
        P("tiles", None),
        P("tiles", "probes"),
        P("tiles"),
    )
    out_specs = (P("tiles", "probes"), P("tiles", "probes"), P(None, "probes", None))
    return jax.shard_map(shards, mesh=mesh, in_specs=in_specs, out_specs=out_specs, check_vma=False)
```

```python
import functools

import jax
import jax.numpy as jnp
from jax import lax
from jax.experimental import pallas as pl
from jax.experimental.pallas import tpu as pltpu
from jax.sharding import PartitionSpec as P

HALO = 512
POWER = 2
RIM = 64
LANES = 128
RADIX = 256
EDGE = HALO // RADIX
SHRINK = 2.0**-40
VMEM_BYTES = 16 * 1024 * 1024

F32 = jnp.float32
BF16 = jnp.bfloat16


def dot(a, b):
    return lax.dot_general(a, b, (((1,), (0,)), ((), ())), preferred_element_type=F32)


def dot_nt(a, b):
    return lax.dot_general(a, b, (((1,), (1,)), ((), ())), preferred_element_type=F32)


def split(x):
    hi = x.astype(BF16)
    return hi, (x - hi.astype(F32)).astype(BF16)


def rows_iota(shape):
    return lax.broadcasted_iota(jnp.int32, shape, 0)


def lanes_iota(shape):
    return lax.broadcasted_iota(jnp.int32, shape, 1)


def spread_matrix(node_slots, padded_order):
    shape = (2 * node_slots, 2 * padded_order)
    row = rows_iota(shape)
    start = (row // node_slots) * padded_order + 3 * (row % node_slots)
    gap = lanes_iota(shape) - start
    return jnp.where((gap >= 0) & (gap < 3), F32(1), F32(0)).astype(BF16)


def order_matrix(node_slots, padded_order):
    pair = 2 * node_slots
    shape = (2 * padded_order, 3 * pair)
    col = lanes_iota(shape)
    inner = col % pair
    source = (inner // node_slots) * padded_order + 3 * (inner % node_slots) + col // pair
    return jnp.where(rows_iota(shape) == source, F32(1), F32(0)).astype(BF16)


def colour_of(ids):
    return (ids % 2) == (rows_iota(ids.shape) % 2)


def by_side(tile, a, b):
    even = tile % 2 == 0
    return jnp.where(even, a, b), jnp.where(even, b, a)


def to_swaps(tile, for_next, for_previous):
    even = tile % 2 == 0
    return jnp.where(even, for_next, for_previous), jnp.where(even, for_previous, for_next)


def setup_kernel(
    conn_in,
    cell_in,
    friction_ref,
    conn_ref,
    cell_ref,
    fr_ref,
    node_hot_ref,
    cell_hot_ref,
    spread_ref,
    order_ref,
):
    pairs = conn_ref.shape[0]
    slots, padded_order = fr_ref.shape
    node_slots = conn_in.shape[1]
    window = 3 * LANES

    def paired(ref):
        return jnp.concatenate(
            [ref[pl.ds(0, pairs, stride=2), :], ref[pl.ds(1, pairs, stride=2), :]], axis=1
        )

    conn = paired(conn_in)
    cells = paired(cell_in)
    cells = jnp.where(cells < RIM, cells + (window - RIM), cells - RIM)
    conn_ref[...] = conn
    cell_ref[...] = cells
    rows = rows_iota((RADIX, LANES))
    for m in range(pairs):
        at = pl.ds(m * LANES, LANES)
        hot = rows == conn[m : m + 1, :] % RADIX
        node_hot_ref[:, at] = jnp.where(hot, F32(1), F32(0)).astype(BF16)
        hot = rows[:LANES] == cells[m : m + 1, :] % LANES
        cell_hot_ref[:, at] = jnp.where(hot, F32(1), F32(0)).astype(BF16)
    spread_ref[...] = spread_matrix(node_slots, padded_order)
    order_ref[...] = order_matrix(node_slots, padded_order)

    shape = (node_slots, padded_order)
    total = jnp.zeros((slots, padded_order), F32)
    for c in range(3):
        place = lanes_iota(shape) == 3 * rows_iota(shape) + c
        place = jnp.where(place, F32(1), F32(0)).astype(BF16)
        rest = friction_ref[c]
        for _ in range(3):
            part = rest.astype(BF16)
            total = total + dot(part, place)
            rest = rest - part.astype(F32)
    fr_ref[...] = total


def edge_levels(levels):
    return list(range(EDGE)) + list(range(levels - EDGE, levels))


def forward_kernel(step, tiles, levels, *refs):
    scalars, block_ref, block_a, block_b, *refs = refs
    first = step == 0
    if not first:
        basal_ref, rim_a, rim_b, *refs = refs
    conn_ref, cell_ref, fr_ref, blocks, node_hot, cell_hot, spread_ref, order_ref, *refs = refs
    ordered_ref, a_ref, b_ref, *refs = refs
    if not first:
        squares_ref, *refs = refs
    if step == 1:
        field_ref, *refs = refs
    f_ref, v_ref = refs

    order = blocks.shape[1]
    padded_order = f_ref.shape[1] // 2
    pairs = blocks.shape[0] // 2
    tile = scalars[0]
    count = scalars[1]

    lane = lanes_iota((8, LANES))
    low = lane < RIM
    after, before = by_side(tile, block_a[:8, :], block_b[:8, :])
    starts = [
        block_ref[:8, :LANES],
        block_ref[:8, LANES:],
        jnp.where(low, after[:, :LANES], before[:, LANES:]),
    ]
    if first:
        parts = starts
    else:
        after, before = by_side(tile, rim_a[...], rim_b[...])
        parts = [basal_ref[:, i * LANES : (i + 1) * LANES] for i in range(3)]
        parts[0] = parts[0] + jnp.where(low, before, F32(0))
        parts[1] = parts[1] + jnp.where(low, F32(0), after)
        parts[2] = parts[2] + jnp.where(low, after, before)
        there = (low & (tile < tiles - 1)) | (~low & (tile > 0))
        parts[2] = jnp.where(there, parts[2], F32(0))
        kept = [(start != 0) if step % 2 == 0 else (start == 0) for start in starts]
        parts = [jnp.where(keep, part, F32(0)) for keep, part in zip(kept, parts)]
        if step == 1:
            field_ref[:, :LANES] = parts[0]
            field_ref[:, LANES:] = parts[1]
        squares_ref[...] = parts[0] * parts[0] + parts[1] * parts[1]
    window = jnp.concatenate(parts, axis=0)
    if step == 1:
        window = window * F32(SHRINK)

    cells = cell_ref[...]
    hi, lo = split(window)
    picked = dot(jnp.concatenate([hi, lo], axis=0), cell_hot[...])
    tops = []
    rests = []
    for m in range(pairs):
        part = picked[:, m * LANES : (m + 1) * LANES]
        which = cells[m : m + 1, :] // LANES
        for base, out in ((0, tops), (24, rests)):
            chosen = jnp.where(which == 0, part[base : base + 8], F32(0))
            for level in (1, 2):
                at = base + 8 * level
                chosen = jnp.where(which == level, part[at : at + 8], chosen)
            out.append(chosen)
    stacked = jnp.concatenate(tops + rests, axis=0).astype(BF16)
    spread = dot(stacked, spread_ref[...])
    half = 8 * pairs
    spread = spread[:half] + spread[half:]

    f_ref[...] = jnp.zeros_like(f_ref)
    for m in range(pairs):
        for side in range(2):
            at = side * padded_order
            slot = 2 * m + side
            inputs = spread[8 * m : 8 * m + 8, at : at + order] * fr_ref[slot : slot + 1, :order]
            if first:
                out = dot_nt(inputs.astype(BF16), blocks[slot])
            else:
                hi = inputs.astype(BF16).astype(F32)
                both = jnp.concatenate([hi, inputs - hi], axis=0).astype(BF16)
                out = dot_nt(both, blocks[slot])
                out = out[:8] + out[8:]
            out = jnp.where(slot < count, out, F32(0))
            hi = out.astype(BF16).astype(F32)
            f_ref[16 * m : 16 * m + 8, at : at + order] = hi
            f_ref[16 * m + 8 : 16 * m + 16, at : at + order] = out - hi

    ordered = dot(f_ref[...].astype(BF16), order_ref[...])
    ordered_ref[...] = ordered
    conn = conn_ref[...]
    edges = edge_levels(levels)
    for m in range(pairs):
        which = conn[m : m + 1, :] // RADIX
        rows = [
            jnp.where(
                which == level,
                ordered[16 * m : 16 * m + 16, c * LANES : (c + 1) * LANES],
                F32(0),
            )
            for level in edges
            for c in range(3)
        ]
        v_ref[:, m * LANES : (m + 1) * LANES] = jnp.concatenate(rows, axis=0).astype(BF16)
    rim = dot_nt(v_ref[...], node_hot[...])
    sums = [
        rim[16 * i : 16 * i + 8] + rim[16 * i + 8 : 16 * i + 16] for i in range(3 * len(edges))
    ]
    half = len(sums) // 2
    for i in range(half):
        lead, spill = sums[i], sums[half + i]
        a_ref[8 * i : 8 * i + 8, :], b_ref[8 * i : 8 * i + 8, :] = to_swaps(tile, spill, lead)


def inner_kernel(levels, ordered_ref, weight_ref, conn_ref, node_hot, picked_ref, v_ref):
    pairs = conn_ref.shape[0]
    conn = conn_ref[...]
    inside = list(range(EDGE, levels - EDGE))
    for m in range(pairs):
        which = conn[m : m + 1, :] // RADIX
        rows = [
            jnp.where(
                which == level,
                ordered_ref[16 * m : 16 * m + 16, c * LANES : (c + 1) * LANES],
                F32(0),
            )
            for level in inside
            for c in range(3)
        ]
        v_ref[:, m * LANES : (m + 1) * LANES] = jnp.concatenate(rows, axis=0).astype(BF16)
    nodes = dot_nt(v_ref[...], node_hot[...])
    rows = []
    for i in range(3 * len(inside)):
        value = nodes[16 * i : 16 * i + 8] + nodes[16 * i + 8 : 16 * i + 16]
        at = inside[i // 3] * RADIX
        rows.append(value * weight_ref[i % 3 : i % 3 + 1, at : at + RADIX])
    weighted = jnp.concatenate(rows, axis=0).astype(BF16)
    step = 2
    for start in range(0, pairs, step):
        found = dot(weighted, node_hot[:, start * LANES : (start + step) * LANES])
        for i in range(step):
            m = start + i
            which = conn[m : m + 1, :] // RADIX
            part = found[:, i * LANES : (i + 1) * LANES]
            chosen = jnp.zeros((24, LANES), F32)
            for at, level in enumerate(inside):
                chosen = jnp.where(which == level, part[24 * at : 24 * at + 24], chosen)
            for c in range(3):
                picked_ref[8 * m : 8 * m + 8, c * LANES : (c + 1) * LANES] = chosen[8 * c : 8 * c + 8]


def adjoint_kernel(last, levels, *refs):
    scalars, block_a, block_b, own_a, own_b, new_a, new_b, inner_ref, weight_ref, *refs = refs
    conn_ref, cell_ref, fr_ref, blocks, node_hot, cell_hot, spread_ref, order_ref, *refs = refs
    if last:
        squares_1, squares_2, ids_ref, *refs = refs
        basal_ref, out_ref, p_ref, n_ref, v_ref = refs
    else:
        basal_ref, a_ref, b_ref, p_ref, n_ref, v_ref = refs

    order = blocks.shape[1]
    padded_order = p_ref.shape[1] // 2
    pairs = blocks.shape[0] // 2
    tile = scalars[0]
    count = scalars[1]

    spill, lead = by_side(tile, own_a[...] + new_a[...], own_b[...] + new_b[...])
    after, _ = by_side(tile, block_a[8:16, :], block_b[8:16, :])
    rows = []
    for i in range(3 * EDGE):
        at = (i // 3) * RADIX
        rows.append(lead[8 * i : 8 * i + 8] * weight_ref[i % 3 : i % 3 + 1, at : at + RADIX])
    for i in range(3 * EDGE):
        rows.append(spill[8 * i : 8 * i + 8] * after[i : i + 1, :])
    weighted = jnp.concatenate(rows, axis=0).astype(BF16)

    conn = conn_ref[...]
    edges = edge_levels(levels)
    step = 2
    for start in range(0, pairs, step):
        found = dot(weighted, node_hot[:, start * LANES : (start + step) * LANES])
        for i in range(step):
            m = start + i
            which = conn[m : m + 1, :] // RADIX
            part = found[:, i * LANES : (i + 1) * LANES]
            for c in range(3):
                value = inner_ref[8 * m : 8 * m + 8, c * LANES : (c + 1) * LANES]
                for at, level in enumerate(edges):
                    row = 24 * at + 8 * c
                    value = jnp.where(which == level, part[row : row + 8], value)
                n_ref[8 * m : 8 * m + 8, c * LANES : (c + 1) * LANES] = value
    natural = dot_nt(n_ref[...].astype(BF16), order_ref[...])
    p_ref[...] = jnp.zeros_like(p_ref)
    for m in range(pairs):
        for side in range(2):
            at = side * padded_order
            slot = 2 * m + side
            out = dot(natural[8 * m : 8 * m + 8, at : at + order].astype(BF16), blocks[slot])
            out = out * fr_ref[slot : slot + 1, :order]
            p_ref[8 * m : 8 * m + 8, at : at + order] = jnp.where(slot < count, out, F32(0))

    hi, lo = split(p_ref[...])
    partial = dot_nt(jnp.concatenate([hi, lo], axis=0), spread_ref[...])
    half = 8 * pairs
    partial = partial[:half] + partial[half:]
    cells = cell_ref[...]
    for m in range(pairs):
        which = cells[m : m + 1, :] // LANES
        value = partial[8 * m : 8 * m + 8, :]
        rows = jnp.concatenate([jnp.where(which == level, value, F32(0)) for level in range(3)], axis=0)
        hi = rows.astype(BF16).astype(F32)
        both = jnp.concatenate([hi, rows - hi], axis=0)
        v_ref[:, m * LANES : (m + 1) * LANES] = both.astype(BF16)
    basal = dot_nt(v_ref[...], cell_hot[...])
    basal = basal[:24] + basal[24:]
    parts = [basal[8 * i : 8 * i + 8] for i in range(3)]
    for i in range(3):
        basal_ref[:, i * LANES : (i + 1) * LANES] = parts[i]
    lane = lanes_iota((8, LANES))
    if not last:
        for_next = jnp.where(lane < RIM, parts[2], parts[1])
        for_previous = jnp.where(lane < RIM, parts[0], parts[2])
        a_ref[...], b_ref[...] = to_swaps(tile, for_next, for_previous)
        return

    ids = ids_ref[...].astype(F32)
    row = rows_iota((8, LANES))
    ids = jnp.where(row == 0, ids[:, :LANES], jnp.where(row == 1, ids[:, LANES:], F32(0)))
    extra = jnp.zeros((8, LANES), F32)
    for i, ref in enumerate((squares_1, squares_2)):
        rest = jnp.sum(ref[...], axis=1, keepdims=True)
        for j in range(3):
            piece = rest.astype(BF16).astype(F32)
            extra = jnp.where(lane == 3 * i + j, piece, extra)
            rest = rest - piece
    message = jnp.concatenate(parts + [ids, extra], axis=1).astype(BF16)
    for t in range(out_ref.shape[0]):
        out_ref[t] = message


def gram_kernel(keep_same, tiles, groups, scalars, g_ref, own_ref, field_ref, gram_ref):
    tile = scalars[0]
    group = scalars[2]
    clusters = gram_ref.shape[0]
    cell_count = tiles * 2 * LANES
    low = lanes_iota((8, LANES)) < RIM

    def factor_of(p):
        def add(t, acc):
            return acc + g_ref[t, p][:, 4 * LANES :].astype(F32)

        sums = lax.fori_loop(0, tiles, add, jnp.zeros((8, LANES), F32), unroll=tiles <= 8)
        first = jnp.sum(sums[:, :3], axis=1, keepdims=True)
        second = jnp.sum(sums[:, 3:6], axis=1, keepdims=True)
        scale = jnp.sqrt(first / cell_count + F32(1e-06))
        size = jnp.sqrt(second / cell_count) * F32(1 / SHRINK) / scale
        return F32(1 / SHRINK) / (scale * jnp.sqrt(size * size + F32(1e-06)))

    def ids_of(t):
        rows = g_ref[t, 0][:, 3 * LANES : 4 * LANES].astype(F32).astype(jnp.int32)
        return [jnp.broadcast_to(rows[i : i + 1, :], (8, LANES)) for i in range(2)]

    def field(t, p, ids, own=None):
        before = g_ref[jnp.maximum(t - 1, 0), p][:, 2 * LANES : 3 * LANES].astype(F32)
        after = g_ref[jnp.minimum(t + 1, tiles - 1), p][:, 2 * LANES : 3 * LANES].astype(F32)
        if own is None:
            own = g_ref[t, p][:, : 2 * LANES].astype(F32)
        parts = [
            own[:, :LANES] + jnp.where(low & (t > 0), before, F32(0)),
            own[:, LANES : 2 * LANES] + jnp.where(~low & (t < tiles - 1), after, F32(0)),
        ]
        return [
            jnp.where(colour_of(i) if keep_same else ~colour_of(i), part, F32(0))
            for i, part in zip(ids, parts)
        ]

    factors = [factor_of(p) for p in range(groups)]
    mine_factor = factors[0]
    for p in range(1, groups):
        mine_factor = jnp.where(group == p, factors[p], mine_factor)
    own = field(tile, group, ids_of(tile), own_ref[...])
    field_ref[:, :LANES] = own[0] * mine_factor
    field_ref[:, LANES:] = own[1] * mine_factor

    def add_tile(t, acc):
        ids = ids_of(t)
        every = [
            jnp.concatenate(field(t, p, ids), axis=1) * factors[p] for p in range(groups)
        ]
        mine = every[0]
        for p in range(1, groups):
            mine = jnp.where(group == p, every[p], mine)
        ids = jnp.concatenate(ids, axis=1)
        left = jnp.concatenate([jnp.where(ids == k, mine, F32(0)) for k in range(clusters)], axis=0)
        return acc + lax.dot_general(
            left,
            jnp.concatenate(every, axis=0),
            (((1,), (1,)), ((), ())),
            precision=lax.Precision.HIGHEST,
            preferred_element_type=F32,
        )

    acc = jnp.zeros((8 * clusters, 8 * groups), F32)
    acc = lax.fori_loop(0, tiles, add_tile, acc, unroll=tiles <= 8)
    gram_ref[...] = acc.reshape(gram_ref.shape)


def shards(
    blocks, connectivity, basal_map, friction, elem_counts, obs_weight, sign_bits, cluster_ids
):
    slots = blocks.shape[0]
    node_slots = connectivity.shape[1]
    node_count = obs_weight.shape[0]
    cell_count, group_size = sign_bits.shape
    tiles = lax.axis_size("tiles")
    groups = lax.axis_size("probes")
    pairs = slots * node_slots // LANES
    refs = pairs * LANES
    levels = (node_count + HALO) // RADIX
    padded_order = 2 * LANES
    window = cell_count + 2 * RIM

    smem = pl.BlockSpec(memory_space=pltpu.SMEM)
    vmem = pl.BlockSpec(memory_space=pltpu.VMEM)
    params = pltpu.CompilerParams(vmem_limit_bytes=VMEM_BYTES)
    shaped = jax.ShapeDtypeStruct

    def call(kernel, name, out_shape, operands, scratch=(), scalar=True):
        return pl.pallas_call(
            kernel,
            out_shape=out_shape,
            in_specs=[smem] * scalar + [vmem] * (len(operands) - scalar),
            out_specs=jax.tree.map(lambda _: vmem, out_shape),
            scratch_shapes=list(scratch),
            compiler_params=params,
            name=name,
        )(*operands)

    evens = range(0, tiles - 1, 2)
    odds = range(1, tiles - 1, 2)
    pairs_a = [(i, i + 1) for i in evens] + [(i + 1, i) for i in evens]
    pairs_b = [(i, i + 1) for i in odds] + [(i + 1, i) for i in odds]

    def swapped(a, b):
        return lax.ppermute(a, "tiles", pairs_a), lax.ppermute(b, "tiles", pairs_b)

    weight = obs_weight.T
    parity = jnp.arange(group_size, dtype=jnp.int32) % 2
    same = (cluster_ids % 2)[None, :] == parity[:, None]
    probes = jnp.where(same, (2 * sign_bits.T - 1).astype(F32), F32(0))
    lead = [weight[:, i * RADIX : (i + 1) * RADIX] for i in range(EDGE)]
    spare = jnp.zeros((8 - 3 * EDGE, RADIX), F32)
    block = jnp.concatenate([probes, *lead, spare], axis=0)
    block_a, block_b = swapped(block, block)

    conn, cells, fr, node_hot, cell_hot, spread, order_map = call(
        setup_kernel,
        "setup",
        [
            shaped((pairs, LANES), jnp.int32),
            shaped((pairs, LANES), jnp.int32),
            shaped((slots, padded_order), F32),
            shaped((RADIX, refs), BF16),
            shaped((LANES, refs), BF16),
            shaped((LANES, 2 * padded_order), BF16),
            shaped((2 * padded_order, 3 * LANES), BF16),
        ],
        [connectivity, basal_map, friction.transpose(2, 0, 1)],
        scalar=False,
    )
    scalars = jnp.stack(
        [lax.axis_index("tiles"), elem_counts[0], lax.axis_index("probes")]
    ).astype(jnp.int32)
    shared = [conn, cells, fr, blocks, node_hot, cell_hot, spread, order_map]

    edge = shaped((24 * EDGE, RADIX), F32)
    rim = shaped((group_size, LANES), F32)
    whole = shaped((group_size, window), F32)
    field = shaped((group_size, cell_count), F32)
    everyone = ("tiles", "probes")

    carried = []
    squares = []
    samples = None
    for step in range(POWER + 1):
        last = step == POWER
        out_shape = [shaped((16 * pairs, 3 * LANES), F32), edge, edge]
        out_shape += [rim] * (step > 0) + [field] * (step == 1)
        ordered, own_a, own_b, *extra = call(
            functools.partial(forward_kernel, step, tiles, levels),
            "forward",
            out_shape,
            [scalars, block, block_a, block_b] + carried + shared,
            [
                pltpu.VMEM((16 * pairs, 2 * padded_order), F32),
                pltpu.VMEM((96 * EDGE, refs), BF16),
            ],
        )
        squares += extra[:1]
        if step == 1:
            samples = extra[1].T
        new_a, new_b = swapped(own_a, own_b)
        inner = call(
            functools.partial(inner_kernel, levels),
            "inner",
            shaped((8 * pairs, 3 * LANES), F32),
            [ordered, weight, conn, node_hot],
            [pltpu.VMEM((48 * (levels - 2 * EDGE), refs), BF16)],
            scalar=False,
        )
        operands = [scalars, block_a, block_b, own_a, own_b, new_a, new_b, inner, weight] + shared
        if last:
            operands += squares + [cluster_ids.reshape(1, cell_count)]
            message = shaped((lax.axis_size(everyone), group_size, window + 2 * LANES), BF16)
            out_shape = [whole, message]
        else:
            out_shape = [whole, rim, rim]
        basal, *messages = call(
            functools.partial(adjoint_kernel, last, levels),
            "adjoint",
            out_shape,
            operands,
            [
                pltpu.VMEM((8 * pairs, 2 * padded_order), F32),
                pltpu.VMEM((8 * pairs, 3 * LANES), F32),
                pltpu.VMEM((48, refs), BF16),
            ],
        )
        if not last:
            carried = [basal, *swapped(*messages)]

    gathered = lax.all_to_all(messages[0], everyone, 0, 0)
    gathered = gathered.reshape(tiles, groups, *gathered.shape[1:])
    refined, gram = call(
        functools.partial(gram_kernel, POWER % 2 == 1, tiles, groups),
        "gram",
        [field, shaped((tiles, group_size, groups * group_size), F32)],
        [scalars, gathered, basal],
    )
    return (samples, refined.T, gram)


def solution(mesh):
    in_specs = (
        P("tiles", None, None),
        P("tiles", None),
        P("tiles", None),
        P("tiles", None, None),
        P("tiles"),
        P("tiles", None),
        P("tiles", "probes"),
        P("tiles"),
    )
    out_specs = (P("tiles", "probes"), P("tiles", "probes"), P(None, "probes", None))
    return jax.shard_map(shards, mesh=mesh, in_specs=in_specs, out_specs=out_specs, check_vma=False)
```

```python
import functools

import jax
import jax.numpy as jnp
from jax import lax
from jax.experimental import pallas as pl
from jax.experimental.pallas import tpu as pltpu
from jax.sharding import PartitionSpec as P

HALO = 512
POWER = 2
RIM = 64
LANES = 128
RADIX = 256
EDGE = HALO // RADIX
SHRINK = 2.0**-40
VMEM_BYTES = 16 * 1024 * 1024

F32 = jnp.float32
BF16 = jnp.bfloat16


def dot(a, b):
    return lax.dot_general(a, b, (((1,), (0,)), ((), ())), preferred_element_type=F32)


def dot_nt(a, b):
    return lax.dot_general(a, b, (((1,), (1,)), ((), ())), preferred_element_type=F32)


def split(x):
    hi = x.astype(BF16)
    return hi, (x - hi.astype(F32)).astype(BF16)


def rows_iota(shape):
    return lax.broadcasted_iota(jnp.int32, shape, 0)


def lanes_iota(shape):
    return lax.broadcasted_iota(jnp.int32, shape, 1)


def spread_matrix(node_slots, padded_order):
    shape = (2 * node_slots, 2 * padded_order)
    row = rows_iota(shape)
    start = (row // node_slots) * padded_order + 3 * (row % node_slots)
    gap = lanes_iota(shape) - start
    return jnp.where((gap >= 0) & (gap < 3), F32(1), F32(0)).astype(BF16)


def order_matrix(node_slots, padded_order):
    pair = 2 * node_slots
    shape = (2 * padded_order, 3 * pair)
    col = lanes_iota(shape)
    inner = col % pair
    source = (inner // node_slots) * padded_order + 3 * (inner % node_slots) + col // pair
    return jnp.where(rows_iota(shape) == source, F32(1), F32(0)).astype(BF16)


def colour_of(ids):
    return (ids % 2) == (rows_iota(ids.shape) % 2)


def by_side(tile, a, b):
    even = tile % 2 == 0
    return jnp.where(even, b, a), jnp.where(even, a, b)


def to_swaps(tile, for_next, for_previous):
    even = tile % 2 == 0
    return jnp.where(even, for_previous, for_next), jnp.where(even, for_next, for_previous)


def announce_kernel(signs_hbm, ids_hbm, weight_hbm, out_ref, signs, ids, lead, sems):
    loads = [
        pltpu.make_async_copy(signs_hbm, signs, sems.at[0]),
        pltpu.make_async_copy(ids_hbm, ids, sems.at[1]),
        pltpu.make_async_copy(weight_hbm.at[:, pl.ds(0, HALO)], lead, sems.at[2]),
    ]
    for load in loads:
        load.start()
    for load in loads:
        load.wait()
    colours = jnp.broadcast_to(ids[...], signs.shape)
    probes = jnp.where(colour_of(colours), (2 * signs[...] - 1).astype(F32), F32(0))
    out_ref[:8, :] = probes
    out_ref[8:, :] = jnp.zeros((8, RADIX), F32)
    for i in range(EDGE):
        out_ref[8 + 3 * i : 11 + 3 * i, :] = lead[:, i * RADIX : (i + 1) * RADIX]


def setup_kernel(
    conn_hbm,
    cell_hbm,
    friction_hbm,
    blocks_hbm,
    conn_ref,
    cell_ref,
    fr_ref,
    blocks_ref,
    node_hot_ref,
    level_hot_ref,
    cell_hot_ref,
    spread_ref,
    order_ref,
    conn_in,
    cell_in,
    friction_in,
    sems,
):
    loads = [
        pltpu.make_async_copy(conn_hbm, conn_in, sems.at[0]),
        pltpu.make_async_copy(cell_hbm, cell_in, sems.at[1]),
        pltpu.make_async_copy(friction_hbm, friction_in, sems.at[2]),
        pltpu.make_async_copy(blocks_hbm, blocks_ref, sems.at[3]),
    ]
    for load in loads:
        load.start()
    pairs = conn_ref.shape[0]
    slots, padded_order = fr_ref.shape
    node_slots = conn_in.shape[1]
    levels = level_hot_ref.shape[0] // 16
    window = 3 * LANES

    spread_ref[...] = spread_matrix(node_slots, padded_order)
    order_ref[...] = order_matrix(node_slots, padded_order)

    def paired(ref):
        return jnp.concatenate(
            [ref[pl.ds(0, pairs, stride=2), :], ref[pl.ds(1, pairs, stride=2), :]], axis=1
        )

    loads[0].wait()
    conn = paired(conn_in)
    conn_ref[...] = conn
    loads[1].wait()
    cells = paired(cell_in)
    cells = jnp.where(cells < RIM, cells + (window - RIM), cells - RIM)
    cell_ref[...] = cells
    rows = rows_iota((RADIX, LANES))
    for m in range(pairs):
        at = pl.ds(m * LANES, LANES)
        hot = rows == conn[m : m + 1, :] % RADIX
        node_hot_ref[:, at] = jnp.where(hot, F32(1), F32(0)).astype(BF16)
        which = jnp.broadcast_to(conn[m : m + 1, :] // RADIX, (16, LANES))
        for level in range(levels):
            hot = jnp.where(which == level, F32(1), F32(0)).astype(BF16)
            level_hot_ref[16 * level : 16 * level + 16, at] = hot
        hot = rows[:LANES] == cells[m : m + 1, :] % LANES
        cell_hot_ref[:, at] = jnp.where(hot, F32(1), F32(0)).astype(BF16)

    loads[2].wait()
    shape = (node_slots, padded_order)
    total = jnp.zeros((slots, padded_order), F32)
    for c in range(3):
        place = lanes_iota(shape) == 3 * rows_iota(shape) + c
        place = jnp.where(place, F32(1), F32(0)).astype(BF16)
        rest = friction_in[c]
        for _ in range(3):
            part = rest.astype(BF16)
            total = total + dot(part, place)
            rest = rest - part.astype(F32)
    fr_ref[...] = total
    loads[3].wait()


def spread_levels(v_ref, ordered, level_hot, levels, pairs):
    for m in range(pairs):
        at = pl.ds(m * LANES, LANES)
        values = [ordered[16 * m : 16 * m + 16, c * LANES : (c + 1) * LANES] for c in range(3)]
        for i, level in enumerate(levels):
            mask = level_hot[16 * level : 16 * level + 16, at]
            for c in range(3):
                row = 48 * i + 16 * c
                v_ref[row : row + 16, at] = values[c] * mask


def edge_levels(levels):
    return list(range(EDGE)) + list(range(levels - EDGE, levels))


def forward_kernel(step, tiles, levels, *refs):
    scalars, block_ref, block_a, block_b, *refs = refs
    first = step == 0
    if not first:
        basal_ref, rim_a, rim_b, *refs = refs
    conn_ref, cell_ref, fr_ref, blocks, node_hot, level_hot, cell_hot, *refs = refs
    spread_ref, order_ref, *refs = refs
    ordered_ref, a_ref, b_ref, *refs = refs
    if not first:
        squares_ref, *refs = refs
    if step == 1:
        field_ref, *refs = refs
    f_ref, v_ref = refs

    order = blocks.shape[1]
    padded_order = f_ref.shape[1] // 2
    pairs = blocks.shape[0] // 2
    tile = scalars[0]
    count = scalars[1]

    lane = lanes_iota((8, LANES))
    low = lane < RIM
    after, before = by_side(tile, block_a[:8, :], block_b[:8, :])
    starts = [
        block_ref[:8, :LANES],
        block_ref[:8, LANES:],
        jnp.where(low, after[:, :LANES], before[:, LANES:]),
    ]
    if first:
        parts = starts
    else:
        after, before = by_side(tile, rim_a[...], rim_b[...])
        parts = [basal_ref[:, i * LANES : (i + 1) * LANES] for i in range(3)]
        parts[0] = parts[0] + jnp.where(low, before, F32(0))
        parts[1] = parts[1] + jnp.where(low, F32(0), after)
        parts[2] = parts[2] + jnp.where(low, after, before)
        there = (low & (tile < tiles - 1)) | (~low & (tile > 0))
        parts[2] = jnp.where(there, parts[2], F32(0))
        kept = [(start != 0) if step % 2 == 0 else (start == 0) for start in starts]
        parts = [jnp.where(keep, part, F32(0)) for keep, part in zip(kept, parts)]
        if step == 1:
            field_ref[:, :LANES] = parts[0]
            field_ref[:, LANES:] = parts[1]
        squares_ref[...] = parts[0] * parts[0] + parts[1] * parts[1]
    window = jnp.concatenate(parts, axis=0)
    if step == 1:
        window = window * F32(SHRINK)

    cells = cell_ref[...]
    hi, lo = split(window)
    picked = dot(jnp.concatenate([hi, lo], axis=0), cell_hot[...])
    tops = []
    rests = []
    for m in range(pairs):
        part = picked[:, m * LANES : (m + 1) * LANES]
        which = cells[m : m + 1, :] // LANES
        for base, out in ((0, tops), (24, rests)):
            chosen = jnp.where(which == 0, part[base : base + 8], F32(0))
            for level in (1, 2):
                at = base + 8 * level
                chosen = jnp.where(which == level, part[at : at + 8], chosen)
            out.append(chosen)
    stacked = jnp.concatenate(tops + rests, axis=0).astype(BF16)
    spread = dot(stacked, spread_ref[...])
    half = 8 * pairs
    spread = spread[:half] + spread[half:]

    f_ref[...] = jnp.zeros_like(f_ref)
    for m in range(pairs):
        for side in range(2):
            at = side * padded_order
            slot = 2 * m + side
            inputs = spread[8 * m : 8 * m + 8, at : at + order] * fr_ref[slot : slot + 1, :order]
            if first:
                out = dot_nt(inputs.astype(BF16), blocks[slot])
            else:
                hi = inputs.astype(BF16).astype(F32)
                both = jnp.concatenate([hi, inputs - hi], axis=0).astype(BF16)
                out = dot_nt(both, blocks[slot])
                out = out[:8] + out[8:]
            out = jnp.where(slot < count, out, F32(0))
            hi = out.astype(BF16).astype(F32)
            f_ref[16 * m : 16 * m + 8, at : at + order] = hi
            f_ref[16 * m + 8 : 16 * m + 16, at : at + order] = out - hi

    ordered = dot(f_ref[...].astype(BF16), order_ref[...]).astype(BF16)
    ordered_ref[...] = ordered
    edges = edge_levels(levels)
    spread_levels(v_ref, ordered, level_hot, edges, pairs)
    rim = dot_nt(v_ref[...], node_hot[...])
    sums = [
        rim[16 * i : 16 * i + 8] + rim[16 * i + 8 : 16 * i + 16] for i in range(3 * len(edges))
    ]
    half = len(sums) // 2
    for i in range(half):
        lead, spill = sums[i], sums[half + i]
        a_ref[8 * i : 8 * i + 8, :], b_ref[8 * i : 8 * i + 8, :] = to_swaps(tile, spill, lead)


def inner_kernel(
    levels, ordered_ref, weight_ref, conn_ref, node_hot, level_hot, picked_ref, v_ref
):
    pairs = conn_ref.shape[0]
    conn = conn_ref[...]
    inside = list(range(EDGE, levels - EDGE))
    spread_levels(v_ref, ordered_ref, level_hot, inside, pairs)
    nodes = dot_nt(v_ref[...], node_hot[...])
    rows = []
    for i in range(3 * len(inside)):
        value = nodes[16 * i : 16 * i + 8] + nodes[16 * i + 8 : 16 * i + 16]
        at = inside[i // 3] * RADIX
        rows.append(value * weight_ref[i % 3 : i % 3 + 1, at : at + RADIX])
    weighted = jnp.concatenate(rows, axis=0).astype(BF16)
    step = 2
    for start in range(0, pairs, step):
        found = dot(weighted, node_hot[:, start * LANES : (start + step) * LANES])
        for i in range(step):
            m = start + i
            which = conn[m : m + 1, :] // RADIX
            part = found[:, i * LANES : (i + 1) * LANES]
            chosen = jnp.zeros((24, LANES), F32)
            for at, level in enumerate(inside):
                chosen = jnp.where(which == level, part[24 * at : 24 * at + 24], chosen)
            for c in range(3):
                picked_ref[8 * m : 8 * m + 8, c * LANES : (c + 1) * LANES] = chosen[8 * c : 8 * c + 8]


def adjoint_kernel(last, clusters, levels, *refs):
    scalars, block_a, block_b, own_a, own_b, new_a, new_b, inner_ref, weight_ref, *refs = refs
    conn_ref, cell_ref, fr_ref, blocks, node_hot, _, cell_hot, spread_ref, order_ref, *refs = refs
    if last:
        squares_1, squares_2, ids_ref, *refs = refs
        basal_ref, out_ref, p_ref, n_ref, v_ref = refs
    else:
        basal_ref, a_ref, b_ref, p_ref, n_ref, v_ref = refs

    order = blocks.shape[1]
    padded_order = p_ref.shape[1] // 2
    pairs = blocks.shape[0] // 2
    tile = scalars[0]
    count = scalars[1]

    spill, lead = by_side(tile, own_a[...] + new_a[...], own_b[...] + new_b[...])
    after, _ = by_side(tile, block_a[8:16, :], block_b[8:16, :])
    rows = []
    for i in range(3 * EDGE):
        at = (i // 3) * RADIX
        rows.append(lead[8 * i : 8 * i + 8] * weight_ref[i % 3 : i % 3 + 1, at : at + RADIX])
    for i in range(3 * EDGE):
        rows.append(spill[8 * i : 8 * i + 8] * after[i : i + 1, :])
    weighted = jnp.concatenate(rows, axis=0).astype(BF16)

    conn = conn_ref[...]
    edges = edge_levels(levels)
    step = 2
    for start in range(0, pairs, step):
        found = dot(weighted, node_hot[:, start * LANES : (start + step) * LANES])
        for i in range(step):
            m = start + i
            which = conn[m : m + 1, :] // RADIX
            part = found[:, i * LANES : (i + 1) * LANES]
            for c in range(3):
                value = inner_ref[8 * m : 8 * m + 8, c * LANES : (c + 1) * LANES]
                for at, level in enumerate(edges):
                    row = 24 * at + 8 * c
                    value = jnp.where(which == level, part[row : row + 8], value)
                n_ref[8 * m : 8 * m + 8, c * LANES : (c + 1) * LANES] = value
    natural = dot_nt(n_ref[...].astype(BF16), order_ref[...])
    p_ref[...] = jnp.zeros_like(p_ref)
    for m in range(pairs):
        for side in range(2):
            at = side * padded_order
            slot = 2 * m + side
            out = dot(natural[8 * m : 8 * m + 8, at : at + order].astype(BF16), blocks[slot])
            out = out * fr_ref[slot : slot + 1, :order]
            p_ref[8 * m : 8 * m + 8, at : at + order] = jnp.where(slot < count, out, F32(0))

    hi, lo = split(p_ref[...])
    partial = dot_nt(jnp.concatenate([hi, lo], axis=0), spread_ref[...])
    half = 8 * pairs
    partial = partial[:half] + partial[half:]
    cells = cell_ref[...]
    for m in range(pairs):
        which = cells[m : m + 1, :] // LANES
        value = partial[8 * m : 8 * m + 8, :]
        rows = jnp.concatenate([jnp.where(which == level, value, F32(0)) for level in range(3)], axis=0)
        hi = rows.astype(BF16).astype(F32)
        both = jnp.concatenate([hi, rows - hi], axis=0)
        v_ref[:, m * LANES : (m + 1) * LANES] = both.astype(BF16)
    basal = dot_nt(v_ref[...], cell_hot[...])
    basal = basal[:24] + basal[24:]
    parts = [basal[8 * i : 8 * i + 8] for i in range(3)]
    for i in range(3):
        basal_ref[:, i * LANES : (i + 1) * LANES] = parts[i]
    lane = lanes_iota((8, LANES))
    if not last:
        for_next = jnp.where(lane < RIM, parts[2], parts[1])
        for_previous = jnp.where(lane < RIM, parts[0], parts[2])
        a_ref[...], b_ref[...] = to_swaps(tile, for_next, for_previous)
        return

    ids = ids_ref[...]
    extra = jnp.zeros((8, LANES), F32)
    for i, ref in enumerate((squares_1, squares_2)):
        rest = jnp.sum(ref[...], axis=1, keepdims=True)
        for j in range(3):
            piece = rest.astype(BF16).astype(F32)
            extra = jnp.where(lane == 3 * i + j, piece, extra)
            rest = rest - piece
    for k in range(1, clusters):
        below = jnp.sum((ids < k).astype(F32), axis=1, keepdims=True)
        extra = jnp.where(lane == 8 + k, below, extra)
    message = jnp.concatenate(parts + [extra], axis=1).astype(BF16)
    for t in range(out_ref.shape[0]):
        out_ref[t] = message


def gram_kernel(keep_same, tiles, groups, scalars, g_ref, own_ref, field_ref, gram_ref):
    tile = scalars[0]
    group = scalars[2]
    clusters = gram_ref.shape[0]
    cell_count = tiles * 2 * LANES
    low = lanes_iota((8, LANES)) < RIM

    def factor_of(p):
        def add(t, acc):
            return acc + g_ref[t, p][:, 3 * LANES :].astype(F32)

        sums = lax.fori_loop(0, tiles, add, jnp.zeros((8, LANES), F32), unroll=tiles <= 8)
        first = jnp.sum(sums[:, :3], axis=1, keepdims=True)
        second = jnp.sum(sums[:, 3:6], axis=1, keepdims=True)
        scale = jnp.sqrt(first / cell_count + F32(1e-06))
        size = jnp.sqrt(second / cell_count) * F32(1 / SHRINK) / scale
        return F32(1 / SHRINK) / (scale * jnp.sqrt(size * size + F32(1e-06)))

    def ids_of(t):
        starts = g_ref[t, 0][:, 3 * LANES :].astype(F32)
        cell = lanes_iota((8, 2 * LANES)).astype(F32)
        ids = jnp.zeros(cell.shape, jnp.int32)
        for k in range(1, clusters):
            ids = ids + (cell >= starts[:, 8 + k : 9 + k]).astype(jnp.int32)
        return [ids[:, :LANES], ids[:, LANES:]]

    def field(t, p, ids, own=None):
        before = g_ref[jnp.maximum(t - 1, 0), p][:, 2 * LANES : 3 * LANES].astype(F32)
        after = g_ref[jnp.minimum(t + 1, tiles - 1), p][:, 2 * LANES : 3 * LANES].astype(F32)
        if own is None:
            own = g_ref[t, p][:, : 2 * LANES].astype(F32)
        parts = [
            own[:, :LANES] + jnp.where(low & (t > 0), before, F32(0)),
            own[:, LANES : 2 * LANES] + jnp.where(~low & (t < tiles - 1), after, F32(0)),
        ]
        return [
            jnp.where(colour_of(i) if keep_same else ~colour_of(i), part, F32(0))
            for i, part in zip(ids, parts)
        ]

    factors = [factor_of(p) for p in range(groups)]
    mine_factor = factors[0]
    for p in range(1, groups):
        mine_factor = jnp.where(group == p, factors[p], mine_factor)
    own = field(tile, group, ids_of(tile), own_ref[...])
    field_ref[:, :LANES] = own[0] * mine_factor
    field_ref[:, LANES:] = own[1] * mine_factor

    def add_tile(t, acc):
        ids = ids_of(t)
        every = [
            jnp.concatenate(field(t, p, ids), axis=1) * factors[p] for p in range(groups)
        ]
        mine = every[0]
        for p in range(1, groups):
            mine = jnp.where(group == p, every[p], mine)
        ids = jnp.concatenate(ids, axis=1)
        left = jnp.concatenate([jnp.where(ids == k, mine, F32(0)) for k in range(clusters)], axis=0)
        return acc + lax.dot_general(
            left,
            jnp.concatenate(every, axis=0),
            (((1,), (1,)), ((), ())),
            precision=lax.Precision.HIGHEST,
            preferred_element_type=F32,
        )

    acc = jnp.zeros((8 * clusters, 8 * groups), F32)
    acc = lax.fori_loop(0, tiles, add_tile, acc, unroll=tiles <= 8)
    gram_ref[...] = acc.reshape(gram_ref.shape)


def shards(
    blocks, connectivity, basal_map, friction, elem_counts, obs_weight, sign_bits, cluster_ids
):
    slots = blocks.shape[0]
    node_slots = connectivity.shape[1]
    node_count = obs_weight.shape[0]
    cell_count, group_size = sign_bits.shape
    tiles = lax.axis_size("tiles")
    groups = lax.axis_size("probes")
    pairs = slots * node_slots // LANES
    refs = pairs * LANES
    levels = (node_count + HALO) // RADIX
    padded_order = 2 * LANES
    window = cell_count + 2 * RIM

    smem = pl.BlockSpec(memory_space=pltpu.SMEM)
    vmem = pl.BlockSpec(memory_space=pltpu.VMEM)
    params = pltpu.CompilerParams(vmem_limit_bytes=VMEM_BYTES)
    shaped = jax.ShapeDtypeStruct

    hbm = pl.BlockSpec(memory_space=pltpu.HBM)

    def call(kernel, name, out_shape, operands, scratch=(), in_specs=None):
        if in_specs and in_specs[0] is hbm:
            operands = [pltpu.with_memory_space_constraint(x, pltpu.HBM) for x in operands]
        return pl.pallas_call(
            kernel,
            out_shape=out_shape,
            in_specs=in_specs or [smem] + [vmem] * (len(operands) - 1),
            out_specs=jax.tree.map(lambda _: vmem, out_shape),
            scratch_shapes=list(scratch),
            compiler_params=params,
            name=name,
        )(*operands)

    evens = range(0, tiles - 1, 2)
    odds = range(1, tiles - 1, 2)
    pairs_a = [(i, i + 1) for i in odds] + [(i + 1, i) for i in odds]
    pairs_b = [(i, i + 1) for i in evens] + [(i + 1, i) for i in evens]

    def swapped(a, b):
        return lax.ppermute(a, "tiles", pairs_a), lax.ppermute(b, "tiles", pairs_b)

    weight = obs_weight.T
    block = call(
        announce_kernel,
        "announce",
        shaped((16, cell_count), F32),
        [sign_bits.T, cluster_ids.reshape(1, cell_count), weight],
        [
            pltpu.VMEM((group_size, cell_count), jnp.int32),
            pltpu.VMEM((1, cell_count), jnp.int32),
            pltpu.VMEM((3, HALO), F32),
            pltpu.SemaphoreType.DMA((3,)),
        ],
        [hbm] * 3,
    )
    block_a, block_b = swapped(block, block)

    shared = call(
        setup_kernel,
        "setup",
        [
            shaped((pairs, LANES), jnp.int32),
            shaped((pairs, LANES), jnp.int32),
            shaped((slots, padded_order), F32),
            shaped(blocks.shape, BF16),
            shaped((RADIX, refs), BF16),
            shaped((16 * levels, refs), BF16),
            shaped((LANES, refs), BF16),
            shaped((LANES, 2 * padded_order), BF16),
            shaped((2 * padded_order, 3 * LANES), BF16),
        ],
        [connectivity, basal_map, friction.transpose(2, 0, 1), blocks],
        [
            pltpu.VMEM(connectivity.shape, jnp.int32),
            pltpu.VMEM(basal_map.shape, jnp.int32),
            pltpu.VMEM((3, slots, node_slots), F32),
            pltpu.SemaphoreType.DMA((4,)),
        ],
        [hbm] * 4,
    )
    scalars = jnp.stack(
        [lax.axis_index("tiles"), elem_counts[0], lax.axis_index("probes")]
    ).astype(jnp.int32)
    conn, node_hot, level_hot = shared[0], shared[4], shared[5]

    edge = shaped((24 * EDGE, RADIX), F32)
    rim = shaped((group_size, LANES), F32)
    whole = shaped((group_size, window), F32)
    field = shaped((group_size, cell_count), F32)
    everyone = ("tiles", "probes")

    carried = []
    squares = []
    samples = None
    for step in range(POWER + 1):
        last = step == POWER
        out_shape = [shaped((16 * pairs, 3 * LANES), BF16), edge, edge]
        out_shape += [rim] * (step > 0) + [field] * (step == 1)
        ordered, own_a, own_b, *extra = call(
            functools.partial(forward_kernel, step, tiles, levels),
            "forward",
            out_shape,
            [scalars, block, block_a, block_b] + carried + [*shared],
            [
                pltpu.VMEM((16 * pairs, 2 * padded_order), F32),
                pltpu.VMEM((96 * EDGE, refs), BF16),
            ],
        )
        squares += extra[:1]
        if step == 1:
            samples = extra[1].T
        new_a, new_b = swapped(own_a, own_b)
        inner = call(
            functools.partial(inner_kernel, levels),
            "inner",
            shaped((8 * pairs, 3 * LANES), F32),
            [ordered, weight, conn, node_hot, level_hot],
            [pltpu.VMEM((48 * (levels - 2 * EDGE), refs), BF16)],
            [vmem] * 5,
        )
        operands = [scalars, block_a, block_b, own_a, own_b, new_a, new_b, inner, weight, *shared]
        if last:
            operands += squares + [cluster_ids.reshape(1, cell_count)]
            message = shaped((lax.axis_size(everyone), group_size, window + LANES), BF16)
            out_shape = [whole, message]
        else:
            out_shape = [whole, rim, rim]
        basal, *messages = call(
            functools.partial(adjoint_kernel, last, tiles, levels),
            "adjoint",
            out_shape,
            operands,
            [
                pltpu.VMEM((8 * pairs, 2 * padded_order), F32),
                pltpu.VMEM((8 * pairs, 3 * LANES), F32),
                pltpu.VMEM((48, refs), BF16),
            ],
        )
        if not last:
            carried = [basal, *swapped(*messages)]

    gathered = lax.all_to_all(messages[0], everyone, 0, 0)
    gathered = gathered.reshape(tiles, groups, *gathered.shape[1:])
    refined, gram = call(
        functools.partial(gram_kernel, POWER % 2 == 1, tiles, groups),
        "gram",
        [field, shaped((tiles, group_size, groups * group_size), F32)],
        [scalars, gathered, basal],
    )
    return (samples, refined.T, gram)


def solution(mesh):
    in_specs = (
        P("tiles", None, None),
        P("tiles", None),
        P("tiles", None),
        P("tiles", None, None),
        P("tiles"),
        P("tiles", None),
        P("tiles", "probes"),
        P("tiles"),
    )
    out_specs = (P("tiles", "probes"), P("tiles", "probes"), P(None, "probes", None))
    return jax.shard_map(shards, mesh=mesh, in_specs=in_specs, out_specs=out_specs, check_vma=False)
```

```python
import functools

import jax
import jax.numpy as jnp
from jax import lax
from jax.experimental import pallas as pl
from jax.experimental.pallas import tpu as pltpu
from jax.sharding import PartitionSpec as P

HALO = 512
POWER = 2
RIM = 64
LANES = 128
RADIX = 512
EDGE = HALO // RADIX
SHRINK = 2.0**-40
VMEM_BYTES = 16 * 1024 * 1024

F32 = jnp.float32
BF16 = jnp.bfloat16


def dot(a, b):
    return lax.dot_general(a, b, (((1,), (0,)), ((), ())), preferred_element_type=F32)


def dot_nt(a, b):
    return lax.dot_general(a, b, (((1,), (1,)), ((), ())), preferred_element_type=F32)


def split(x):
    hi = x.astype(BF16)
    return hi, (x - hi.astype(F32)).astype(BF16)


def rows_iota(shape):
    return lax.broadcasted_iota(jnp.int32, shape, 0)


def lanes_iota(shape):
    return lax.broadcasted_iota(jnp.int32, shape, 1)


def spread_matrix(node_slots, padded_order):
    shape = (2 * node_slots, 2 * padded_order)
    row = rows_iota(shape)
    start = (row // node_slots) * padded_order + 3 * (row % node_slots)
    gap = lanes_iota(shape) - start
    return jnp.where((gap >= 0) & (gap < 3), F32(1), F32(0)).astype(BF16)


def order_matrix(node_slots, padded_order):
    pair = 2 * node_slots
    shape = (2 * padded_order, 3 * pair)
    col = lanes_iota(shape)
    inner = col % pair
    source = (inner // node_slots) * padded_order + 3 * (inner % node_slots) + col // pair
    return jnp.where(rows_iota(shape) == source, F32(1), F32(0)).astype(BF16)


def colour_of(ids):
    return (ids % 2) == (rows_iota(ids.shape) % 2)


def by_side(tile, a, b):
    even = tile % 2 == 0
    return jnp.where(even, b, a), jnp.where(even, a, b)


def to_swaps(tile, for_next, for_previous):
    even = tile % 2 == 0
    return jnp.where(even, for_previous, for_next), jnp.where(even, for_next, for_previous)


def announce_kernel(signs_hbm, ids_hbm, weight_hbm, out_ref, signs, ids, lead, sems):
    loads = [
        pltpu.make_async_copy(signs_hbm, signs, sems.at[0]),
        pltpu.make_async_copy(ids_hbm, ids, sems.at[1]),
        pltpu.make_async_copy(weight_hbm.at[:, pl.ds(0, HALO)], lead, sems.at[2]),
    ]
    for load in loads:
        load.start()
    for load in loads:
        load.wait()
    colours = jnp.broadcast_to(ids[...], signs.shape)
    probes = jnp.where(colour_of(colours), (2 * signs[...] - 1).astype(F32), F32(0))
    out_ref[:8, :] = probes
    out_ref[8:, :] = jnp.zeros_like(probes)
    half = HALO // 2
    out_ref[8:11, :] = lead[:, :half]
    out_ref[11:14, :] = lead[:, half:]


def setup_kernel(
    counts,
    conn_hbm,
    cell_hbm,
    friction_hbm,
    blocks_hbm,
    conn_ref,
    cell_ref,
    fr_ref,
    blocks_ref,
    turned_ref,
    node_hot_ref,
    level_hot_ref,
    cell_hot_ref,
    spread_ref,
    order_ref,
    conn_in,
    cell_in,
    friction_in,
    sems,
):
    loads = [
        pltpu.make_async_copy(conn_hbm, conn_in, sems.at[0]),
        pltpu.make_async_copy(cell_hbm, cell_in, sems.at[1]),
        pltpu.make_async_copy(friction_hbm, friction_in, sems.at[2]),
        pltpu.make_async_copy(blocks_hbm, blocks_ref, sems.at[3]),
    ]
    for load in loads:
        load.start()
    pairs = conn_ref.shape[0]
    slots, padded_order = fr_ref.shape
    node_slots = conn_in.shape[1]
    levels = level_hot_ref.shape[0] // 16
    window = 3 * LANES

    spread_ref[...] = spread_matrix(node_slots, padded_order)
    order_ref[...] = order_matrix(node_slots, padded_order)

    def paired(ref):
        return jnp.concatenate(
            [ref[pl.ds(0, pairs, stride=2), :], ref[pl.ds(1, pairs, stride=2), :]], axis=1
        )

    loads[0].wait()
    conn = paired(conn_in)
    conn_ref[...] = conn
    loads[1].wait()
    cells = paired(cell_in)
    cells = jnp.where(cells < RIM, cells + (window - RIM), cells - RIM)
    cell_ref[...] = cells
    rows = rows_iota((RADIX, LANES))
    for m in range(pairs):
        at = pl.ds(m * LANES, LANES)
        hot = rows == conn[m : m + 1, :] % RADIX
        node_hot_ref[:, at] = jnp.where(hot, F32(1), F32(0)).astype(BF16)
        which = jnp.broadcast_to(conn[m : m + 1, :] // RADIX, (16, LANES))
        for level in range(levels):
            hot = jnp.where(which == level, F32(1), F32(0)).astype(BF16)
            level_hot_ref[16 * level : 16 * level + 16, at] = hot
        hot = rows[:LANES] == cells[m : m + 1, :] % LANES
        cell_hot_ref[:, at] = jnp.where(hot, F32(1), F32(0)).astype(BF16)

    loads[2].wait()
    shape = (node_slots, padded_order)
    total = jnp.zeros((slots, padded_order), F32)
    for c in range(3):
        place = lanes_iota(shape) == 3 * rows_iota(shape) + c
        place = jnp.where(place, F32(1), F32(0)).astype(BF16)
        rest = friction_in[c]
        for _ in range(3):
            part = rest.astype(BF16)
            total = total + dot(part, place)
            rest = rest - part.astype(F32)
    fr_ref[...] = jnp.where(rows_iota(total.shape) < counts[0], total, F32(0))
    loads[3].wait()
    for slot in range(slots):
        turned_ref[slot] = blocks_ref[slot].T


def spread_levels(v_ref, ordered, level_hot, levels, pairs):
    for m in range(pairs):
        at = pl.ds(m * LANES, LANES)
        values = [ordered[16 * m : 16 * m + 16, c * LANES : (c + 1) * LANES] for c in range(3)]
        for i, level in enumerate(levels):
            mask = level_hot[16 * level : 16 * level + 16, at]
            for c in range(3):
                row = 48 * i + 16 * c
                v_ref[row : row + 16, at] = values[c] * mask


def edge_levels(levels):
    return list(range(EDGE)) + list(range(levels - EDGE, levels))


def forward_kernel(step, tiles, levels, *refs):
    block_ref, block_a, block_b, *refs = refs
    first = step == 0
    if not first:
        basal_ref, rim_a, rim_b, *refs = refs
    conn_ref, cell_ref, fr_ref, _, turned, node_hot, level_hot, cell_hot, *refs = refs
    spread_ref, order_ref, *refs = refs
    ordered_ref, a_ref, b_ref, *refs = refs
    if not first:
        squares_ref, *refs = refs
    if step == 1:
        field_ref, *refs = refs
    f_ref, v_ref = refs

    order = turned.shape[1]
    padded_order = f_ref.shape[1] // 2
    pairs = turned.shape[0] // 2
    tile = lax.axis_index("tiles")

    lane = lanes_iota((8, LANES))
    low = lane < RIM
    after, before = by_side(tile, block_a[:8, :], block_b[:8, :])
    starts = [
        block_ref[:8, :LANES],
        block_ref[:8, LANES:],
        jnp.where(low, after[:, :LANES], before[:, LANES:]),
    ]
    if first:
        parts = starts
    else:
        after, before = by_side(tile, rim_a[...], rim_b[...])
        parts = [basal_ref[:, i * LANES : (i + 1) * LANES] for i in range(3)]
        parts[0] = parts[0] + jnp.where(low, before, F32(0))
        parts[1] = parts[1] + jnp.where(low, F32(0), after)
        parts[2] = parts[2] + jnp.where(low, after, before)
        there = (low & (tile < tiles - 1)) | (~low & (tile > 0))
        parts[2] = jnp.where(there, parts[2], F32(0))
        kept = [(start != 0) if step % 2 == 0 else (start == 0) for start in starts]
        parts = [jnp.where(keep, part, F32(0)) for keep, part in zip(kept, parts)]
        if step == 1:
            field_ref[:, :LANES] = parts[0]
            field_ref[:, LANES:] = parts[1]
        squares_ref[...] = parts[0] * parts[0] + parts[1] * parts[1]
    window = jnp.concatenate(parts, axis=0)
    if step == 1:
        window = window * F32(SHRINK)

    cells = cell_ref[...]
    hi, lo = split(window)
    picked = dot(jnp.concatenate([hi, lo], axis=0), cell_hot[...])
    tops = []
    rests = []
    for m in range(pairs):
        part = picked[:, m * LANES : (m + 1) * LANES]
        which = cells[m : m + 1, :] // LANES
        for base, out in ((0, tops), (24, rests)):
            chosen = jnp.where(which == 0, part[base : base + 8], F32(0))
            for level in (1, 2):
                at = base + 8 * level
                chosen = jnp.where(which == level, part[at : at + 8], chosen)
            out.append(chosen)
    stacked = jnp.concatenate(tops + rests, axis=0).astype(BF16)
    spread = dot(stacked, spread_ref[...])
    half = 8 * pairs
    spread = spread[:half] + spread[half:]

    f_ref[...] = jnp.zeros_like(f_ref)
    for m in range(pairs):
        for side in range(2):
            at = side * padded_order
            slot = 2 * m + side
            inputs = spread[8 * m : 8 * m + 8, at : at + order] * fr_ref[slot : slot + 1, :order]
            if first:
                out = dot(inputs.astype(BF16), turned[slot])
            else:
                hi = inputs.astype(BF16).astype(F32)
                both = jnp.concatenate([hi, inputs - hi], axis=0).astype(BF16)
                out = dot(both, turned[slot])
                out = out[:8] + out[8:]
            hi = out.astype(BF16).astype(F32)
            f_ref[16 * m : 16 * m + 8, at : at + order] = hi
            f_ref[16 * m + 8 : 16 * m + 16, at : at + order] = out - hi

    ordered = dot(f_ref[...].astype(BF16), order_ref[...]).astype(BF16)
    ordered_ref[...] = ordered
    edges = edge_levels(levels)
    spread_levels(v_ref, ordered, level_hot, edges, pairs)
    rim = dot_nt(v_ref[...], node_hot[...])
    sums = [
        rim[16 * i : 16 * i + 8] + rim[16 * i + 8 : 16 * i + 16] for i in range(3 * len(edges))
    ]
    half = len(sums) // 2
    for i in range(half):
        lead, spill = sums[i], sums[half + i]
        a_ref[8 * i : 8 * i + 8, :], b_ref[8 * i : 8 * i + 8, :] = to_swaps(tile, spill, lead)


def inner_kernel(
    levels, ordered_ref, weight_ref, conn_ref, node_hot, level_hot, picked_ref, v_ref
):
    pairs = conn_ref.shape[0]
    conn = conn_ref[...]
    inside = list(range(EDGE, levels - EDGE))
    spread_levels(v_ref, ordered_ref, level_hot, inside, pairs)
    nodes = dot_nt(v_ref[...], node_hot[...])
    rows = []
    for i in range(3 * len(inside)):
        value = nodes[16 * i : 16 * i + 8] + nodes[16 * i + 8 : 16 * i + 16]
        at = inside[i // 3] * RADIX
        rows.append(value * weight_ref[i % 3 : i % 3 + 1, at : at + RADIX])
    weighted = jnp.concatenate(rows, axis=0).astype(BF16)
    step = 2
    for start in range(0, pairs, step):
        found = dot(weighted, node_hot[:, start * LANES : (start + step) * LANES])
        for i in range(step):
            m = start + i
            which = conn[m : m + 1, :] // RADIX
            part = found[:, i * LANES : (i + 1) * LANES]
            chosen = jnp.zeros((24, LANES), F32)
            for at, level in enumerate(inside):
                chosen = jnp.where(which == level, part[24 * at : 24 * at + 24], chosen)
            for c in range(3):
                picked_ref[8 * m : 8 * m + 8, c * LANES : (c + 1) * LANES] = chosen[8 * c : 8 * c + 8]


def adjoint_kernel(last, clusters, levels, *refs):
    block_ref, block_a, block_b, own_a, own_b, new_a, new_b, inner_ref, weight_ref, *refs = refs
    conn_ref, cell_ref, fr_ref, blocks, _, node_hot, _, cell_hot, *refs = refs
    spread_ref, order_ref, *refs = refs
    if last:
        squares_1, squares_2, ids_ref, *refs = refs
        basal_ref, out_ref, p_ref, n_ref, v_ref = refs
    else:
        basal_ref, a_ref, b_ref, p_ref, n_ref, v_ref = refs

    order = blocks.shape[1]
    padded_order = p_ref.shape[1] // 2
    pairs = blocks.shape[0] // 2
    tile = lax.axis_index("tiles")

    spill, lead = by_side(tile, own_a[...] + new_a[...], own_b[...] + new_b[...])
    after, before = by_side(tile, block_a[...], block_b[...])
    rows = [lead[8 * c : 8 * c + 8] * weight_ref[c : c + 1, :HALO] for c in range(3)]
    for c in range(3):
        weight = jnp.concatenate([after[8 + c : 9 + c, :], after[11 + c : 12 + c, :]], axis=1)
        rows.append(spill[8 * c : 8 * c + 8] * weight)
    weighted = jnp.concatenate(rows, axis=0).astype(BF16)

    conn = conn_ref[...]
    edges = edge_levels(levels)
    step = 2
    for start in range(0, pairs, step):
        found = dot(weighted, node_hot[:, start * LANES : (start + step) * LANES])
        for i in range(step):
            m = start + i
            which = conn[m : m + 1, :] // RADIX
            part = found[:, i * LANES : (i + 1) * LANES]
            for c in range(3):
                value = inner_ref[8 * m : 8 * m + 8, c * LANES : (c + 1) * LANES]
                for at, level in enumerate(edges):
                    row = 24 * at + 8 * c
                    value = jnp.where(which == level, part[row : row + 8], value)
                n_ref[8 * m : 8 * m + 8, c * LANES : (c + 1) * LANES] = value
    natural = dot_nt(n_ref[...].astype(BF16), order_ref[...])
    p_ref[...] = jnp.zeros_like(p_ref)
    for m in range(pairs):
        for side in range(2):
            at = side * padded_order
            slot = 2 * m + side
            out = dot(natural[8 * m : 8 * m + 8, at : at + order].astype(BF16), blocks[slot])
            out = out * fr_ref[slot : slot + 1, :order]
            p_ref[8 * m : 8 * m + 8, at : at + order] = out

    hi, lo = split(p_ref[...])
    partial = dot_nt(jnp.concatenate([hi, lo], axis=0), spread_ref[...])
    half = 8 * pairs
    partial = partial[:half] + partial[half:]
    cells = cell_ref[...]
    for m in range(pairs):
        which = cells[m : m + 1, :] // LANES
        value = partial[8 * m : 8 * m + 8, :]
        rows = jnp.concatenate([jnp.where(which == level, value, F32(0)) for level in range(3)], axis=0)
        hi = rows.astype(BF16).astype(F32)
        both = jnp.concatenate([hi, rows - hi], axis=0)
        v_ref[:, m * LANES : (m + 1) * LANES] = both.astype(BF16)
    basal = dot_nt(v_ref[...], cell_hot[...])
    basal = basal[:24] + basal[24:]
    parts = [basal[8 * i : 8 * i + 8] for i in range(3)]
    for i in range(3):
        basal_ref[:, i * LANES : (i + 1) * LANES] = parts[i]
    lane = lanes_iota((8, LANES))
    if not last:
        for_next = jnp.where(lane < RIM, parts[2], parts[1])
        for_previous = jnp.where(lane < RIM, parts[0], parts[2])
        a_ref[...], b_ref[...] = to_swaps(tile, for_next, for_previous)
        return

    starts = [
        block_ref[:1, :LANES],
        block_ref[:1, LANES:],
        jnp.where(lane[:1] < RIM, after[:1, :LANES], before[:1, LANES:]),
    ]
    packed = []
    for start, part in zip(starts, parts):
        even = start != 0
        rows = [jnp.where(even, part[r + 1 : r + 2], part[r : r + 1]) for r in range(0, 8, 2)]
        packed.append(jnp.concatenate(rows, axis=0))
    extra = jnp.zeros((8, LANES), F32)
    for i, ref in enumerate((squares_1, squares_2)):
        rest = jnp.sum(ref[...], axis=1, keepdims=True)
        for j in range(3):
            piece = rest.astype(BF16).astype(F32)
            extra = jnp.where(lane == 3 * i + j, piece, extra)
            rest = rest - piece
    moved = pltpu.roll(extra, 8, 1)
    rows = [extra[r : r + 1] + moved[r + 1 : r + 2] for r in range(0, 8, 2)]
    extra = jnp.concatenate(rows, axis=0)
    ids = ids_ref[...]
    for k in range(1, clusters):
        below = jnp.sum((ids < k).astype(F32), axis=1, keepdims=True)
        extra = jnp.where(lane[:4] == 16 + k, below, extra)
    top = jnp.concatenate([packed[0], packed[1]], axis=1)
    message = jnp.concatenate([top, jnp.concatenate([packed[2], extra], axis=1)], axis=0)
    message = message.astype(BF16)
    for t in range(out_ref.shape[0]):
        out_ref[t] = message


def gram_kernel(keep_same, tiles, groups, g_ref, own_ref, field_ref, gram_ref):
    tile = lax.axis_index("tiles")
    group = lax.axis_index("probes")
    clusters = gram_ref.shape[0]
    cell_count = tiles * 2 * LANES
    low = lanes_iota((8, LANES)) < RIM
    row = rows_iota((8, LANES))

    def twice(x):
        out = jnp.broadcast_to(x[:1], (8, LANES))
        for r in range(1, 4):
            out = jnp.where(row >= 2 * r, jnp.broadcast_to(x[r : r + 1], (8, LANES)), out)
        return out

    def piece_of(t, p, lower, at):
        part = g_ref[t, p].astype(F32)
        return twice(part[4 * lower : 4 * lower + 4, at * LANES : (at + 1) * LANES])

    def factor_of(p):
        def add(t, acc):
            return acc + g_ref[t, p].astype(F32)[4:, LANES:]

        sums = lax.fori_loop(0, tiles, add, jnp.zeros((4, LANES), F32), unroll=tiles <= 8)
        sums = twice(sums)
        sums = jnp.where(row % 2 == 0, sums, pltpu.roll(sums, LANES - 8, 1))
        first = jnp.sum(sums[:, :3], axis=1, keepdims=True)
        second = jnp.sum(sums[:, 3:6], axis=1, keepdims=True)
        scale = jnp.sqrt(first / cell_count + F32(1e-06))
        size = jnp.sqrt(second / cell_count) * F32(1 / SHRINK) / scale
        return F32(1 / SHRINK) / (scale * jnp.sqrt(size * size + F32(1e-06)))

    def ids_of(t):
        starts = piece_of(t, 0, 1, 1)
        cell = lanes_iota((8, 2 * LANES)).astype(F32)
        ids = jnp.zeros(cell.shape, jnp.int32)
        for k in range(1, clusters):
            ids = ids + (cell >= starts[:, 16 + k : 17 + k]).astype(jnp.int32)
        return [ids[:, :LANES], ids[:, LANES:]]

    def field(t, p, ids, own=None):
        before = piece_of(jnp.maximum(t - 1, 0), p, 1, 0)
        after = piece_of(jnp.minimum(t + 1, tiles - 1), p, 1, 0)
        if own is None:
            own = [piece_of(t, p, 0, at) for at in range(2)]
        parts = [
            own[0] + jnp.where(low & (t > 0), before, F32(0)),
            own[1] + jnp.where(~low & (t < tiles - 1), after, F32(0)),
        ]
        return [
            jnp.where(colour_of(i) if keep_same else ~colour_of(i), part, F32(0))
            for i, part in zip(ids, parts)
        ]

    factors = [factor_of(p) for p in range(groups)]
    mine_factor = factors[0]
    for p in range(1, groups):
        mine_factor = jnp.where(group == p, factors[p], mine_factor)
    own = [own_ref[:, at * LANES : (at + 1) * LANES] for at in range(2)]
    own = field(tile, group, ids_of(tile), own)
    field_ref[:, :LANES] = own[0] * mine_factor
    field_ref[:, LANES:] = own[1] * mine_factor

    def add_tile(t, acc):
        ids = ids_of(t)
        every = [
            jnp.concatenate(field(t, p, ids), axis=1) * factors[p] for p in range(groups)
        ]
        mine = every[0]
        for p in range(1, groups):
            mine = jnp.where(group == p, every[p], mine)
        ids = jnp.concatenate(ids, axis=1)
        left = jnp.concatenate([jnp.where(ids == k, mine, F32(0)) for k in range(clusters)], axis=0)
        return acc + lax.dot_general(
            left,
            jnp.concatenate(every, axis=0),
            (((1,), (1,)), ((), ())),
            precision=lax.Precision.HIGHEST,
            preferred_element_type=F32,
        )

    acc = jnp.zeros((8 * clusters, 8 * groups), F32)
    acc = lax.fori_loop(0, tiles, add_tile, acc, unroll=tiles <= 8)
    gram_ref[...] = acc.reshape(gram_ref.shape)


def shards(
    blocks, connectivity, basal_map, friction, elem_counts, obs_weight, sign_bits, cluster_ids
):
    slots = blocks.shape[0]
    node_slots = connectivity.shape[1]
    node_count = obs_weight.shape[0]
    cell_count, group_size = sign_bits.shape
    tiles = lax.axis_size("tiles")
    groups = lax.axis_size("probes")
    pairs = slots * node_slots // LANES
    refs = pairs * LANES
    levels = (node_count + HALO) // RADIX
    padded_order = 2 * LANES
    window = cell_count + 2 * RIM

    smem = pl.BlockSpec(memory_space=pltpu.SMEM)
    vmem = pl.BlockSpec(memory_space=pltpu.VMEM)
    params = pltpu.CompilerParams(vmem_limit_bytes=VMEM_BYTES)
    shaped = jax.ShapeDtypeStruct

    hbm = pl.BlockSpec(memory_space=pltpu.HBM)

    def call(kernel, name, out_shape, operands, scratch=(), in_specs=None):
        in_specs = in_specs or [vmem] * len(operands)
        operands = [
            pltpu.with_memory_space_constraint(x, pltpu.HBM) if spec is hbm else x
            for x, spec in zip(operands, in_specs)
        ]
        return pl.pallas_call(
            kernel,
            out_shape=out_shape,
            in_specs=in_specs,
            out_specs=jax.tree.map(lambda _: vmem, out_shape),
            scratch_shapes=list(scratch),
            compiler_params=params,
            name=name,
        )(*operands)

    evens = range(0, tiles - 1, 2)
    odds = range(1, tiles - 1, 2)
    pairs_a = [(i, i + 1) for i in odds] + [(i + 1, i) for i in odds]
    pairs_b = [(i, i + 1) for i in evens] + [(i + 1, i) for i in evens]

    def swapped(a, b):
        return lax.ppermute(a, "tiles", pairs_a), lax.ppermute(b, "tiles", pairs_b)

    weight = obs_weight.T
    block = call(
        announce_kernel,
        "announce",
        shaped((16, cell_count), F32),
        [sign_bits.T, cluster_ids.reshape(1, cell_count), weight],
        [
            pltpu.VMEM((group_size, cell_count), jnp.int32),
            pltpu.VMEM((1, cell_count), jnp.int32),
            pltpu.VMEM((3, HALO), F32),
            pltpu.SemaphoreType.DMA((3,)),
        ],
        [hbm] * 3,
    )
    block_a, block_b = swapped(block, block)

    shared = call(
        setup_kernel,
        "setup",
        [
            shaped((pairs, LANES), jnp.int32),
            shaped((pairs, LANES), jnp.int32),
            shaped((slots, padded_order), F32),
            shaped(blocks.shape, BF16),
            shaped(blocks.shape, BF16),
            shaped((RADIX, refs), BF16),
            shaped((16 * levels, refs), BF16),
            shaped((LANES, refs), BF16),
            shaped((LANES, 2 * padded_order), BF16),
            shaped((2 * padded_order, 3 * LANES), BF16),
        ],
        [elem_counts, connectivity, basal_map, friction.transpose(2, 0, 1), blocks],
        [
            pltpu.VMEM(connectivity.shape, jnp.int32),
            pltpu.VMEM(basal_map.shape, jnp.int32),
            pltpu.VMEM((3, slots, node_slots), F32),
            pltpu.SemaphoreType.DMA((4,)),
        ],
        [smem] + [hbm] * 4,
    )
    conn, node_hot, level_hot = shared[0], shared[5], shared[6]

    edge = shaped((24 * EDGE, RADIX), F32)
    rim = shaped((group_size, LANES), F32)
    whole = shaped((group_size, window), F32)
    field = shaped((group_size, cell_count), F32)
    everyone = ("tiles", "probes")

    carried = []
    squares = []
    samples = None
    for step in range(POWER + 1):
        last = step == POWER
        out_shape = [shaped((16 * pairs, 3 * LANES), BF16), edge, edge]
        out_shape += [rim] * (step > 0) + [field] * (step == 1)
        ordered, own_a, own_b, *extra = call(
            functools.partial(forward_kernel, step, tiles, levels),
            "forward",
            out_shape,
            [block, block_a, block_b] + carried + [*shared],
            [
                pltpu.VMEM((16 * pairs, 2 * padded_order), F32),
                pltpu.VMEM((96 * EDGE, refs), BF16),
            ],
        )
        squares += extra[:1]
        if step == 1:
            samples = extra[1].T
        new_a, new_b = swapped(own_a, own_b)
        inner = call(
            functools.partial(inner_kernel, levels),
            "inner",
            shaped((8 * pairs, 3 * LANES), F32),
            [ordered, weight, conn, node_hot, level_hot],
            [pltpu.VMEM((48 * (levels - 2 * EDGE), refs), BF16)],
        )
        operands = [block, block_a, block_b, own_a, own_b, new_a, new_b, inner, weight, *shared]
        if last:
            operands += squares + [cluster_ids.reshape(1, cell_count)]
            message = shaped((lax.axis_size(everyone), group_size, 2 * LANES), BF16)
            out_shape = [whole, message]
        else:
            out_shape = [whole, rim, rim]
        basal, *messages = call(
            functools.partial(adjoint_kernel, last, tiles, levels),
            "adjoint",
            out_shape,
            operands,
            [
                pltpu.VMEM((8 * pairs, 2 * padded_order), F32),
                pltpu.VMEM((8 * pairs, 3 * LANES), F32),
                pltpu.VMEM((48, refs), BF16),
            ],
        )
        if not last:
            carried = [basal, *swapped(*messages)]

    gathered = lax.all_to_all(messages[0], everyone, 0, 0)
    gathered = gathered.reshape(tiles, groups, *gathered.shape[1:])
    refined, gram = call(
        functools.partial(gram_kernel, POWER % 2 == 1, tiles, groups),
        "gram",
        [field, shaped((tiles, group_size, groups * group_size), F32)],
        [gathered, basal],
    )
    return (samples, refined.T, gram)


def solution(mesh):
    in_specs = (
        P("tiles", None, None),
        P("tiles", None),
        P("tiles", None),
        P("tiles", None, None),
        P("tiles"),
        P("tiles", None),
        P("tiles", "probes"),
        P("tiles"),
    )
    out_specs = (P("tiles", "probes"), P("tiles", "probes"), P(None, "probes", None))
    return jax.shard_map(shards, mesh=mesh, in_specs=in_specs, out_specs=out_specs, check_vma=False)
```

```python
import functools

import jax
import jax.numpy as jnp
from jax import lax
from jax.experimental import pallas as pl
from jax.experimental.pallas import tpu as pltpu
from jax.sharding import PartitionSpec as P

HALO = 512
POWER = 2
RIM = 64
LANES = 128
RADIX = 512
EDGE = HALO // RADIX
SHRINK = 2.0**-40
VMEM_BYTES = 16 * 1024 * 1024

F32 = jnp.float32
BF16 = jnp.bfloat16


def dot(a, b):
    return lax.dot_general(a, b, (((1,), (0,)), ((), ())), preferred_element_type=F32)


def dot_nt(a, b):
    return lax.dot_general(a, b, (((1,), (1,)), ((), ())), preferred_element_type=F32)


def split(x):
    hi = x.astype(BF16)
    return hi, (x - hi.astype(F32)).astype(BF16)


def rows_iota(shape):
    return lax.broadcasted_iota(jnp.int32, shape, 0)


def lanes_iota(shape):
    return lax.broadcasted_iota(jnp.int32, shape, 1)


def spread_matrix(node_slots, padded_order):
    shape = (2 * node_slots, 2 * padded_order)
    row = rows_iota(shape)
    start = (row // node_slots) * padded_order + 3 * (row % node_slots)
    gap = lanes_iota(shape) - start
    return jnp.where((gap >= 0) & (gap < 3), F32(1), F32(0)).astype(BF16)


def order_matrix(node_slots, padded_order):
    pair = 2 * node_slots
    shape = (2 * padded_order, 3 * pair)
    col = lanes_iota(shape)
    inner = col % pair
    source = (inner // node_slots) * padded_order + 3 * (inner % node_slots) + col // pair
    return jnp.where(rows_iota(shape) == source, F32(1), F32(0)).astype(BF16)


def colour_of(ids):
    return (ids % 2) == (rows_iota(ids.shape) % 2)


def by_side(tile, a, b):
    even = tile % 2 == 0
    return jnp.where(even, b, a), jnp.where(even, a, b)


def to_swaps(tile, for_next, for_previous):
    even = tile % 2 == 0
    return jnp.where(even, for_previous, for_next), jnp.where(even, for_next, for_previous)


def announce_kernel(signs_hbm, ids_hbm, weight_hbm, out_ref, signs, ids, lead, sems):
    loads = [
        pltpu.make_async_copy(signs_hbm, signs, sems.at[0]),
        pltpu.make_async_copy(ids_hbm, ids, sems.at[1]),
        pltpu.make_async_copy(weight_hbm.at[:, pl.ds(0, HALO)], lead, sems.at[2]),
    ]
    for load in loads:
        load.start()
    for load in loads:
        load.wait()
    colours = jnp.broadcast_to(ids[...], signs.shape)
    probes = jnp.where(colour_of(colours), (2 * signs[...] - 1).astype(F32), F32(0))
    out_ref[:8, :] = probes
    out_ref[8:, :] = jnp.zeros_like(probes)
    half = HALO // 2
    out_ref[8:11, :] = lead[:, :half]
    out_ref[11:14, :] = lead[:, half:]


def setup_kernel(
    counts,
    conn_hbm,
    cell_hbm,
    friction_hbm,
    blocks_hbm,
    conn_ref,
    cell_ref,
    fr_ref,
    blocks_ref,
    turned_ref,
    node_hot_ref,
    level_hot_ref,
    cell_hot_ref,
    spread_ref,
    order_ref,
    conn_in,
    cell_in,
    friction_in,
    sems,
):
    loads = [
        pltpu.make_async_copy(conn_hbm, conn_in, sems.at[0]),
        pltpu.make_async_copy(cell_hbm, cell_in, sems.at[1]),
        pltpu.make_async_copy(friction_hbm, friction_in, sems.at[2]),
        pltpu.make_async_copy(blocks_hbm, blocks_ref, sems.at[3]),
    ]
    for load in loads:
        load.start()
    pairs = conn_ref.shape[0]
    slots, padded_order = fr_ref.shape
    node_slots = conn_in.shape[1]
    levels = level_hot_ref.shape[0] // 16
    window = 3 * LANES

    spread_ref[...] = spread_matrix(node_slots, padded_order)
    order_ref[...] = order_matrix(node_slots, padded_order)

    def paired(ref):
        return jnp.concatenate(
            [ref[pl.ds(0, pairs, stride=2), :], ref[pl.ds(1, pairs, stride=2), :]], axis=1
        )

    loads[0].wait()
    conn = paired(conn_in)
    conn_ref[...] = conn
    loads[1].wait()
    cells = paired(cell_in)
    cells = jnp.where(cells < RIM, cells + (window - RIM), cells - RIM)
    cell_ref[...] = cells
    rows = rows_iota((RADIX, LANES))
    for m in range(pairs):
        at = pl.ds(m * LANES, LANES)
        hot = rows == conn[m : m + 1, :] % RADIX
        node_hot_ref[:, at] = jnp.where(hot, F32(1), F32(0)).astype(BF16)
        which = jnp.broadcast_to(conn[m : m + 1, :] // RADIX, (16, LANES))
        for level in range(levels):
            hot = jnp.where(which == level, F32(1), F32(0)).astype(BF16)
            level_hot_ref[16 * level : 16 * level + 16, at] = hot
        hot = rows[:LANES] == cells[m : m + 1, :] % LANES
        cell_hot_ref[:, at] = jnp.where(hot, F32(1), F32(0)).astype(BF16)

    loads[2].wait()
    shape = (node_slots, padded_order)
    total = jnp.zeros((slots, padded_order), F32)
    for c in range(3):
        place = lanes_iota(shape) == 3 * rows_iota(shape) + c
        place = jnp.where(place, F32(1), F32(0)).astype(BF16)
        rest = friction_in[c]
        for _ in range(3):
            part = rest.astype(BF16)
            total = total + dot(part, place)
            rest = rest - part.astype(F32)
    fr_ref[...] = jnp.where(rows_iota(total.shape) < counts[0], total, F32(0))
    loads[3].wait()
    for slot in range(slots):
        turned_ref[slot] = blocks_ref[slot].T


def spread_levels(v_ref, ordered, level_hot, levels, pairs):
    for m in range(pairs):
        at = pl.ds(m * LANES, LANES)
        values = [ordered[16 * m : 16 * m + 16, c * LANES : (c + 1) * LANES] for c in range(3)]
        for i, level in enumerate(levels):
            mask = level_hot[16 * level : 16 * level + 16, at]
            for c in range(3):
                row = 48 * i + 16 * c
                v_ref[row : row + 16, at] = values[c] * mask


def edge_levels(levels):
    return list(range(EDGE)) + list(range(levels - EDGE, levels))


def forward_kernel(step, tiles, levels, *refs):
    block_ref, block_a, block_b, *refs = refs
    first = step == 0
    if not first:
        basal_ref, rims, *refs = refs
    conn_ref, cell_ref, fr_ref, _, turned, node_hot, level_hot, cell_hot, *refs = refs
    spread_ref, order_ref, *refs = refs
    ordered_ref, a_ref, b_ref, *refs = refs
    if not first:
        squares_ref, *refs = refs
    if step == 1:
        field_ref, *refs = refs
    f_ref, v_ref = refs

    order = turned.shape[1]
    padded_order = f_ref.shape[1] // 2
    pairs = turned.shape[0] // 2
    tile = lax.axis_index("tiles")

    lane = lanes_iota((8, LANES))
    low = lane < RIM
    after, before = by_side(tile, block_a[:8, :], block_b[:8, :])
    starts = [
        block_ref[:8, :LANES],
        block_ref[:8, LANES:],
        jnp.where(low, after[:, :LANES], before[:, LANES:]),
    ]
    if first:
        parts = starts
    else:
        after, before = by_side(tile, rims[8:, :], rims[:8, :])
        parts = [basal_ref[:, i * LANES : (i + 1) * LANES] for i in range(3)]
        parts[0] = parts[0] + jnp.where(low, before, F32(0))
        parts[1] = parts[1] + jnp.where(low, F32(0), after)
        parts[2] = parts[2] + jnp.where(low, after, before)
        there = (low & (tile < tiles - 1)) | (~low & (tile > 0))
        parts[2] = jnp.where(there, parts[2], F32(0))
        kept = [(start != 0) if step % 2 == 0 else (start == 0) for start in starts]
        parts = [jnp.where(keep, part, F32(0)) for keep, part in zip(kept, parts)]
        if step == 1:
            field_ref[:, :LANES] = parts[0]
            field_ref[:, LANES:] = parts[1]
        squares_ref[...] = parts[0] * parts[0] + parts[1] * parts[1]
    window = jnp.concatenate(parts, axis=0)
    if step == 1:
        window = window * F32(SHRINK)

    cells = cell_ref[...]
    hi, lo = split(window)
    picked = dot(jnp.concatenate([hi, lo], axis=0), cell_hot[...])
    tops = []
    rests = []
    for m in range(pairs):
        part = picked[:, m * LANES : (m + 1) * LANES]
        which = cells[m : m + 1, :] // LANES
        for base, out in ((0, tops), (24, rests)):
            chosen = jnp.where(which == 0, part[base : base + 8], F32(0))
            for level in (1, 2):
                at = base + 8 * level
                chosen = jnp.where(which == level, part[at : at + 8], chosen)
            out.append(chosen)
    stacked = jnp.concatenate(tops + rests, axis=0).astype(BF16)
    spread = dot(stacked, spread_ref[...])
    half = 8 * pairs
    spread = spread[:half] + spread[half:]

    f_ref[...] = jnp.zeros_like(f_ref)
    for m in range(pairs):
        for side in range(2):
            at = side * padded_order
            slot = 2 * m + side
            inputs = spread[8 * m : 8 * m + 8, at : at + order] * fr_ref[slot : slot + 1, :order]
            if first:
                out = dot(inputs.astype(BF16), turned[slot])
            else:
                hi = inputs.astype(BF16).astype(F32)
                both = jnp.concatenate([hi, inputs - hi], axis=0).astype(BF16)
                out = dot(both, turned[slot])
                out = out[:8] + out[8:]
            hi = out.astype(BF16).astype(F32)
            f_ref[16 * m : 16 * m + 8, at : at + order] = hi
            f_ref[16 * m + 8 : 16 * m + 16, at : at + order] = out - hi

    ordered = dot(f_ref[...].astype(BF16), order_ref[...]).astype(BF16)
    ordered_ref[...] = ordered
    edges = edge_levels(levels)
    spread_levels(v_ref, ordered, level_hot, edges, pairs)
    rim = dot_nt(v_ref[...], node_hot[...])
    sums = [
        rim[16 * i : 16 * i + 8] + rim[16 * i + 8 : 16 * i + 16] for i in range(3 * len(edges))
    ]
    half = len(sums) // 2
    for i in range(half):
        lead, spill = sums[i], sums[half + i]
        a_ref[8 * i : 8 * i + 8, :], b_ref[8 * i : 8 * i + 8, :] = to_swaps(tile, spill, lead)


def inner_scatter_kernel(
    levels, ordered_ref, weight_ref, node_hot, level_hot, weighted_ref, v_ref
):
    pairs = v_ref.shape[1] // LANES
    inside = list(range(EDGE, levels - EDGE))
    spread_levels(v_ref, ordered_ref, level_hot, inside, pairs)
    nodes = dot_nt(v_ref[...], node_hot[...])
    rows = []
    for i in range(3 * len(inside)):
        value = nodes[16 * i : 16 * i + 8] + nodes[16 * i + 8 : 16 * i + 16]
        at = inside[i // 3] * RADIX
        rows.append(value * weight_ref[i % 3 : i % 3 + 1, at : at + RADIX])
    weighted_ref[...] = jnp.concatenate(rows, axis=0).astype(BF16)


def inner_gather_kernel(levels, weighted_ref, conn_ref, node_hot, picked_ref):
    pairs = conn_ref.shape[0]
    conn = conn_ref[...]
    inside = list(range(EDGE, levels - EDGE))
    weighted = weighted_ref[...]
    step = 2
    for start in range(0, pairs, step):
        found = dot(weighted, node_hot[:, start * LANES : (start + step) * LANES])
        for i in range(step):
            m = start + i
            which = conn[m : m + 1, :] // RADIX
            part = found[:, i * LANES : (i + 1) * LANES]
            chosen = jnp.zeros((24, LANES), F32)
            for at, level in enumerate(inside):
                chosen = jnp.where(which == level, part[24 * at : 24 * at + 24], chosen)
            for c in range(3):
                picked_ref[8 * m : 8 * m + 8, c * LANES : (c + 1) * LANES] = chosen[8 * c : 8 * c + 8]


def adjoint_kernel(last, clusters, levels, *refs):
    block_ref, block_a, block_b, own_a, own_b, new, inner_ref, weight_ref, *refs = refs
    conn_ref, cell_ref, fr_ref, blocks, _, node_hot, _, cell_hot, *refs = refs
    spread_ref, order_ref, *refs = refs
    if last:
        squares_1, squares_2, ids_ref, *refs = refs
        basal_ref, out_ref, p_ref, n_ref, v_ref = refs
    else:
        basal_ref, a_ref, b_ref, p_ref, n_ref, v_ref = refs

    order = blocks.shape[1]
    padded_order = p_ref.shape[1] // 2
    pairs = blocks.shape[0] // 2
    tile = lax.axis_index("tiles")

    spill, lead = by_side(tile, own_a[...] + new[24 * EDGE :, :], own_b[...] + new[: 24 * EDGE, :])
    after, before = by_side(tile, block_a[...], block_b[...])
    rows = [lead[8 * c : 8 * c + 8] * weight_ref[c : c + 1, :HALO] for c in range(3)]
    for c in range(3):
        weight = jnp.concatenate([after[8 + c : 9 + c, :], after[11 + c : 12 + c, :]], axis=1)
        rows.append(spill[8 * c : 8 * c + 8] * weight)
    weighted = jnp.concatenate(rows, axis=0).astype(BF16)

    conn = conn_ref[...]
    edges = edge_levels(levels)
    step = 2
    for start in range(0, pairs, step):
        found = dot(weighted, node_hot[:, start * LANES : (start + step) * LANES])
        for i in range(step):
            m = start + i
            which = conn[m : m + 1, :] // RADIX
            part = found[:, i * LANES : (i + 1) * LANES]
            for c in range(3):
                value = inner_ref[8 * m : 8 * m + 8, c * LANES : (c + 1) * LANES]
                for at, level in enumerate(edges):
                    row = 24 * at + 8 * c
                    value = jnp.where(which == level, part[row : row + 8], value)
                n_ref[8 * m : 8 * m + 8, c * LANES : (c + 1) * LANES] = value
    natural = dot_nt(n_ref[...].astype(BF16), order_ref[...])
    p_ref[...] = jnp.zeros_like(p_ref)
    for m in range(pairs):
        for side in range(2):
            at = side * padded_order
            slot = 2 * m + side
            out = dot(natural[8 * m : 8 * m + 8, at : at + order].astype(BF16), blocks[slot])
            out = out * fr_ref[slot : slot + 1, :order]
            p_ref[8 * m : 8 * m + 8, at : at + order] = out

    hi, lo = split(p_ref[...])
    partial = dot_nt(jnp.concatenate([hi, lo], axis=0), spread_ref[...])
    half = 8 * pairs
    partial = partial[:half] + partial[half:]
    cells = cell_ref[...]
    for m in range(pairs):
        which = cells[m : m + 1, :] // LANES
        value = partial[8 * m : 8 * m + 8, :]
        rows = jnp.concatenate([jnp.where(which == level, value, F32(0)) for level in range(3)], axis=0)
        hi = rows.astype(BF16).astype(F32)
        both = jnp.concatenate([hi, rows - hi], axis=0)
        v_ref[:, m * LANES : (m + 1) * LANES] = both.astype(BF16)
    basal = dot_nt(v_ref[...], cell_hot[...])
    basal = basal[:24] + basal[24:]
    parts = [basal[8 * i : 8 * i + 8] for i in range(3)]
    for i in range(3):
        basal_ref[:, i * LANES : (i + 1) * LANES] = parts[i]
    lane = lanes_iota((8, LANES))
    if not last:
        for_next = jnp.where(lane < RIM, parts[2], parts[1])
        for_previous = jnp.where(lane < RIM, parts[0], parts[2])
        a_ref[...], b_ref[...] = to_swaps(tile, for_next, for_previous)
        return

    starts = [
        block_ref[:1, :LANES],
        block_ref[:1, LANES:],
        jnp.where(lane[:1] < RIM, after[:1, :LANES], before[:1, LANES:]),
    ]
    packed = []
    for start, part in zip(starts, parts):
        even = start != 0
        rows = [jnp.where(even, part[r + 1 : r + 2], part[r : r + 1]) for r in range(0, 8, 2)]
        packed.append(jnp.concatenate(rows, axis=0))
    extra = jnp.zeros((8, LANES), F32)
    for i, ref in enumerate((squares_1, squares_2)):
        rest = jnp.sum(ref[...], axis=1, keepdims=True)
        for j in range(3):
            piece = rest.astype(BF16).astype(F32)
            extra = jnp.where(lane == 3 * i + j, piece, extra)
            rest = rest - piece
    moved = pltpu.roll(extra, 8, 1)
    rows = [extra[r : r + 1] + moved[r + 1 : r + 2] for r in range(0, 8, 2)]
    extra = jnp.concatenate(rows, axis=0)
    ids = ids_ref[...]
    for k in range(1, clusters):
        below = jnp.sum((ids < k).astype(F32), axis=1, keepdims=True)
        extra = jnp.where(lane[:4] == 16 + k, below, extra)
    top = jnp.concatenate([packed[0], packed[1]], axis=1)
    message = jnp.concatenate([top, jnp.concatenate([packed[2], extra], axis=1)], axis=0)
    message = message.astype(BF16)
    for t in range(out_ref.shape[0]):
        out_ref[t] = message


def gram_kernel(keep_same, tiles, groups, g_ref, own_ref, field_ref, gram_ref):
    tile = lax.axis_index("tiles")
    group = lax.axis_index("probes")
    clusters = gram_ref.shape[0]
    cell_count = tiles * 2 * LANES
    low = lanes_iota((8, LANES)) < RIM
    row = rows_iota((8, LANES))

    def twice(x):
        out = jnp.broadcast_to(x[:1], (8, LANES))
        for r in range(1, 4):
            out = jnp.where(row >= 2 * r, jnp.broadcast_to(x[r : r + 1], (8, LANES)), out)
        return out

    def piece_of(t, p, lower, at):
        part = g_ref[t, p].astype(F32)
        return twice(part[4 * lower : 4 * lower + 4, at * LANES : (at + 1) * LANES])

    def factor_of(p):
        def add(t, acc):
            return acc + g_ref[t, p].astype(F32)[4:, LANES:]

        sums = lax.fori_loop(0, tiles, add, jnp.zeros((4, LANES), F32), unroll=tiles <= 8)
        sums = twice(sums)
        sums = jnp.where(row % 2 == 0, sums, pltpu.roll(sums, LANES - 8, 1))
        first = jnp.sum(sums[:, :3], axis=1, keepdims=True)
        second = jnp.sum(sums[:, 3:6], axis=1, keepdims=True)
        scale = jnp.sqrt(first / cell_count + F32(1e-06))
        size = jnp.sqrt(second / cell_count) * F32(1 / SHRINK) / scale
        return F32(1 / SHRINK) / (scale * jnp.sqrt(size * size + F32(1e-06)))

    def ids_of(t):
        starts = piece_of(t, 0, 1, 1)
        cell = lanes_iota((8, 2 * LANES)).astype(F32)
        ids = jnp.zeros(cell.shape, jnp.int32)
        for k in range(1, clusters):
            ids = ids + (cell >= starts[:, 16 + k : 17 + k]).astype(jnp.int32)
        return [ids[:, :LANES], ids[:, LANES:]]

    def field(t, p, ids, own=None):
        before = piece_of(jnp.maximum(t - 1, 0), p, 1, 0)
        after = piece_of(jnp.minimum(t + 1, tiles - 1), p, 1, 0)
        if own is None:
            own = [piece_of(t, p, 0, at) for at in range(2)]
        parts = [
            own[0] + jnp.where(low & (t > 0), before, F32(0)),
            own[1] + jnp.where(~low & (t < tiles - 1), after, F32(0)),
        ]
        return [
            jnp.where(colour_of(i) if keep_same else ~colour_of(i), part, F32(0))
            for i, part in zip(ids, parts)
        ]

    factors = [factor_of(p) for p in range(groups)]
    mine_factor = factors[0]
    for p in range(1, groups):
        mine_factor = jnp.where(group == p, factors[p], mine_factor)
    own = [own_ref[:, at * LANES : (at + 1) * LANES] for at in range(2)]
    own = field(tile, group, ids_of(tile), own)
    field_ref[:, :LANES] = own[0] * mine_factor
    field_ref[:, LANES:] = own[1] * mine_factor

    def add_tile(t, acc):
        ids = ids_of(t)
        every = [
            jnp.concatenate(field(t, p, ids), axis=1) * factors[p] for p in range(groups)
        ]
        mine = every[0]
        for p in range(1, groups):
            mine = jnp.where(group == p, every[p], mine)
        ids = jnp.concatenate(ids, axis=1)
        left = jnp.concatenate([jnp.where(ids == k, mine, F32(0)) for k in range(clusters)], axis=0)
        return acc + lax.dot_general(
            left,
            jnp.concatenate(every, axis=0),
            (((1,), (1,)), ((), ())),
            precision=lax.Precision.HIGHEST,
            preferred_element_type=F32,
        )

    acc = jnp.zeros((8 * clusters, 8 * groups), F32)
    acc = lax.fori_loop(0, tiles, add_tile, acc, unroll=tiles <= 8)
    gram_ref[...] = acc.reshape(gram_ref.shape)


def shards(
    blocks, connectivity, basal_map, friction, elem_counts, obs_weight, sign_bits, cluster_ids
):
    slots = blocks.shape[0]
    node_slots = connectivity.shape[1]
    node_count = obs_weight.shape[0]
    cell_count, group_size = sign_bits.shape
    tiles = lax.axis_size("tiles")
    groups = lax.axis_size("probes")
    pairs = slots * node_slots // LANES
    refs = pairs * LANES
    levels = (node_count + HALO) // RADIX
    padded_order = 2 * LANES
    window = cell_count + 2 * RIM

    smem = pl.BlockSpec(memory_space=pltpu.SMEM)
    vmem = pl.BlockSpec(memory_space=pltpu.VMEM)
    params = pltpu.CompilerParams(vmem_limit_bytes=VMEM_BYTES)
    shaped = jax.ShapeDtypeStruct

    hbm = pl.BlockSpec(memory_space=pltpu.HBM)

    def call(kernel, name, out_shape, operands, scratch=(), in_specs=None):
        in_specs = in_specs or [vmem] * len(operands)
        operands = [
            pltpu.with_memory_space_constraint(x, pltpu.HBM) if spec is hbm else x
            for x, spec in zip(operands, in_specs)
        ]
        return pl.pallas_call(
            kernel,
            out_shape=out_shape,
            in_specs=in_specs,
            out_specs=jax.tree.map(lambda _: vmem, out_shape),
            scratch_shapes=list(scratch),
            compiler_params=params,
            name=name,
        )(*operands)

    evens = range(0, tiles - 1, 2)
    odds = range(1, tiles - 1, 2)
    pairs_a = [(i, i + 1) for i in odds] + [(i + 1, i) for i in odds]
    pairs_b = [(i, i + 1) for i in evens] + [(i + 1, i) for i in evens]

    def swapped(a, b):
        return lax.ppermute(a, "tiles", pairs_a), lax.ppermute(b, "tiles", pairs_b)

    relay = [(i, i + 2) for i in range(1, tiles - 2, 2)]
    relay += [(i, i - 2) for i in range(2, tiles, 2)]

    def passed(far):
        return lax.ppermute(far, "tiles", relay)

    def arrived(near, far):
        return lax.ppermute(jnp.concatenate([near, far], axis=0), "tiles", pairs_b)

    weight = obs_weight.T
    block = call(
        announce_kernel,
        "announce",
        shaped((16, cell_count), F32),
        [sign_bits.T, cluster_ids.reshape(1, cell_count), weight],
        [
            pltpu.VMEM((group_size, cell_count), jnp.int32),
            pltpu.VMEM((1, cell_count), jnp.int32),
            pltpu.VMEM((3, HALO), F32),
            pltpu.SemaphoreType.DMA((3,)),
        ],
        [hbm] * 3,
    )
    block_a, block_b = swapped(block, block)

    shared = call(
        setup_kernel,
        "setup",
        [
            shaped((pairs, LANES), jnp.int32),
            shaped((pairs, LANES), jnp.int32),
            shaped((slots, padded_order), F32),
            shaped(blocks.shape, BF16),
            shaped(blocks.shape, BF16),
            shaped((RADIX, refs), BF16),
            shaped((16 * levels, refs), BF16),
            shaped((LANES, refs), BF16),
            shaped((LANES, 2 * padded_order), BF16),
            shaped((2 * padded_order, 3 * LANES), BF16),
        ],
        [elem_counts, connectivity, basal_map, friction.transpose(2, 0, 1), blocks],
        [
            pltpu.VMEM(connectivity.shape, jnp.int32),
            pltpu.VMEM(basal_map.shape, jnp.int32),
            pltpu.VMEM((3, slots, node_slots), F32),
            pltpu.SemaphoreType.DMA((4,)),
        ],
        [smem] + [hbm] * 4,
    )
    conn, node_hot, level_hot = shared[0], shared[5], shared[6]

    edge = shaped((24 * EDGE, RADIX), F32)
    rim = shaped((group_size, LANES), F32)
    whole = shaped((group_size, window), F32)
    field = shaped((group_size, cell_count), F32)
    everyone = ("tiles", "probes")

    carried = []
    squares = []
    samples = None
    for step in range(POWER + 1):
        last = step == POWER
        out_shape = [shaped((16 * pairs, 3 * LANES), BF16), edge, edge]
        out_shape += [rim] * (step > 0) + [field] * (step == 1)
        ordered, own_a, own_b, *extra = call(
            functools.partial(forward_kernel, step, tiles, levels),
            "forward",
            out_shape,
            [block, block_a, block_b] + carried + [*shared],
            [
                pltpu.VMEM((16 * pairs, 2 * padded_order), F32),
                pltpu.VMEM((96 * EDGE, refs), BF16),
            ],
        )
        squares += extra[:1]
        if step == 1:
            samples = extra[1].T
        far = passed(own_a)
        weighted = call(
            functools.partial(inner_scatter_kernel, levels),
            "inner_scatter",
            shaped((24 * (levels - 2 * EDGE), RADIX), BF16),
            [ordered, weight, node_hot, level_hot],
            [pltpu.VMEM((48 * (levels - 2 * EDGE), refs), BF16)],
        )
        far, weighted = lax.optimization_barrier((far, weighted))
        new = arrived(own_b, far)
        inner = call(
            functools.partial(inner_gather_kernel, levels),
            "inner_gather",
            shaped((8 * pairs, 3 * LANES), F32),
            [weighted, conn, node_hot],
        )
        operands = [block, block_a, block_b, own_a, own_b, new, inner, weight, *shared]
        if last:
            operands += squares + [cluster_ids.reshape(1, cell_count)]
            message = shaped((lax.axis_size(everyone), group_size, 2 * LANES), BF16)
            out_shape = [whole, message]
        else:
            out_shape = [whole, rim, rim]
        basal, *messages = call(
            functools.partial(adjoint_kernel, last, tiles, levels),
            "adjoint",
            out_shape,
            operands,
            [
                pltpu.VMEM((8 * pairs, 2 * padded_order), F32),
                pltpu.VMEM((8 * pairs, 3 * LANES), F32),
                pltpu.VMEM((48, refs), BF16),
            ],
        )
        if not last:
            carried = [basal, arrived(messages[1], passed(messages[0]))]

    gathered = lax.all_to_all(messages[0], everyone, 0, 0)
    gathered = gathered.reshape(tiles, groups, *gathered.shape[1:])
    refined, gram = call(
        functools.partial(gram_kernel, POWER % 2 == 1, tiles, groups),
        "gram",
        [field, shaped((tiles, group_size, groups * group_size), F32)],
        [gathered, basal],
    )
    return (samples, refined.T, gram)


def solution(mesh):
    in_specs = (
        P("tiles", None, None),
        P("tiles", None),
        P("tiles", None),
        P("tiles", None, None),
        P("tiles"),
        P("tiles", None),
        P("tiles", "probes"),
        P("tiles"),
    )
    out_specs = (P("tiles", "probes"), P("tiles", "probes"), P(None, "probes", None))
    return jax.shard_map(shards, mesh=mesh, in_specs=in_specs, out_specs=out_specs, check_vma=False)
```

```python
import functools

import jax
import jax.numpy as jnp
from jax import lax
from jax.experimental import pallas as pl
from jax.experimental.pallas import tpu as pltpu
from jax.sharding import PartitionSpec as P

HALO = 512
POWER = 2
RIM = 64
LANES = 128
RADIX = 512
CHUNKS = 4
EDGE = HALO // RADIX
SHRINK = 2.0**-40
VMEM_BYTES = 16 * 1024 * 1024

F32 = jnp.float32
BF16 = jnp.bfloat16


def dot(a, b):
    return lax.dot_general(a, b, (((1,), (0,)), ((), ())), preferred_element_type=F32)


def split(x):
    hi = x.astype(BF16)
    return hi, (x - hi.astype(F32)).astype(BF16)


def rows_iota(shape):
    return lax.broadcasted_iota(jnp.int32, shape, 0)


def lanes_iota(shape):
    return lax.broadcasted_iota(jnp.int32, shape, 1)


def hot(mask):
    return jnp.where(mask, F32(1), F32(0)).astype(BF16)


def spread_matrix(node_slots, padded_order, turned=False):
    shape = (2 * node_slots, 2 * padded_order)
    row, col = rows_iota(shape), lanes_iota(shape)
    if turned:
        row, col = lanes_iota(shape[::-1]), rows_iota(shape[::-1])
    gap = col - ((row // node_slots) * padded_order + 3 * (row % node_slots))
    return hot((gap >= 0) & (gap < 3))


def order_matrix(node_slots, padded_order, turned=False):
    pair = 2 * node_slots
    shape = (2 * padded_order, 3 * pair)
    row, col = rows_iota(shape), lanes_iota(shape)
    if turned:
        row, col = lanes_iota(shape[::-1]), rows_iota(shape[::-1])
    inner = col % pair
    source = (inner // node_slots) * padded_order + 3 * (inner % node_slots) + col // pair
    return hot(row == source)


def colour_of(ids):
    return (ids % 2) == (rows_iota(ids.shape) % 2)


def by_side(tile, a, b):
    even = tile % 2 == 0
    return jnp.where(even, b, a), jnp.where(even, a, b)


def to_swaps(tile, for_next, for_previous):
    even = tile % 2 == 0
    return jnp.where(even, for_previous, for_next), jnp.where(even, for_next, for_previous)


def announce_kernel(signs_hbm, ids_hbm, weight_hbm, out_ref, signs, ids, lead, sems):
    loads = [
        pltpu.make_async_copy(signs_hbm, signs, sems.at[0]),
        pltpu.make_async_copy(ids_hbm, ids, sems.at[1]),
        pltpu.make_async_copy(weight_hbm.at[:, pl.ds(0, HALO)], lead, sems.at[2]),
    ]
    for load in loads:
        load.start()
    for load in loads:
        load.wait()
    colours = jnp.broadcast_to(ids[...], signs.shape)
    probes = jnp.where(colour_of(colours), (2 * signs[...] - 1).astype(F32), F32(0))
    out_ref[:8, :] = probes
    out_ref[8:, :] = jnp.zeros_like(probes)
    half = HALO // 2
    out_ref[8:11, :] = lead[:, :half]
    out_ref[11:14, :] = lead[:, half:]


def setup_kernel(
    counts,
    conn_hbm,
    cell_hbm,
    friction_hbm,
    blocks_hbm,
    conn_ref,
    cell_ref,
    fr_ref,
    blocks_ref,
    turned_ref,
    node_hot_ref,
    node_turn_ref,
    level_hot_ref,
    cell_hot_ref,
    cell_turn_ref,
    spread_ref,
    spread_turn_ref,
    order_ref,
    order_turn_ref,
    conn_in,
    cell_in,
    friction_in,
    sems,
):
    pairs = conn_ref.shape[0]
    slots, padded_order = fr_ref.shape
    node_slots = conn_in.shape[1]
    levels = level_hot_ref.shape[0] // 16
    window = 3 * LANES
    chunks = sems.shape[0] - 3
    chunk = slots // chunks

    loads = [
        pltpu.make_async_copy(source, target, sems.at[i])
        for i, (source, target) in enumerate(
            [
                (conn_hbm, conn_in),
                (cell_hbm, cell_in),
                (friction_hbm, friction_in),
            ]
        )
    ]
    for i in range(chunks):
        at = pl.ds(i * chunk, chunk)
        loads.append(pltpu.make_async_copy(blocks_hbm.at[at], blocks_ref.at[at], sems.at[3 + i]))
    for load in loads:
        load.start()

    spread_ref[...] = spread_matrix(node_slots, padded_order)
    spread_turn_ref[...] = spread_matrix(node_slots, padded_order, True)
    order_ref[...] = order_matrix(node_slots, padded_order)
    order_turn_ref[...] = order_matrix(node_slots, padded_order, True)

    def paired(ref):
        return jnp.concatenate(
            [ref[pl.ds(0, pairs, stride=2), :], ref[pl.ds(1, pairs, stride=2), :]], axis=1
        )

    for load in loads[:3]:
        load.wait()
    conn = paired(conn_in)
    conn_ref[...] = conn
    cells = paired(cell_in)
    cells = jnp.where(cells < RIM, cells + (window - RIM), cells - RIM)
    cell_ref[...] = cells
    node_low = conn % RADIX
    cell_low = cells % LANES
    node_column = node_low.astype(F32).T
    cell_column = cell_low.astype(F32).T

    shape = (node_slots, padded_order)
    total = jnp.zeros((slots, padded_order), F32)
    for c in range(3):
        place = hot(lanes_iota(shape) == 3 * rows_iota(shape) + c)
        rest = friction_in[c]
        for _ in range(3):
            part = rest.astype(BF16)
            total = total + dot(part, place)
            rest = rest - part.astype(F32)
    live = rows_iota(total.shape) < counts[0]
    fr_ref[...] = jnp.where(live, total, F32(0))

    rows = rows_iota((RADIX, LANES))
    lanes = lanes_iota((LANES, RADIX)).astype(F32)
    for i in range(chunks):
        loads[3 + i].wait()
        for slot in range(i * chunk, (i + 1) * chunk):
            turned_ref[slot] = blocks_ref[slot].T
            if slot % 2:
                continue
            m = slot // 2
            at = pl.ds(m * LANES, LANES)
            node_hot_ref[:, at] = hot(rows == node_low[m : m + 1, :])
            node_turn_ref[at, :] = hot(lanes == node_column[:, m : m + 1])
            which = jnp.broadcast_to(conn[m : m + 1, :] // RADIX, (16, LANES))
            for level in range(levels):
                level_hot_ref[16 * level : 16 * level + 16, at] = hot(which == level)
            cell_hot_ref[:, at] = hot(rows[:LANES] == cell_low[m : m + 1, :])
            cell_turn_ref[at, :] = hot(lanes[:, :LANES] == cell_column[:, m : m + 1])


def spread_levels(v_ref, ordered, level_hot, levels, pairs):
    for m in range(pairs):
        at = pl.ds(m * LANES, LANES)
        values = [ordered[16 * m : 16 * m + 16, c * LANES : (c + 1) * LANES] for c in range(3)]
        for i, level in enumerate(levels):
            mask = level_hot[16 * level : 16 * level + 16, at]
            for c in range(3):
                row = 48 * i + 16 * c
                v_ref[row : row + 16, at] = values[c] * mask


def edge_levels(levels):
    return list(range(EDGE)) + list(range(levels - EDGE, levels))


def forward_kernel(step, tiles, levels, *refs):
    block_ref, block_a, block_b, *refs = refs
    first = step == 0
    if not first:
        basal_ref, rim_a, rim_b, *refs = refs
    _, cell_ref, fr_ref, _, turned, _, node_turn, level_hot, cell_hot, _, *refs = refs
    spread_ref, _, order_ref, _, *refs = refs
    ordered_ref, a_ref, b_ref, *refs = refs
    if not first:
        squares_ref, *refs = refs
    if step == 1:
        field_ref, *refs = refs
    f_ref, v_ref = refs

    order = turned.shape[1]
    padded_order = f_ref.shape[1] // 2
    pairs = turned.shape[0] // 2
    tile = lax.axis_index("tiles")

    lane = lanes_iota((8, LANES))
    low = lane < RIM
    after, before = by_side(tile, block_a[:8, :], block_b[:8, :])
    starts = [
        block_ref[:8, :LANES],
        block_ref[:8, LANES:],
        jnp.where(low, after[:, :LANES], before[:, LANES:]),
    ]
    if first:
        parts = starts
    else:
        after, before = by_side(tile, rim_a[...], rim_b[...])
        parts = [basal_ref[:, i * LANES : (i + 1) * LANES] for i in range(3)]
        parts[0] = parts[0] + jnp.where(low, before, F32(0))
        parts[1] = parts[1] + jnp.where(low, F32(0), after)
        parts[2] = parts[2] + jnp.where(low, after, before)
        there = (low & (tile < tiles - 1)) | (~low & (tile > 0))
        parts[2] = jnp.where(there, parts[2], F32(0))
        kept = [(start != 0) if step % 2 == 0 else (start == 0) for start in starts]
        parts = [jnp.where(keep, part, F32(0)) for keep, part in zip(kept, parts)]
        if step == 1:
            field_ref[:, :LANES] = parts[0]
            field_ref[:, LANES:] = parts[1]
        squares_ref[...] = parts[0] * parts[0] + parts[1] * parts[1]
    window = jnp.concatenate(parts, axis=0)
    if step == 1:
        window = window * F32(SHRINK)

    cells = cell_ref[...]
    hi, lo = split(window)
    picked = dot(jnp.concatenate([hi, lo], axis=0), cell_hot[...])
    tops = []
    rests = []
    for m in range(pairs):
        part = picked[:, m * LANES : (m + 1) * LANES]
        which = cells[m : m + 1, :] // LANES
        for base, out in ((0, tops), (24, rests)):
            chosen = jnp.where(which == 0, part[base : base + 8], F32(0))
            for level in (1, 2):
                at = base + 8 * level
                chosen = jnp.where(which == level, part[at : at + 8], chosen)
            out.append(chosen)
    stacked = jnp.concatenate(tops + rests, axis=0).astype(BF16)
    spread = dot(stacked, spread_ref[...])
    half = 8 * pairs
    spread = spread[:half] + spread[half:]

    f_ref[...] = jnp.zeros_like(f_ref)
    for m in range(pairs):
        for side in range(2):
            at = side * padded_order
            slot = 2 * m + side
            inputs = spread[8 * m : 8 * m + 8, at : at + order] * fr_ref[slot : slot + 1, :order]
            if first:
                out = dot(inputs.astype(BF16), turned[slot])
            else:
                hi = inputs.astype(BF16).astype(F32)
                both = jnp.concatenate([hi, inputs - hi], axis=0).astype(BF16)
                out = dot(both, turned[slot])
                out = out[:8] + out[8:]
            hi = out.astype(BF16).astype(F32)
            f_ref[16 * m : 16 * m + 8, at : at + order] = hi
            f_ref[16 * m + 8 : 16 * m + 16, at : at + order] = out - hi

    ordered = dot(f_ref[...].astype(BF16), order_ref[...]).astype(BF16)
    ordered_ref[...] = ordered
    edges = edge_levels(levels)
    spread_levels(v_ref, ordered, level_hot, edges, pairs)
    rim = dot(v_ref[...], node_turn[...])
    sums = [
        rim[16 * i : 16 * i + 8] + rim[16 * i + 8 : 16 * i + 16] for i in range(3 * len(edges))
    ]
    half = len(sums) // 2
    for i in range(half):
        lead, spill = sums[i], sums[half + i]
        a_ref[8 * i : 8 * i + 8, :], b_ref[8 * i : 8 * i + 8, :] = to_swaps(tile, spill, lead)


def inner_kernel(
    levels, ordered_ref, weight_ref, conn_ref, node_hot, node_turn, level_hot, picked_ref, v_ref
):
    pairs = conn_ref.shape[0]
    conn = conn_ref[...]
    inside = list(range(EDGE, levels - EDGE))
    spread_levels(v_ref, ordered_ref, level_hot, inside, pairs)
    nodes = dot(v_ref[...], node_turn[...])
    rows = []
    for i in range(3 * len(inside)):
        value = nodes[16 * i : 16 * i + 8] + nodes[16 * i + 8 : 16 * i + 16]
        at = inside[i // 3] * RADIX
        rows.append(value * weight_ref[i % 3 : i % 3 + 1, at : at + RADIX])
    weighted = jnp.concatenate(rows, axis=0).astype(BF16)
    step = 2
    for start in range(0, pairs, step):
        found = dot(weighted, node_hot[:, start * LANES : (start + step) * LANES])
        for i in range(step):
            m = start + i
            which = conn[m : m + 1, :] // RADIX
            part = found[:, i * LANES : (i + 1) * LANES]
            chosen = jnp.zeros((24, LANES), F32)
            for at, level in enumerate(inside):
                chosen = jnp.where(which == level, part[24 * at : 24 * at + 24], chosen)
            for c in range(3):
                picked_ref[8 * m : 8 * m + 8, c * LANES : (c + 1) * LANES] = chosen[8 * c : 8 * c + 8]


def adjoint_kernel(last, clusters, levels, *refs):
    block_ref, block_a, block_b, own_a, own_b, new_a, new_b, inner_ref, weight_ref, *refs = refs
    conn_ref, cell_ref, fr_ref, blocks, _, node_hot, _, _, _, cell_turn, *refs = refs
    _, spread_turn, _, order_turn, *refs = refs
    if last:
        squares_1, squares_2, ids_ref, *refs = refs
        basal_ref, out_ref, p_ref, n_ref, v_ref = refs
    else:
        basal_ref, a_ref, b_ref, p_ref, n_ref, v_ref = refs

    order = blocks.shape[1]
    padded_order = p_ref.shape[1] // 2
    pairs = blocks.shape[0] // 2
    tile = lax.axis_index("tiles")

    spill, lead = by_side(tile, own_a[...] + new_a[...], own_b[...] + new_b[...])
    after, before = by_side(tile, block_a[...], block_b[...])
    rows = [lead[8 * c : 8 * c + 8] * weight_ref[c : c + 1, :HALO] for c in range(3)]
    for c in range(3):
        weight = jnp.concatenate([after[8 + c : 9 + c, :], after[11 + c : 12 + c, :]], axis=1)
        rows.append(spill[8 * c : 8 * c + 8] * weight)
    weighted = jnp.concatenate(rows, axis=0).astype(BF16)

    conn = conn_ref[...]
    edges = edge_levels(levels)
    step = 2
    for start in range(0, pairs, step):
        found = dot(weighted, node_hot[:, start * LANES : (start + step) * LANES])
        for i in range(step):
            m = start + i
            which = conn[m : m + 1, :] // RADIX
            part = found[:, i * LANES : (i + 1) * LANES]
            for c in range(3):
                value = inner_ref[8 * m : 8 * m + 8, c * LANES : (c + 1) * LANES]
                for at, level in enumerate(edges):
                    row = 24 * at + 8 * c
                    value = jnp.where(which == level, part[row : row + 8], value)
                n_ref[8 * m : 8 * m + 8, c * LANES : (c + 1) * LANES] = value
    natural = dot(n_ref[...].astype(BF16), order_turn[...])
    p_ref[...] = jnp.zeros_like(p_ref)
    for m in range(pairs):
        for side in range(2):
            at = side * padded_order
            slot = 2 * m + side
            out = dot(natural[8 * m : 8 * m + 8, at : at + order].astype(BF16), blocks[slot])
            out = out * fr_ref[slot : slot + 1, :order]
            p_ref[8 * m : 8 * m + 8, at : at + order] = out

    hi, lo = split(p_ref[...])
    partial = dot(jnp.concatenate([hi, lo], axis=0), spread_turn[...])
    half = 8 * pairs
    partial = partial[:half] + partial[half:]
    cells = cell_ref[...]
    for m in range(pairs):
        which = cells[m : m + 1, :] // LANES
        value = partial[8 * m : 8 * m + 8, :]
        rows = jnp.concatenate([jnp.where(which == level, value, F32(0)) for level in range(3)], axis=0)
        hi = rows.astype(BF16).astype(F32)
        both = jnp.concatenate([hi, rows - hi], axis=0)
        v_ref[:, m * LANES : (m + 1) * LANES] = both.astype(BF16)
    basal = dot(v_ref[...], cell_turn[...])
    basal = basal[:24] + basal[24:]
    parts = [basal[8 * i : 8 * i + 8] for i in range(3)]
    for i in range(3):
        basal_ref[:, i * LANES : (i + 1) * LANES] = parts[i]
    lane = lanes_iota((8, LANES))
    if not last:
        for_next = jnp.where(lane < RIM, parts[2], parts[1])
        for_previous = jnp.where(lane < RIM, parts[0], parts[2])
        a_ref[...], b_ref[...] = to_swaps(tile, for_next, for_previous)
        return

    starts = [
        block_ref[:1, :LANES],
        block_ref[:1, LANES:],
        jnp.where(lane[:1] < RIM, after[:1, :LANES], before[:1, LANES:]),
    ]
    packed = []
    for start, part in zip(starts, parts):
        even = start != 0
        rows = [jnp.where(even, part[r + 1 : r + 2], part[r : r + 1]) for r in range(0, 8, 2)]
        packed.append(jnp.concatenate(rows, axis=0))
    extra = jnp.zeros((8, LANES), F32)
    for i, ref in enumerate((squares_1, squares_2)):
        rest = jnp.sum(ref[...], axis=1, keepdims=True)
        for j in range(3):
            piece = rest.astype(BF16).astype(F32)
            extra = jnp.where(lane == 3 * i + j, piece, extra)
            rest = rest - piece
    moved = pltpu.roll(extra, 8, 1)
    rows = [extra[r : r + 1] + moved[r + 1 : r + 2] for r in range(0, 8, 2)]
    extra = jnp.concatenate(rows, axis=0)
    ids = ids_ref[...]
    for k in range(1, clusters):
        below = jnp.sum((ids < k).astype(F32), axis=1, keepdims=True)
        extra = jnp.where(lane[:4] == 16 + k, below, extra)
    top = jnp.concatenate([packed[0], packed[1]], axis=1)
    message = jnp.concatenate([top, jnp.concatenate([packed[2], extra], axis=1)], axis=0)
    message = message.astype(BF16)
    for t in range(out_ref.shape[0]):
        out_ref[t] = message


def gram_kernel(
    keep_same, tiles, groups, g_ref, own_ref, samples_in, samples_ref, field_ref, gram_ref
):
    samples_ref[...] = samples_in[...]
    tile = lax.axis_index("tiles")
    group = lax.axis_index("probes")
    clusters = gram_ref.shape[0]
    cell_count = tiles * 2 * LANES
    low = lanes_iota((8, LANES)) < RIM
    row = rows_iota((8, LANES))

    def twice(x):
        out = jnp.broadcast_to(x[:1], (8, LANES))
        for r in range(1, 4):
            out = jnp.where(row >= 2 * r, jnp.broadcast_to(x[r : r + 1], (8, LANES)), out)
        return out

    def piece_of(t, p, lower, at):
        part = g_ref[t, p].astype(F32)
        return twice(part[4 * lower : 4 * lower + 4, at * LANES : (at + 1) * LANES])

    def factor_of(p):
        def add(t, acc):
            return acc + g_ref[t, p].astype(F32)[4:, LANES:]

        sums = lax.fori_loop(0, tiles, add, jnp.zeros((4, LANES), F32), unroll=tiles <= 8)
        sums = twice(sums)
        sums = jnp.where(row % 2 == 0, sums, pltpu.roll(sums, LANES - 8, 1))
        first = jnp.sum(sums[:, :3], axis=1, keepdims=True)
        second = jnp.sum(sums[:, 3:6], axis=1, keepdims=True)
        scale = jnp.sqrt(first / cell_count + F32(1e-06))
        size = jnp.sqrt(second / cell_count) * F32(1 / SHRINK) / scale
        return F32(1 / SHRINK) / (scale * jnp.sqrt(size * size + F32(1e-06)))

    def ids_of(t):
        starts = piece_of(t, 0, 1, 1)
        cell = lanes_iota((8, 2 * LANES)).astype(F32)
        ids = jnp.zeros(cell.shape, jnp.int32)
        for k in range(1, clusters):
            ids = ids + (cell >= starts[:, 16 + k : 17 + k]).astype(jnp.int32)
        return [ids[:, :LANES], ids[:, LANES:]]

    def field(t, p, ids, own=None):
        before = piece_of(jnp.maximum(t - 1, 0), p, 1, 0)
        after = piece_of(jnp.minimum(t + 1, tiles - 1), p, 1, 0)
        if own is None:
            own = [piece_of(t, p, 0, at) for at in range(2)]
        parts = [
            own[0] + jnp.where(low & (t > 0), before, F32(0)),
            own[1] + jnp.where(~low & (t < tiles - 1), after, F32(0)),
        ]
        return [
            jnp.where(colour_of(i) if keep_same else ~colour_of(i), part, F32(0))
            for i, part in zip(ids, parts)
        ]

    factors = [factor_of(p) for p in range(groups)]
    mine_factor = factors[0]
    for p in range(1, groups):
        mine_factor = jnp.where(group == p, factors[p], mine_factor)
    own = [own_ref[:, at * LANES : (at + 1) * LANES] for at in range(2)]
    own = field(tile, group, ids_of(tile), own)
    field_ref[:, :LANES] = own[0] * mine_factor
    field_ref[:, LANES:] = own[1] * mine_factor

    def add_tile(t, acc):
        ids = ids_of(t)
        every = [
            jnp.concatenate(field(t, p, ids), axis=1) * factors[p] for p in range(groups)
        ]
        mine = every[0]
        for p in range(1, groups):
            mine = jnp.where(group == p, every[p], mine)
        ids = jnp.concatenate(ids, axis=1)
        left = jnp.concatenate([jnp.where(ids == k, mine, F32(0)) for k in range(clusters)], axis=0)
        return acc + lax.dot_general(
            left,
            jnp.concatenate(every, axis=0),
            (((1,), (1,)), ((), ())),
            precision=lax.Precision.HIGHEST,
            preferred_element_type=F32,
        )

    acc = jnp.zeros((8 * clusters, 8 * groups), F32)
    acc = lax.fori_loop(0, tiles, add_tile, acc, unroll=tiles <= 8)
    gram_ref[...] = acc.reshape(gram_ref.shape)


def shards(
    blocks, connectivity, basal_map, friction, elem_counts, obs_weight, sign_bits, cluster_ids
):
    slots = blocks.shape[0]
    node_slots = connectivity.shape[1]
    node_count = obs_weight.shape[0]
    cell_count, group_size = sign_bits.shape
    tiles = lax.axis_size("tiles")
    groups = lax.axis_size("probes")
    pairs = slots * node_slots // LANES
    refs = pairs * LANES
    levels = (node_count + HALO) // RADIX
    padded_order = 2 * LANES
    window = cell_count + 2 * RIM

    vmem = pl.BlockSpec(memory_space=pltpu.VMEM)
    params = pltpu.CompilerParams(vmem_limit_bytes=VMEM_BYTES)
    shaped = jax.ShapeDtypeStruct

    hbm = pl.BlockSpec(memory_space=pltpu.HBM)
    smem = pl.BlockSpec(memory_space=pltpu.SMEM)

    def call(kernel, name, out_shape, operands, scratch=(), in_specs=None):
        in_specs = in_specs or [vmem] * len(operands)
        operands = [
            pltpu.with_memory_space_constraint(x, pltpu.HBM) if spec is hbm else x
            for x, spec in zip(operands, in_specs)
        ]
        return pl.pallas_call(
            kernel,
            out_shape=out_shape,
            in_specs=in_specs,
            out_specs=jax.tree.map(lambda _: vmem, out_shape),
            scratch_shapes=list(scratch),
            compiler_params=params,
            name=name,
        )(*operands)

    evens = range(0, tiles - 1, 2)
    odds = range(1, tiles - 1, 2)
    pairs_a = [(i, i + 1) for i in odds] + [(i + 1, i) for i in odds]
    pairs_b = [(i, i + 1) for i in evens] + [(i + 1, i) for i in evens]

    def swapped(a, b):
        return lax.ppermute(a, "tiles", pairs_a), lax.ppermute(b, "tiles", pairs_b)

    weight = obs_weight.T
    block = call(
        announce_kernel,
        "announce",
        shaped((16, cell_count), F32),
        [sign_bits.T, cluster_ids.reshape(1, cell_count), weight],
        [
            pltpu.VMEM((group_size, cell_count), jnp.int32),
            pltpu.VMEM((1, cell_count), jnp.int32),
            pltpu.VMEM((3, HALO), F32),
            pltpu.SemaphoreType.DMA((3,)),
        ],
        [hbm] * 3,
    )
    block_a, block_b = swapped(block, block)

    shared = call(
        setup_kernel,
        "setup",
        [
            shaped((pairs, LANES), jnp.int32),
            shaped((pairs, LANES), jnp.int32),
            shaped((slots, padded_order), F32),
            shaped(blocks.shape, BF16),
            shaped(blocks.shape, BF16),
            shaped((RADIX, refs), BF16),
            shaped((refs, RADIX), BF16),
            shaped((16 * levels, refs), BF16),
            shaped((LANES, refs), BF16),
            shaped((refs, LANES), BF16),
            shaped((LANES, 2 * padded_order), BF16),
            shaped((2 * padded_order, LANES), BF16),
            shaped((2 * padded_order, 3 * LANES), BF16),
            shaped((3 * LANES, 2 * padded_order), BF16),
        ],
        [
            elem_counts,
            connectivity,
            basal_map,
            friction.transpose(2, 0, 1),
            blocks,
        ],
        [
            pltpu.VMEM(connectivity.shape, jnp.int32),
            pltpu.VMEM(basal_map.shape, jnp.int32),
            pltpu.VMEM((3, slots, node_slots), F32),
            pltpu.SemaphoreType.DMA((3 + CHUNKS,)),
        ],
        [smem] + [hbm] * 4,
    )
    conn, node_hot, node_turn, level_hot = shared[0], *shared[5:8]

    edge = shaped((24 * EDGE, RADIX), F32)
    rim = shaped((group_size, LANES), F32)
    whole = shaped((group_size, window), F32)
    field = shaped((group_size, cell_count), F32)
    everyone = ("tiles", "probes")

    carried = []
    squares = []
    samples = None
    for step in range(POWER + 1):
        last = step == POWER
        out_shape = [shaped((16 * pairs, 3 * LANES), BF16), edge, edge]
        out_shape += [rim] * (step > 0) + [field] * (step == 1)
        ordered, own_a, own_b, *extra = call(
            functools.partial(forward_kernel, step, tiles, levels),
            "forward",
            out_shape,
            [block, block_a, block_b] + carried + [*shared],
            [
                pltpu.VMEM((16 * pairs, 2 * padded_order), F32),
                pltpu.VMEM((96 * EDGE, refs), BF16),
            ],
        )
        squares += extra[:1]
        if step == 1:
            samples = extra[1]
        new_a, new_b = swapped(own_a, own_b)
        inner = call(
            functools.partial(inner_kernel, levels),
            "inner",
            shaped((8 * pairs, 3 * LANES), F32),
            [ordered, weight, conn, node_hot, node_turn, level_hot],
            [pltpu.VMEM((48 * (levels - 2 * EDGE), refs), BF16)],
        )
        operands = [block, block_a, block_b, own_a, own_b, new_a, new_b, inner, weight, *shared]
        if last:
            operands += squares + [cluster_ids.reshape(1, cell_count)]
            message = shaped((lax.axis_size(everyone), group_size, 2 * LANES), BF16)
            out_shape = [whole, message]
        else:
            out_shape = [whole, rim, rim]
        basal, *messages = call(
            functools.partial(adjoint_kernel, last, tiles, levels),
            "adjoint",
            out_shape,
            operands,
            [
                pltpu.VMEM((8 * pairs, 2 * padded_order), F32),
                pltpu.VMEM((8 * pairs, 3 * LANES), F32),
                pltpu.VMEM((48, refs), BF16),
            ],
        )
        if not last:
            carried = [basal, *swapped(*messages)]

    gathered = lax.all_to_all(messages[0], everyone, 0, 0)
    gathered = gathered.reshape(tiles, groups, *gathered.shape[1:])
    samples, refined, gram = call(
        functools.partial(gram_kernel, POWER % 2 == 1, tiles, groups),
        "gram",
        [field, field, shaped((tiles, group_size, groups * group_size), F32)],
        [gathered, basal, samples],
    )
    return (samples.T, refined.T, gram)


def solution(mesh):
    in_specs = (
        P("tiles", None, None),
        P("tiles", None),
        P("tiles", None),
        P("tiles", None, None),
        P("tiles"),
        P("tiles", None),
        P("tiles", "probes"),
        P("tiles"),
    )
    out_specs = (P("tiles", "probes"), P("tiles", "probes"), P(None, "probes", None))
    return jax.shard_map(shards, mesh=mesh, in_specs=in_specs, out_specs=out_specs, check_vma=False)
```

```python
import functools

import jax
import jax.numpy as jnp
from jax import lax
from jax.experimental import pallas as pl
from jax.experimental.pallas import tpu as pltpu
from jax.sharding import PartitionSpec as P

HALO = 512
POWER = 2
RIM = 64
LANES = 128
RADIX = 512
EDGE_RADIX = 256
EDGE = HALO // EDGE_RADIX
SHRINK = 2.0**-40
VMEM_BYTES = 16 * 1024 * 1024

F32 = jnp.float32
BF16 = jnp.bfloat16


def dot(a, b):
    return lax.dot_general(a, b, (((1,), (0,)), ((), ())), preferred_element_type=F32)


def dot_nt(a, b):
    return lax.dot_general(a, b, (((1,), (1,)), ((), ())), preferred_element_type=F32)


def split(x):
    hi = x.astype(BF16)
    return hi, (x - hi.astype(F32)).astype(BF16)


def rows_iota(shape):
    return lax.broadcasted_iota(jnp.int32, shape, 0)


def lanes_iota(shape):
    return lax.broadcasted_iota(jnp.int32, shape, 1)


def hot(mask):
    return jnp.where(mask, F32(1), F32(0)).astype(BF16)


def spread_matrix(node_slots, padded_order, turned=False):
    shape = (2 * node_slots, 2 * padded_order)
    row, col = rows_iota(shape), lanes_iota(shape)
    if turned:
        row, col = lanes_iota(shape[::-1]), rows_iota(shape[::-1])
    gap = col - ((row // node_slots) * padded_order + 3 * (row % node_slots))
    return hot((gap >= 0) & (gap < 3))


def order_matrix(node_slots, padded_order, turned=False):
    pair = 2 * node_slots
    shape = (2 * padded_order, 3 * pair)
    row, col = rows_iota(shape), lanes_iota(shape)
    if turned:
        row, col = lanes_iota(shape[::-1]), rows_iota(shape[::-1])
    inner = col % pair
    source = (inner // node_slots) * padded_order + 3 * (inner % node_slots) + col // pair
    return hot(row == source)


def colour_of(ids):
    return (ids % 2) == (rows_iota(ids.shape) % 2)


def by_side(tile, a, b):
    even = tile % 2 == 0
    return jnp.where(even, b, a), jnp.where(even, a, b)


def to_swaps(tile, for_next, for_previous):
    even = tile % 2 == 0
    return jnp.where(even, for_previous, for_next), jnp.where(even, for_next, for_previous)


def announce_kernel(signs_hbm, ids_hbm, weight_hbm, out_ref, again_ref, signs, ids, lead, sems):
    loads = [
        pltpu.make_async_copy(signs_hbm, signs, sems.at[0]),
        pltpu.make_async_copy(ids_hbm, ids, sems.at[1]),
        pltpu.make_async_copy(weight_hbm.at[:, pl.ds(0, HALO)], lead, sems.at[2]),
    ]
    for load in loads:
        load.start()
    for load in loads:
        load.wait()
    colours = jnp.broadcast_to(ids[...], signs.shape)
    probes = jnp.where(colour_of(colours), (2 * signs[...] - 1).astype(F32), F32(0))
    out_ref[:8, :] = probes
    out_ref[8:, :] = jnp.zeros_like(probes)
    half = HALO // 2
    out_ref[8:11, :] = lead[:, :half]
    out_ref[11:14, :] = lead[:, half:]
    again_ref[...] = out_ref[...]


def setup_kernel(
    levels,
    counts,
    conn_hbm,
    cell_hbm,
    friction_hbm,
    blocks_hbm,
    conn_ref,
    cell_ref,
    fr_ref,
    blocks_ref,
    node_hot_ref,
    edge_hot_ref,
    edge_turn_ref,
    inside_ref,
    edges_ref,
    cell_hot_ref,
    cell_turn_ref,
    spread_ref,
    spread_turn_ref,
    order_ref,
    order_turn_ref,
    conn_in,
    cell_in,
    friction_in,
    sems,
):
    pairs = conn_ref.shape[0]
    slots, padded_order = fr_ref.shape
    node_slots = conn_in.shape[1]
    inside, edges = levels_of(levels)
    window = 3 * LANES

    loads = [
        pltpu.make_async_copy(source, target, sems.at[i])
        for i, (source, target) in enumerate(
            [
                (conn_hbm, conn_in),
                (cell_hbm, cell_in),
                (friction_hbm, friction_in),
                (blocks_hbm, blocks_ref),
            ]
        )
    ]
    for load in loads:
        load.start()

    spread_ref[...] = spread_matrix(node_slots, padded_order)
    spread_turn_ref[...] = spread_matrix(node_slots, padded_order, True)
    order_ref[...] = order_matrix(node_slots, padded_order)
    order_turn_ref[...] = order_matrix(node_slots, padded_order, True)

    def paired(ref):
        return jnp.concatenate(
            [ref[pl.ds(0, pairs, stride=2), :], ref[pl.ds(1, pairs, stride=2), :]], axis=1
        )

    for load in loads[:3]:
        load.wait()
    conn = paired(conn_in)
    conn_ref[...] = conn
    cells = paired(cell_in)
    cells = jnp.where(cells < RIM, cells + (window - RIM), cells - RIM)
    cell_ref[...] = cells
    node_low = conn % RADIX
    cell_low = cells % LANES
    edge_column = (conn % EDGE_RADIX).astype(F32).T
    cell_column = cell_low.astype(F32).T

    shape = (node_slots, padded_order)
    total = jnp.zeros((slots, padded_order), F32)
    for c in range(3):
        place = hot(lanes_iota(shape) == 3 * rows_iota(shape) + c)
        rest = friction_in[c]
        for _ in range(3):
            part = rest.astype(BF16)
            total = total + dot(part, place)
            rest = rest - part.astype(F32)
    live = rows_iota(total.shape) < counts[0]
    fr_ref[...] = jnp.where(live, total, F32(0))

    rows = rows_iota((RADIX, LANES))
    lanes = lanes_iota((LANES, EDGE_RADIX)).astype(F32)
    for m in range(pairs):
        at = pl.ds(m * LANES, LANES)
        mine = hot(rows == node_low[m : m + 1, :])
        node_hot_ref[:, at] = mine
        edge_hot_ref[:, at] = mine[:EDGE_RADIX] + mine[EDGE_RADIX:]
        edge_turn_ref[at, :] = hot(lanes == edge_column[:, m : m + 1])
        which = jnp.broadcast_to(conn[m : m + 1, :], (16, LANES))
        for i, level in enumerate(inside):
            inside_ref[16 * i : 16 * i + 16, at] = hot(which // RADIX == level)
        for i, level in enumerate(edges):
            edges_ref[16 * i : 16 * i + 16, at] = hot(which // EDGE_RADIX == level)
        cell_hot_ref[:, at] = hot(rows[:LANES] == cell_low[m : m + 1, :])
        cell_turn_ref[at, :] = hot(lanes[:, :LANES] == cell_column[:, m : m + 1])
    loads[3].wait()


def turn_kernel(blocks, turned_ref):
    for slot in range(blocks.shape[0]):
        turned_ref[slot] = blocks[slot].T


def spread_levels(v_ref, ordered, level_hot, pairs):
    for m in range(pairs):
        at = pl.ds(m * LANES, LANES)
        values = [ordered[16 * m : 16 * m + 16, c * LANES : (c + 1) * LANES] for c in range(3)]
        for i in range(level_hot.shape[0] // 16):
            mask = level_hot[16 * i : 16 * i + 16, at]
            for c in range(3):
                row = 48 * i + 16 * c
                v_ref[row : row + 16, at] = values[c] * mask


def levels_of(levels):
    ratio = RADIX // EDGE_RADIX
    ends = list(range(EDGE)) + list(range(ratio * levels - EDGE, ratio * levels))
    return list(range(1, levels - 1)), ends


def forward_kernel(step, tiles, *refs):
    block_ref, block_a, block_b, *refs = refs
    first = step == 0
    if not first:
        basal_ref, rim_a, rim_b, *refs = refs
    cell_ref, fr_ref, factors, edge_turn, edges_ref, cell_hot, spread_ref, order_ref, *refs = refs
    ordered_ref, a_ref, b_ref, *refs = refs
    if not first:
        squares_ref, *refs = refs
    if step == 1:
        field_ref, *refs = refs
    f_ref, v_ref = refs

    order = factors.shape[1]
    padded_order = f_ref.shape[1] // 2
    pairs = factors.shape[0] // 2
    tile = lax.axis_index("tiles")

    lane = lanes_iota((8, LANES))
    low = lane < RIM
    after, before = by_side(tile, block_a[:8, :], block_b[:8, :])
    starts = [
        block_ref[:8, :LANES],
        block_ref[:8, LANES:],
        jnp.where(low, after[:, :LANES], before[:, LANES:]),
    ]
    if first:
        parts = starts
    else:
        after, before = by_side(tile, rim_a[...], rim_b[...])
        parts = [basal_ref[:, i * LANES : (i + 1) * LANES] for i in range(3)]
        parts[0] = parts[0] + jnp.where(low, before, F32(0))
        parts[1] = parts[1] + jnp.where(low, F32(0), after)
        parts[2] = parts[2] + jnp.where(low, after, before)
        there = (low & (tile < tiles - 1)) | (~low & (tile > 0))
        parts[2] = jnp.where(there, parts[2], F32(0))
        kept = [(start != 0) if step % 2 == 0 else (start == 0) for start in starts]
        parts = [jnp.where(keep, part, F32(0)) for keep, part in zip(kept, parts)]
        if step == 1:
            field_ref[:, :LANES] = parts[0]
            field_ref[:, LANES:] = parts[1]
        squares_ref[...] = parts[0] * parts[0] + parts[1] * parts[1]
    window = jnp.concatenate(parts, axis=0)
    if step == 1:
        window = window * F32(SHRINK)

    cells = cell_ref[...]
    hi, lo = split(window)
    picked = dot(jnp.concatenate([hi, lo], axis=0), cell_hot[...])
    tops = []
    rests = []
    for m in range(pairs):
        part = picked[:, m * LANES : (m + 1) * LANES]
        which = cells[m : m + 1, :] // LANES
        for base, out in ((0, tops), (24, rests)):
            chosen = jnp.where(which == 0, part[base : base + 8], F32(0))
            for level in (1, 2):
                at = base + 8 * level
                chosen = jnp.where(which == level, part[at : at + 8], chosen)
            out.append(chosen)
    stacked = jnp.concatenate(tops + rests, axis=0).astype(BF16)
    spread = dot(stacked, spread_ref[...])
    half = 8 * pairs
    spread = spread[:half] + spread[half:]

    f_ref[...] = jnp.zeros_like(f_ref)
    for m in range(pairs):
        for side in range(2):
            at = side * padded_order
            slot = 2 * m + side
            inputs = spread[8 * m : 8 * m + 8, at : at + order] * fr_ref[slot : slot + 1, :order]
            if first:
                out = dot_nt(inputs.astype(BF16), factors[slot])
            else:
                hi = inputs.astype(BF16).astype(F32)
                both = jnp.concatenate([hi, inputs - hi], axis=0).astype(BF16)
                out = dot(both, factors[slot])
                out = out[:8] + out[8:]
            hi = out.astype(BF16).astype(F32)
            f_ref[16 * m : 16 * m + 8, at : at + order] = hi
            f_ref[16 * m + 8 : 16 * m + 16, at : at + order] = out - hi

    ordered = dot(f_ref[...].astype(BF16), order_ref[...]).astype(BF16)
    ordered_ref[...] = ordered
    spread_levels(v_ref, ordered, edges_ref, pairs)
    rim = dot(v_ref[...], edge_turn[...])
    sums = [
        rim[16 * i : 16 * i + 8] + rim[16 * i + 8 : 16 * i + 16] for i in range(6 * EDGE)
    ]
    half = len(sums) // 2
    for i in range(half):
        lead, spill = sums[i], sums[half + i]
        a_ref[8 * i : 8 * i + 8, :], b_ref[8 * i : 8 * i + 8, :] = to_swaps(tile, spill, lead)


def inner_kernel(levels, ordered_ref, weight_ref, conn_ref, node_hot, inside_ref, picked_ref, v_ref):
    pairs = conn_ref.shape[0]
    conn = conn_ref[...]
    inside, _ = levels_of(levels)
    spread_levels(v_ref, ordered_ref, inside_ref, pairs)
    nodes = dot_nt(v_ref[...], node_hot[...])
    rows = []
    for i in range(3 * len(inside)):
        value = nodes[16 * i : 16 * i + 8] + nodes[16 * i + 8 : 16 * i + 16]
        at = inside[i // 3] * RADIX
        rows.append(value * weight_ref[i % 3 : i % 3 + 1, at : at + RADIX])
    weighted = jnp.concatenate(rows, axis=0).astype(BF16)
    step = 2
    for start in range(0, pairs, step):
        found = dot(weighted, node_hot[:, start * LANES : (start + step) * LANES])
        for i in range(step):
            m = start + i
            which = conn[m : m + 1, :] // RADIX
            part = found[:, i * LANES : (i + 1) * LANES]
            chosen = jnp.zeros((24, LANES), F32)
            for at, level in enumerate(inside):
                chosen = jnp.where(which == level, part[24 * at : 24 * at + 24], chosen)
            for c in range(3):
                picked_ref[8 * m : 8 * m + 8, c * LANES : (c + 1) * LANES] = chosen[8 * c : 8 * c + 8]


def adjoint_kernel(last, clusters, levels, *refs):
    block_ref, block_a, block_b, own_a, own_b, new_a, new_b, inner_ref, weight_ref, *refs = refs
    conn_ref, cell_ref, fr_ref, blocks, edge_hot, cell_turn, spread_turn, order_turn, *refs = refs
    if last:
        squares_1, squares_2, ids_ref, *refs = refs
        basal_ref, out_ref, p_ref, n_ref, v_ref = refs
    else:
        basal_ref, a_ref, b_ref, p_ref, n_ref, v_ref = refs

    order = blocks.shape[1]
    padded_order = p_ref.shape[1] // 2
    pairs = blocks.shape[0] // 2
    tile = lax.axis_index("tiles")

    spill, lead = by_side(tile, own_a[...] + new_a[...], own_b[...] + new_b[...])
    after, before = by_side(tile, block_a[...], block_b[...])
    rows = []
    for i in range(3 * EDGE):
        at = (i // 3) * EDGE_RADIX
        rows.append(lead[8 * i : 8 * i + 8] * weight_ref[i % 3 : i % 3 + 1, at : at + EDGE_RADIX])
    for i in range(3 * EDGE):
        rows.append(spill[8 * i : 8 * i + 8] * after[8 + i : 9 + i, :])
    weighted = jnp.concatenate(rows, axis=0).astype(BF16)

    conn = conn_ref[...]
    _, edges = levels_of(levels)
    step = 2
    for start in range(0, pairs, step):
        found = dot(weighted, edge_hot[:, start * LANES : (start + step) * LANES])
        for i in range(step):
            m = start + i
            which = conn[m : m + 1, :] // EDGE_RADIX
            part = found[:, i * LANES : (i + 1) * LANES]
            for c in range(3):
                value = inner_ref[8 * m : 8 * m + 8, c * LANES : (c + 1) * LANES]
                for at, level in enumerate(edges):
                    row = 24 * at + 8 * c
                    value = jnp.where(which == level, part[row : row + 8], value)
                n_ref[8 * m : 8 * m + 8, c * LANES : (c + 1) * LANES] = value
    natural = dot(n_ref[...].astype(BF16), order_turn[...])
    p_ref[...] = jnp.zeros_like(p_ref)
    for m in range(pairs):
        for side in range(2):
            at = side * padded_order
            slot = 2 * m + side
            out = dot(natural[8 * m : 8 * m + 8, at : at + order].astype(BF16), blocks[slot])
            out = out * fr_ref[slot : slot + 1, :order]
            p_ref[8 * m : 8 * m + 8, at : at + order] = out

    hi, lo = split(p_ref[...])
    partial = dot(jnp.concatenate([hi, lo], axis=0), spread_turn[...])
    half = 8 * pairs
    partial = partial[:half] + partial[half:]
    cells = cell_ref[...]
    for m in range(pairs):
        which = cells[m : m + 1, :] // LANES
        value = partial[8 * m : 8 * m + 8, :]
        rows = jnp.concatenate([jnp.where(which == level, value, F32(0)) for level in range(3)], axis=0)
        hi = rows.astype(BF16).astype(F32)
        both = jnp.concatenate([hi, rows - hi], axis=0)
        v_ref[:, m * LANES : (m + 1) * LANES] = both.astype(BF16)
    basal = dot(v_ref[...], cell_turn[...])
    basal = basal[:24] + basal[24:]
    parts = [basal[8 * i : 8 * i + 8] for i in range(3)]
    for i in range(3):
        basal_ref[:, i * LANES : (i + 1) * LANES] = parts[i]
    lane = lanes_iota((8, LANES))
    if not last:
        for_next = jnp.where(lane < RIM, parts[2], parts[1])
        for_previous = jnp.where(lane < RIM, parts[0], parts[2])
        a_ref[...], b_ref[...] = to_swaps(tile, for_next, for_previous)
        return

    starts = [
        block_ref[:1, :LANES],
        block_ref[:1, LANES:],
        jnp.where(lane[:1] < RIM, after[:1, :LANES], before[:1, LANES:]),
    ]
    packed = []
    for start, part in zip(starts, parts):
        even = start != 0
        rows = [jnp.where(even, part[r + 1 : r + 2], part[r : r + 1]) for r in range(0, 8, 2)]
        packed.append(jnp.concatenate(rows, axis=0))
    extra = jnp.zeros((8, LANES), F32)
    for i, ref in enumerate((squares_1, squares_2)):
        rest = jnp.sum(ref[...], axis=1, keepdims=True)
        for j in range(3):
            piece = rest.astype(BF16).astype(F32)
            extra = jnp.where(lane == 3 * i + j, piece, extra)
            rest = rest - piece
    moved = pltpu.roll(extra, 8, 1)
    rows = [extra[r : r + 1] + moved[r + 1 : r + 2] for r in range(0, 8, 2)]
    extra = jnp.concatenate(rows, axis=0)
    ids = ids_ref[...]
    for k in range(1, clusters):
        below = jnp.sum((ids < k).astype(F32), axis=1, keepdims=True)
        extra = jnp.where(lane[:4] == 16 + k, below, extra)
    top = jnp.concatenate([packed[0], packed[1]], axis=1)
    message = jnp.concatenate([top, jnp.concatenate([packed[2], extra], axis=1)], axis=0)
    message = message.astype(BF16)
    for t in range(out_ref.shape[0]):
        out_ref[t] = message


def gram_kernel(
    keep_same, tiles, groups, g_ref, own_ref, samples_in, samples_ref, field_ref, gram_ref
):
    samples_ref[...] = samples_in[...]
    tile = lax.axis_index("tiles")
    group = lax.axis_index("probes")
    clusters = gram_ref.shape[0]
    cell_count = tiles * 2 * LANES
    low = lanes_iota((8, LANES)) < RIM
    row = rows_iota((8, LANES))

    def twice(x):
        out = jnp.broadcast_to(x[:1], (8, LANES))
        for r in range(1, 4):
            out = jnp.where(row >= 2 * r, jnp.broadcast_to(x[r : r + 1], (8, LANES)), out)
        return out

    def piece_of(t, p, lower, at):
        part = g_ref[t, p].astype(F32)
        return twice(part[4 * lower : 4 * lower + 4, at * LANES : (at + 1) * LANES])

    def factor_of(p):
        def add(t, acc):
            return acc + g_ref[t, p].astype(F32)[4:, LANES:]

        sums = lax.fori_loop(0, tiles, add, jnp.zeros((4, LANES), F32), unroll=tiles <= 8)
        sums = twice(sums)
        sums = jnp.where(row % 2 == 0, sums, pltpu.roll(sums, LANES - 8, 1))
        first = jnp.sum(sums[:, :3], axis=1, keepdims=True)
        second = jnp.sum(sums[:, 3:6], axis=1, keepdims=True)
        scale = jnp.sqrt(first / cell_count + F32(1e-06))
        size = jnp.sqrt(second / cell_count) * F32(1 / SHRINK) / scale
        return F32(1 / SHRINK) / (scale * jnp.sqrt(size * size + F32(1e-06)))

    def ids_of(t):
        starts = piece_of(t, 0, 1, 1)
        cell = lanes_iota((8, 2 * LANES)).astype(F32)
        ids = jnp.zeros(cell.shape, jnp.int32)
        for k in range(1, clusters):
            ids = ids + (cell >= starts[:, 16 + k : 17 + k]).astype(jnp.int32)
        return [ids[:, :LANES], ids[:, LANES:]]

    def field(t, p, ids, own=None):
        before = piece_of(jnp.maximum(t - 1, 0), p, 1, 0)
        after = piece_of(jnp.minimum(t + 1, tiles - 1), p, 1, 0)
        if own is None:
            own = [piece_of(t, p, 0, at) for at in range(2)]
        parts = [
            own[0] + jnp.where(low & (t > 0), before, F32(0)),
            own[1] + jnp.where(~low & (t < tiles - 1), after, F32(0)),
        ]
        return [
            jnp.where(colour_of(i) if keep_same else ~colour_of(i), part, F32(0))
            for i, part in zip(ids, parts)
        ]

    factors = [factor_of(p) for p in range(groups)]
    mine_factor = factors[0]
    for p in range(1, groups):
        mine_factor = jnp.where(group == p, factors[p], mine_factor)
    own = [own_ref[:, at * LANES : (at + 1) * LANES] for at in range(2)]
    own = field(tile, group, ids_of(tile), own)
    field_ref[:, :LANES] = own[0] * mine_factor
    field_ref[:, LANES:] = own[1] * mine_factor

    def add_tile(t, acc):
        ids = ids_of(t)
        every = [
            jnp.concatenate(field(t, p, ids), axis=1) * factors[p] for p in range(groups)
        ]
        mine = every[0]
        for p in range(1, groups):
            mine = jnp.where(group == p, every[p], mine)
        ids = jnp.concatenate(ids, axis=1)
        left = jnp.concatenate([jnp.where(ids == k, mine, F32(0)) for k in range(clusters)], axis=0)
        return acc + lax.dot_general(
            left,
            jnp.concatenate(every, axis=0),
            (((1,), (1,)), ((), ())),
            precision=lax.Precision.HIGHEST,
            preferred_element_type=F32,
        )

    acc = jnp.zeros((8 * clusters, 8 * groups), F32)
    acc = lax.fori_loop(0, tiles, add_tile, acc, unroll=tiles <= 8)
    gram_ref[...] = acc.reshape(gram_ref.shape)


def shards(
    blocks, connectivity, basal_map, friction, elem_counts, obs_weight, sign_bits, cluster_ids
):
    slots = blocks.shape[0]
    node_slots = connectivity.shape[1]
    node_count = obs_weight.shape[0]
    cell_count, group_size = sign_bits.shape
    tiles = lax.axis_size("tiles")
    groups = lax.axis_size("probes")
    pairs = slots * node_slots // LANES
    refs = pairs * LANES
    levels = (node_count + HALO) // RADIX
    padded_order = 2 * LANES
    window = cell_count + 2 * RIM

    vmem = pl.BlockSpec(memory_space=pltpu.VMEM)
    params = pltpu.CompilerParams(vmem_limit_bytes=VMEM_BYTES)
    shaped = jax.ShapeDtypeStruct

    hbm = pl.BlockSpec(memory_space=pltpu.HBM)
    smem = pl.BlockSpec(memory_space=pltpu.SMEM)

    def call(kernel, name, out_shape, operands, scratch=(), in_specs=None):
        in_specs = in_specs or [vmem] * len(operands)
        operands = [
            pltpu.with_memory_space_constraint(x, pltpu.HBM) if spec is hbm else x
            for x, spec in zip(operands, in_specs)
        ]
        return pl.pallas_call(
            kernel,
            out_shape=out_shape,
            in_specs=in_specs,
            out_specs=jax.tree.map(lambda _: vmem, out_shape),
            scratch_shapes=list(scratch),
            compiler_params=params,
            name=name,
        )(*operands)

    evens = range(0, tiles - 1, 2)
    odds = range(1, tiles - 1, 2)
    pairs_a = [(i, i + 1) for i in odds] + [(i + 1, i) for i in odds]
    pairs_b = [(i, i + 1) for i in evens] + [(i + 1, i) for i in evens]

    def swapped(a, b):
        return lax.ppermute(a, "tiles", pairs_a), lax.ppermute(b, "tiles", pairs_b)

    weight = obs_weight.T
    block, again = call(
        announce_kernel,
        "announce",
        [shaped((16, cell_count), F32)] * 2,
        [sign_bits.T, cluster_ids.reshape(1, cell_count), weight],
        [
            pltpu.VMEM((group_size, cell_count), jnp.int32),
            pltpu.VMEM((1, cell_count), jnp.int32),
            pltpu.VMEM((3, HALO), F32),
            pltpu.SemaphoreType.DMA((3,)),
        ],
        [hbm] * 3,
    )
    block_a, block_b = swapped(again, block)

    conn, cells, fr, loaded, *hots, cell_hot, cell_turn, spread, spread_turn, order, order_turn = call(
        functools.partial(setup_kernel, levels),
        "setup",
        [
            shaped((pairs, LANES), jnp.int32),
            shaped((pairs, LANES), jnp.int32),
            shaped((slots, padded_order), F32),
            shaped(blocks.shape, BF16),
            shaped((RADIX, refs), BF16),
            shaped((EDGE_RADIX, refs), BF16),
            shaped((refs, EDGE_RADIX), BF16),
            shaped((16 * (levels - 2), refs), BF16),
            shaped((32 * EDGE, refs), BF16),
            shaped((LANES, refs), BF16),
            shaped((refs, LANES), BF16),
            shaped((LANES, 2 * padded_order), BF16),
            shaped((2 * padded_order, LANES), BF16),
            shaped((2 * padded_order, 3 * LANES), BF16),
            shaped((3 * LANES, 2 * padded_order), BF16),
        ],
        [elem_counts, connectivity, basal_map, friction.transpose(2, 0, 1), blocks],
        [
            pltpu.VMEM(connectivity.shape, jnp.int32),
            pltpu.VMEM(basal_map.shape, jnp.int32),
            pltpu.VMEM((3, slots, node_slots), F32),
            pltpu.SemaphoreType.DMA((4,)),
        ],
        [smem] + [hbm] * 4,
    )
    node_hot, edge_hot, edge_turn, inside, edges = hots

    edge = shaped((24 * EDGE, EDGE_RADIX), F32)
    rim = shaped((group_size, LANES), F32)
    whole = shaped((group_size, window), F32)
    field = shaped((group_size, cell_count), F32)
    everyone = ("tiles", "probes")

    carried = []
    factors = loaded
    squares = []
    samples = None
    for step in range(POWER + 1):
        last = step == POWER
        out_shape = [shaped((16 * pairs, 3 * LANES), BF16), edge, edge]
        out_shape += [rim] * (step > 0) + [field] * (step == 1)
        ordered, own_a, own_b, *extra = call(
            functools.partial(forward_kernel, step, tiles),
            "forward",
            out_shape,
            [block, block_a, block_b, *carried]
            + [cells, fr, factors, edge_turn, edges, cell_hot, spread, order],
            [
                pltpu.VMEM((16 * pairs, 2 * padded_order), F32),
                pltpu.VMEM((96 * EDGE, refs), BF16),
            ],
        )
        squares += extra[:1]
        if step == 1:
            samples = extra[1]
        new_a, new_b = swapped(own_a, own_b)
        inner = call(
            functools.partial(inner_kernel, levels),
            "inner",
            shaped((8 * pairs, 3 * LANES), F32),
            [ordered, weight, conn, node_hot, inside],
            [pltpu.VMEM((48 * (levels - 2), refs), BF16)],
        )
        operands = [block, block_a, block_b, own_a, own_b, new_a, new_b, inner, weight]
        operands += [conn, cells, fr, loaded, edge_hot, cell_turn, spread_turn, order_turn]
        if last:
            operands += squares + [cluster_ids.reshape(1, cell_count)]
            message = shaped((lax.axis_size(everyone), group_size, 2 * LANES), BF16)
            out_shape = [whole, message]
        else:
            out_shape = [whole, rim, rim]
        basal, *messages = call(
            functools.partial(adjoint_kernel, last, tiles, levels),
            "adjoint",
            out_shape,
            operands,
            [
                pltpu.VMEM((8 * pairs, 2 * padded_order), F32),
                pltpu.VMEM((8 * pairs, 3 * LANES), F32),
                pltpu.VMEM((48, refs), BF16),
            ],
        )
        if not last:
            if step == 0:
                *messages, settled = lax.optimization_barrier((*messages, loaded))
                factors = call(turn_kernel, "turn", shaped(blocks.shape, BF16), [settled])
            carried = [basal, *swapped(*messages)]

    gathered = lax.all_to_all(messages[0], everyone, 0, 0)
    gathered = gathered.reshape(tiles, groups, *gathered.shape[1:])
    samples, refined, gram = call(
        functools.partial(gram_kernel, POWER % 2 == 1, tiles, groups),
        "gram",
        [field, field, shaped((tiles, group_size, groups * group_size), F32)],
        [gathered, basal, samples],
    )
    return (samples.T, refined.T, gram)


def solution(mesh):
    in_specs = (
        P("tiles", None, None),
        P("tiles", None),
        P("tiles", None),
        P("tiles", None, None),
        P("tiles"),
        P("tiles", None),
        P("tiles", "probes"),
        P("tiles"),
    )
    out_specs = (P("tiles", "probes"), P("tiles", "probes"), P(None, "probes", None))
    return jax.shard_map(shards, mesh=mesh, in_specs=in_specs, out_specs=out_specs, check_vma=False)
```

```python
import functools

import jax
import jax.numpy as jnp
from jax import lax
from jax.experimental import pallas as pl
from jax.experimental.pallas import tpu as pltpu
from jax.sharding import PartitionSpec as P

HALO = 512
POWER = 2
RIM = 64
LANES = 128
RADIX = 512
EDGE_RADIX = 256
EDGE = HALO // EDGE_RADIX
SHRINK = 2.0**-40
VMEM_BYTES = 16 * 1024 * 1024

F32 = jnp.float32
BF16 = jnp.bfloat16


def dot(a, b):
    return lax.dot_general(a, b, (((1,), (0,)), ((), ())), preferred_element_type=F32)


def dot_nt(a, b):
    return lax.dot_general(a, b, (((1,), (1,)), ((), ())), preferred_element_type=F32)


def product(turned):
    return dot if turned else dot_nt


def split(x):
    hi = x.astype(BF16)
    return hi, (x - hi.astype(F32)).astype(BF16)


def rows_iota(shape):
    return lax.broadcasted_iota(jnp.int32, shape, 0)


def lanes_iota(shape):
    return lax.broadcasted_iota(jnp.int32, shape, 1)


def hot(mask):
    return jnp.where(mask, F32(1), F32(0)).astype(BF16)


def hot16(a, b):
    return jnp.where(a == b, jnp.ones((), BF16), jnp.zeros((), BF16))


def spread_matrix(node_slots, padded_order, turned=False):
    shape = (2 * node_slots, 2 * padded_order)
    row, col = rows_iota(shape), lanes_iota(shape)
    if turned:
        row, col = lanes_iota(shape[::-1]), rows_iota(shape[::-1])
    gap = col - ((row // node_slots) * padded_order + 3 * (row % node_slots))
    return hot((gap >= 0) & (gap < 3))


def order_matrix(node_slots, padded_order, turned=False):
    pair = 2 * node_slots
    shape = (2 * padded_order, 3 * pair)
    row, col = rows_iota(shape), lanes_iota(shape)
    if turned:
        row, col = lanes_iota(shape[::-1]), rows_iota(shape[::-1])
    inner = col % pair
    source = (inner // node_slots) * padded_order + 3 * (inner % node_slots) + col // pair
    return hot(row == source)


def colour_of(ids):
    return (ids % 2) == (rows_iota(ids.shape) % 2)


def by_side(tile, a, b):
    even = tile % 2 == 0
    return jnp.where(even, b, a), jnp.where(even, a, b)


def to_swaps(tile, for_next, for_previous):
    even = tile % 2 == 0
    return jnp.where(even, for_previous, for_next), jnp.where(even, for_next, for_previous)


def announce_kernel(signs_hbm, ids_hbm, weight_hbm, out_ref, again_ref, signs, ids, lead, sems):
    loads = [
        pltpu.make_async_copy(signs_hbm, signs, sems.at[0]),
        pltpu.make_async_copy(ids_hbm, ids, sems.at[1]),
        pltpu.make_async_copy(weight_hbm.at[:, pl.ds(0, HALO)], lead, sems.at[2]),
    ]
    for load in loads:
        load.start()
    for load in loads:
        load.wait()
    colours = jnp.broadcast_to(ids[...], signs.shape)
    probes = jnp.where(colour_of(colours), (2 * signs[...] - 1).astype(F32), F32(0))
    out_ref[:8, :] = probes
    out_ref[8:, :] = jnp.zeros_like(probes)
    half = HALO // 2
    out_ref[8:11, :] = lead[:, :half]
    out_ref[11:14, :] = lead[:, half:]
    again_ref[...] = out_ref[...]


def setup_kernel(
    levels,
    counts,
    conn_hbm,
    cell_hbm,
    friction_hbm,
    blocks_hbm,
    conn_ref,
    cell_ref,
    fr_ref,
    blocks_ref,
    node_hot_ref,
    edge_hot_ref,
    level_hot_ref,
    cell_hot_ref,
    spread_ref,
    order_ref,
    conn_in,
    cell_in,
    friction_in,
    sems,
):
    pairs = conn_ref.shape[0]
    slots, padded_order = fr_ref.shape
    node_slots = conn_in.shape[1]
    window = 3 * LANES

    loads = [
        pltpu.make_async_copy(source, target, sems.at[i])
        for i, (source, target) in enumerate(
            [
                (conn_hbm, conn_in),
                (cell_hbm, cell_in),
                (friction_hbm, friction_in),
                (blocks_hbm, blocks_ref),
            ]
        )
    ]
    for load in loads:
        load.start()

    spread_ref[...] = spread_matrix(node_slots, padded_order)
    order_ref[...] = order_matrix(node_slots, padded_order)

    def paired(ref):
        return jnp.concatenate(
            [ref[pl.ds(0, pairs, stride=2), :], ref[pl.ds(1, pairs, stride=2), :]], axis=1
        )

    for load in loads[:3]:
        load.wait()
    conn = paired(conn_in)
    conn_ref[...] = conn
    cells = paired(cell_in)
    cells = jnp.where(cells < RIM, cells + (window - RIM), cells - RIM)
    cell_ref[...] = cells

    shape = (node_slots, padded_order)
    total = jnp.zeros((slots, padded_order), F32)
    for c in range(3):
        place = hot(lanes_iota(shape) == 3 * rows_iota(shape) + c)
        rest = friction_in[c]
        for _ in range(3):
            part = rest.astype(BF16)
            total = total + dot(part, place)
            rest = rest - part.astype(F32)
    live = rows_iota(total.shape) < counts[0]
    fr_ref[...] = jnp.where(live, total, F32(0))

    rows = rows_iota((EDGE_RADIX, LANES)).astype(F32).astype(BF16)
    low = conn % RADIX
    halves = []
    for at in range(0, RADIX, EDGE_RADIX):
        inside = (low >= at) & (low < at + EDGE_RADIX)
        halves.append(jnp.where(inside, low - at, -1).astype(F32))
    which = (conn // RADIX).astype(F32)
    cell_low = (cells % LANES).astype(F32)
    for m in range(pairs):
        at = pl.ds(m * LANES, LANES)
        total = jnp.zeros((EDGE_RADIX, LANES), BF16)
        for i, half in enumerate(halves):
            row = jnp.broadcast_to(half[m : m + 1, :], (EDGE_RADIX, LANES)).astype(BF16)
            mine = hot16(rows, row)
            node_hot_ref[i * EDGE_RADIX : (i + 1) * EDGE_RADIX, at] = mine
            total = total + mine
        edge_hot_ref[:, at] = total
        row = jnp.broadcast_to(which[m : m + 1, :], (16, LANES)).astype(BF16)
        for level in range(levels):
            mine = hot16(row, jnp.full((16, LANES), level, BF16))
            level_hot_ref[16 * level : 16 * level + 16, at] = mine
        row = jnp.broadcast_to(cell_low[m : m + 1, :], (LANES, LANES)).astype(BF16)
        cell_hot_ref[:, at] = hot16(rows[:LANES], row)
    loads[3].wait()


def turn_kernel(
    blocks, conn_ref, cell_ref, turned_ref, node_turn_ref, cell_turn_ref, spread_turn_ref, order_turn_ref
):
    node_slots = blocks.shape[1] // 3
    padded_order = order_turn_ref.shape[1] // 2
    spread_turn_ref[...] = spread_matrix(node_slots, padded_order, True)
    order_turn_ref[...] = order_matrix(node_slots, padded_order, True)
    nodes = (conn_ref[...] % RADIX).astype(F32).T
    cells = (cell_ref[...] % LANES).astype(F32).T
    lanes = lanes_iota((LANES, RADIX)).astype(F32)
    for slot in range(blocks.shape[0]):
        turned_ref[slot] = blocks[slot].T
        if slot % 2:
            continue
        m = slot // 2
        at = pl.ds(m * LANES, LANES)
        node_turn_ref[at, :] = hot(lanes == nodes[:, m : m + 1])
        cell_turn_ref[at, :] = hot(lanes[:, :LANES] == cells[:, m : m + 1])


def spread_levels(v_ref, ordered, level_hot, levels, pairs):
    for m in range(pairs):
        at = pl.ds(m * LANES, LANES)
        values = [ordered[16 * m : 16 * m + 16, c * LANES : (c + 1) * LANES] for c in range(3)]
        for i, level in enumerate(levels):
            mask = level_hot[16 * level : 16 * level + 16, at]
            for c in range(3):
                row = 48 * i + 16 * c
                v_ref[row : row + 16, at] = values[c] * mask


def forward_kernel(step, tiles, levels, *refs):
    block_ref, block_a, block_b, *refs = refs
    first = step == 0
    if not first:
        basal_ref, rim_a, rim_b, *refs = refs
    cell_ref, fr_ref, factors, node_map, level_hot, cell_hot, spread_ref, order_ref, *refs = refs
    ordered_ref, a_ref, b_ref, *refs = refs
    if not first:
        squares_ref, *refs = refs
    if step == 1:
        field_ref, *refs = refs
    f_ref, v_ref = refs

    order = factors.shape[1]
    padded_order = f_ref.shape[1] // 2
    pairs = factors.shape[0] // 2
    tile = lax.axis_index("tiles")

    lane = lanes_iota((8, LANES))
    low = lane < RIM
    after, before = by_side(tile, block_a[:8, :], block_b[:8, :])
    starts = [
        block_ref[:8, :LANES],
        block_ref[:8, LANES:],
        jnp.where(low, after[:, :LANES], before[:, LANES:]),
    ]
    if first:
        parts = starts
    else:
        after, before = by_side(tile, rim_a[...], rim_b[...])
        parts = [basal_ref[:, i * LANES : (i + 1) * LANES] for i in range(3)]
        parts[0] = parts[0] + jnp.where(low, before, F32(0))
        parts[1] = parts[1] + jnp.where(low, F32(0), after)
        parts[2] = parts[2] + jnp.where(low, after, before)
        there = (low & (tile < tiles - 1)) | (~low & (tile > 0))
        parts[2] = jnp.where(there, parts[2], F32(0))
        kept = [(start != 0) if step % 2 == 0 else (start == 0) for start in starts]
        parts = [jnp.where(keep, part, F32(0)) for keep, part in zip(kept, parts)]
        if step == 1:
            field_ref[:, :LANES] = parts[0]
            field_ref[:, LANES:] = parts[1]
        squares_ref[...] = parts[0] * parts[0] + parts[1] * parts[1]
    window = jnp.concatenate(parts, axis=0)
    if step == 1:
        window = window * F32(SHRINK)

    cells = cell_ref[...]
    hi, lo = split(window)
    picked = dot(jnp.concatenate([hi, lo], axis=0), cell_hot[...])
    tops = []
    rests = []
    for m in range(pairs):
        part = picked[:, m * LANES : (m + 1) * LANES]
        which = cells[m : m + 1, :] // LANES
        for base, out in ((0, tops), (24, rests)):
            chosen = jnp.where(which == 0, part[base : base + 8], F32(0))
            for level in (1, 2):
                at = base + 8 * level
                chosen = jnp.where(which == level, part[at : at + 8], chosen)
            out.append(chosen)
    stacked = jnp.concatenate(tops + rests, axis=0).astype(BF16)
    spread = dot(stacked, spread_ref[...])
    half = 8 * pairs
    spread = spread[:half] + spread[half:]

    f_ref[...] = jnp.zeros_like(f_ref)
    for m in range(pairs):
        for side in range(2):
            at = side * padded_order
            slot = 2 * m + side
            inputs = spread[8 * m : 8 * m + 8, at : at + order] * fr_ref[slot : slot + 1, :order]
            if first:
                out = product(step > 0)(inputs.astype(BF16), factors[slot])
            else:
                hi = inputs.astype(BF16).astype(F32)
                both = jnp.concatenate([hi, inputs - hi], axis=0).astype(BF16)
                out = product(step > 0)(both, factors[slot])
                out = out[:8] + out[8:]
            hi = out.astype(BF16).astype(F32)
            f_ref[16 * m : 16 * m + 8, at : at + order] = hi
            f_ref[16 * m + 8 : 16 * m + 16, at : at + order] = out - hi

    ordered = dot(f_ref[...].astype(BF16), order_ref[...]).astype(BF16)
    ordered_ref[...] = ordered
    spread_levels(v_ref, ordered, level_hot, (0, levels - 1), pairs)
    rim = product(step > 0)(v_ref[...], node_map[...])
    sums = [rim[16 * i : 16 * i + 8] + rim[16 * i + 8 : 16 * i + 16] for i in range(6)]
    half = len(sums) // 2
    for i in range(half):
        lead, spill = sums[i], sums[half + i]
        a_ref[8 * i : 8 * i + 8, :], b_ref[8 * i : 8 * i + 8, :] = to_swaps(tile, spill, lead)


def inner_kernel(levels, ordered_ref, weight_ref, conn_ref, node_hot, level_hot, picked_ref, v_ref):
    pairs = conn_ref.shape[0]
    conn = conn_ref[...]
    inside = range(1, levels - 1)
    spread_levels(v_ref, ordered_ref, level_hot, inside, pairs)
    nodes = dot_nt(v_ref[...], node_hot[...])
    rows = []
    for i in range(3 * len(inside)):
        value = nodes[16 * i : 16 * i + 8] + nodes[16 * i + 8 : 16 * i + 16]
        at = inside[i // 3] * RADIX
        rows.append(value * weight_ref[i % 3 : i % 3 + 1, at : at + RADIX])
    weighted = jnp.concatenate(rows, axis=0).astype(BF16)
    step = 2
    for start in range(0, pairs, step):
        found = dot(weighted, node_hot[:, start * LANES : (start + step) * LANES])
        for i in range(step):
            m = start + i
            which = conn[m : m + 1, :] // RADIX
            part = found[:, i * LANES : (i + 1) * LANES]
            chosen = jnp.zeros((24, LANES), F32)
            for at, level in enumerate(inside):
                chosen = jnp.where(which == level, part[24 * at : 24 * at + 24], chosen)
            for c in range(3):
                picked_ref[8 * m : 8 * m + 8, c * LANES : (c + 1) * LANES] = chosen[8 * c : 8 * c + 8]


def adjoint_kernel(step, last, clusters, levels, *refs):
    block_ref, block_a, block_b, own_a, own_b, new_a, new_b, inner_ref, weight_ref, *refs = refs
    conn_ref, cell_ref, fr_ref, blocks, edge_hot, cell_map, spread_map, order_map, *refs = refs
    if last:
        squares_1, squares_2, ids_ref, *refs = refs
        basal_ref, out_ref, p_ref, n_ref, v_ref = refs
    else:
        basal_ref, a_ref, b_ref, p_ref, n_ref, v_ref = refs

    order = blocks.shape[1]
    padded_order = p_ref.shape[1] // 2
    pairs = blocks.shape[0] // 2
    tile = lax.axis_index("tiles")

    spill, lead = by_side(tile, own_a[...] + new_a[...], own_b[...] + new_b[...])
    after, before = by_side(tile, block_a[...], block_b[...])
    rows = []
    for i in range(3 * EDGE):
        c, at = i % 3, (i // 3) * EDGE_RADIX
        value = lead[8 * c : 8 * c + 8, at : at + EDGE_RADIX]
        rows.append(value * weight_ref[c : c + 1, at : at + EDGE_RADIX])
    for i in range(3 * EDGE):
        c, at = i % 3, (i // 3) * EDGE_RADIX
        value = spill[8 * c : 8 * c + 8, at : at + EDGE_RADIX]
        rows.append(value * after[8 + i : 9 + i, :])
    weighted = jnp.concatenate(rows, axis=0).astype(BF16)

    conn = conn_ref[...]
    first = levels * RADIX // EDGE_RADIX - EDGE
    edges = [*range(EDGE), *range(first, first + EDGE)]
    width = 2
    for start in range(0, pairs, width):
        found = dot(weighted, edge_hot[:, start * LANES : (start + width) * LANES])
        for i in range(width):
            m = start + i
            which = conn[m : m + 1, :] // EDGE_RADIX
            part = found[:, i * LANES : (i + 1) * LANES]
            for c in range(3):
                value = inner_ref[8 * m : 8 * m + 8, c * LANES : (c + 1) * LANES]
                for at, level in enumerate(edges):
                    row = 24 * at + 8 * c
                    value = jnp.where(which == level, part[row : row + 8], value)
                n_ref[8 * m : 8 * m + 8, c * LANES : (c + 1) * LANES] = value
    natural = product(step > 0)(n_ref[...].astype(BF16), order_map[...])
    p_ref[...] = jnp.zeros_like(p_ref)
    for m in range(pairs):
        for side in range(2):
            at = side * padded_order
            slot = 2 * m + side
            out = dot(natural[8 * m : 8 * m + 8, at : at + order].astype(BF16), blocks[slot])
            out = out * fr_ref[slot : slot + 1, :order]
            p_ref[8 * m : 8 * m + 8, at : at + order] = out

    hi, lo = split(p_ref[...])
    partial = product(step > 0)(jnp.concatenate([hi, lo], axis=0), spread_map[...])
    half = 8 * pairs
    partial = partial[:half] + partial[half:]
    cells = cell_ref[...]
    for m in range(pairs):
        which = cells[m : m + 1, :] // LANES
        value = partial[8 * m : 8 * m + 8, :]
        rows = jnp.concatenate([jnp.where(which == level, value, F32(0)) for level in range(3)], axis=0)
        hi = rows.astype(BF16).astype(F32)
        both = jnp.concatenate([hi, rows - hi], axis=0)
        v_ref[:, m * LANES : (m + 1) * LANES] = both.astype(BF16)
    basal = product(step > 0)(v_ref[...], cell_map[...])
    basal = basal[:24] + basal[24:]
    parts = [basal[8 * i : 8 * i + 8] for i in range(3)]
    for i in range(3):
        basal_ref[:, i * LANES : (i + 1) * LANES] = parts[i]
    lane = lanes_iota((8, LANES))
    if not last:
        for_next = jnp.where(lane < RIM, parts[2], parts[1])
        for_previous = jnp.where(lane < RIM, parts[0], parts[2])
        a_ref[...], b_ref[...] = to_swaps(tile, for_next, for_previous)
        return

    starts = [
        block_ref[:1, :LANES],
        block_ref[:1, LANES:],
        jnp.where(lane[:1] < RIM, after[:1, :LANES], before[:1, LANES:]),
    ]
    packed = []
    for start, part in zip(starts, parts):
        even = start != 0
        rows = [jnp.where(even, part[r + 1 : r + 2], part[r : r + 1]) for r in range(0, 8, 2)]
        packed.append(jnp.concatenate(rows, axis=0))
    extra = jnp.zeros((8, LANES), F32)
    for i, ref in enumerate((squares_1, squares_2)):
        rest = jnp.sum(ref[...], axis=1, keepdims=True)
        for j in range(3):
            piece = rest.astype(BF16).astype(F32)
            extra = jnp.where(lane == 3 * i + j, piece, extra)
            rest = rest - piece
    moved = pltpu.roll(extra, 8, 1)
    rows = [extra[r : r + 1] + moved[r + 1 : r + 2] for r in range(0, 8, 2)]
    extra = jnp.concatenate(rows, axis=0)
    ids = ids_ref[...]
    for k in range(1, clusters):
        below = jnp.sum((ids < k).astype(F32), axis=1, keepdims=True)
        extra = jnp.where(lane[:4] == 16 + k, below, extra)
    top = jnp.concatenate([packed[0], packed[1]], axis=1)
    message = jnp.concatenate([top, jnp.concatenate([packed[2], extra], axis=1)], axis=0)
    message = message.astype(BF16)
    for t in range(out_ref.shape[0]):
        out_ref[t] = message


def gram_kernel(
    keep_same, tiles, groups, g_ref, own_ref, samples_in, samples_ref, field_ref, gram_ref
):
    samples_ref[...] = samples_in[...]
    tile = lax.axis_index("tiles")
    group = lax.axis_index("probes")
    clusters = gram_ref.shape[0]
    cell_count = tiles * 2 * LANES
    low = lanes_iota((8, LANES)) < RIM
    row = rows_iota((8, LANES))

    def twice(x):
        out = jnp.broadcast_to(x[:1], (8, LANES))
        for r in range(1, 4):
            out = jnp.where(row >= 2 * r, jnp.broadcast_to(x[r : r + 1], (8, LANES)), out)
        return out

    def piece_of(t, p, lower, at):
        part = g_ref[t, p].astype(F32)
        return twice(part[4 * lower : 4 * lower + 4, at * LANES : (at + 1) * LANES])

    def factor_of(p):
        def add(t, acc):
            return acc + g_ref[t, p].astype(F32)[4:, LANES:]

        sums = lax.fori_loop(0, tiles, add, jnp.zeros((4, LANES), F32), unroll=tiles <= 8)
        sums = twice(sums)
        sums = jnp.where(row % 2 == 0, sums, pltpu.roll(sums, LANES - 8, 1))
        first = jnp.sum(sums[:, :3], axis=1, keepdims=True)
        second = jnp.sum(sums[:, 3:6], axis=1, keepdims=True)
        scale = jnp.sqrt(first / cell_count + F32(1e-06))
        size = jnp.sqrt(second / cell_count) * F32(1 / SHRINK) / scale
        return F32(1 / SHRINK) / (scale * jnp.sqrt(size * size + F32(1e-06)))

    def ids_of(t):
        starts = piece_of(t, 0, 1, 1)
        cell = lanes_iota((8, 2 * LANES)).astype(F32)
        ids = jnp.zeros(cell.shape, jnp.int32)
        for k in range(1, clusters):
            ids = ids + (cell >= starts[:, 16 + k : 17 + k]).astype(jnp.int32)
        return [ids[:, :LANES], ids[:, LANES:]]

    def field(t, p, ids, own=None):
        before = piece_of(jnp.maximum(t - 1, 0), p, 1, 0)
        after = piece_of(jnp.minimum(t + 1, tiles - 1), p, 1, 0)
        if own is None:
            own = [piece_of(t, p, 0, at) for at in range(2)]
        parts = [
            own[0] + jnp.where(low & (t > 0), before, F32(0)),
            own[1] + jnp.where(~low & (t < tiles - 1), after, F32(0)),
        ]
        return [
            jnp.where(colour_of(i) if keep_same else ~colour_of(i), part, F32(0))
            for i, part in zip(ids, parts)
        ]

    factors = [factor_of(p) for p in range(groups)]
    mine_factor = factors[0]
    for p in range(1, groups):
        mine_factor = jnp.where(group == p, factors[p], mine_factor)
    own = [own_ref[:, at * LANES : (at + 1) * LANES] for at in range(2)]
    own = field(tile, group, ids_of(tile), own)
    field_ref[:, :LANES] = own[0] * mine_factor
    field_ref[:, LANES:] = own[1] * mine_factor

    def add_tile(t, acc):
        ids = ids_of(t)
        every = [
            jnp.concatenate(field(t, p, ids), axis=1) * factors[p] for p in range(groups)
        ]
        mine = every[0]
        for p in range(1, groups):
            mine = jnp.where(group == p, every[p], mine)
        ids = jnp.concatenate(ids, axis=1)
        left = jnp.concatenate([jnp.where(ids == k, mine, F32(0)) for k in range(clusters)], axis=0)
        return acc + lax.dot_general(
            left,
            jnp.concatenate(every, axis=0),
            (((1,), (1,)), ((), ())),
            precision=lax.Precision.HIGHEST,
            preferred_element_type=F32,
        )

    acc = jnp.zeros((8 * clusters, 8 * groups), F32)
    acc = lax.fori_loop(0, tiles, add_tile, acc, unroll=tiles <= 8)
    gram_ref[...] = acc.reshape(gram_ref.shape)


def shards(
    blocks, connectivity, basal_map, friction, elem_counts, obs_weight, sign_bits, cluster_ids
):
    slots = blocks.shape[0]
    node_slots = connectivity.shape[1]
    node_count = obs_weight.shape[0]
    cell_count, group_size = sign_bits.shape
    tiles = lax.axis_size("tiles")
    groups = lax.axis_size("probes")
    pairs = slots * node_slots // LANES
    refs = pairs * LANES
    levels = (node_count + HALO) // RADIX
    padded_order = 2 * LANES
    window = cell_count + 2 * RIM

    vmem = pl.BlockSpec(memory_space=pltpu.VMEM)
    params = pltpu.CompilerParams(vmem_limit_bytes=VMEM_BYTES)
    shaped = jax.ShapeDtypeStruct

    hbm = pl.BlockSpec(memory_space=pltpu.HBM)
    smem = pl.BlockSpec(memory_space=pltpu.SMEM)

    def call(kernel, name, out_shape, operands, scratch=(), in_specs=None):
        in_specs = in_specs or [vmem] * len(operands)
        operands = [
            pltpu.with_memory_space_constraint(x, pltpu.HBM) if spec is hbm else x
            for x, spec in zip(operands, in_specs)
        ]
        return pl.pallas_call(
            kernel,
            out_shape=out_shape,
            in_specs=in_specs,
            out_specs=jax.tree.map(lambda _: vmem, out_shape),
            scratch_shapes=list(scratch),
            compiler_params=params,
            name=name,
        )(*operands)

    evens = range(0, tiles - 1, 2)
    odds = range(1, tiles - 1, 2)
    pairs_a = [(i, i + 1) for i in odds] + [(i + 1, i) for i in odds]
    pairs_b = [(i, i + 1) for i in evens] + [(i + 1, i) for i in evens]

    def swapped(a, b):
        return lax.ppermute(a, "tiles", pairs_a), lax.ppermute(b, "tiles", pairs_b)

    weight = obs_weight.T
    block, again = call(
        announce_kernel,
        "announce",
        [shaped((16, cell_count), F32)] * 2,
        [sign_bits.T, cluster_ids.reshape(1, cell_count), weight],
        [
            pltpu.VMEM((group_size, cell_count), jnp.int32),
            pltpu.VMEM((1, cell_count), jnp.int32),
            pltpu.VMEM((3, HALO), F32),
            pltpu.SemaphoreType.DMA((3,)),
        ],
        [hbm] * 3,
    )
    block_a, block_b = swapped(again, block)

    conn, cells, fr, loaded, node_hot, edge_hot, level_hot, cell_hot, spread, order = call(
        functools.partial(setup_kernel, levels),
        "setup",
        [
            shaped((pairs, LANES), jnp.int32),
            shaped((pairs, LANES), jnp.int32),
            shaped((slots, padded_order), F32),
            shaped(blocks.shape, BF16),
            shaped((RADIX, refs), BF16),
            shaped((EDGE_RADIX, refs), BF16),
            shaped((16 * levels, refs), BF16),
            shaped((LANES, refs), BF16),
            shaped((LANES, 2 * padded_order), BF16),
            shaped((2 * padded_order, 3 * LANES), BF16),
        ],
        [elem_counts, connectivity, basal_map, friction.transpose(2, 0, 1), blocks],
        [
            pltpu.VMEM(connectivity.shape, jnp.int32),
            pltpu.VMEM(basal_map.shape, jnp.int32),
            pltpu.VMEM((3, slots, node_slots), F32),
            pltpu.SemaphoreType.DMA((4,)),
        ],
        [smem] + [hbm] * 4,
    )
    factors, node_map, cell_map, spread_map, order_map = loaded, node_hot, cell_hot, spread, order

    edge = shaped((24, HALO), F32)
    rim = shaped((group_size, LANES), F32)
    whole = shaped((group_size, window), F32)
    field = shaped((group_size, cell_count), F32)
    everyone = ("tiles", "probes")

    carried = []
    factors = loaded
    squares = []
    samples = None
    for step in range(POWER + 1):
        last = step == POWER
        out_shape = [shaped((16 * pairs, 3 * LANES), BF16), edge, edge]
        out_shape += [rim] * (step > 0) + [field] * (step == 1)
        ordered, own_a, own_b, *extra = call(
            functools.partial(forward_kernel, step, tiles, levels),
            "forward",
            out_shape,
            [block, block_a, block_b, *carried]
            + [cells, fr, factors, node_map, level_hot, cell_hot, spread, order],
            [
                pltpu.VMEM((16 * pairs, 2 * padded_order), F32),
                pltpu.VMEM((96, refs), BF16),
            ],
        )
        squares += extra[:1]
        if step == 1:
            samples = extra[1]
        new_a, new_b = swapped(own_a, own_b)
        inner = call(
            functools.partial(inner_kernel, levels),
            "inner",
            shaped((8 * pairs, 3 * LANES), F32),
            [ordered, weight, conn, node_hot, level_hot],
            [pltpu.VMEM((48 * (levels - 2), refs), BF16)],
        )
        operands = [block, block_a, block_b, own_a, own_b, new_a, new_b, inner, weight]
        operands += [conn, cells, fr, loaded, edge_hot, cell_map, spread_map, order_map]
        if last:
            operands += squares + [cluster_ids.reshape(1, cell_count)]
            message = shaped((lax.axis_size(everyone), group_size, 2 * LANES), BF16)
            out_shape = [whole, message]
        else:
            out_shape = [whole, rim, rim]
        basal, *messages = call(
            functools.partial(adjoint_kernel, step, last, tiles, levels),
            "adjoint",
            out_shape,
            operands,
            [
                pltpu.VMEM((8 * pairs, 2 * padded_order), F32),
                pltpu.VMEM((8 * pairs, 3 * LANES), F32),
                pltpu.VMEM((48, refs), BF16),
            ],
        )
        if not last:
            if step == 0:
                *messages, settled = lax.optimization_barrier((*messages, loaded))
                factors, node_map, cell_map, spread_map, order_map = call(
                    turn_kernel,
                    "turn",
                    [
                        shaped(blocks.shape, BF16),
                        shaped((refs, RADIX), BF16),
                        shaped((refs, LANES), BF16),
                        shaped((2 * padded_order, LANES), BF16),
                        shaped((3 * LANES, 2 * padded_order), BF16),
                    ],
                    [settled, conn, cells],
                )
            carried = [basal, *swapped(*messages)]

    gathered = lax.all_to_all(messages[0], everyone, 0, 0)
    gathered = gathered.reshape(tiles, groups, *gathered.shape[1:])
    samples, refined, gram = call(
        functools.partial(gram_kernel, POWER % 2 == 1, tiles, groups),
        "gram",
        [field, field, shaped((tiles, group_size, groups * group_size), F32)],
        [gathered, basal, samples],
    )
    return (samples.T, refined.T, gram)


def solution(mesh):
    in_specs = (
        P("tiles", None, None),
        P("tiles", None),
        P("tiles", None),
        P("tiles", None, None),
        P("tiles"),
        P("tiles", None),
        P("tiles", "probes"),
        P("tiles"),
    )
    out_specs = (P("tiles", "probes"), P("tiles", "probes"), P(None, "probes", None))
    return jax.shard_map(shards, mesh=mesh, in_specs=in_specs, out_specs=out_specs, check_vma=False)
```

```python
import functools

import jax
import jax.numpy as jnp
from jax import lax
from jax.experimental import pallas as pl
from jax.experimental.pallas import tpu as pltpu
from jax.sharding import PartitionSpec as P

HALO = 512
POWER = 2
RIM = 64
LANES = 128
RADIX = 512
EDGE_RADIX = 256
EDGE = HALO // EDGE_RADIX
SHRINK = 2.0**-40
VMEM_BYTES = 16 * 1024 * 1024

F32 = jnp.float32
BF16 = jnp.bfloat16


def dot(a, b):
    return lax.dot_general(a, b, (((1,), (0,)), ((), ())), preferred_element_type=F32)


def dot_nt(a, b):
    return lax.dot_general(a, b, (((1,), (1,)), ((), ())), preferred_element_type=F32)


def product(turned):
    return dot if turned else dot_nt


def split(x):
    hi = x.astype(BF16)
    return hi, (x - hi.astype(F32)).astype(BF16)


def rows_iota(shape):
    return lax.broadcasted_iota(jnp.int32, shape, 0)


def lanes_iota(shape):
    return lax.broadcasted_iota(jnp.int32, shape, 1)


def hot(mask):
    return jnp.where(mask, F32(1), F32(0)).astype(BF16)


def hot16(a, b):
    return jnp.where(a == b, jnp.ones((), BF16), jnp.zeros((), BF16))


def lane_tiles(count, tile):
    return jnp.concatenate([tile(i * LANES) for i in range(count)], axis=1)


def spread_matrix(node_slots, padded_order, turned=False):
    pair, wide = 2 * node_slots, 2 * padded_order

    def start(at):
        return (at // node_slots) * padded_order + 3 * (at % node_slots)

    def near(gap):
        return hot((gap >= 0) & (gap < 3))

    if turned:
        return near(rows_iota((wide, pair)) - start(lanes_iota((1, pair))))
    gap = lanes_iota((pair, LANES)) - start(rows_iota((pair, LANES)))
    return lane_tiles(wide // LANES, lambda at: near(gap + at))


def order_matrix(node_slots, padded_order, turned=False):
    pair, wide = 2 * node_slots, 2 * padded_order

    def source(at):
        inner = at % pair
        return (inner // node_slots) * padded_order + 3 * (inner % node_slots) + at // pair

    if not turned:
        return hot(rows_iota((wide, 3 * pair)) == source(lanes_iota((1, 3 * pair))))
    gap = lanes_iota((3 * pair, LANES)) - source(rows_iota((3 * pair, LANES)))
    return lane_tiles(wide // LANES, lambda at: hot(gap + at == 0))


def colour_of(ids):
    return (ids % 2) == (rows_iota(ids.shape) % 2)


def by_side(tile, a, b):
    even = tile % 2 == 0
    return jnp.where(even, b, a), jnp.where(even, a, b)


def to_swaps(tile, for_next, for_previous):
    even = tile % 2 == 0
    return jnp.where(even, for_previous, for_next), jnp.where(even, for_next, for_previous)


def announce_kernel(signs_hbm, ids_hbm, weight_hbm, out_ref, again_ref, signs, ids, lead, sems):
    loads = [
        pltpu.make_async_copy(signs_hbm, signs, sems.at[0]),
        pltpu.make_async_copy(ids_hbm, ids, sems.at[1]),
        pltpu.make_async_copy(weight_hbm.at[:, pl.ds(0, HALO)], lead, sems.at[2]),
    ]
    for load in loads:
        load.start()
    for load in loads:
        load.wait()
    colours = jnp.broadcast_to(ids[...], signs.shape)
    probes = jnp.where(colour_of(colours), (2 * signs[...] - 1).astype(F32), F32(0))
    out_ref[:8, :] = probes
    out_ref[8:, :] = jnp.zeros_like(probes)
    half = HALO // 2
    out_ref[8:11, :] = lead[:, :half]
    out_ref[11:14, :] = lead[:, half:]
    again_ref[...] = out_ref[...]


def halves_of(conn):
    low = conn % RADIX
    halves = []
    for at in range(0, RADIX, EDGE_RADIX):
        inside = (low >= at) & (low < at + EDGE_RADIX)
        halves.append(jnp.where(inside, low - at, -1).astype(F32))
    return halves


def setup_kernel(
    levels,
    counts,
    conn_hbm,
    cell_hbm,
    friction_hbm,
    blocks_hbm,
    conn_ref,
    cell_ref,
    fr_ref,
    blocks_ref,
    node_hot_ref,
    edge_hot_ref,
    level_hot_ref,
    cell_hot_ref,
    spread_ref,
    order_ref,
    conn_in,
    cell_in,
    friction_in,
    sems,
):
    pairs = conn_ref.shape[0]
    slots, padded_order = fr_ref.shape
    node_slots = conn_in.shape[1]
    window = 3 * LANES

    loads = [
        pltpu.make_async_copy(source, target, sems.at[i])
        for i, (source, target) in enumerate(
            [
                (conn_hbm, conn_in),
                (cell_hbm, cell_in),
                (friction_hbm, friction_in),
                (blocks_hbm, blocks_ref),
            ]
        )
    ]
    for load in loads:
        load.start()

    spread_ref[...] = spread_matrix(node_slots, padded_order)
    order_ref[...] = order_matrix(node_slots, padded_order)

    def paired(ref):
        return jnp.concatenate(
            [ref[pl.ds(0, pairs, stride=2), :], ref[pl.ds(1, pairs, stride=2), :]], axis=1
        )

    for load in loads[:3]:
        load.wait()
    conn = paired(conn_in)
    conn_ref[...] = conn
    cells = paired(cell_in)
    cells = jnp.where(cells < RIM, cells + (window - RIM), cells - RIM)
    cell_ref[...] = cells

    shape = (node_slots, padded_order)
    total = jnp.zeros((slots, padded_order), F32)
    for c in range(3):
        place = hot(lanes_iota(shape) == 3 * rows_iota(shape) + c)
        rest = friction_in[c]
        for _ in range(3):
            part = rest.astype(BF16)
            total = total + dot(part, place)
            rest = rest - part.astype(F32)
    live = rows_iota(total.shape) < counts[0]
    fr_ref[...] = jnp.where(live, total, F32(0))

    rows = rows_iota((EDGE_RADIX, LANES)).astype(F32).astype(BF16)
    halves = halves_of(conn)
    which = (conn // RADIX).astype(F32)
    cell_low = (cells % LANES).astype(F32)
    for m in range(pairs):
        at = pl.ds(m * LANES, LANES)
        total = jnp.zeros((EDGE_RADIX, LANES), BF16)
        for i, half in enumerate(halves):
            row = jnp.broadcast_to(half[m : m + 1, :], (EDGE_RADIX, LANES)).astype(BF16)
            mine = hot16(rows, row)
            node_hot_ref[i * EDGE_RADIX : (i + 1) * EDGE_RADIX, at] = mine
            total = total + mine
        edge_hot_ref[:, at] = total
        row = jnp.broadcast_to(which[m : m + 1, :], (16, LANES)).astype(BF16)
        for level in range(levels):
            mine = hot16(row, jnp.full((16, LANES), level, BF16))
            level_hot_ref[16 * level : 16 * level + 16, at] = mine
        row = jnp.broadcast_to(cell_low[m : m + 1, :], (LANES, LANES)).astype(BF16)
        cell_hot_ref[:, at] = hot16(rows[:LANES], row)
    loads[3].wait()


def turn_nodes_kernel(conn_ref, node_turn_ref):
    columns = [half.T for half in halves_of(conn_ref[...])]
    lanes = lanes_iota((LANES, EDGE_RADIX)).astype(F32).astype(BF16)
    for m in range(conn_ref.shape[0]):
        for i, column in enumerate(columns):
            row = jnp.broadcast_to(column[:, m : m + 1], (LANES, LANES)).astype(BF16)
            row = jnp.concatenate([row] * (EDGE_RADIX // LANES), axis=1)
            at = pl.ds(i * EDGE_RADIX, EDGE_RADIX)
            node_turn_ref[m * LANES : (m + 1) * LANES, at] = hot16(lanes, row)


def turn_kernel(blocks, cell_ref, turned_ref, cell_turn_ref, spread_turn_ref, order_turn_ref):
    node_slots = blocks.shape[1] // 3
    padded_order = order_turn_ref.shape[1] // 2
    spread_turn_ref[...] = spread_matrix(node_slots, padded_order, True)
    order_turn_ref[...] = order_matrix(node_slots, padded_order, True)
    cells = (cell_ref[...] % LANES).astype(F32).T
    lanes = lanes_iota((LANES, LANES)).astype(F32).astype(BF16)
    for slot in range(blocks.shape[0]):
        turned_ref[slot] = blocks[slot].T
        if slot % 2:
            continue
        m = slot // 2
        row = jnp.broadcast_to(cells[:, m : m + 1], (LANES, LANES)).astype(BF16)
        cell_turn_ref[m * LANES : (m + 1) * LANES, :] = hot16(lanes, row)


def spread_levels(v_ref, ordered, level_hot, levels, pairs):
    for m in range(pairs):
        at = pl.ds(m * LANES, LANES)
        values = [ordered[16 * m : 16 * m + 16, c * LANES : (c + 1) * LANES] for c in range(3)]
        for i, level in enumerate(levels):
            mask = level_hot[16 * level : 16 * level + 16, at]
            for c in range(3):
                row = 48 * i + 16 * c
                v_ref[row : row + 16, at] = values[c] * mask


def forward_kernel(step, tiles, levels, *refs):
    block_ref, block_a, block_b, *refs = refs
    first = step == 0
    if not first:
        basal_ref, rim_a, rim_b, *refs = refs
    cell_ref, fr_ref, factors, node_map, level_hot, cell_hot, spread_ref, order_ref, *refs = refs
    ordered_ref, a_ref, b_ref, *refs = refs
    if not first:
        squares_ref, *refs = refs
    if step == 1:
        field_ref, *refs = refs
    f_ref, v_ref = refs

    order = factors.shape[1]
    padded_order = f_ref.shape[1] // 2
    pairs = factors.shape[0] // 2
    tile = lax.axis_index("tiles")

    lane = lanes_iota((8, LANES))
    low = lane < RIM
    after, before = by_side(tile, block_a[:8, :], block_b[:8, :])
    starts = [
        block_ref[:8, :LANES],
        block_ref[:8, LANES:],
        jnp.where(low, after[:, :LANES], before[:, LANES:]),
    ]
    if first:
        parts = starts
    else:
        after, before = by_side(tile, rim_a[...], rim_b[...])
        parts = [basal_ref[:, i * LANES : (i + 1) * LANES] for i in range(3)]
        parts[0] = parts[0] + jnp.where(low, before, F32(0))
        parts[1] = parts[1] + jnp.where(low, F32(0), after)
        parts[2] = parts[2] + jnp.where(low, after, before)
        there = (low & (tile < tiles - 1)) | (~low & (tile > 0))
        parts[2] = jnp.where(there, parts[2], F32(0))
        kept = [(start != 0) if step % 2 == 0 else (start == 0) for start in starts]
        parts = [jnp.where(keep, part, F32(0)) for keep, part in zip(kept, parts)]
        if step == 1:
            field_ref[:, :LANES] = parts[0]
            field_ref[:, LANES:] = parts[1]
        squares_ref[...] = parts[0] * parts[0] + parts[1] * parts[1]
    window = jnp.concatenate(parts, axis=0)
    if step == 1:
        window = window * F32(SHRINK)

    cells = cell_ref[...]
    hi, lo = split(window)
    picked = dot(jnp.concatenate([hi, lo], axis=0), cell_hot[...])
    tops = []
    rests = []
    for m in range(pairs):
        part = picked[:, m * LANES : (m + 1) * LANES]
        which = cells[m : m + 1, :] // LANES
        for base, out in ((0, tops), (24, rests)):
            chosen = jnp.where(which == 0, part[base : base + 8], F32(0))
            for level in (1, 2):
                at = base + 8 * level
                chosen = jnp.where(which == level, part[at : at + 8], chosen)
            out.append(chosen)
    stacked = jnp.concatenate(tops + rests, axis=0).astype(BF16)
    spread = dot(stacked, spread_ref[...])
    half = 8 * pairs
    spread = spread[:half] + spread[half:]

    f_ref[...] = jnp.zeros_like(f_ref)
    for m in range(pairs):
        for side in range(2):
            at = side * padded_order
            slot = 2 * m + side
            inputs = spread[8 * m : 8 * m + 8, at : at + order] * fr_ref[slot : slot + 1, :order]
            if first:
                out = product(step > 0)(inputs.astype(BF16), factors[slot])
            else:
                hi = inputs.astype(BF16).astype(F32)
                both = jnp.concatenate([hi, inputs - hi], axis=0).astype(BF16)
                out = product(step > 0)(both, factors[slot])
                out = out[:8] + out[8:]
            hi = out.astype(BF16).astype(F32)
            f_ref[16 * m : 16 * m + 8, at : at + order] = hi
            f_ref[16 * m + 8 : 16 * m + 16, at : at + order] = out - hi

    ordered = dot(f_ref[...].astype(BF16), order_ref[...]).astype(BF16)
    ordered_ref[...] = ordered
    spread_levels(v_ref, ordered, level_hot, (0, levels - 1), pairs)
    rim = product(step > 0)(v_ref[...], node_map[...])
    sums = [rim[16 * i : 16 * i + 8] + rim[16 * i + 8 : 16 * i + 16] for i in range(6)]
    half = len(sums) // 2
    for i in range(half):
        lead, spill = sums[i], sums[half + i]
        a_ref[8 * i : 8 * i + 8, :], b_ref[8 * i : 8 * i + 8, :] = to_swaps(tile, spill, lead)


def inner_kernel(levels, ordered_ref, weight_ref, conn_ref, node_hot, level_hot, picked_ref, v_ref):
    pairs = conn_ref.shape[0]
    conn = conn_ref[...]
    inside = range(1, levels - 1)
    spread_levels(v_ref, ordered_ref, level_hot, inside, pairs)
    nodes = dot_nt(v_ref[...], node_hot[...])
    rows = []
    for i in range(3 * len(inside)):
        value = nodes[16 * i : 16 * i + 8] + nodes[16 * i + 8 : 16 * i + 16]
        at = inside[i // 3] * RADIX
        rows.append(value * weight_ref[i % 3 : i % 3 + 1, at : at + RADIX])
    weighted = jnp.concatenate(rows, axis=0).astype(BF16)
    step = 2
    for start in range(0, pairs, step):
        found = dot(weighted, node_hot[:, start * LANES : (start + step) * LANES])
        for i in range(step):
            m = start + i
            which = conn[m : m + 1, :] // RADIX
            part = found[:, i * LANES : (i + 1) * LANES]
            chosen = jnp.zeros((24, LANES), F32)
            for at, level in enumerate(inside):
                chosen = jnp.where(which == level, part[24 * at : 24 * at + 24], chosen)
            for c in range(3):
                picked_ref[8 * m : 8 * m + 8, c * LANES : (c + 1) * LANES] = chosen[8 * c : 8 * c + 8]


def adjoint_kernel(step, last, clusters, levels, *refs):
    block_ref, block_a, block_b, own_a, own_b, new_a, new_b, inner_ref, weight_ref, *refs = refs
    conn_ref, cell_ref, fr_ref, blocks, edge_hot, cell_map, spread_map, order_map, *refs = refs
    if last:
        squares_1, squares_2, ids_ref, *refs = refs
        basal_ref, out_ref, p_ref, n_ref, v_ref = refs
    else:
        basal_ref, a_ref, b_ref, p_ref, n_ref, v_ref = refs

    order = blocks.shape[1]
    padded_order = p_ref.shape[1] // 2
    pairs = blocks.shape[0] // 2
    tile = lax.axis_index("tiles")

    spill, lead = by_side(tile, own_a[...] + new_a[...], own_b[...] + new_b[...])
    after, before = by_side(tile, block_a[...], block_b[...])
    rows = []
    for i in range(3 * EDGE):
        c, at = i % 3, (i // 3) * EDGE_RADIX
        value = lead[8 * c : 8 * c + 8, at : at + EDGE_RADIX]
        rows.append(value * weight_ref[c : c + 1, at : at + EDGE_RADIX])
    for i in range(3 * EDGE):
        c, at = i % 3, (i // 3) * EDGE_RADIX
        value = spill[8 * c : 8 * c + 8, at : at + EDGE_RADIX]
        rows.append(value * after[8 + i : 9 + i, :])
    weighted = jnp.concatenate(rows, axis=0).astype(BF16)

    conn = conn_ref[...]
    first = levels * RADIX // EDGE_RADIX - EDGE
    edges = [*range(EDGE), *range(first, first + EDGE)]
    width = 2
    for start in range(0, pairs, width):
        found = dot(weighted, edge_hot[:, start * LANES : (start + width) * LANES])
        for i in range(width):
            m = start + i
            which = conn[m : m + 1, :] // EDGE_RADIX
            part = found[:, i * LANES : (i + 1) * LANES]
            for c in range(3):
                value = inner_ref[8 * m : 8 * m + 8, c * LANES : (c + 1) * LANES]
                for at, level in enumerate(edges):
                    row = 24 * at + 8 * c
                    value = jnp.where(which == level, part[row : row + 8], value)
                n_ref[8 * m : 8 * m + 8, c * LANES : (c + 1) * LANES] = value
    natural = product(step > 0)(n_ref[...].astype(BF16), order_map[...])
    p_ref[...] = jnp.zeros_like(p_ref)
    for m in range(pairs):
        for side in range(2):
            at = side * padded_order
            slot = 2 * m + side
            out = dot(natural[8 * m : 8 * m + 8, at : at + order].astype(BF16), blocks[slot])
            out = out * fr_ref[slot : slot + 1, :order]
            p_ref[8 * m : 8 * m + 8, at : at + order] = out

    hi, lo = split(p_ref[...])
    partial = product(step > 0)(jnp.concatenate([hi, lo], axis=0), spread_map[...])
    half = 8 * pairs
    partial = partial[:half] + partial[half:]
    cells = cell_ref[...]
    for m in range(pairs):
        which = cells[m : m + 1, :] // LANES
        value = partial[8 * m : 8 * m + 8, :]
        rows = jnp.concatenate([jnp.where(which == level, value, F32(0)) for level in range(3)], axis=0)
        hi = rows.astype(BF16).astype(F32)
        both = jnp.concatenate([hi, rows - hi], axis=0)
        v_ref[:, m * LANES : (m + 1) * LANES] = both.astype(BF16)
    basal = product(step > 0)(v_ref[...], cell_map[...])
    basal = basal[:24] + basal[24:]
    parts = [basal[8 * i : 8 * i + 8] for i in range(3)]
    for i in range(3):
        basal_ref[:, i * LANES : (i + 1) * LANES] = parts[i]
    lane = lanes_iota((8, LANES))
    if not last:
        for_next = jnp.where(lane < RIM, parts[2], parts[1])
        for_previous = jnp.where(lane < RIM, parts[0], parts[2])
        a_ref[...], b_ref[...] = to_swaps(tile, for_next, for_previous)
        return

    starts = [
        block_ref[:1, :LANES],
        block_ref[:1, LANES:],
        jnp.where(lane[:1] < RIM, after[:1, :LANES], before[:1, LANES:]),
    ]
    packed = []
    for start, part in zip(starts, parts):
        even = start != 0
        rows = [jnp.where(even, part[r + 1 : r + 2], part[r : r + 1]) for r in range(0, 8, 2)]
        packed.append(jnp.concatenate(rows, axis=0))
    extra = jnp.zeros((8, LANES), F32)
    for i, ref in enumerate((squares_1, squares_2)):
        rest = jnp.sum(ref[...], axis=1, keepdims=True)
        for j in range(3):
            piece = rest.astype(BF16).astype(F32)
            extra = jnp.where(lane == 3 * i + j, piece, extra)
            rest = rest - piece
    moved = pltpu.roll(extra, 8, 1)
    rows = [extra[r : r + 1] + moved[r + 1 : r + 2] for r in range(0, 8, 2)]
    extra = jnp.concatenate(rows, axis=0)
    ids = ids_ref[...]
    for k in range(1, clusters):
        below = jnp.sum((ids < k).astype(F32), axis=1, keepdims=True)
        extra = jnp.where(lane[:4] == 16 + k, below, extra)
    top = jnp.concatenate([packed[0], packed[1]], axis=1)
    message = jnp.concatenate([top, jnp.concatenate([packed[2], extra], axis=1)], axis=0)
    message = message.astype(BF16)
    for t in range(out_ref.shape[0]):
        out_ref[t] = message


def gram_kernel(
    keep_same, tiles, groups, g_ref, own_ref, samples_in, samples_ref, field_ref, gram_ref
):
    samples_ref[...] = samples_in[...]
    tile = lax.axis_index("tiles")
    group = lax.axis_index("probes")
    clusters = gram_ref.shape[0]
    cell_count = tiles * 2 * LANES
    low = lanes_iota((8, LANES)) < RIM
    row = rows_iota((8, LANES))

    def twice(x):
        out = jnp.broadcast_to(x[:1], (8, LANES))
        for r in range(1, 4):
            out = jnp.where(row >= 2 * r, jnp.broadcast_to(x[r : r + 1], (8, LANES)), out)
        return out

    def piece_of(t, p, lower, at):
        part = g_ref[t, p].astype(F32)
        return twice(part[4 * lower : 4 * lower + 4, at * LANES : (at + 1) * LANES])

    def factor_of(p):
        def add(t, acc):
            return acc + g_ref[t, p].astype(F32)[4:, LANES:]

        sums = lax.fori_loop(0, tiles, add, jnp.zeros((4, LANES), F32), unroll=tiles <= 8)
        sums = twice(sums)
        sums = jnp.where(row % 2 == 0, sums, pltpu.roll(sums, LANES - 8, 1))
        first = jnp.sum(sums[:, :3], axis=1, keepdims=True)
        second = jnp.sum(sums[:, 3:6], axis=1, keepdims=True)
        scale = jnp.sqrt(first / cell_count + F32(1e-06))
        size = jnp.sqrt(second / cell_count) * F32(1 / SHRINK) / scale
        return F32(1 / SHRINK) / (scale * jnp.sqrt(size * size + F32(1e-06)))

    def ids_of(t):
        starts = piece_of(t, 0, 1, 1)
        cell = lanes_iota((8, 2 * LANES)).astype(F32)
        ids = jnp.zeros(cell.shape, jnp.int32)
        for k in range(1, clusters):
            ids = ids + (cell >= starts[:, 16 + k : 17 + k]).astype(jnp.int32)
        return [ids[:, :LANES], ids[:, LANES:]]

    def field(t, p, ids, own=None):
        before = piece_of(jnp.maximum(t - 1, 0), p, 1, 0)
        after = piece_of(jnp.minimum(t + 1, tiles - 1), p, 1, 0)
        if own is None:
            own = [piece_of(t, p, 0, at) for at in range(2)]
        parts = [
            own[0] + jnp.where(low & (t > 0), before, F32(0)),
            own[1] + jnp.where(~low & (t < tiles - 1), after, F32(0)),
        ]
        return [
            jnp.where(colour_of(i) if keep_same else ~colour_of(i), part, F32(0))
            for i, part in zip(ids, parts)
        ]

    factors = [factor_of(p) for p in range(groups)]
    mine_factor = factors[0]
    for p in range(1, groups):
        mine_factor = jnp.where(group == p, factors[p], mine_factor)
    own = [own_ref[:, at * LANES : (at + 1) * LANES] for at in range(2)]
    own = field(tile, group, ids_of(tile), own)
    field_ref[:, :LANES] = own[0] * mine_factor
    field_ref[:, LANES:] = own[1] * mine_factor

    def add_tile(t, acc):
        ids = ids_of(t)
        every = [
            jnp.concatenate(field(t, p, ids), axis=1) * factors[p] for p in range(groups)
        ]
        mine = every[0]
        for p in range(1, groups):
            mine = jnp.where(group == p, every[p], mine)
        ids = jnp.concatenate(ids, axis=1)
        left = jnp.concatenate([jnp.where(ids == k, mine, F32(0)) for k in range(clusters)], axis=0)
        return acc + lax.dot_general(
            left,
            jnp.concatenate(every, axis=0),
            (((1,), (1,)), ((), ())),
            precision=lax.Precision.HIGHEST,
            preferred_element_type=F32,
        )

    acc = jnp.zeros((8 * clusters, 8 * groups), F32)
    acc = lax.fori_loop(0, tiles, add_tile, acc, unroll=tiles <= 8)
    gram_ref[...] = acc.reshape(gram_ref.shape)


def shards(
    blocks, connectivity, basal_map, friction, elem_counts, obs_weight, sign_bits, cluster_ids
):
    slots = blocks.shape[0]
    node_slots = connectivity.shape[1]
    node_count = obs_weight.shape[0]
    cell_count, group_size = sign_bits.shape
    tiles = lax.axis_size("tiles")
    groups = lax.axis_size("probes")
    pairs = slots * node_slots // LANES
    refs = pairs * LANES
    levels = (node_count + HALO) // RADIX
    padded_order = 2 * LANES
    window = cell_count + 2 * RIM

    vmem = pl.BlockSpec(memory_space=pltpu.VMEM)
    params = pltpu.CompilerParams(vmem_limit_bytes=VMEM_BYTES)
    shaped = jax.ShapeDtypeStruct

    hbm = pl.BlockSpec(memory_space=pltpu.HBM)
    smem = pl.BlockSpec(memory_space=pltpu.SMEM)

    def call(kernel, name, out_shape, operands, scratch=(), in_specs=None):
        in_specs = in_specs or [vmem] * len(operands)
        operands = [
            pltpu.with_memory_space_constraint(x, pltpu.HBM) if spec is hbm else x
            for x, spec in zip(operands, in_specs)
        ]
        return pl.pallas_call(
            kernel,
            out_shape=out_shape,
            in_specs=in_specs,
            out_specs=jax.tree.map(lambda _: vmem, out_shape),
            scratch_shapes=list(scratch),
            compiler_params=params,
            name=name,
        )(*operands)

    evens = range(0, tiles - 1, 2)
    odds = range(1, tiles - 1, 2)
    pairs_a = [(i, i + 1) for i in odds] + [(i + 1, i) for i in odds]
    pairs_b = [(i, i + 1) for i in evens] + [(i + 1, i) for i in evens]

    def swapped(a, b):
        return lax.ppermute(a, "tiles", pairs_a), lax.ppermute(b, "tiles", pairs_b)

    weight = obs_weight.T
    block, again = call(
        announce_kernel,
        "announce",
        [shaped((16, cell_count), F32)] * 2,
        [sign_bits.T, cluster_ids.reshape(1, cell_count), weight],
        [
            pltpu.VMEM((group_size, cell_count), jnp.int32),
            pltpu.VMEM((1, cell_count), jnp.int32),
            pltpu.VMEM((3, HALO), F32),
            pltpu.SemaphoreType.DMA((3,)),
        ],
        [hbm] * 3,
    )
    block_a, block_b = swapped(again, block)

    conn, cells, fr, loaded, node_hot, edge_hot, level_hot, cell_hot, spread, order = call(
        functools.partial(setup_kernel, levels),
        "setup",
        [
            shaped((pairs, LANES), jnp.int32),
            shaped((pairs, LANES), jnp.int32),
            shaped((slots, padded_order), F32),
            shaped(blocks.shape, BF16),
            shaped((RADIX, refs), BF16),
            shaped((EDGE_RADIX, refs), BF16),
            shaped((16 * levels, refs), BF16),
            shaped((LANES, refs), BF16),
            shaped((LANES, 2 * padded_order), BF16),
            shaped((2 * padded_order, 3 * LANES), BF16),
        ],
        [elem_counts, connectivity, basal_map, friction.transpose(2, 0, 1), blocks],
        [
            pltpu.VMEM(connectivity.shape, jnp.int32),
            pltpu.VMEM(basal_map.shape, jnp.int32),
            pltpu.VMEM((3, slots, node_slots), F32),
            pltpu.SemaphoreType.DMA((4,)),
        ],
        [smem] + [hbm] * 4,
    )
    factors, node_map, cell_map, spread_map, order_map = loaded, node_hot, cell_hot, spread, order

    edge = shaped((24, HALO), F32)
    rim = shaped((group_size, LANES), F32)
    whole = shaped((group_size, window), F32)
    field = shaped((group_size, cell_count), F32)
    everyone = ("tiles", "probes")

    carried = []
    factors = loaded
    squares = []
    samples = None
    for step in range(POWER + 1):
        last = step == POWER
        out_shape = [shaped((16 * pairs, 3 * LANES), BF16), edge, edge]
        out_shape += [rim] * (step > 0) + [field] * (step == 1)
        ordered, own_a, own_b, *extra = call(
            functools.partial(forward_kernel, step, tiles, levels),
            "forward",
            out_shape,
            [block, block_a, block_b, *carried]
            + [cells, fr, factors, node_map, level_hot, cell_hot, spread, order],
            [
                pltpu.VMEM((16 * pairs, 2 * padded_order), F32),
                pltpu.VMEM((96, refs), BF16),
            ],
        )
        squares += extra[:1]
        if step == 1:
            samples = extra[1]
        if step == 0:
            own_a, own_b, settled = lax.optimization_barrier((own_a, own_b, conn))
            shape = shaped((refs, RADIX), BF16)
            node_map = call(turn_nodes_kernel, "turn_nodes", shape, [settled])
        new_a, new_b = swapped(own_a, own_b)
        inner = call(
            functools.partial(inner_kernel, levels),
            "inner",
            shaped((8 * pairs, 3 * LANES), F32),
            [ordered, weight, conn, node_hot, level_hot],
            [pltpu.VMEM((48 * (levels - 2), refs), BF16)],
        )
        if step == 0:
            inner, node_map = lax.optimization_barrier((inner, node_map))
        operands = [block, block_a, block_b, own_a, own_b, new_a, new_b, inner, weight]
        operands += [conn, cells, fr, loaded, edge_hot, cell_map, spread_map, order_map]
        if last:
            operands += squares + [cluster_ids.reshape(1, cell_count)]
            message = shaped((lax.axis_size(everyone), group_size, 2 * LANES), BF16)
            out_shape = [whole, message]
        else:
            out_shape = [whole, rim, rim]
        basal, *messages = call(
            functools.partial(adjoint_kernel, step, last, tiles, levels),
            "adjoint",
            out_shape,
            operands,
            [
                pltpu.VMEM((8 * pairs, 2 * padded_order), F32),
                pltpu.VMEM((8 * pairs, 3 * LANES), F32),
                pltpu.VMEM((48, refs), BF16),
            ],
        )
        if not last:
            if step == 0:
                *messages, settled = lax.optimization_barrier((*messages, loaded))
                factors, cell_map, spread_map, order_map = call(
                    turn_kernel,
                    "turn",
                    [
                        shaped(blocks.shape, BF16),
                        shaped((refs, LANES), BF16),
                        shaped((2 * padded_order, LANES), BF16),
                        shaped((3 * LANES, 2 * padded_order), BF16),
                    ],
                    [settled, cells],
                )
            carried = [basal, *swapped(*messages)]

    gathered = lax.all_to_all(messages[0], everyone, 0, 0)
    gathered = gathered.reshape(tiles, groups, *gathered.shape[1:])
    samples, refined, gram = call(
        functools.partial(gram_kernel, POWER % 2 == 1, tiles, groups),
        "gram",
        [field, field, shaped((tiles, group_size, groups * group_size), F32)],
        [gathered, basal, samples],
    )
    return (samples.T, refined.T, gram)


def solution(mesh):
    in_specs = (
        P("tiles", None, None),
        P("tiles", None),
        P("tiles", None),
        P("tiles", None, None),
        P("tiles"),
        P("tiles", None),
        P("tiles", "probes"),
        P("tiles"),
    )
    out_specs = (P("tiles", "probes"), P("tiles", "probes"), P(None, "probes", None))
    return jax.shard_map(shards, mesh=mesh, in_specs=in_specs, out_specs=out_specs, check_vma=False)
```

```python
import functools

import jax
import jax.numpy as jnp
from jax import lax
from jax.experimental import pallas as pl
from jax.experimental.pallas import tpu as pltpu
from jax.sharding import PartitionSpec as P

HALO = 512
POWER = 2
RIM = 64
LANES = 128
RADIX = 512
EDGE_RADIX = 256
EDGE = HALO // EDGE_RADIX
SHRINK = 2.0**-40
VMEM_BYTES = 16 * 1024 * 1024

F32 = jnp.float32
BF16 = jnp.bfloat16


def dot(a, b):
    return lax.dot_general(a, b, (((1,), (0,)), ((), ())), preferred_element_type=F32)


def dot_nt(a, b):
    return lax.dot_general(a, b, (((1,), (1,)), ((), ())), preferred_element_type=F32)


def product(turned):
    return dot if turned else dot_nt


def split(x):
    hi = x.astype(BF16)
    return hi, (x - hi.astype(F32)).astype(BF16)


def rows_iota(shape):
    return lax.broadcasted_iota(jnp.int32, shape, 0)


def lanes_iota(shape):
    return lax.broadcasted_iota(jnp.int32, shape, 1)


def hot(mask):
    return jnp.where(mask, F32(1), F32(0)).astype(BF16)


def hot16(a, b):
    return jnp.where(a == b, jnp.ones((), BF16), jnp.zeros((), BF16))


def lane_tiles(count, tile):
    return jnp.concatenate([tile(i * LANES) for i in range(count)], axis=1)


def spread_matrix(node_slots, padded_order, turned=False):
    pair, wide = 2 * node_slots, 2 * padded_order

    def start(at):
        return (at // node_slots) * padded_order + 3 * (at % node_slots)

    def near(gap):
        return hot((gap >= 0) & (gap < 3))

    if turned:
        return near(rows_iota((wide, pair)) - start(lanes_iota((1, pair))))
    gap = lanes_iota((pair, LANES)) - start(rows_iota((pair, LANES)))
    return lane_tiles(wide // LANES, lambda at: near(gap + at))


def order_matrix(node_slots, padded_order, turned=False):
    pair, wide = 2 * node_slots, 2 * padded_order

    def source(at):
        inner = at % pair
        return (inner // node_slots) * padded_order + 3 * (inner % node_slots) + at // pair

    if not turned:
        return hot(rows_iota((wide, 3 * pair)) == source(lanes_iota((1, 3 * pair))))
    gap = lanes_iota((3 * pair, LANES)) - source(rows_iota((3 * pair, LANES)))
    return lane_tiles(wide // LANES, lambda at: hot(gap + at == 0))


def colour_of(ids):
    return (ids % 2) == (rows_iota(ids.shape) % 2)


def by_side(tile, a, b):
    even = tile % 2 == 0
    return jnp.where(even, b, a), jnp.where(even, a, b)


def to_swaps(tile, for_next, for_previous):
    even = tile % 2 == 0
    return jnp.where(even, for_previous, for_next), jnp.where(even, for_next, for_previous)


def announce_kernel(signs_hbm, ids_hbm, weight_hbm, out_ref, again_ref, signs, ids, lead, sems):
    loads = [
        pltpu.make_async_copy(signs_hbm, signs, sems.at[0]),
        pltpu.make_async_copy(ids_hbm, ids, sems.at[1]),
        pltpu.make_async_copy(weight_hbm.at[:, pl.ds(0, HALO)], lead, sems.at[2]),
    ]
    for load in loads:
        load.start()
    for load in loads:
        load.wait()
    colours = jnp.broadcast_to(ids[...], signs.shape)
    probes = jnp.where(colour_of(colours), (2 * signs[...] - 1).astype(F32), F32(0))
    out_ref[:8, :] = probes
    out_ref[8:, :] = jnp.zeros_like(probes)
    half = HALO // 2
    out_ref[8:11, :] = lead[:, :half]
    out_ref[11:14, :] = lead[:, half:]
    again_ref[...] = out_ref[...]


def halves_of(conn):
    low = conn % RADIX
    halves = []
    for at in range(0, RADIX, EDGE_RADIX):
        inside = (low >= at) & (low < at + EDGE_RADIX)
        halves.append(jnp.where(inside, low - at, -1).astype(F32))
    return halves


def setup_kernel(
    levels,
    counts,
    conn_hbm,
    cell_hbm,
    friction_hbm,
    blocks_hbm,
    conn_ref,
    cell_ref,
    fr_ref,
    blocks_ref,
    node_hot_ref,
    edge_hot_ref,
    level_hot_ref,
    cell_hot_ref,
    spread_ref,
    order_ref,
    conn_in,
    cell_in,
    friction_in,
    sems,
):
    pairs = conn_ref.shape[0]
    slots, padded_order = fr_ref.shape
    node_slots = conn_in.shape[1]
    window = 3 * LANES

    loads = [
        pltpu.make_async_copy(source, target, sems.at[i])
        for i, (source, target) in enumerate(
            [
                (conn_hbm, conn_in),
                (cell_hbm, cell_in),
                (friction_hbm, friction_in),
                (blocks_hbm, blocks_ref),
            ]
        )
    ]
    for load in loads:
        load.start()

    spread_ref[...] = spread_matrix(node_slots, padded_order)
    order_ref[...] = order_matrix(node_slots, padded_order)

    def paired(ref):
        return jnp.concatenate(
            [ref[pl.ds(0, pairs, stride=2), :], ref[pl.ds(1, pairs, stride=2), :]], axis=1
        )

    for load in loads[:3]:
        load.wait()
    conn = paired(conn_in)
    conn_ref[...] = conn
    cells = paired(cell_in)
    cells = jnp.where(cells < RIM, cells + (window - RIM), cells - RIM)
    cell_ref[...] = cells

    shape = (node_slots, padded_order)
    total = jnp.zeros((slots, padded_order), F32)
    for c in range(3):
        place = hot(lanes_iota(shape) == 3 * rows_iota(shape) + c)
        rest = friction_in[c]
        for _ in range(3):
            part = rest.astype(BF16)
            total = total + dot(part, place)
            rest = rest - part.astype(F32)
    live = rows_iota(total.shape) < counts[0]
    fr_ref[...] = jnp.where(live, total, F32(0))

    rows = rows_iota((EDGE_RADIX, LANES)).astype(F32).astype(BF16)
    halves = halves_of(conn)
    which = (conn // RADIX).astype(F32)
    cell_low = (cells % LANES).astype(F32)
    for m in range(pairs):
        at = pl.ds(m * LANES, LANES)
        total = jnp.zeros((EDGE_RADIX, LANES), BF16)
        for i, half in enumerate(halves):
            row = jnp.broadcast_to(half[m : m + 1, :], (EDGE_RADIX, LANES)).astype(BF16)
            mine = hot16(rows, row)
            node_hot_ref[i * EDGE_RADIX : (i + 1) * EDGE_RADIX, at] = mine
            total = total + mine
        edge_hot_ref[:, at] = total
        row = jnp.broadcast_to(which[m : m + 1, :], (16, LANES)).astype(BF16)
        for level in range(levels):
            mine = hot16(row, jnp.full((16, LANES), level, BF16))
            level_hot_ref[16 * level : 16 * level + 16, at] = mine
        row = jnp.broadcast_to(cell_low[m : m + 1, :], (LANES, LANES)).astype(BF16)
        cell_hot_ref[:, at] = hot16(rows[:LANES], row)
    loads[3].wait()


def turn_nodes_kernel(conn_ref, node_turn_ref):
    columns = [half.T for half in halves_of(conn_ref[...])]
    lanes = lanes_iota((LANES, EDGE_RADIX)).astype(F32).astype(BF16)
    for m in range(conn_ref.shape[0]):
        for i, column in enumerate(columns):
            row = jnp.broadcast_to(column[:, m : m + 1], (LANES, LANES)).astype(BF16)
            row = jnp.concatenate([row] * (EDGE_RADIX // LANES), axis=1)
            at = pl.ds(i * EDGE_RADIX, EDGE_RADIX)
            node_turn_ref[m * LANES : (m + 1) * LANES, at] = hot16(lanes, row)


def turn_blocks_kernel(blocks, turned_ref):
    for slot in range(blocks.shape[0]):
        turned_ref[slot] = blocks[slot].T


def turn_cells_kernel(node_slots, cell_ref, cell_turn_ref, spread_turn_ref, order_turn_ref):
    padded_order = order_turn_ref.shape[1] // 2
    spread_turn_ref[...] = spread_matrix(node_slots, padded_order, True)
    order_turn_ref[...] = order_matrix(node_slots, padded_order, True)
    cells = (cell_ref[...] % LANES).astype(F32).T
    lanes = lanes_iota((LANES, LANES)).astype(F32).astype(BF16)
    for m in range(cell_ref.shape[0]):
        row = jnp.broadcast_to(cells[:, m : m + 1], (LANES, LANES)).astype(BF16)
        cell_turn_ref[m * LANES : (m + 1) * LANES, :] = hot16(lanes, row)


def spread_levels(v_ref, ordered, level_hot, levels, pairs):
    for m in range(pairs):
        at = pl.ds(m * LANES, LANES)
        values = [ordered[16 * m : 16 * m + 16, c * LANES : (c + 1) * LANES] for c in range(3)]
        for i, level in enumerate(levels):
            mask = level_hot[16 * level : 16 * level + 16, at]
            for c in range(3):
                row = 48 * i + 16 * c
                v_ref[row : row + 16, at] = values[c] * mask


def forward_kernel(step, tiles, levels, *refs):
    block_ref, block_a, block_b, *refs = refs
    first = step == 0
    if not first:
        basal_ref, rim_a, rim_b, *refs = refs
    cell_ref, fr_ref, factors, node_map, level_hot, cell_hot, spread_ref, order_ref, *refs = refs
    ordered_ref, a_ref, b_ref, far_ref, near_ref, *refs = refs
    if not first:
        squares_ref, *refs = refs
    if step == 1:
        field_ref, *refs = refs
    f_ref, v_ref = refs

    order = factors.shape[1]
    padded_order = f_ref.shape[1] // 2
    pairs = factors.shape[0] // 2
    tile = lax.axis_index("tiles")

    lane = lanes_iota((8, LANES))
    low = lane < RIM
    after, before = by_side(tile, block_a[:8, :], block_b[:8, :])
    starts = [
        block_ref[:8, :LANES],
        block_ref[:8, LANES:],
        jnp.where(low, after[:, :LANES], before[:, LANES:]),
    ]
    if first:
        parts = starts
    else:
        after, before = by_side(tile, rim_a[...], rim_b[...])
        parts = [basal_ref[:, i * LANES : (i + 1) * LANES] for i in range(3)]
        parts[0] = parts[0] + jnp.where(low, before, F32(0))
        parts[1] = parts[1] + jnp.where(low, F32(0), after)
        parts[2] = parts[2] + jnp.where(low, after, before)
        there = (low & (tile < tiles - 1)) | (~low & (tile > 0))
        parts[2] = jnp.where(there, parts[2], F32(0))
        kept = [(start != 0) if step % 2 == 0 else (start == 0) for start in starts]
        parts = [jnp.where(keep, part, F32(0)) for keep, part in zip(kept, parts)]
        if step == 1:
            field_ref[:, :LANES] = parts[0]
            field_ref[:, LANES:] = parts[1]
        squares_ref[...] = parts[0] * parts[0] + parts[1] * parts[1]
    window = jnp.concatenate(parts, axis=0)
    if step == 1:
        window = window * F32(SHRINK)

    cells = cell_ref[...]
    hi, lo = split(window)
    picked = dot(jnp.concatenate([hi, lo], axis=0), cell_hot[...])
    tops = []
    rests = []
    for m in range(pairs):
        part = picked[:, m * LANES : (m + 1) * LANES]
        which = cells[m : m + 1, :] // LANES
        for base, out in ((0, tops), (24, rests)):
            chosen = jnp.where(which == 0, part[base : base + 8], F32(0))
            for level in (1, 2):
                at = base + 8 * level
                chosen = jnp.where(which == level, part[at : at + 8], chosen)
            out.append(chosen)
    stacked = jnp.concatenate(tops + rests, axis=0).astype(BF16)
    spread = dot(stacked, spread_ref[...])
    half = 8 * pairs
    spread = spread[:half] + spread[half:]

    f_ref[...] = jnp.zeros_like(f_ref)
    for m in range(pairs):
        for side in range(2):
            at = side * padded_order
            slot = 2 * m + side
            inputs = spread[8 * m : 8 * m + 8, at : at + order] * fr_ref[slot : slot + 1, :order]
            if first:
                out = product(step > 0)(inputs.astype(BF16), factors[slot])
            else:
                hi = inputs.astype(BF16).astype(F32)
                both = jnp.concatenate([hi, inputs - hi], axis=0).astype(BF16)
                out = product(step > 0)(both, factors[slot])
                out = out[:8] + out[8:]
            hi = out.astype(BF16).astype(F32)
            f_ref[16 * m : 16 * m + 8, at : at + order] = hi
            f_ref[16 * m + 8 : 16 * m + 16, at : at + order] = out - hi

    ordered = dot(f_ref[...].astype(BF16), order_ref[...]).astype(BF16)
    ordered_ref[...] = ordered
    spread_levels(v_ref, ordered, level_hot, (0, levels - 1), pairs)
    rim = product(step > 0)(v_ref[...], node_map[...])
    sums = [rim[16 * i : 16 * i + 8] + rim[16 * i + 8 : 16 * i + 16] for i in range(6)]
    lead, spill = (jnp.concatenate(part, axis=0) for part in (sums[:3], sums[3:]))
    for ref, message, value in zip((a_ref, b_ref), (far_ref, near_ref), to_swaps(tile, spill, lead)):
        ref[...] = value
        pieces = [value[:, i * EDGE_RADIX : (i + 1) * EDGE_RADIX] for i in range(EDGE)]
        message[...] = jnp.concatenate(pieces, axis=0).astype(BF16)


def inner_kernel(levels, ordered_ref, weight_ref, conn_ref, node_hot, level_hot, picked_ref, v_ref):
    pairs = conn_ref.shape[0]
    conn = conn_ref[...]
    inside = range(1, levels - 1)
    spread_levels(v_ref, ordered_ref, level_hot, inside, pairs)
    nodes = dot_nt(v_ref[...], node_hot[...])
    rows = []
    for i in range(3 * len(inside)):
        value = nodes[16 * i : 16 * i + 8] + nodes[16 * i + 8 : 16 * i + 16]
        at = inside[i // 3] * RADIX
        rows.append(value * weight_ref[i % 3 : i % 3 + 1, at : at + RADIX])
    weighted = jnp.concatenate(rows, axis=0).astype(BF16)
    step = 2
    for start in range(0, pairs, step):
        found = dot(weighted, node_hot[:, start * LANES : (start + step) * LANES])
        for i in range(step):
            m = start + i
            which = conn[m : m + 1, :] // RADIX
            part = found[:, i * LANES : (i + 1) * LANES]
            chosen = jnp.zeros((24, LANES), F32)
            for at, level in enumerate(inside):
                chosen = jnp.where(which == level, part[24 * at : 24 * at + 24], chosen)
            for c in range(3):
                picked_ref[8 * m : 8 * m + 8, c * LANES : (c + 1) * LANES] = chosen[8 * c : 8 * c + 8]


def adjoint_kernel(step, last, clusters, levels, *refs):
    block_ref, block_a, block_b, own_a, own_b, new_a, new_b, inner_ref, weight_ref, *refs = refs
    conn_ref, cell_ref, fr_ref, blocks, edge_hot, cell_map, spread_map, order_map, *refs = refs
    if last:
        squares_1, squares_2, ids_ref, *refs = refs
        basal_ref, out_ref, p_ref, n_ref, v_ref = refs
    else:
        basal_ref, a_ref, b_ref, p_ref, n_ref, v_ref = refs

    order = blocks.shape[1]
    padded_order = p_ref.shape[1] // 2
    pairs = blocks.shape[0] // 2
    tile = lax.axis_index("tiles")

    spill, lead = by_side(tile, own_a[...], own_b[...])
    new_spill, new_lead = by_side(tile, new_a[...].astype(F32), new_b[...].astype(F32))
    after, before = by_side(tile, block_a[...], block_b[...])
    rows = []
    for i in range(3 * EDGE):
        c, at = i % 3, (i // 3) * EDGE_RADIX
        value = lead[8 * c : 8 * c + 8, at : at + EDGE_RADIX] + new_lead[8 * i : 8 * i + 8]
        rows.append(value * weight_ref[c : c + 1, at : at + EDGE_RADIX])
    for i in range(3 * EDGE):
        c, at = i % 3, (i // 3) * EDGE_RADIX
        value = spill[8 * c : 8 * c + 8, at : at + EDGE_RADIX] + new_spill[8 * i : 8 * i + 8]
        rows.append(value * after[8 + i : 9 + i, :])
    weighted = jnp.concatenate(rows, axis=0).astype(BF16)

    conn = conn_ref[...]
    first = levels * RADIX // EDGE_RADIX - EDGE
    edges = [*range(EDGE), *range(first, first + EDGE)]
    width = 2
    for start in range(0, pairs, width):
        found = dot(weighted, edge_hot[:, start * LANES : (start + width) * LANES])
        for i in range(width):
            m = start + i
            which = conn[m : m + 1, :] // EDGE_RADIX
            part = found[:, i * LANES : (i + 1) * LANES]
            for c in range(3):
                value = inner_ref[8 * m : 8 * m + 8, c * LANES : (c + 1) * LANES]
                for at, level in enumerate(edges):
                    row = 24 * at + 8 * c
                    value = jnp.where(which == level, part[row : row + 8], value)
                n_ref[8 * m : 8 * m + 8, c * LANES : (c + 1) * LANES] = value
    natural = product(step > 0)(n_ref[...].astype(BF16), order_map[...])
    p_ref[...] = jnp.zeros_like(p_ref)
    for m in range(pairs):
        for side in range(2):
            at = side * padded_order
            slot = 2 * m + side
            out = dot(natural[8 * m : 8 * m + 8, at : at + order].astype(BF16), blocks[slot])
            out = out * fr_ref[slot : slot + 1, :order]
            p_ref[8 * m : 8 * m + 8, at : at + order] = out

    hi, lo = split(p_ref[...])
    partial = product(step > 0)(jnp.concatenate([hi, lo], axis=0), spread_map[...])
    half = 8 * pairs
    partial = partial[:half] + partial[half:]
    cells = cell_ref[...]
    for m in range(pairs):
        which = cells[m : m + 1, :] // LANES
        value = partial[8 * m : 8 * m + 8, :]
        rows = jnp.concatenate([jnp.where(which == level, value, F32(0)) for level in range(3)], axis=0)
        hi = rows.astype(BF16).astype(F32)
        both = jnp.concatenate([hi, rows - hi], axis=0)
        v_ref[:, m * LANES : (m + 1) * LANES] = both.astype(BF16)
    basal = product(step > 0)(v_ref[...], cell_map[...])
    basal = basal[:24] + basal[24:]
    parts = [basal[8 * i : 8 * i + 8] for i in range(3)]
    for i in range(3):
        basal_ref[:, i * LANES : (i + 1) * LANES] = parts[i]
    lane = lanes_iota((8, LANES))
    if not last:
        for_next = jnp.where(lane < RIM, parts[2], parts[1])
        for_previous = jnp.where(lane < RIM, parts[0], parts[2])
        a_ref[...], b_ref[...] = to_swaps(tile, for_next, for_previous)
        return

    starts = [
        block_ref[:1, :LANES],
        block_ref[:1, LANES:],
        jnp.where(lane[:1] < RIM, after[:1, :LANES], before[:1, LANES:]),
    ]
    packed = []
    for start, part in zip(starts, parts):
        even = start != 0
        rows = [jnp.where(even, part[r + 1 : r + 2], part[r : r + 1]) for r in range(0, 8, 2)]
        packed.append(jnp.concatenate(rows, axis=0))
    extra = jnp.zeros((8, LANES), F32)
    for i, ref in enumerate((squares_1, squares_2)):
        rest = jnp.sum(ref[...], axis=1, keepdims=True)
        for j in range(3):
            piece = rest.astype(BF16).astype(F32)
            extra = jnp.where(lane == 3 * i + j, piece, extra)
            rest = rest - piece
    moved = pltpu.roll(extra, 8, 1)
    rows = [extra[r : r + 1] + moved[r + 1 : r + 2] for r in range(0, 8, 2)]
    extra = jnp.concatenate(rows, axis=0)
    ids = ids_ref[...]
    for k in range(1, clusters):
        below = jnp.sum((ids < k).astype(F32), axis=1, keepdims=True)
        extra = jnp.where(lane[:4] == 16 + k, below, extra)
    top = jnp.concatenate([packed[0], packed[1]], axis=1)
    message = jnp.concatenate([top, jnp.concatenate([packed[2], extra], axis=1)], axis=0)
    message = message.astype(BF16)
    for t in range(out_ref.shape[0]):
        out_ref[t] = message


def gram_kernel(
    keep_same, tiles, groups, g_ref, own_ref, samples_in, samples_ref, field_ref, gram_ref
):
    samples_ref[...] = samples_in[...]
    tile = lax.axis_index("tiles")
    group = lax.axis_index("probes")
    clusters = gram_ref.shape[0]
    cell_count = tiles * 2 * LANES
    low = lanes_iota((8, LANES)) < RIM
    row = rows_iota((8, LANES))

    def twice(x):
        out = jnp.broadcast_to(x[:1], (8, LANES))
        for r in range(1, 4):
            out = jnp.where(row >= 2 * r, jnp.broadcast_to(x[r : r + 1], (8, LANES)), out)
        return out

    def piece_of(t, p, lower, at):
        part = g_ref[t, p].astype(F32)
        return twice(part[4 * lower : 4 * lower + 4, at * LANES : (at + 1) * LANES])

    def factor_of(p):
        def add(t, acc):
            return acc + g_ref[t, p].astype(F32)[4:, LANES:]

        sums = lax.fori_loop(0, tiles, add, jnp.zeros((4, LANES), F32), unroll=tiles <= 8)
        sums = twice(sums)
        sums = jnp.where(row % 2 == 0, sums, pltpu.roll(sums, LANES - 8, 1))
        first = jnp.sum(sums[:, :3], axis=1, keepdims=True)
        second = jnp.sum(sums[:, 3:6], axis=1, keepdims=True)
        scale = jnp.sqrt(first / cell_count + F32(1e-06))
        size = jnp.sqrt(second / cell_count) * F32(1 / SHRINK) / scale
        return F32(1 / SHRINK) / (scale * jnp.sqrt(size * size + F32(1e-06)))

    def ids_of(t):
        starts = piece_of(t, 0, 1, 1)
        cell = lanes_iota((8, 2 * LANES)).astype(F32)
        ids = jnp.zeros(cell.shape, jnp.int32)
        for k in range(1, clusters):
            ids = ids + (cell >= starts[:, 16 + k : 17 + k]).astype(jnp.int32)
        return [ids[:, :LANES], ids[:, LANES:]]

    def field(t, p, ids, own=None):
        before = piece_of(jnp.maximum(t - 1, 0), p, 1, 0)
        after = piece_of(jnp.minimum(t + 1, tiles - 1), p, 1, 0)
        if own is None:
            own = [piece_of(t, p, 0, at) for at in range(2)]
        parts = [
            own[0] + jnp.where(low & (t > 0), before, F32(0)),
            own[1] + jnp.where(~low & (t < tiles - 1), after, F32(0)),
        ]
        return [
            jnp.where(colour_of(i) if keep_same else ~colour_of(i), part, F32(0))
            for i, part in zip(ids, parts)
        ]

    factors = [factor_of(p) for p in range(groups)]
    mine_factor = factors[0]
    for p in range(1, groups):
        mine_factor = jnp.where(group == p, factors[p], mine_factor)
    own = [own_ref[:, at * LANES : (at + 1) * LANES] for at in range(2)]
    own = field(tile, group, ids_of(tile), own)
    field_ref[:, :LANES] = own[0] * mine_factor
    field_ref[:, LANES:] = own[1] * mine_factor

    def add_tile(t, acc):
        ids = ids_of(t)
        every = [
            jnp.concatenate(field(t, p, ids), axis=1) * factors[p] for p in range(groups)
        ]
        mine = every[0]
        for p in range(1, groups):
            mine = jnp.where(group == p, every[p], mine)
        ids = jnp.concatenate(ids, axis=1)
        left = jnp.concatenate([jnp.where(ids == k, mine, F32(0)) for k in range(clusters)], axis=0)
        return acc + lax.dot_general(
            left,
            jnp.concatenate(every, axis=0),
            (((1,), (1,)), ((), ())),
            precision=lax.Precision.HIGHEST,
            preferred_element_type=F32,
        )

    acc = jnp.zeros((8 * clusters, 8 * groups), F32)
    acc = lax.fori_loop(0, tiles, add_tile, acc, unroll=tiles <= 8)
    gram_ref[...] = acc.reshape(gram_ref.shape)


def shards(
    blocks, connectivity, basal_map, friction, elem_counts, obs_weight, sign_bits, cluster_ids
):
    slots = blocks.shape[0]
    node_slots = connectivity.shape[1]
    node_count = obs_weight.shape[0]
    cell_count, group_size = sign_bits.shape
    tiles = lax.axis_size("tiles")
    groups = lax.axis_size("probes")
    pairs = slots * node_slots // LANES
    refs = pairs * LANES
    levels = (node_count + HALO) // RADIX
    padded_order = 2 * LANES
    window = cell_count + 2 * RIM

    vmem = pl.BlockSpec(memory_space=pltpu.VMEM)
    params = pltpu.CompilerParams(vmem_limit_bytes=VMEM_BYTES)
    shaped = jax.ShapeDtypeStruct

    hbm = pl.BlockSpec(memory_space=pltpu.HBM)
    smem = pl.BlockSpec(memory_space=pltpu.SMEM)

    def call(kernel, name, out_shape, operands, scratch=(), in_specs=None):
        in_specs = in_specs or [vmem] * len(operands)
        operands = [
            pltpu.with_memory_space_constraint(x, pltpu.HBM) if spec is hbm else x
            for x, spec in zip(operands, in_specs)
        ]
        return pl.pallas_call(
            kernel,
            out_shape=out_shape,
            in_specs=in_specs,
            out_specs=jax.tree.map(lambda _: vmem, out_shape),
            scratch_shapes=list(scratch),
            compiler_params=params,
            name=name,
        )(*operands)

    evens = range(0, tiles - 1, 2)
    odds = range(1, tiles - 1, 2)
    pairs_a = [(i, i + 1) for i in odds] + [(i + 1, i) for i in odds]
    pairs_b = [(i, i + 1) for i in evens] + [(i + 1, i) for i in evens]

    def swapped(a, b):
        return lax.ppermute(a, "tiles", pairs_a), lax.ppermute(b, "tiles", pairs_b)

    weight = obs_weight.T
    block, again = call(
        announce_kernel,
        "announce",
        [shaped((16, cell_count), F32)] * 2,
        [sign_bits.T, cluster_ids.reshape(1, cell_count), weight],
        [
            pltpu.VMEM((group_size, cell_count), jnp.int32),
            pltpu.VMEM((1, cell_count), jnp.int32),
            pltpu.VMEM((3, HALO), F32),
            pltpu.SemaphoreType.DMA((3,)),
        ],
        [hbm] * 3,
    )
    block_a, block_b = swapped(again, block)

    conn, cells, fr, loaded, node_hot, edge_hot, level_hot, cell_hot, spread, order = call(
        functools.partial(setup_kernel, levels),
        "setup",
        [
            shaped((pairs, LANES), jnp.int32),
            shaped((pairs, LANES), jnp.int32),
            shaped((slots, padded_order), F32),
            shaped(blocks.shape, BF16),
            shaped((RADIX, refs), BF16),
            shaped((EDGE_RADIX, refs), BF16),
            shaped((16 * levels, refs), BF16),
            shaped((LANES, refs), BF16),
            shaped((LANES, 2 * padded_order), BF16),
            shaped((2 * padded_order, 3 * LANES), BF16),
        ],
        [elem_counts, connectivity, basal_map, friction.transpose(2, 0, 1), blocks],
        [
            pltpu.VMEM(connectivity.shape, jnp.int32),
            pltpu.VMEM(basal_map.shape, jnp.int32),
            pltpu.VMEM((3, slots, node_slots), F32),
            pltpu.SemaphoreType.DMA((4,)),
        ],
        [smem] + [hbm] * 4,
    )
    factors, node_map, cell_map, spread_map, order_map = loaded, node_hot, cell_hot, spread, order

    edge = shaped((24, HALO), F32)
    message = shaped((24 * EDGE, EDGE_RADIX), BF16)
    rim = shaped((group_size, LANES), F32)
    whole = shaped((group_size, window), F32)
    field = shaped((group_size, cell_count), F32)
    everyone = ("tiles", "probes")

    carried = []
    factors = loaded
    squares = []
    samples = None
    for step in range(POWER + 1):
        last = step == POWER
        out_shape = [shaped((16 * pairs, 3 * LANES), BF16), edge, edge, message, message]
        out_shape += [rim] * (step > 0) + [field] * (step == 1)
        ordered, own_a, own_b, far, near, *extra = call(
            functools.partial(forward_kernel, step, tiles, levels),
            "forward",
            out_shape,
            [block, block_a, block_b, *carried]
            + [cells, fr, factors, node_map, level_hot, cell_hot, spread, order],
            [
                pltpu.VMEM((16 * pairs, 2 * padded_order), F32),
                pltpu.VMEM((96, refs), BF16),
            ],
        )
        squares += extra[:1]
        if step == 1:
            samples = extra[1]
        if step == 0:
            far, near, settled = lax.optimization_barrier((far, near, conn))
            shape = shaped((refs, RADIX), BF16)
            node_map = call(turn_nodes_kernel, "turn_nodes", shape, [settled])
        if step == 1:
            far, near, settled = lax.optimization_barrier((far, near, cells))
            cell_map, spread_map, order_map = call(
                functools.partial(turn_cells_kernel, node_slots),
                "turn_cells",
                [
                    shaped((refs, LANES), BF16),
                    shaped((2 * padded_order, LANES), BF16),
                    shaped((3 * LANES, 2 * padded_order), BF16),
                ],
                [settled],
            )
        new_a, new_b = swapped(far, near)
        inner = call(
            functools.partial(inner_kernel, levels),
            "inner",
            shaped((8 * pairs, 3 * LANES), F32),
            [ordered, weight, conn, node_hot, level_hot],
            [pltpu.VMEM((48 * (levels - 2), refs), BF16)],
        )
        if step == 0:
            inner, node_map = lax.optimization_barrier((inner, node_map))
        operands = [block, block_a, block_b, own_a, own_b, new_a, new_b, inner, weight]
        operands += [conn, cells, fr, loaded, edge_hot, cell_map, spread_map, order_map]
        if last:
            operands += squares + [cluster_ids.reshape(1, cell_count)]
            packed = shaped((lax.axis_size(everyone), group_size, 2 * LANES), BF16)
            out_shape = [whole, packed]
        else:
            out_shape = [whole, rim, rim]
        basal, *messages = call(
            functools.partial(adjoint_kernel, step, last, tiles, levels),
            "adjoint",
            out_shape,
            operands,
            [
                pltpu.VMEM((8 * pairs, 2 * padded_order), F32),
                pltpu.VMEM((8 * pairs, 3 * LANES), F32),
                pltpu.VMEM((48, refs), BF16),
            ],
        )
        if not last:
            if step == 0:
                *messages, settled = lax.optimization_barrier((*messages, loaded))
                shape = shaped(blocks.shape, BF16)
                factors = call(turn_blocks_kernel, "turn_blocks", shape, [settled])
            carried = [basal, *swapped(*messages)]

    gathered = lax.all_to_all(messages[0], everyone, 0, 0)
    gathered = gathered.reshape(tiles, groups, *gathered.shape[1:])
    samples, refined, gram = call(
        functools.partial(gram_kernel, POWER % 2 == 1, tiles, groups),
        "gram",
        [field, field, shaped((tiles, group_size, groups * group_size), F32)],
        [gathered, basal, samples],
    )
    return (samples.T, refined.T, gram)


def solution(mesh):
    in_specs = (
        P("tiles", None, None),
        P("tiles", None),
        P("tiles", None),
        P("tiles", None, None),
        P("tiles"),
        P("tiles", None),
        P("tiles", "probes"),
        P("tiles"),
    )
    out_specs = (P("tiles", "probes"), P("tiles", "probes"), P(None, "probes", None))
    return jax.shard_map(shards, mesh=mesh, in_specs=in_specs, out_specs=out_specs, check_vma=False)
```

```python
import functools

import jax
import jax.numpy as jnp
from jax import lax
from jax.experimental import pallas as pl
from jax.experimental.pallas import tpu as pltpu
from jax.sharding import PartitionSpec as P

HALO = 512
POWER = 2
RIM = 64
LANES = 128
RADIX = 512
EDGE_RADIX = 256
EDGE = HALO // EDGE_RADIX
SHRINK = 2.0**-40
VMEM_BYTES = 16 * 1024 * 1024

F32 = jnp.float32
BF16 = jnp.bfloat16


def dot(a, b):
    return lax.dot_general(a, b, (((1,), (0,)), ((), ())), preferred_element_type=F32)


def dot_nt(a, b):
    return lax.dot_general(a, b, (((1,), (1,)), ((), ())), preferred_element_type=F32)


def product(turned):
    return dot if turned else dot_nt


def split(x):
    hi = x.astype(BF16)
    return hi, (x - hi.astype(F32)).astype(BF16)


def rows_iota(shape):
    return lax.broadcasted_iota(jnp.int32, shape, 0)


def lanes_iota(shape):
    return lax.broadcasted_iota(jnp.int32, shape, 1)


def hot(mask):
    return jnp.where(mask, F32(1), F32(0)).astype(BF16)


def hot16(a, b):
    return jnp.where(a == b, jnp.ones((), BF16), jnp.zeros((), BF16))


def lane_tiles(count, tile):
    return jnp.concatenate([tile(i * LANES) for i in range(count)], axis=1)


def spread_matrix(node_slots, padded_order, turned=False):
    pair, wide = 2 * node_slots, 2 * padded_order

    def start(at):
        return (at // node_slots) * padded_order + 3 * (at % node_slots)

    def near(gap):
        return hot((gap >= 0) & (gap < 3))

    if turned:
        return near(rows_iota((wide, pair)) - start(lanes_iota((1, pair))))
    gap = lanes_iota((pair, LANES)) - start(rows_iota((pair, LANES)))
    return lane_tiles(wide // LANES, lambda at: near(gap + at))


def order_matrix(node_slots, padded_order, turned=False):
    pair, wide = 2 * node_slots, 2 * padded_order

    def source(at):
        inner = at % pair
        return (inner // node_slots) * padded_order + 3 * (inner % node_slots) + at // pair

    if not turned:
        return hot(rows_iota((wide, 3 * pair)) == source(lanes_iota((1, 3 * pair))))
    gap = lanes_iota((3 * pair, LANES)) - source(rows_iota((3 * pair, LANES)))
    return lane_tiles(wide // LANES, lambda at: hot(gap + at == 0))


def colour_of(ids):
    return (ids % 2) == (rows_iota(ids.shape) % 2)


def by_side(tile, a, b):
    even = tile % 2 == 0
    return jnp.where(even, b, a), jnp.where(even, a, b)


def to_swaps(tile, for_next, for_previous):
    even = tile % 2 == 0
    return jnp.where(even, for_previous, for_next), jnp.where(even, for_next, for_previous)


def announce_kernel(signs_hbm, ids_hbm, weight_hbm, out_ref, again_ref, signs, ids, lead, sems):
    loads = [
        pltpu.make_async_copy(signs_hbm, signs, sems.at[0]),
        pltpu.make_async_copy(ids_hbm, ids, sems.at[1]),
        pltpu.make_async_copy(weight_hbm.at[:, pl.ds(0, HALO)], lead, sems.at[2]),
    ]
    for load in loads:
        load.start()
    for load in loads:
        load.wait()
    colours = jnp.broadcast_to(ids[...], signs.shape)
    probes = jnp.where(colour_of(colours), (2 * signs[...] - 1).astype(F32), F32(0))
    out_ref[:8, :] = probes
    out_ref[8:, :] = jnp.zeros_like(probes)
    half = HALO // 2
    out_ref[8:11, :] = lead[:, :half]
    out_ref[11:14, :] = lead[:, half:]
    again_ref[...] = out_ref[...]


def halves_of(conn):
    low = conn % RADIX
    halves = []
    for at in range(0, RADIX, EDGE_RADIX):
        inside = (low >= at) & (low < at + EDGE_RADIX)
        halves.append(jnp.where(inside, low - at, -1).astype(F32))
    return halves


def setup_kernel(
    levels,
    counts,
    conn_hbm,
    cell_hbm,
    friction_hbm,
    blocks_hbm,
    conn_ref,
    cell_ref,
    fr_ref,
    blocks_ref,
    node_hot_ref,
    edge_hot_ref,
    level_hot_ref,
    cell_hot_ref,
    spread_ref,
    order_ref,
    conn_in,
    cell_in,
    friction_in,
    sems,
):
    pairs = conn_ref.shape[0]
    slots, padded_order = fr_ref.shape
    node_slots = conn_in.shape[1]
    window = 3 * LANES

    loads = [
        pltpu.make_async_copy(source, target, sems.at[i])
        for i, (source, target) in enumerate(
            [
                (conn_hbm, conn_in),
                (cell_hbm, cell_in),
                (friction_hbm, friction_in),
                (blocks_hbm, blocks_ref),
            ]
        )
    ]
    for load in loads:
        load.start()

    spread_ref[...] = spread_matrix(node_slots, padded_order)
    order_ref[...] = order_matrix(node_slots, padded_order)

    def paired(ref):
        return jnp.concatenate(
            [ref[pl.ds(0, pairs, stride=2), :], ref[pl.ds(1, pairs, stride=2), :]], axis=1
        )

    for load in loads[:3]:
        load.wait()
    conn = paired(conn_in)
    conn_ref[...] = conn
    cells = paired(cell_in)
    cells = jnp.where(cells < RIM, cells + (window - RIM), cells - RIM)
    cell_ref[...] = cells

    shape = (node_slots, padded_order)
    total = jnp.zeros((slots, padded_order), F32)
    for c in range(3):
        place = hot(lanes_iota(shape) == 3 * rows_iota(shape) + c)
        rest = friction_in[c]
        for _ in range(3):
            part = rest.astype(BF16)
            total = total + dot(part, place)
            rest = rest - part.astype(F32)
    live = rows_iota(total.shape) < counts[0]
    fr_ref[...] = jnp.where(live, total, F32(0))

    rows = rows_iota((EDGE_RADIX, LANES)).astype(F32).astype(BF16)
    halves = halves_of(conn)
    which = (conn // RADIX).astype(F32)
    cell_low = (cells % LANES).astype(F32)
    for m in range(pairs):
        at = pl.ds(m * LANES, LANES)
        total = jnp.zeros((EDGE_RADIX, LANES), BF16)
        for i, half in enumerate(halves):
            row = jnp.broadcast_to(half[m : m + 1, :], (EDGE_RADIX, LANES)).astype(BF16)
            mine = hot16(rows, row)
            node_hot_ref[i * EDGE_RADIX : (i + 1) * EDGE_RADIX, at] = mine
            total = total + mine
        edge_hot_ref[:, at] = total
        row = jnp.broadcast_to(which[m : m + 1, :], (16, LANES)).astype(BF16)
        for level in range(levels):
            mine = hot16(row, jnp.full((16, LANES), level, BF16))
            level_hot_ref[16 * level : 16 * level + 16, at] = mine
        row = jnp.broadcast_to(cell_low[m : m + 1, :], (LANES, LANES)).astype(BF16)
        cell_hot_ref[:, at] = hot16(rows[:LANES], row)
    loads[3].wait()


def turn_nodes_kernel(conn_ref, node_turn_ref):
    columns = [half.T for half in halves_of(conn_ref[...])]
    lanes = lanes_iota((LANES, EDGE_RADIX)).astype(F32).astype(BF16)
    for m in range(conn_ref.shape[0]):
        for i, column in enumerate(columns):
            row = jnp.broadcast_to(column[:, m : m + 1], (LANES, LANES)).astype(BF16)
            row = jnp.concatenate([row] * (EDGE_RADIX // LANES), axis=1)
            at = pl.ds(i * EDGE_RADIX, EDGE_RADIX)
            node_turn_ref[m * LANES : (m + 1) * LANES, at] = hot16(lanes, row)


def turn_blocks_kernel(blocks, turned_ref):
    for slot in range(blocks.shape[0]):
        turned_ref[slot] = blocks[slot].T


def turn_cells_kernel(node_slots, cell_ref, cell_turn_ref, spread_turn_ref, order_turn_ref):
    padded_order = order_turn_ref.shape[1] // 2
    spread_turn_ref[...] = spread_matrix(node_slots, padded_order, True)
    order_turn_ref[...] = order_matrix(node_slots, padded_order, True)
    cells = (cell_ref[...] % LANES).astype(F32).T
    lanes = lanes_iota((LANES, LANES)).astype(F32).astype(BF16)
    for m in range(cell_ref.shape[0]):
        row = jnp.broadcast_to(cells[:, m : m + 1], (LANES, LANES)).astype(BF16)
        cell_turn_ref[m * LANES : (m + 1) * LANES, :] = hot16(lanes, row)


def spread_levels(v_ref, ordered, level_hot, levels, pairs):
    for m in range(pairs):
        at = pl.ds(m * LANES, LANES)
        values = [ordered[16 * m : 16 * m + 16, c * LANES : (c + 1) * LANES] for c in range(3)]
        for i, level in enumerate(levels):
            mask = level_hot[16 * level : 16 * level + 16, at]
            for c in range(3):
                row = 48 * i + 16 * c
                v_ref[row : row + 16, at] = values[c] * mask


def forward_kernel(step, tiles, levels, *refs):
    block_ref, block_a, block_b, *refs = refs
    first = step == 0
    if not first:
        basal_ref, rim_a, rim_b, *refs = refs
    cell_ref, fr_ref, factors, node_map, level_hot, cell_hot, spread_ref, order_ref, *refs = refs
    ordered_ref, a_ref, b_ref, far_ref, near_ref, *refs = refs
    if not first:
        squares_ref, *refs = refs
    if step == 1:
        field_ref, *refs = refs
    f_ref, v_ref = refs

    order = factors.shape[1]
    padded_order = f_ref.shape[1] // 2
    pairs = factors.shape[0] // 2
    tile = lax.axis_index("tiles")

    lane = lanes_iota((8, LANES))
    low = lane < RIM
    after, before = by_side(tile, block_a[:8, :], block_b[:8, :])
    starts = [
        block_ref[:8, :LANES],
        block_ref[:8, LANES:],
        jnp.where(low, after[:, :LANES], before[:, LANES:]),
    ]
    if first:
        parts = starts
    else:
        after, before = by_side(tile, rim_a[...], rim_b[...])
        parts = [basal_ref[:, i * LANES : (i + 1) * LANES] for i in range(3)]
        parts[0] = parts[0] + jnp.where(low, before, F32(0))
        parts[1] = parts[1] + jnp.where(low, F32(0), after)
        parts[2] = parts[2] + jnp.where(low, after, before)
        there = (low & (tile < tiles - 1)) | (~low & (tile > 0))
        parts[2] = jnp.where(there, parts[2], F32(0))
        kept = [(start != 0) if step % 2 == 0 else (start == 0) for start in starts]
        parts = [jnp.where(keep, part, F32(0)) for keep, part in zip(kept, parts)]
        if step == 1:
            field_ref[:, :LANES] = parts[0]
            field_ref[:, LANES:] = parts[1]
        squares_ref[...] = parts[0] * parts[0] + parts[1] * parts[1]
    window = jnp.concatenate(parts, axis=0)
    if step == 1:
        window = window * F32(SHRINK)

    cells = cell_ref[...]
    hi, lo = split(window)
    picked = dot(jnp.concatenate([hi, lo], axis=0), cell_hot[...])
    tops = []
    rests = []
    for m in range(pairs):
        part = picked[:, m * LANES : (m + 1) * LANES]
        which = cells[m : m + 1, :] // LANES
        for base, out in ((0, tops), (24, rests)):
            chosen = jnp.where(which == 0, part[base : base + 8], F32(0))
            for level in (1, 2):
                at = base + 8 * level
                chosen = jnp.where(which == level, part[at : at + 8], chosen)
            out.append(chosen)
    stacked = jnp.concatenate(tops + rests, axis=0).astype(BF16)
    spread = dot(stacked, spread_ref[...])
    half = 8 * pairs
    spread = spread[:half] + spread[half:]

    f_ref[...] = jnp.zeros_like(f_ref)
    for m in range(pairs):
        for side in range(2):
            at = side * padded_order
            slot = 2 * m + side
            inputs = spread[8 * m : 8 * m + 8, at : at + order] * fr_ref[slot : slot + 1, :order]
            if first:
                out = product(step > 0)(inputs.astype(BF16), factors[slot])
            else:
                hi = inputs.astype(BF16).astype(F32)
                both = jnp.concatenate([hi, inputs - hi], axis=0).astype(BF16)
                out = product(step > 0)(both, factors[slot])
                out = out[:8] + out[8:]
            hi = out.astype(BF16).astype(F32)
            f_ref[16 * m : 16 * m + 8, at : at + order] = hi
            f_ref[16 * m + 8 : 16 * m + 16, at : at + order] = out - hi

    ordered = dot(f_ref[...].astype(BF16), order_ref[...]).astype(BF16)
    ordered_ref[...] = ordered
    spread_levels(v_ref, ordered, level_hot, (0, levels - 1), pairs)
    rim = product(step > 0)(v_ref[...], node_map[...])
    sums = [rim[16 * i : 16 * i + 8] + rim[16 * i + 8 : 16 * i + 16] for i in range(6)]
    lead, spill = (jnp.concatenate(part, axis=0) for part in (sums[:3], sums[3:]))
    for ref, message, value in zip((a_ref, b_ref), (far_ref, near_ref), to_swaps(tile, spill, lead)):
        ref[...] = value
        pieces = [value[:, i * EDGE_RADIX : (i + 1) * EDGE_RADIX] for i in range(EDGE)]
        message[...] = jnp.concatenate(pieces, axis=0).astype(BF16)


def inner_kernel(levels, ordered_ref, weight_ref, conn_ref, node_hot, level_hot, picked_ref, v_ref):
    pairs = conn_ref.shape[0]
    conn = conn_ref[...]
    inside = range(1, levels - 1)
    spread_levels(v_ref, ordered_ref, level_hot, inside, pairs)
    nodes = dot_nt(v_ref[...], node_hot[...])
    rows = []
    for i in range(3 * len(inside)):
        value = nodes[16 * i : 16 * i + 8] + nodes[16 * i + 8 : 16 * i + 16]
        at = inside[i // 3] * RADIX
        rows.append(value * weight_ref[i % 3 : i % 3 + 1, at : at + RADIX])
    weighted = jnp.concatenate(rows, axis=0).astype(BF16)
    step = 2
    for start in range(0, pairs, step):
        found = dot(weighted, node_hot[:, start * LANES : (start + step) * LANES])
        for i in range(step):
            m = start + i
            which = conn[m : m + 1, :] // RADIX
            part = found[:, i * LANES : (i + 1) * LANES]
            chosen = jnp.zeros((24, LANES), F32)
            for at, level in enumerate(inside):
                chosen = jnp.where(which == level, part[24 * at : 24 * at + 24], chosen)
            for c in range(3):
                picked_ref[8 * m : 8 * m + 8, c * LANES : (c + 1) * LANES] = chosen[8 * c : 8 * c + 8]


def adjoint_kernel(last, clusters, levels, *refs):
    block_ref, block_a, block_b, own_a, own_b, new_a, new_b, inner_ref, weight_ref, *refs = refs
    conn_ref, cell_ref, fr_ref, blocks, edge_hot, cell_map, spread_map, order_map, *refs = refs
    if last:
        squares_1, squares_2, ids_ref, *refs = refs
        basal_ref, out_ref, p_ref, n_ref, v_ref = refs
    else:
        basal_ref, a_ref, b_ref, p_ref, n_ref, v_ref = refs

    order = blocks.shape[1]
    padded_order = p_ref.shape[1] // 2
    pairs = blocks.shape[0] // 2
    tile = lax.axis_index("tiles")

    spill, lead = by_side(tile, own_a[...], own_b[...])
    new_spill, new_lead = by_side(tile, new_a[...].astype(F32), new_b[...].astype(F32))
    after, before = by_side(tile, block_a[...], block_b[...])
    rows = []
    for i in range(3 * EDGE):
        c, at = i % 3, (i // 3) * EDGE_RADIX
        value = lead[8 * c : 8 * c + 8, at : at + EDGE_RADIX] + new_lead[8 * i : 8 * i + 8]
        rows.append(value * weight_ref[c : c + 1, at : at + EDGE_RADIX])
    for i in range(3 * EDGE):
        c, at = i % 3, (i // 3) * EDGE_RADIX
        value = spill[8 * c : 8 * c + 8, at : at + EDGE_RADIX] + new_spill[8 * i : 8 * i + 8]
        rows.append(value * after[8 + i : 9 + i, :])
    weighted = jnp.concatenate(rows, axis=0).astype(BF16)

    conn = conn_ref[...]
    first = levels * RADIX // EDGE_RADIX - EDGE
    edges = [*range(EDGE), *range(first, first + EDGE)]
    width = 2
    for start in range(0, pairs, width):
        found = dot(weighted, edge_hot[:, start * LANES : (start + width) * LANES])
        for i in range(width):
            m = start + i
            which = conn[m : m + 1, :] // EDGE_RADIX
            part = found[:, i * LANES : (i + 1) * LANES]
            for c in range(3):
                value = inner_ref[8 * m : 8 * m + 8, c * LANES : (c + 1) * LANES]
                for at, level in enumerate(edges):
                    row = 24 * at + 8 * c
                    value = jnp.where(which == level, part[row : row + 8], value)
                n_ref[8 * m : 8 * m + 8, c * LANES : (c + 1) * LANES] = value
    natural = product(last)(n_ref[...].astype(BF16), order_map[...])
    p_ref[...] = jnp.zeros_like(p_ref)
    for m in range(pairs):
        for side in range(2):
            at = side * padded_order
            slot = 2 * m + side
            out = dot(natural[8 * m : 8 * m + 8, at : at + order].astype(BF16), blocks[slot])
            out = out * fr_ref[slot : slot + 1, :order]
            p_ref[8 * m : 8 * m + 8, at : at + order] = out

    hi, lo = split(p_ref[...])
    partial = product(last)(jnp.concatenate([hi, lo], axis=0), spread_map[...])
    half = 8 * pairs
    partial = partial[:half] + partial[half:]
    cells = cell_ref[...]
    for m in range(pairs):
        which = cells[m : m + 1, :] // LANES
        value = partial[8 * m : 8 * m + 8, :]
        rows = jnp.concatenate([jnp.where(which == level, value, F32(0)) for level in range(3)], axis=0)
        hi = rows.astype(BF16).astype(F32)
        both = jnp.concatenate([hi, rows - hi], axis=0)
        v_ref[:, m * LANES : (m + 1) * LANES] = both.astype(BF16)
    basal = product(last)(v_ref[...], cell_map[...])
    basal = basal[:24] + basal[24:]
    parts = [basal[8 * i : 8 * i + 8] for i in range(3)]
    for i in range(3):
        basal_ref[:, i * LANES : (i + 1) * LANES] = parts[i]
    lane = lanes_iota((8, LANES))
    if not last:
        for_next = jnp.where(lane < RIM, parts[2], parts[1])
        for_previous = jnp.where(lane < RIM, parts[0], parts[2])
        a_ref[...], b_ref[...] = to_swaps(tile, for_next, for_previous)
        return

    starts = [
        block_ref[:1, :LANES],
        block_ref[:1, LANES:],
        jnp.where(lane[:1] < RIM, after[:1, :LANES], before[:1, LANES:]),
    ]
    packed = []
    for start, part in zip(starts, parts):
        even = start != 0
        rows = [jnp.where(even, part[r + 1 : r + 2], part[r : r + 1]) for r in range(0, 8, 2)]
        packed.append(jnp.concatenate(rows, axis=0))
    extra = jnp.zeros((8, LANES), F32)
    for i, ref in enumerate((squares_1, squares_2)):
        rest = jnp.sum(ref[...], axis=1, keepdims=True)
        for j in range(3):
            piece = rest.astype(BF16).astype(F32)
            extra = jnp.where(lane == 3 * i + j, piece, extra)
            rest = rest - piece
    moved = pltpu.roll(extra, 8, 1)
    rows = [extra[r : r + 1] + moved[r + 1 : r + 2] for r in range(0, 8, 2)]
    extra = jnp.concatenate(rows, axis=0)
    ids = ids_ref[...]
    for k in range(1, clusters):
        below = jnp.sum((ids < k).astype(F32), axis=1, keepdims=True)
        extra = jnp.where(lane[:4] == 16 + k, below, extra)
    top = jnp.concatenate([packed[0], packed[1]], axis=1)
    message = jnp.concatenate([top, jnp.concatenate([packed[2], extra], axis=1)], axis=0)
    message = message.astype(BF16)
    for t in range(out_ref.shape[0]):
        out_ref[t] = message


def gram_kernel(
    keep_same, tiles, groups, g_ref, own_ref, samples_in, samples_ref, field_ref, gram_ref
):
    samples_ref[...] = samples_in[...]
    tile = lax.axis_index("tiles")
    group = lax.axis_index("probes")
    clusters = gram_ref.shape[0]
    cell_count = tiles * 2 * LANES
    low = lanes_iota((8, LANES)) < RIM
    row = rows_iota((8, LANES))

    def twice(x):
        out = jnp.broadcast_to(x[:1], (8, LANES))
        for r in range(1, 4):
            out = jnp.where(row >= 2 * r, jnp.broadcast_to(x[r : r + 1], (8, LANES)), out)
        return out

    def piece_of(t, p, lower, at):
        part = g_ref[t, p].astype(F32)
        return twice(part[4 * lower : 4 * lower + 4, at * LANES : (at + 1) * LANES])

    def factor_of(p):
        def add(t, acc):
            return acc + g_ref[t, p].astype(F32)[4:, LANES:]

        sums = lax.fori_loop(0, tiles, add, jnp.zeros((4, LANES), F32), unroll=tiles <= 8)
        sums = twice(sums)
        sums = jnp.where(row % 2 == 0, sums, pltpu.roll(sums, LANES - 8, 1))
        first = jnp.sum(sums[:, :3], axis=1, keepdims=True)
        second = jnp.sum(sums[:, 3:6], axis=1, keepdims=True)
        scale = jnp.sqrt(first / cell_count + F32(1e-06))
        size = jnp.sqrt(second / cell_count) * F32(1 / SHRINK) / scale
        return F32(1 / SHRINK) / (scale * jnp.sqrt(size * size + F32(1e-06)))

    def ids_of(t):
        starts = piece_of(t, 0, 1, 1)
        cell = lanes_iota((8, 2 * LANES)).astype(F32)
        ids = jnp.zeros(cell.shape, jnp.int32)
        for k in range(1, clusters):
            ids = ids + (cell >= starts[:, 16 + k : 17 + k]).astype(jnp.int32)
        return [ids[:, :LANES], ids[:, LANES:]]

    def field(t, p, ids, own=None):
        before = piece_of(jnp.maximum(t - 1, 0), p, 1, 0)
        after = piece_of(jnp.minimum(t + 1, tiles - 1), p, 1, 0)
        if own is None:
            own = [piece_of(t, p, 0, at) for at in range(2)]
        parts = [
            own[0] + jnp.where(low & (t > 0), before, F32(0)),
            own[1] + jnp.where(~low & (t < tiles - 1), after, F32(0)),
        ]
        return [
            jnp.where(colour_of(i) if keep_same else ~colour_of(i), part, F32(0))
            for i, part in zip(ids, parts)
        ]

    factors = [factor_of(p) for p in range(groups)]
    mine_factor = factors[0]
    for p in range(1, groups):
        mine_factor = jnp.where(group == p, factors[p], mine_factor)
    own = [own_ref[:, at * LANES : (at + 1) * LANES] for at in range(2)]
    own = field(tile, group, ids_of(tile), own)
    field_ref[:, :LANES] = own[0] * mine_factor
    field_ref[:, LANES:] = own[1] * mine_factor

    def add_tile(t, acc):
        ids = ids_of(t)
        every = [
            jnp.concatenate(field(t, p, ids), axis=1) * factors[p] for p in range(groups)
        ]
        mine = every[0]
        for p in range(1, groups):
            mine = jnp.where(group == p, every[p], mine)
        ids = jnp.concatenate(ids, axis=1)
        left = jnp.concatenate([jnp.where(ids == k, mine, F32(0)) for k in range(clusters)], axis=0)
        return acc + lax.dot_general(
            left,
            jnp.concatenate(every, axis=0),
            (((1,), (1,)), ((), ())),
            precision=lax.Precision.HIGHEST,
            preferred_element_type=F32,
        )

    acc = jnp.zeros((8 * clusters, 8 * groups), F32)
    acc = lax.fori_loop(0, tiles, add_tile, acc, unroll=tiles <= 8)
    gram_ref[...] = acc.reshape(gram_ref.shape)


def shards(
    blocks, connectivity, basal_map, friction, elem_counts, obs_weight, sign_bits, cluster_ids
):
    slots = blocks.shape[0]
    node_slots = connectivity.shape[1]
    node_count = obs_weight.shape[0]
    cell_count, group_size = sign_bits.shape
    tiles = lax.axis_size("tiles")
    groups = lax.axis_size("probes")
    pairs = slots * node_slots // LANES
    refs = pairs * LANES
    levels = (node_count + HALO) // RADIX
    padded_order = 2 * LANES
    window = cell_count + 2 * RIM

    vmem = pl.BlockSpec(memory_space=pltpu.VMEM)
    params = pltpu.CompilerParams(vmem_limit_bytes=VMEM_BYTES)
    shaped = jax.ShapeDtypeStruct

    hbm = pl.BlockSpec(memory_space=pltpu.HBM)
    smem = pl.BlockSpec(memory_space=pltpu.SMEM)

    def call(kernel, name, out_shape, operands, scratch=(), in_specs=None):
        in_specs = in_specs or [vmem] * len(operands)
        operands = [
            pltpu.with_memory_space_constraint(x, pltpu.HBM) if spec is hbm else x
            for x, spec in zip(operands, in_specs)
        ]
        return pl.pallas_call(
            kernel,
            out_shape=out_shape,
            in_specs=in_specs,
            out_specs=jax.tree.map(lambda _: vmem, out_shape),
            scratch_shapes=list(scratch),
            compiler_params=params,
            name=name,
        )(*operands)

    evens = range(0, tiles - 1, 2)
    odds = range(1, tiles - 1, 2)
    pairs_a = [(i, i + 1) for i in odds] + [(i + 1, i) for i in odds]
    pairs_b = [(i, i + 1) for i in evens] + [(i + 1, i) for i in evens]

    def swapped(a, b):
        return lax.ppermute(a, "tiles", pairs_a), lax.ppermute(b, "tiles", pairs_b)

    weight = obs_weight.T
    block, again = call(
        announce_kernel,
        "announce",
        [shaped((16, cell_count), F32)] * 2,
        [sign_bits.T, cluster_ids.reshape(1, cell_count), weight],
        [
            pltpu.VMEM((group_size, cell_count), jnp.int32),
            pltpu.VMEM((1, cell_count), jnp.int32),
            pltpu.VMEM((3, HALO), F32),
            pltpu.SemaphoreType.DMA((3,)),
        ],
        [hbm] * 3,
    )
    block_a, block_b = swapped(again, block)

    conn, cells, fr, loaded, node_hot, edge_hot, level_hot, cell_hot, spread, order = call(
        functools.partial(setup_kernel, levels),
        "setup",
        [
            shaped((pairs, LANES), jnp.int32),
            shaped((pairs, LANES), jnp.int32),
            shaped((slots, padded_order), F32),
            shaped(blocks.shape, BF16),
            shaped((RADIX, refs), BF16),
            shaped((EDGE_RADIX, refs), BF16),
            shaped((16 * levels, refs), BF16),
            shaped((LANES, refs), BF16),
            shaped((LANES, 2 * padded_order), BF16),
            shaped((2 * padded_order, 3 * LANES), BF16),
        ],
        [elem_counts, connectivity, basal_map, friction.transpose(2, 0, 1), blocks],
        [
            pltpu.VMEM(connectivity.shape, jnp.int32),
            pltpu.VMEM(basal_map.shape, jnp.int32),
            pltpu.VMEM((3, slots, node_slots), F32),
            pltpu.SemaphoreType.DMA((4,)),
        ],
        [smem] + [hbm] * 4,
    )
    factors, node_map, cell_map, spread_map, order_map = loaded, node_hot, cell_hot, spread, order

    edge = shaped((24, HALO), F32)
    message = shaped((24 * EDGE, EDGE_RADIX), BF16)
    rim = shaped((group_size, LANES), F32)
    whole = shaped((group_size, window), F32)
    field = shaped((group_size, cell_count), F32)
    everyone = ("tiles", "probes")

    carried = []
    factors = loaded
    squares = []
    samples = None
    for step in range(POWER + 1):
        last = step == POWER
        out_shape = [shaped((16 * pairs, 3 * LANES), BF16), edge, edge, message, message]
        out_shape += [rim] * (step > 0) + [field] * (step == 1)
        ordered, own_a, own_b, far, near, *extra = call(
            functools.partial(forward_kernel, step, tiles, levels),
            "forward",
            out_shape,
            [block, block_a, block_b, *carried]
            + [cells, fr, factors, node_map, level_hot, cell_hot, spread, order],
            [
                pltpu.VMEM((16 * pairs, 2 * padded_order), F32),
                pltpu.VMEM((96, refs), BF16),
            ],
        )
        squares += extra[:1]
        if step == 1:
            samples = extra[1]
        new_a, new_b = swapped(far, near)
        inner = call(
            functools.partial(inner_kernel, levels),
            "inner",
            shaped((8 * pairs, 3 * LANES), F32),
            [ordered, weight, conn, node_hot, level_hot],
            [pltpu.VMEM((48 * (levels - 2), refs), BF16)],
        )
        operands = [block, block_a, block_b, own_a, own_b, new_a, new_b, inner, weight]
        operands += [conn, cells, fr, loaded, edge_hot, cell_map, spread_map, order_map]
        if last:
            operands += squares + [cluster_ids.reshape(1, cell_count)]
            packed = shaped((lax.axis_size(everyone), group_size, 2 * LANES), BF16)
            out_shape = [whole, packed]
        else:
            out_shape = [whole, rim, rim]
        basal, *messages = call(
            functools.partial(adjoint_kernel, last, tiles, levels),
            "adjoint",
            out_shape,
            operands,
            [
                pltpu.VMEM((8 * pairs, 2 * padded_order), F32),
                pltpu.VMEM((8 * pairs, 3 * LANES), F32),
                pltpu.VMEM((48, refs), BF16),
            ],
        )
        if not last:
            if step == 0:
                *messages, source, ids = lax.optimization_barrier((*messages, loaded, conn))
                shape = shaped(blocks.shape, BF16)
                factors = call(turn_blocks_kernel, "turn_blocks", shape, [source])
                shape = shaped((refs, RADIX), BF16)
                node_map = call(turn_nodes_kernel, "turn_nodes", shape, [ids])
            if step == POWER - 1:
                *messages, ids = lax.optimization_barrier((*messages, cells))
                cell_map, spread_map, order_map = call(
                    functools.partial(turn_cells_kernel, node_slots),
                    "turn_cells",
                    [
                        shaped((refs, LANES), BF16),
                        shaped((2 * padded_order, LANES), BF16),
                        shaped((3 * LANES, 2 * padded_order), BF16),
                    ],
                    [ids],
                )
                basal, cell_map = lax.optimization_barrier((basal, cell_map))
            carried = [basal, *swapped(*messages)]

    gathered = lax.all_to_all(messages[0], everyone, 0, 0)
    gathered = gathered.reshape(tiles, groups, *gathered.shape[1:])
    samples, refined, gram = call(
        functools.partial(gram_kernel, POWER % 2 == 1, tiles, groups),
        "gram",
        [field, field, shaped((tiles, group_size, groups * group_size), F32)],
        [gathered, basal, samples],
    )
    return (samples.T, refined.T, gram)


def solution(mesh):
    in_specs = (
        P("tiles", None, None),
        P("tiles", None),
        P("tiles", None),
        P("tiles", None, None),
        P("tiles"),
        P("tiles", None),
        P("tiles", "probes"),
        P("tiles"),
    )
    out_specs = (P("tiles", "probes"), P("tiles", "probes"), P(None, "probes", None))
    return jax.shard_map(shards, mesh=mesh, in_specs=in_specs, out_specs=out_specs, check_vma=False)
```

```python
import functools

import jax
import jax.numpy as jnp
from jax import lax
from jax.experimental import pallas as pl
from jax.experimental.pallas import tpu as pltpu
from jax.sharding import PartitionSpec as P

HALO = 512
POWER = 2
RIM = 64
LANES = 128
RADIX = 512
EDGE_RADIX = 256
EDGE = HALO // EDGE_RADIX
SHRINK = 2.0**-40
VMEM_BYTES = 16 * 1024 * 1024

F32 = jnp.float32
BF16 = jnp.bfloat16


def dot(a, b):
    return lax.dot_general(a, b, (((1,), (0,)), ((), ())), preferred_element_type=F32)


def dot_nt(a, b):
    return lax.dot_general(a, b, (((1,), (1,)), ((), ())), preferred_element_type=F32)


def product(turned):
    return dot if turned else dot_nt


def split(x):
    hi = x.astype(BF16)
    return hi, (x - hi.astype(F32)).astype(BF16)


def rows_iota(shape):
    return lax.broadcasted_iota(jnp.int32, shape, 0)


def lanes_iota(shape):
    return lax.broadcasted_iota(jnp.int32, shape, 1)


def hot(mask):
    return jnp.where(mask, F32(1), F32(0)).astype(BF16)


def hot16(a, b):
    return jnp.where(a == b, jnp.ones((), BF16), jnp.zeros((), BF16))


def lane_tiles(count, tile):
    return jnp.concatenate([tile(i * LANES) for i in range(count)], axis=1)


def spread_matrix(node_slots, padded_order, turned=False):
    pair, wide = 2 * node_slots, 2 * padded_order

    def start(at):
        return (at // node_slots) * padded_order + 3 * (at % node_slots)

    def near(gap):
        return hot((gap >= 0) & (gap < 3))

    if turned:
        return near(rows_iota((wide, pair)) - start(lanes_iota((1, pair))))
    gap = lanes_iota((pair, LANES)) - start(rows_iota((pair, LANES)))
    return lane_tiles(wide // LANES, lambda at: near(gap + at))


def order_matrix(node_slots, padded_order, turned=False):
    pair, wide = 2 * node_slots, 2 * padded_order

    def source(at):
        inner = at % pair
        return (inner // node_slots) * padded_order + 3 * (inner % node_slots) + at // pair

    if not turned:
        return hot(rows_iota((wide, 3 * pair)) == source(lanes_iota((1, 3 * pair))))
    gap = lanes_iota((3 * pair, LANES)) - source(rows_iota((3 * pair, LANES)))
    return lane_tiles(wide // LANES, lambda at: hot(gap + at == 0))


def colour_of(ids):
    return (ids % 2) == (rows_iota(ids.shape) % 2)


def by_side(tile, a, b):
    even = tile % 2 == 0
    return jnp.where(even, b, a), jnp.where(even, a, b)


def to_swaps(tile, for_next, for_previous):
    even = tile % 2 == 0
    return jnp.where(even, for_previous, for_next), jnp.where(even, for_next, for_previous)


def announce_kernel(signs_hbm, ids_hbm, weight_hbm, out_ref, again_ref, signs, ids, lead, sems):
    loads = [
        pltpu.make_async_copy(signs_hbm, signs, sems.at[0]),
        pltpu.make_async_copy(ids_hbm, ids, sems.at[1]),
        pltpu.make_async_copy(weight_hbm.at[:, pl.ds(0, HALO)], lead, sems.at[2]),
    ]
    for load in loads:
        load.start()
    for load in loads:
        load.wait()
    colours = jnp.broadcast_to(ids[...], signs.shape)
    probes = jnp.where(colour_of(colours), (2 * signs[...] - 1).astype(F32), F32(0))
    out_ref[:8, :] = probes
    out_ref[8:, :] = jnp.zeros_like(probes)
    half = HALO // 2
    out_ref[8:11, :] = lead[:, :half]
    out_ref[11:14, :] = lead[:, half:]
    again_ref[...] = out_ref[...]


def halves_of(conn):
    low = conn % RADIX
    halves = []
    for at in range(0, RADIX, EDGE_RADIX):
        inside = (low >= at) & (low < at + EDGE_RADIX)
        halves.append(jnp.where(inside, low - at, -1).astype(F32))
    return halves


def setup_kernel(
    levels,
    counts,
    conn_hbm,
    cell_hbm,
    friction_hbm,
    blocks_hbm,
    conn_ref,
    cell_ref,
    fr_ref,
    blocks_ref,
    node_hot_ref,
    edge_hot_ref,
    level_hot_ref,
    cell_hot_ref,
    spread_ref,
    order_ref,
    conn_in,
    cell_in,
    friction_in,
    sems,
):
    pairs = conn_ref.shape[0]
    slots, padded_order = fr_ref.shape
    node_slots = conn_in.shape[1]
    window = 3 * LANES

    loads = [
        pltpu.make_async_copy(source, target, sems.at[i])
        for i, (source, target) in enumerate(
            [
                (conn_hbm, conn_in),
                (cell_hbm, cell_in),
                (friction_hbm, friction_in),
                (blocks_hbm, blocks_ref),
            ]
        )
    ]
    for load in loads:
        load.start()

    spread_ref[...] = spread_matrix(node_slots, padded_order)
    order_ref[...] = order_matrix(node_slots, padded_order)

    def paired(ref):
        return jnp.concatenate(
            [ref[pl.ds(0, pairs, stride=2), :], ref[pl.ds(1, pairs, stride=2), :]], axis=1
        )

    for load in loads[:3]:
        load.wait()
    conn = paired(conn_in)
    conn_ref[...] = conn
    cells = paired(cell_in)
    cells = jnp.where(cells < RIM, cells + (window - RIM), cells - RIM)
    cell_ref[...] = cells

    shape = (node_slots, padded_order)
    total = jnp.zeros((slots, padded_order), F32)
    for c in range(3):
        place = hot(lanes_iota(shape) == 3 * rows_iota(shape) + c)
        rest = friction_in[c]
        for _ in range(3):
            part = rest.astype(BF16)
            total = total + dot(part, place)
            rest = rest - part.astype(F32)
    live = rows_iota(total.shape) < counts[0]
    fr_ref[...] = jnp.where(live, total, F32(0))

    rows = rows_iota((EDGE_RADIX, LANES)).astype(F32).astype(BF16)
    halves = halves_of(conn)
    which = (conn // RADIX).astype(F32)
    cell_low = (cells % LANES).astype(F32)
    for m in range(pairs):
        at = pl.ds(m * LANES, LANES)
        total = jnp.zeros((EDGE_RADIX, LANES), BF16)
        for i, half in enumerate(halves):
            row = jnp.broadcast_to(half[m : m + 1, :], (EDGE_RADIX, LANES)).astype(BF16)
            mine = hot16(rows, row)
            node_hot_ref[i * EDGE_RADIX : (i + 1) * EDGE_RADIX, at] = mine
            total = total + mine
        edge_hot_ref[:, at] = total
        row = jnp.broadcast_to(which[m : m + 1, :], (16, LANES)).astype(BF16)
        for level in range(levels):
            mine = hot16(row, jnp.full((16, LANES), level, BF16))
            level_hot_ref[16 * level : 16 * level + 16, at] = mine
        row = jnp.broadcast_to(cell_low[m : m + 1, :], (LANES, LANES)).astype(BF16)
        cell_hot_ref[:, at] = hot16(rows[:LANES], row)
    loads[3].wait()


def turn_nodes_kernel(conn_ref, node_turn_ref):
    columns = [half.T for half in halves_of(conn_ref[...])]
    lanes = lanes_iota((LANES, EDGE_RADIX)).astype(F32).astype(BF16)
    for m in range(conn_ref.shape[0]):
        for i, column in enumerate(columns):
            row = jnp.broadcast_to(column[:, m : m + 1], (LANES, LANES)).astype(BF16)
            row = jnp.concatenate([row] * (EDGE_RADIX // LANES), axis=1)
            at = pl.ds(i * EDGE_RADIX, EDGE_RADIX)
            node_turn_ref[m * LANES : (m + 1) * LANES, at] = hot16(lanes, row)


def turn_blocks_kernel(blocks, turned_ref):
    for slot in range(blocks.shape[0]):
        turned_ref[slot] = blocks[slot].T


def turn_cells_kernel(node_slots, cell_ref, cell_turn_ref, spread_turn_ref, order_turn_ref):
    padded_order = order_turn_ref.shape[1] // 2
    spread_turn_ref[...] = spread_matrix(node_slots, padded_order, True)
    order_turn_ref[...] = order_matrix(node_slots, padded_order, True)
    cells = (cell_ref[...] % LANES).astype(F32).T
    lanes = lanes_iota((LANES, LANES)).astype(F32).astype(BF16)
    for m in range(cell_ref.shape[0]):
        row = jnp.broadcast_to(cells[:, m : m + 1], (LANES, LANES)).astype(BF16)
        cell_turn_ref[m * LANES : (m + 1) * LANES, :] = hot16(lanes, row)


def spread_levels(v_ref, ordered, level_hot, levels, pairs):
    for m in range(pairs):
        at = pl.ds(m * LANES, LANES)
        values = [ordered[16 * m : 16 * m + 16, c * LANES : (c + 1) * LANES] for c in range(3)]
        for i, level in enumerate(levels):
            mask = level_hot[16 * level : 16 * level + 16, at]
            for c in range(3):
                row = 48 * i + 16 * c
                v_ref[row : row + 16, at] = values[c] * mask


def both_parts(x):
    hi = x.astype(BF16).astype(F32)
    return jnp.concatenate([hi, x - hi], axis=0).astype(BF16)


def clear_padding(ref, padded_order):
    for half in range(2):
        end = (half + 1) * padded_order
        ref[:, end - LANES : end] = jnp.zeros((ref.shape[0], LANES), BF16)


def forward_kernel(step, tiles, levels, *refs):
    block_ref, block_a, block_b, *refs = refs
    first = step == 0
    if not first:
        basal_ref, rim_a, rim_b, *refs = refs
    cell_ref, fr_ref, factors, node_map, level_hot, cell_hot, spread_ref, order_ref, *refs = refs
    ordered_ref, a_ref, b_ref, far_ref, near_ref, *refs = refs
    if not first:
        squares_ref, *refs = refs
    if step == 1:
        field_ref, *refs = refs
    f_ref, v_ref = refs

    order = factors.shape[1]
    padded_order = f_ref.shape[1] // 2
    pairs = factors.shape[0] // 2
    tile = lax.axis_index("tiles")

    lane = lanes_iota((8, LANES))
    low = lane < RIM
    after, before = by_side(tile, block_a[:8, :], block_b[:8, :])
    starts = [
        block_ref[:8, :LANES],
        block_ref[:8, LANES:],
        jnp.where(low, after[:, :LANES], before[:, LANES:]),
    ]
    if first:
        parts = starts
    else:
        after, before = by_side(tile, rim_a[...], rim_b[...])
        parts = [basal_ref[:, i * LANES : (i + 1) * LANES] for i in range(3)]
        parts[0] = parts[0] + jnp.where(low, before, F32(0))
        parts[1] = parts[1] + jnp.where(low, F32(0), after)
        parts[2] = parts[2] + jnp.where(low, after, before)
        there = (low & (tile < tiles - 1)) | (~low & (tile > 0))
        parts[2] = jnp.where(there, parts[2], F32(0))
        kept = [(start != 0) if step % 2 == 0 else (start == 0) for start in starts]
        parts = [jnp.where(keep, part, F32(0)) for keep, part in zip(kept, parts)]
        if step == 1:
            field_ref[:, :LANES] = parts[0]
            field_ref[:, LANES:] = parts[1]
        squares_ref[...] = parts[0] * parts[0] + parts[1] * parts[1]
    window = jnp.concatenate(parts, axis=0)
    if step == 1:
        window = window * F32(SHRINK)

    cells = cell_ref[...]
    hi, lo = split(window)
    picked = dot(jnp.concatenate([hi, lo], axis=0), cell_hot[...])
    tops = []
    rests = []
    for m in range(pairs):
        part = picked[:, m * LANES : (m + 1) * LANES]
        which = cells[m : m + 1, :] // LANES
        for base, out in ((0, tops), (24, rests)):
            chosen = jnp.where(which == 0, part[base : base + 8], F32(0))
            for level in (1, 2):
                at = base + 8 * level
                chosen = jnp.where(which == level, part[at : at + 8], chosen)
            out.append(chosen)
    stacked = jnp.concatenate(tops + rests, axis=0).astype(BF16)
    spread = dot(stacked, spread_ref[...])
    half = 8 * pairs
    spread = spread[:half] + spread[half:]

    clear_padding(f_ref, padded_order)
    for m in range(pairs):
        for side in range(2):
            at = side * padded_order
            slot = 2 * m + side
            inputs = spread[8 * m : 8 * m + 8, at : at + order] * fr_ref[slot : slot + 1, :order]
            if first:
                out = product(step > 0)(inputs.astype(BF16), factors[slot])
            else:
                out = product(step > 0)(both_parts(inputs), factors[slot])
                out = out[:8] + out[8:]
            f_ref[16 * m : 16 * m + 16, at : at + order] = both_parts(out)

    ordered = dot(f_ref[...], order_ref[...]).astype(BF16)
    ordered_ref[...] = ordered
    spread_levels(v_ref, ordered, level_hot, (0, levels - 1), pairs)
    rim = product(step > 0)(v_ref[...], node_map[...])
    sums = [rim[16 * i : 16 * i + 8] + rim[16 * i + 8 : 16 * i + 16] for i in range(6)]
    lead, spill = (jnp.concatenate(part, axis=0) for part in (sums[:3], sums[3:]))
    for ref, message, value in zip((a_ref, b_ref), (far_ref, near_ref), to_swaps(tile, spill, lead)):
        ref[...] = value
        pieces = [value[:, i * EDGE_RADIX : (i + 1) * EDGE_RADIX] for i in range(EDGE)]
        message[...] = jnp.concatenate(pieces, axis=0).astype(BF16)


def inner_kernel(levels, ordered_ref, weight_ref, conn_ref, node_hot, level_hot, picked_ref, v_ref):
    pairs = conn_ref.shape[0]
    conn = conn_ref[...]
    inside = range(1, levels - 1)
    spread_levels(v_ref, ordered_ref, level_hot, inside, pairs)
    nodes = dot_nt(v_ref[...], node_hot[...])
    rows = []
    for i in range(3 * len(inside)):
        value = nodes[16 * i : 16 * i + 8] + nodes[16 * i + 8 : 16 * i + 16]
        at = inside[i // 3] * RADIX
        rows.append(value * weight_ref[i % 3 : i % 3 + 1, at : at + RADIX])
    weighted = jnp.concatenate(rows, axis=0).astype(BF16)
    step = 2
    for start in range(0, pairs, step):
        found = dot(weighted, node_hot[:, start * LANES : (start + step) * LANES])
        for i in range(step):
            m = start + i
            which = conn[m : m + 1, :] // RADIX
            part = found[:, i * LANES : (i + 1) * LANES]
            chosen = jnp.zeros((24, LANES), F32)
            for at, level in enumerate(inside):
                chosen = jnp.where(which == level, part[24 * at : 24 * at + 24], chosen)
            for c in range(3):
                picked_ref[8 * m : 8 * m + 8, c * LANES : (c + 1) * LANES] = chosen[8 * c : 8 * c + 8]


def adjoint_kernel(last, clusters, levels, *refs):
    block_ref, block_a, block_b, own_a, own_b, new_a, new_b, inner_ref, weight_ref, *refs = refs
    conn_ref, cell_ref, fr_ref, blocks, edge_hot, cell_map, spread_map, order_map, *refs = refs
    if last:
        squares_1, squares_2, ids_ref, *refs = refs
        basal_ref, out_ref, p_ref, n_ref, v_ref = refs
    else:
        basal_ref, a_ref, b_ref, p_ref, n_ref, v_ref = refs

    order = blocks.shape[1]
    padded_order = p_ref.shape[1] // 2
    pairs = blocks.shape[0] // 2
    tile = lax.axis_index("tiles")

    spill, lead = by_side(tile, own_a[...], own_b[...])
    new_spill, new_lead = by_side(tile, new_a[...].astype(F32), new_b[...].astype(F32))
    after, before = by_side(tile, block_a[...], block_b[...])
    rows = []
    for i in range(3 * EDGE):
        c, at = i % 3, (i // 3) * EDGE_RADIX
        value = lead[8 * c : 8 * c + 8, at : at + EDGE_RADIX] + new_lead[8 * i : 8 * i + 8]
        rows.append(value * weight_ref[c : c + 1, at : at + EDGE_RADIX])
    for i in range(3 * EDGE):
        c, at = i % 3, (i // 3) * EDGE_RADIX
        value = spill[8 * c : 8 * c + 8, at : at + EDGE_RADIX] + new_spill[8 * i : 8 * i + 8]
        rows.append(value * after[8 + i : 9 + i, :])
    weighted = jnp.concatenate(rows, axis=0).astype(BF16)

    conn = conn_ref[...]
    first = levels * RADIX // EDGE_RADIX - EDGE
    edges = [*range(EDGE), *range(first, first + EDGE)]
    width = 2
    for start in range(0, pairs, width):
        found = dot(weighted, edge_hot[:, start * LANES : (start + width) * LANES])
        values = [[] for _ in range(3)]
        for i in range(width):
            m = start + i
            which = conn[m : m + 1, :] // EDGE_RADIX
            part = found[:, i * LANES : (i + 1) * LANES]
            for c in range(3):
                value = inner_ref[8 * m : 8 * m + 8, c * LANES : (c + 1) * LANES]
                for at, level in enumerate(edges):
                    row = 24 * at + 8 * c
                    value = jnp.where(which == level, part[row : row + 8], value)
                values[c].append(value)
        for c in range(3):
            rows = jnp.concatenate(values[c], axis=0).astype(BF16)
            n_ref[8 * start : 8 * (start + width), c * LANES : (c + 1) * LANES] = rows
    natural = product(last)(n_ref[...], order_map[...])
    clear_padding(p_ref, padded_order)
    for m in range(pairs):
        for side in range(2):
            at = side * padded_order
            slot = 2 * m + side
            out = dot(natural[8 * m : 8 * m + 8, at : at + order].astype(BF16), blocks[slot])
            out = out * fr_ref[slot : slot + 1, :order]
            p_ref[16 * m : 16 * m + 16, at : at + order] = both_parts(out)

    partial = product(last)(p_ref[...], spread_map[...])
    cells = cell_ref[...]
    for m in range(pairs):
        which = cells[m : m + 1, :] // LANES
        value = partial[16 * m : 16 * m + 8, :] + partial[16 * m + 8 : 16 * m + 16, :]
        rows = jnp.concatenate([jnp.where(which == level, value, F32(0)) for level in range(3)], axis=0)
        hi = rows.astype(BF16).astype(F32)
        both = jnp.concatenate([hi, rows - hi], axis=0)
        v_ref[:, m * LANES : (m + 1) * LANES] = both.astype(BF16)
    basal = product(last)(v_ref[...], cell_map[...])
    basal = basal[:24] + basal[24:]
    parts = [basal[8 * i : 8 * i + 8] for i in range(3)]
    for i in range(3):
        basal_ref[:, i * LANES : (i + 1) * LANES] = parts[i]
    lane = lanes_iota((8, LANES))
    if not last:
        for_next = jnp.where(lane < RIM, parts[2], parts[1])
        for_previous = jnp.where(lane < RIM, parts[0], parts[2])
        a_ref[...], b_ref[...] = to_swaps(tile, for_next, for_previous)
        return

    starts = [
        block_ref[:1, :LANES],
        block_ref[:1, LANES:],
        jnp.where(lane[:1] < RIM, after[:1, :LANES], before[:1, LANES:]),
    ]
    packed = []
    for start, part in zip(starts, parts):
        even = start != 0
        rows = [jnp.where(even, part[r + 1 : r + 2], part[r : r + 1]) for r in range(0, 8, 2)]
        packed.append(jnp.concatenate(rows, axis=0))
    extra = jnp.zeros((8, LANES), F32)
    for i, ref in enumerate((squares_1, squares_2)):
        rest = jnp.sum(ref[...], axis=1, keepdims=True)
        for j in range(3):
            piece = rest.astype(BF16).astype(F32)
            extra = jnp.where(lane == 3 * i + j, piece, extra)
            rest = rest - piece
    moved = pltpu.roll(extra, 8, 1)
    rows = [extra[r : r + 1] + moved[r + 1 : r + 2] for r in range(0, 8, 2)]
    extra = jnp.concatenate(rows, axis=0)
    ids = ids_ref[...]
    for k in range(1, clusters):
        below = jnp.sum((ids < k).astype(F32), axis=1, keepdims=True)
        extra = jnp.where(lane[:4] == 16 + k, below, extra)
    top = jnp.concatenate([packed[0], packed[1]], axis=1)
    message = jnp.concatenate([top, jnp.concatenate([packed[2], extra], axis=1)], axis=0)
    message = message.astype(BF16)
    for t in range(out_ref.shape[0]):
        out_ref[t] = message


def gram_kernel(
    keep_same, tiles, groups, g_ref, own_ref, samples_in, samples_ref, field_ref, gram_ref
):
    samples_ref[...] = samples_in[...]
    tile = lax.axis_index("tiles")
    group = lax.axis_index("probes")
    clusters = gram_ref.shape[0]
    cell_count = tiles * 2 * LANES
    low = lanes_iota((8, LANES)) < RIM
    row = rows_iota((8, LANES))

    def twice(x):
        out = jnp.broadcast_to(x[:1], (8, LANES))
        for r in range(1, 4):
            out = jnp.where(row >= 2 * r, jnp.broadcast_to(x[r : r + 1], (8, LANES)), out)
        return out

    def piece_of(t, p, lower, at):
        part = g_ref[t, p].astype(F32)
        return part[4 * lower : 4 * lower + 4, at * LANES : (at + 1) * LANES]

    def factor_of(p):
        def add(t, acc):
            return acc + g_ref[t, p].astype(F32)[4:, LANES:]

        sums = lax.fori_loop(0, tiles, add, jnp.zeros((4, LANES), F32), unroll=tiles <= 8)
        sums = twice(sums)
        sums = jnp.where(row % 2 == 0, sums, pltpu.roll(sums, LANES - 8, 1))
        first = jnp.sum(sums[:, :3], axis=1, keepdims=True)
        second = jnp.sum(sums[:, 3:6], axis=1, keepdims=True)
        scale = jnp.sqrt(first / cell_count + F32(1e-06))
        size = jnp.sqrt(second / cell_count) * F32(1 / SHRINK) / scale
        return F32(1 / SHRINK) / (scale * jnp.sqrt(size * size + F32(1e-06)))

    def ids_of(t):
        starts = twice(piece_of(t, 0, 1, 1))
        cell = lanes_iota((8, 2 * LANES)).astype(F32)
        ids = jnp.zeros(cell.shape, jnp.int32)
        for k in range(1, clusters):
            ids = ids + (cell >= starts[:, 16 + k : 17 + k]).astype(jnp.int32)
        return [ids[:, :LANES], ids[:, LANES:]]

    def field(t, p, ids, own=None):
        before = piece_of(jnp.maximum(t - 1, 0), p, 1, 0)
        before = jnp.where(low[:4] & (t > 0), before, F32(0))
        after = piece_of(jnp.minimum(t + 1, tiles - 1), p, 1, 0)
        after = jnp.where(~low[:4] & (t < tiles - 1), after, F32(0))
        if own is None:
            parts = [twice(piece_of(t, p, 0, 0) + before), twice(piece_of(t, p, 0, 1) + after)]
        else:
            parts = [own[0] + twice(before), own[1] + twice(after)]
        return [
            jnp.where(colour_of(i) if keep_same else ~colour_of(i), part, F32(0))
            for i, part in zip(ids, parts)
        ]

    factors = [factor_of(p) for p in range(groups)]
    mine_factor = factors[0]
    for p in range(1, groups):
        mine_factor = jnp.where(group == p, factors[p], mine_factor)
    own = [own_ref[:, at * LANES : (at + 1) * LANES] for at in range(2)]
    own = field(tile, group, ids_of(tile), own)
    field_ref[:, :LANES] = own[0] * mine_factor
    field_ref[:, LANES:] = own[1] * mine_factor

    def add_tile(t, acc):
        ids = ids_of(t)
        every = [
            jnp.concatenate(field(t, p, ids), axis=1) * factors[p] for p in range(groups)
        ]
        mine = every[0]
        for p in range(1, groups):
            mine = jnp.where(group == p, every[p], mine)
        ids = jnp.concatenate(ids, axis=1)
        left = jnp.concatenate([jnp.where(ids == k, mine, F32(0)) for k in range(clusters)], axis=0)
        return acc + lax.dot_general(
            left,
            jnp.concatenate(every, axis=0),
            (((1,), (1,)), ((), ())),
            precision=lax.Precision.HIGHEST,
            preferred_element_type=F32,
        )

    acc = jnp.zeros((8 * clusters, 8 * groups), F32)
    acc = lax.fori_loop(0, tiles, add_tile, acc, unroll=tiles <= 8)
    gram_ref[...] = acc.reshape(gram_ref.shape)


def shards(
    blocks, connectivity, basal_map, friction, elem_counts, obs_weight, sign_bits, cluster_ids
):
    slots = blocks.shape[0]
    node_slots = connectivity.shape[1]
    node_count = obs_weight.shape[0]
    cell_count, group_size = sign_bits.shape
    tiles = lax.axis_size("tiles")
    groups = lax.axis_size("probes")
    pairs = slots * node_slots // LANES
    refs = pairs * LANES
    levels = (node_count + HALO) // RADIX
    padded_order = 2 * LANES
    window = cell_count + 2 * RIM

    vmem = pl.BlockSpec(memory_space=pltpu.VMEM)
    params = pltpu.CompilerParams(vmem_limit_bytes=VMEM_BYTES)
    shaped = jax.ShapeDtypeStruct

    hbm = pl.BlockSpec(memory_space=pltpu.HBM)
    smem = pl.BlockSpec(memory_space=pltpu.SMEM)

    def call(kernel, name, out_shape, operands, scratch=(), in_specs=None):
        in_specs = in_specs or [vmem] * len(operands)
        operands = [
            pltpu.with_memory_space_constraint(x, pltpu.HBM) if spec is hbm else x
            for x, spec in zip(operands, in_specs)
        ]
        return pl.pallas_call(
            kernel,
            out_shape=out_shape,
            in_specs=in_specs,
            out_specs=jax.tree.map(lambda _: vmem, out_shape),
            scratch_shapes=list(scratch),
            compiler_params=params,
            name=name,
        )(*operands)

    evens = range(0, tiles - 1, 2)
    odds = range(1, tiles - 1, 2)
    pairs_a = [(i, i + 1) for i in odds] + [(i + 1, i) for i in odds]
    pairs_b = [(i, i + 1) for i in evens] + [(i + 1, i) for i in evens]

    def swapped(a, b):
        return lax.ppermute(a, "tiles", pairs_a), lax.ppermute(b, "tiles", pairs_b)

    weight = obs_weight.T
    block, again = call(
        announce_kernel,
        "announce",
        [shaped((16, cell_count), F32)] * 2,
        [sign_bits.T, cluster_ids.reshape(1, cell_count), weight],
        [
            pltpu.VMEM((group_size, cell_count), jnp.int32),
            pltpu.VMEM((1, cell_count), jnp.int32),
            pltpu.VMEM((3, HALO), F32),
            pltpu.SemaphoreType.DMA((3,)),
        ],
        [hbm] * 3,
    )
    block_a, block_b = swapped(again, block)

    conn, cells, fr, loaded, node_hot, edge_hot, level_hot, cell_hot, spread, order = call(
        functools.partial(setup_kernel, levels),
        "setup",
        [
            shaped((pairs, LANES), jnp.int32),
            shaped((pairs, LANES), jnp.int32),
            shaped((slots, padded_order), F32),
            shaped(blocks.shape, BF16),
            shaped((RADIX, refs), BF16),
            shaped((EDGE_RADIX, refs), BF16),
            shaped((16 * levels, refs), BF16),
            shaped((LANES, refs), BF16),
            shaped((LANES, 2 * padded_order), BF16),
            shaped((2 * padded_order, 3 * LANES), BF16),
        ],
        [elem_counts, connectivity, basal_map, friction.transpose(2, 0, 1), blocks],
        [
            pltpu.VMEM(connectivity.shape, jnp.int32),
            pltpu.VMEM(basal_map.shape, jnp.int32),
            pltpu.VMEM((3, slots, node_slots), F32),
            pltpu.SemaphoreType.DMA((4,)),
        ],
        [smem] + [hbm] * 4,
    )
    factors, node_map, cell_map, spread_map, order_map = loaded, node_hot, cell_hot, spread, order

    edge = shaped((24, HALO), F32)
    message = shaped((24 * EDGE, EDGE_RADIX), BF16)
    rim = shaped((group_size, LANES), F32)
    whole = shaped((group_size, window), F32)
    field = shaped((group_size, cell_count), F32)
    everyone = ("tiles", "probes")

    carried = []
    factors = loaded
    squares = []
    samples = None
    for step in range(POWER + 1):
        last = step == POWER
        out_shape = [shaped((16 * pairs, 3 * LANES), BF16), edge, edge, message, message]
        out_shape += [rim] * (step > 0) + [field] * (step == 1)
        ordered, own_a, own_b, far, near, *extra = call(
            functools.partial(forward_kernel, step, tiles, levels),
            "forward",
            out_shape,
            [block, block_a, block_b, *carried]
            + [cells, fr, factors, node_map, level_hot, cell_hot, spread, order],
            [
                pltpu.VMEM((16 * pairs, 2 * padded_order), BF16),
                pltpu.VMEM((96, refs), BF16),
            ],
        )
        squares += extra[:1]
        if step == 1:
            samples = extra[1]
        new_a, new_b = swapped(far, near)
        inner = call(
            functools.partial(inner_kernel, levels),
            "inner",
            shaped((8 * pairs, 3 * LANES), F32),
            [ordered, weight, conn, node_hot, level_hot],
            [pltpu.VMEM((48 * (levels - 2), refs), BF16)],
        )
        operands = [block, block_a, block_b, own_a, own_b, new_a, new_b, inner, weight]
        operands += [conn, cells, fr, loaded, edge_hot, cell_map, spread_map, order_map]
        if last:
            operands += squares + [cluster_ids.reshape(1, cell_count)]
            packed = shaped((lax.axis_size(everyone), group_size, 2 * LANES), BF16)
            out_shape = [whole, packed]
        else:
            out_shape = [whole, rim, rim]
        basal, *messages = call(
            functools.partial(adjoint_kernel, last, tiles, levels),
            "adjoint",
            out_shape,
            operands,
            [
                pltpu.VMEM((16 * pairs, 2 * padded_order), BF16),
                pltpu.VMEM((8 * pairs, 3 * LANES), BF16),
                pltpu.VMEM((48, refs), BF16),
            ],
        )
        if not last:
            if step == 0:
                *messages, source, ids = lax.optimization_barrier((*messages, loaded, conn))
                shape = shaped(blocks.shape, BF16)
                factors = call(turn_blocks_kernel, "turn_blocks", shape, [source])
                shape = shaped((refs, RADIX), BF16)
                node_map = call(turn_nodes_kernel, "turn_nodes", shape, [ids])
            if step == POWER - 1:
                *messages, ids = lax.optimization_barrier((*messages, cells))
                cell_map, spread_map, order_map = call(
                    functools.partial(turn_cells_kernel, node_slots),
                    "turn_cells",
                    [
                        shaped((refs, LANES), BF16),
                        shaped((2 * padded_order, LANES), BF16),
                        shaped((3 * LANES, 2 * padded_order), BF16),
                    ],
                    [ids],
                )
                basal, cell_map = lax.optimization_barrier((basal, cell_map))
            carried = [basal, *swapped(*messages)]

    gathered = lax.all_to_all(messages[0], everyone, 0, 0)
    gathered = gathered.reshape(tiles, groups, *gathered.shape[1:])
    samples, refined, gram = call(
        functools.partial(gram_kernel, POWER % 2 == 1, tiles, groups),
        "gram",
        [field, field, shaped((tiles, group_size, groups * group_size), F32)],
        [gathered, basal, samples],
    )
    return (samples.T, refined.T, gram)


def solution(mesh):
    in_specs = (
        P("tiles", None, None),
        P("tiles", None),
        P("tiles", None),
        P("tiles", None, None),
        P("tiles"),
        P("tiles", None),
        P("tiles", "probes"),
        P("tiles"),
    )
    out_specs = (P("tiles", "probes"), P("tiles", "probes"), P(None, "probes", None))
    return jax.shard_map(shards, mesh=mesh, in_specs=in_specs, out_specs=out_specs, check_vma=False)
```

```python
import functools

import jax
import jax.numpy as jnp
from jax import lax
from jax.experimental import pallas as pl
from jax.experimental.pallas import tpu as pltpu
from jax.sharding import PartitionSpec as P

HALO = 512
POWER = 2
RIM = 64
LANES = 128
RADIX = 512
EDGE_RADIX = 256
EDGE = HALO // EDGE_RADIX
SHRINK = 2.0**-40
VMEM_BYTES = 16 * 1024 * 1024

F32 = jnp.float32
BF16 = jnp.bfloat16


def dot(a, b):
    return lax.dot_general(a, b, (((1,), (0,)), ((), ())), preferred_element_type=F32)


def dot_nt(a, b):
    return lax.dot_general(a, b, (((1,), (1,)), ((), ())), preferred_element_type=F32)


def product(turned):
    return dot if turned else dot_nt


def split(x):
    hi = x.astype(BF16)
    return hi, (x - hi.astype(F32)).astype(BF16)


def rows_iota(shape):
    return lax.broadcasted_iota(jnp.int32, shape, 0)


def lanes_iota(shape):
    return lax.broadcasted_iota(jnp.int32, shape, 1)


def hot(mask):
    return jnp.where(mask, F32(1), F32(0)).astype(BF16)


def hot16(a, b):
    return jnp.where(a == b, jnp.ones((), BF16), jnp.zeros((), BF16))


def lane_tiles(count, tile):
    return jnp.concatenate([tile(i * LANES) for i in range(count)], axis=1)


def spread_matrix(node_slots, padded_order, turned=False):
    pair, wide = 2 * node_slots, 2 * padded_order

    def start(at):
        return (at // node_slots) * padded_order + 3 * (at % node_slots)

    def near(gap):
        return hot((gap >= 0) & (gap < 3))

    if turned:
        return near(rows_iota((wide, pair)) - start(lanes_iota((1, pair))))
    gap = lanes_iota((pair, LANES)) - start(rows_iota((pair, LANES)))
    return lane_tiles(wide // LANES, lambda at: near(gap + at))


def order_matrix(node_slots, padded_order, turned=False):
    pair, wide = 2 * node_slots, 2 * padded_order

    def source(at):
        inner = at % pair
        return (inner // node_slots) * padded_order + 3 * (inner % node_slots) + at // pair

    if not turned:
        return hot(rows_iota((wide, 3 * pair)) == source(lanes_iota((1, 3 * pair))))
    gap = lanes_iota((3 * pair, LANES)) - source(rows_iota((3 * pair, LANES)))
    return lane_tiles(wide // LANES, lambda at: hot(gap + at == 0))


def colour_of(ids):
    return (ids % 2) == (rows_iota(ids.shape) % 2)


def by_side(tile, a, b):
    even = tile % 2 == 0
    return jnp.where(even, b, a), jnp.where(even, a, b)


def to_swaps(tile, for_next, for_previous):
    even = tile % 2 == 0
    return jnp.where(even, for_previous, for_next), jnp.where(even, for_next, for_previous)


def announce_kernel(signs_hbm, ids_hbm, weight_hbm, out_ref, again_ref, signs, ids, lead, sems):
    loads = [
        pltpu.make_async_copy(signs_hbm, signs, sems.at[0]),
        pltpu.make_async_copy(ids_hbm, ids, sems.at[1]),
        pltpu.make_async_copy(weight_hbm.at[:, pl.ds(0, HALO)], lead, sems.at[2]),
    ]
    for load in loads:
        load.start()
    for load in loads:
        load.wait()
    colours = jnp.broadcast_to(ids[...], signs.shape)
    probes = jnp.where(colour_of(colours), (2 * signs[...] - 1).astype(F32), F32(0))
    out_ref[:8, :] = probes
    out_ref[8:, :] = jnp.zeros_like(probes)
    half = HALO // 2
    out_ref[8:11, :] = lead[:, :half]
    out_ref[11:14, :] = lead[:, half:]
    again_ref[...] = out_ref[...]


def halves_of(conn):
    low = conn % RADIX
    halves = []
    for at in range(0, RADIX, EDGE_RADIX):
        inside = (low >= at) & (low < at + EDGE_RADIX)
        halves.append(jnp.where(inside, low - at, -1).astype(F32))
    return halves


def setup_kernel(
    levels,
    counts,
    conn_hbm,
    cell_hbm,
    friction_hbm,
    blocks_hbm,
    conn_ref,
    cell_ref,
    fr_ref,
    blocks_ref,
    node_hot_ref,
    edge_hot_ref,
    level_hot_ref,
    cell_hot_ref,
    spread_ref,
    order_ref,
    conn_in,
    cell_in,
    friction_in,
    sems,
):
    pairs = conn_ref.shape[0]
    slots, padded_order = fr_ref.shape
    node_slots = conn_in.shape[1]
    window = 3 * LANES

    loads = [
        pltpu.make_async_copy(source, target, sems.at[i])
        for i, (source, target) in enumerate(
            [
                (conn_hbm, conn_in),
                (cell_hbm, cell_in),
                (friction_hbm, friction_in),
                (blocks_hbm, blocks_ref),
            ]
        )
    ]
    for load in loads:
        load.start()

    spread_ref[...] = spread_matrix(node_slots, padded_order)
    order_ref[...] = order_matrix(node_slots, padded_order)

    def paired(ref):
        return jnp.concatenate(
            [ref[pl.ds(0, pairs, stride=2), :], ref[pl.ds(1, pairs, stride=2), :]], axis=1
        )

    for load in loads[:3]:
        load.wait()
    conn = paired(conn_in)
    conn_ref[...] = conn
    cells = paired(cell_in)
    cells = jnp.where(cells < RIM, cells + (window - RIM), cells - RIM)
    cell_ref[...] = cells

    shape = (node_slots, padded_order)
    total = jnp.zeros((slots, padded_order), F32)
    for c in range(3):
        place = hot(lanes_iota(shape) == 3 * rows_iota(shape) + c)
        rest = friction_in[c]
        for _ in range(3):
            part = rest.astype(BF16)
            total = total + dot(part, place)
            rest = rest - part.astype(F32)
    live = rows_iota(total.shape) < counts[0]
    fr_ref[...] = jnp.where(live, total, F32(0))

    rows = rows_iota((EDGE_RADIX, LANES)).astype(F32).astype(BF16)
    halves = halves_of(conn)
    which = (conn // RADIX).astype(F32)
    ends = jnp.where(rows_iota((16, LANES)) < 8, F32(0), F32(levels - 1)).astype(BF16)
    cell_low = (cells % LANES).astype(F32)
    for m in range(pairs):
        at = pl.ds(m * LANES, LANES)
        total = jnp.zeros((EDGE_RADIX, LANES), BF16)
        for i, half in enumerate(halves):
            row = jnp.broadcast_to(half[m : m + 1, :], (EDGE_RADIX, LANES)).astype(BF16)
            mine = hot16(rows, row)
            node_hot_ref[i * EDGE_RADIX : (i + 1) * EDGE_RADIX, at] = mine
            total = total + mine
        edge_hot_ref[:, at] = total
        row = jnp.broadcast_to(which[m : m + 1, :], (16, LANES)).astype(BF16)
        for level in range(levels):
            mine = hot16(row, jnp.full((16, LANES), level, BF16))
            level_hot_ref[16 * level : 16 * level + 16, at] = mine
        level_hot_ref[16 * levels : 16 * levels + 16, at] = hot16(row, ends)
        row = jnp.broadcast_to(cell_low[m : m + 1, :], (LANES, LANES)).astype(BF16)
        cell_hot_ref[:, at] = hot16(rows[:LANES], row)
    loads[3].wait()


def turn_nodes_kernel(conn_ref, node_turn_ref):
    columns = [half.T for half in halves_of(conn_ref[...])]
    lanes = lanes_iota((LANES, EDGE_RADIX)).astype(F32).astype(BF16)
    for m in range(conn_ref.shape[0]):
        for i, column in enumerate(columns):
            row = jnp.broadcast_to(column[:, m : m + 1], (LANES, LANES)).astype(BF16)
            row = jnp.concatenate([row] * (EDGE_RADIX // LANES), axis=1)
            at = pl.ds(i * EDGE_RADIX, EDGE_RADIX)
            node_turn_ref[m * LANES : (m + 1) * LANES, at] = hot16(lanes, row)


def turn_blocks_kernel(blocks, turned_ref):
    for slot in range(blocks.shape[0]):
        turned_ref[slot] = blocks[slot].T


def turn_cells_kernel(node_slots, cell_ref, cell_turn_ref, spread_turn_ref, order_turn_ref):
    padded_order = order_turn_ref.shape[1] // 2
    spread_turn_ref[...] = spread_matrix(node_slots, padded_order, True)
    order_turn_ref[...] = order_matrix(node_slots, padded_order, True)
    cells = (cell_ref[...] % LANES).astype(F32).T
    lanes = lanes_iota((LANES, LANES)).astype(F32).astype(BF16)
    for m in range(cell_ref.shape[0]):
        row = jnp.broadcast_to(cells[:, m : m + 1], (LANES, LANES)).astype(BF16)
        cell_turn_ref[m * LANES : (m + 1) * LANES, :] = hot16(lanes, row)


def spread_levels(v_ref, ordered, level_hot, levels, pairs):
    for m in range(pairs):
        at = pl.ds(m * LANES, LANES)
        values = [ordered[16 * m : 16 * m + 16, c * LANES : (c + 1) * LANES] for c in range(3)]
        for i, level in enumerate(levels):
            mask = level_hot[16 * level : 16 * level + 16, at]
            for c in range(3):
                row = 48 * i + 16 * c
                v_ref[row : row + 16, at] = values[c] * mask


def both_parts(x):
    hi = x.astype(BF16).astype(F32)
    return jnp.concatenate([hi, x - hi], axis=0).astype(BF16)


def clear_padding(ref, padded_order):
    for half in range(2):
        end = (half + 1) * padded_order
        ref[:, end - LANES : end] = jnp.zeros((ref.shape[0], LANES), BF16)


def forward_kernel(step, tiles, levels, *refs):
    block_ref, block_a, block_b, *refs = refs
    first = step == 0
    if not first:
        basal_ref, rim_a, rim_b, *refs = refs
    cell_ref, fr_ref, factors, node_map, level_hot, cell_hot, spread_ref, order_ref, *refs = refs
    ordered_ref, a_ref, b_ref, far_ref, near_ref, *refs = refs
    if not first:
        squares_ref, *refs = refs
    if step == 1:
        field_ref, *refs = refs
    f_ref, v_ref = refs

    order = factors.shape[1]
    padded_order = f_ref.shape[1] // 2
    pairs = factors.shape[0] // 2
    tile = lax.axis_index("tiles")

    lane = lanes_iota((8, LANES))
    low = lane < RIM
    after, before = by_side(tile, block_a[:8, :], block_b[:8, :])
    starts = [
        block_ref[:8, :LANES],
        block_ref[:8, LANES:],
        jnp.where(low, after[:, :LANES], before[:, LANES:]),
    ]
    if first:
        parts = starts
    else:
        after, before = by_side(tile, rim_a[...], rim_b[...])
        parts = [basal_ref[:, i * LANES : (i + 1) * LANES] for i in range(3)]
        parts[0] = parts[0] + jnp.where(low, before, F32(0))
        parts[1] = parts[1] + jnp.where(low, F32(0), after)
        parts[2] = parts[2] + jnp.where(low, after, before)
        there = (low & (tile < tiles - 1)) | (~low & (tile > 0))
        parts[2] = jnp.where(there, parts[2], F32(0))
        kept = [(start != 0) if step % 2 == 0 else (start == 0) for start in starts]
        parts = [jnp.where(keep, part, F32(0)) for keep, part in zip(kept, parts)]
        if step == 1:
            field_ref[:, :LANES] = parts[0]
            field_ref[:, LANES:] = parts[1]
        squares_ref[...] = parts[0] * parts[0] + parts[1] * parts[1]
    window = jnp.concatenate(parts, axis=0)
    if step == 1:
        window = window * F32(SHRINK)

    cells = cell_ref[...]
    hi, lo = split(window)
    picked = dot(jnp.concatenate([hi, lo], axis=0), cell_hot[...])
    tops = []
    rests = []
    for m in range(pairs):
        part = picked[:, m * LANES : (m + 1) * LANES]
        which = cells[m : m + 1, :] // LANES
        for base, out in ((0, tops), (24, rests)):
            chosen = jnp.where(which == 0, part[base : base + 8], F32(0))
            for level in (1, 2):
                at = base + 8 * level
                chosen = jnp.where(which == level, part[at : at + 8], chosen)
            out.append(chosen)
    stacked = jnp.concatenate(tops + rests, axis=0).astype(BF16)
    spread = dot(stacked, spread_ref[...])
    half = 8 * pairs
    spread = spread[:half] + spread[half:]

    clear_padding(f_ref, padded_order)
    for m in range(pairs):
        for side in range(2):
            at = side * padded_order
            slot = 2 * m + side
            inputs = spread[8 * m : 8 * m + 8, at : at + order] * fr_ref[slot : slot + 1, :order]
            if first:
                out = product(step > 0)(inputs.astype(BF16), factors[slot])
            else:
                out = product(step > 0)(both_parts(inputs), factors[slot])
                out = out[:8] + out[8:]
            f_ref[16 * m : 16 * m + 16, at : at + order] = both_parts(out)

    ordered = dot(f_ref[...], order_ref[...])
    ordered_ref[...] = ordered.astype(BF16)
    for m in range(pairs):
        at = pl.ds(m * LANES, LANES)
        mask = level_hot[16 * levels : 16 * levels + 16, at]
        for c in range(3):
            value = ordered[16 * m : 16 * m + 8, c * LANES : (c + 1) * LANES]
            value = jnp.concatenate([value, value], axis=0).astype(BF16)
            v_ref[16 * c : 16 * c + 16, at] = value * mask
    rim = product(step > 0)(v_ref[...], node_map[...])
    lead = jnp.concatenate([rim[16 * c : 16 * c + 8] for c in range(3)], axis=0)
    spill = jnp.concatenate([rim[16 * c + 8 : 16 * c + 16] for c in range(3)], axis=0)
    for ref, message, value in zip((a_ref, b_ref), (far_ref, near_ref), to_swaps(tile, spill, lead)):
        ref[...] = value
        pieces = [value[:, i * EDGE_RADIX : (i + 1) * EDGE_RADIX] for i in range(EDGE)]
        message[...] = jnp.concatenate(pieces, axis=0).astype(BF16)


def inner_kernel(levels, ordered_ref, weight_ref, conn_ref, node_hot, level_hot, picked_ref, v_ref):
    pairs = conn_ref.shape[0]
    conn = conn_ref[...]
    inside = range(1, levels - 1)
    spread_levels(v_ref, ordered_ref, level_hot, inside, pairs)
    nodes = dot_nt(v_ref[...], node_hot[...])
    rows = []
    for i in range(3 * len(inside)):
        value = nodes[16 * i : 16 * i + 8] + nodes[16 * i + 8 : 16 * i + 16]
        at = inside[i // 3] * RADIX
        rows.append(value * weight_ref[i % 3 : i % 3 + 1, at : at + RADIX])
    weighted = jnp.concatenate(rows, axis=0).astype(BF16)
    step = 2
    for start in range(0, pairs, step):
        found = dot(weighted, node_hot[:, start * LANES : (start + step) * LANES])
        for i in range(step):
            m = start + i
            which = conn[m : m + 1, :] // RADIX
            part = found[:, i * LANES : (i + 1) * LANES]
            chosen = jnp.zeros((24, LANES), F32)
            for at, level in enumerate(inside):
                chosen = jnp.where(which == level, part[24 * at : 24 * at + 24], chosen)
            for c in range(3):
                picked_ref[8 * m : 8 * m + 8, c * LANES : (c + 1) * LANES] = chosen[8 * c : 8 * c + 8]


def adjoint_kernel(last, clusters, levels, *refs):
    block_ref, block_a, block_b, own_a, own_b, new_a, new_b, inner_ref, weight_ref, *refs = refs
    conn_ref, cell_ref, fr_ref, blocks, edge_hot, cell_map, spread_map, order_map, *refs = refs
    if last:
        squares_1, squares_2, ids_ref, *refs = refs
        basal_ref, out_ref, p_ref, n_ref, v_ref = refs
    else:
        basal_ref, a_ref, b_ref, p_ref, n_ref, v_ref = refs

    order = blocks.shape[1]
    padded_order = p_ref.shape[1] // 2
    pairs = blocks.shape[0] // 2
    tile = lax.axis_index("tiles")

    spill, lead = by_side(tile, own_a[...], own_b[...])
    new_spill, new_lead = by_side(tile, new_a[...].astype(F32), new_b[...].astype(F32))
    after, before = by_side(tile, block_a[...], block_b[...])
    rows = []
    for i in range(3 * EDGE):
        c, at = i % 3, (i // 3) * EDGE_RADIX
        value = lead[8 * c : 8 * c + 8, at : at + EDGE_RADIX] + new_lead[8 * i : 8 * i + 8]
        rows.append(value * weight_ref[c : c + 1, at : at + EDGE_RADIX])
    for i in range(3 * EDGE):
        c, at = i % 3, (i // 3) * EDGE_RADIX
        value = spill[8 * c : 8 * c + 8, at : at + EDGE_RADIX] + new_spill[8 * i : 8 * i + 8]
        rows.append(value * after[8 + i : 9 + i, :])
    weighted = jnp.concatenate(rows, axis=0).astype(BF16)

    conn = conn_ref[...]
    first = levels * RADIX // EDGE_RADIX - EDGE
    edges = [*range(EDGE), *range(first, first + EDGE)]
    width = 2
    for start in range(0, pairs, width):
        found = dot(weighted, edge_hot[:, start * LANES : (start + width) * LANES])
        values = [[] for _ in range(3)]
        for i in range(width):
            m = start + i
            which = conn[m : m + 1, :] // EDGE_RADIX
            part = found[:, i * LANES : (i + 1) * LANES]
            for c in range(3):
                value = inner_ref[8 * m : 8 * m + 8, c * LANES : (c + 1) * LANES]
                for at, level in enumerate(edges):
                    row = 24 * at + 8 * c
                    value = jnp.where(which == level, part[row : row + 8], value)
                values[c].append(value)
        for c in range(3):
            rows = jnp.concatenate(values[c], axis=0).astype(BF16)
            n_ref[8 * start : 8 * (start + width), c * LANES : (c + 1) * LANES] = rows
    natural = product(last)(n_ref[...], order_map[...])
    clear_padding(p_ref, padded_order)
    for m in range(pairs):
        for side in range(2):
            at = side * padded_order
            slot = 2 * m + side
            out = dot(natural[8 * m : 8 * m + 8, at : at + order].astype(BF16), blocks[slot])
            out = out * fr_ref[slot : slot + 1, :order]
            p_ref[16 * m : 16 * m + 16, at : at + order] = both_parts(out)

    partial = product(last)(p_ref[...], spread_map[...])
    cells = cell_ref[...]
    for m in range(pairs):
        which = cells[m : m + 1, :] // LANES
        value = partial[16 * m : 16 * m + 8, :] + partial[16 * m + 8 : 16 * m + 16, :]
        rows = jnp.concatenate([jnp.where(which == level, value, F32(0)) for level in range(3)], axis=0)
        hi = rows.astype(BF16).astype(F32)
        both = jnp.concatenate([hi, rows - hi], axis=0)
        v_ref[:, m * LANES : (m + 1) * LANES] = both.astype(BF16)
    basal = product(last)(v_ref[...], cell_map[...])
    basal = basal[:24] + basal[24:]
    parts = [basal[8 * i : 8 * i + 8] for i in range(3)]
    for i in range(3):
        basal_ref[:, i * LANES : (i + 1) * LANES] = parts[i]
    lane = lanes_iota((8, LANES))
    if not last:
        for_next = jnp.where(lane < RIM, parts[2], parts[1])
        for_previous = jnp.where(lane < RIM, parts[0], parts[2])
        a_ref[...], b_ref[...] = to_swaps(tile, for_next, for_previous)
        return

    starts = [
        block_ref[:1, :LANES],
        block_ref[:1, LANES:],
        jnp.where(lane[:1] < RIM, after[:1, :LANES], before[:1, LANES:]),
    ]
    packed = []
    for start, part in zip(starts, parts):
        even = start != 0
        rows = [jnp.where(even, part[r + 1 : r + 2], part[r : r + 1]) for r in range(0, 8, 2)]
        packed.append(jnp.concatenate(rows, axis=0))
    extra = jnp.zeros((8, LANES), F32)
    for i, ref in enumerate((squares_1, squares_2)):
        rest = jnp.sum(ref[...], axis=1, keepdims=True)
        for j in range(3):
            piece = rest.astype(BF16).astype(F32)
            extra = jnp.where(lane == 3 * i + j, piece, extra)
            rest = rest - piece
    moved = pltpu.roll(extra, 8, 1)
    rows = [extra[r : r + 1] + moved[r + 1 : r + 2] for r in range(0, 8, 2)]
    extra = jnp.concatenate(rows, axis=0)
    ids = ids_ref[...]
    for k in range(1, clusters):
        below = jnp.sum((ids < k).astype(F32), axis=1, keepdims=True)
        extra = jnp.where(lane[:4] == 16 + k, below, extra)
    top = jnp.concatenate([packed[0], packed[1]], axis=1)
    message = jnp.concatenate([top, jnp.concatenate([packed[2], extra], axis=1)], axis=0)
    message = message.astype(BF16)
    for t in range(out_ref.shape[0]):
        out_ref[t] = message


def gram_kernel(
    keep_same, tiles, groups, g_ref, own_ref, samples_in, samples_ref, field_ref, gram_ref
):
    samples_ref[...] = samples_in[...]
    tile = lax.axis_index("tiles")
    group = lax.axis_index("probes")
    clusters = gram_ref.shape[0]
    cell_count = tiles * 2 * LANES
    low = lanes_iota((8, LANES)) < RIM
    row = rows_iota((8, LANES))

    def twice(x):
        out = jnp.broadcast_to(x[:1], (8, LANES))
        for r in range(1, 4):
            out = jnp.where(row >= 2 * r, jnp.broadcast_to(x[r : r + 1], (8, LANES)), out)
        return out

    def piece_of(t, p, lower, at):
        part = g_ref[t, p].astype(F32)
        return part[4 * lower : 4 * lower + 4, at * LANES : (at + 1) * LANES]

    def factor_of(p):
        def add(t, acc):
            return acc + g_ref[t, p].astype(F32)[4:, LANES:]

        sums = lax.fori_loop(0, tiles, add, jnp.zeros((4, LANES), F32), unroll=tiles <= 8)
        sums = twice(sums)
        sums = jnp.where(row % 2 == 0, sums, pltpu.roll(sums, LANES - 8, 1))
        first = jnp.sum(sums[:, :3], axis=1, keepdims=True)
        second = jnp.sum(sums[:, 3:6], axis=1, keepdims=True)
        scale = jnp.sqrt(first / cell_count + F32(1e-06))
        size = jnp.sqrt(second / cell_count) * F32(1 / SHRINK) / scale
        return F32(1 / SHRINK) / (scale * jnp.sqrt(size * size + F32(1e-06)))

    def ids_of(t):
        starts = twice(piece_of(t, 0, 1, 1))
        cell = lanes_iota((8, 2 * LANES)).astype(F32)
        ids = jnp.zeros(cell.shape, jnp.int32)
        for k in range(1, clusters):
            ids = ids + (cell >= starts[:, 16 + k : 17 + k]).astype(jnp.int32)
        return [ids[:, :LANES], ids[:, LANES:]]

    def field(t, p, ids, own=None):
        before = piece_of(jnp.maximum(t - 1, 0), p, 1, 0)
        before = jnp.where(low[:4] & (t > 0), before, F32(0))
        after = piece_of(jnp.minimum(t + 1, tiles - 1), p, 1, 0)
        after = jnp.where(~low[:4] & (t < tiles - 1), after, F32(0))
        if own is None:
            parts = [twice(piece_of(t, p, 0, 0) + before), twice(piece_of(t, p, 0, 1) + after)]
        else:
            parts = [own[0] + twice(before), own[1] + twice(after)]
        return [
            jnp.where(colour_of(i) if keep_same else ~colour_of(i), part, F32(0))
            for i, part in zip(ids, parts)
        ]

    factors = [factor_of(p) for p in range(groups)]
    mine_factor = factors[0]
    for p in range(1, groups):
        mine_factor = jnp.where(group == p, factors[p], mine_factor)
    own = [own_ref[:, at * LANES : (at + 1) * LANES] for at in range(2)]
    own = field(tile, group, ids_of(tile), own)
    field_ref[:, :LANES] = own[0] * mine_factor
    field_ref[:, LANES:] = own[1] * mine_factor

    def add_tile(t, acc):
        ids = ids_of(t)
        every = [
            jnp.concatenate(field(t, p, ids), axis=1) * factors[p] for p in range(groups)
        ]
        mine = every[0]
        for p in range(1, groups):
            mine = jnp.where(group == p, every[p], mine)
        ids = jnp.concatenate(ids, axis=1)
        left = jnp.concatenate([jnp.where(ids == k, mine, F32(0)) for k in range(clusters)], axis=0)
        return acc + lax.dot_general(
            left,
            jnp.concatenate(every, axis=0),
            (((1,), (1,)), ((), ())),
            precision=lax.Precision.HIGHEST,
            preferred_element_type=F32,
        )

    acc = jnp.zeros((8 * clusters, 8 * groups), F32)
    acc = lax.fori_loop(0, tiles, add_tile, acc, unroll=tiles <= 8)
    gram_ref[...] = acc.reshape(gram_ref.shape)


def shards(
    blocks, connectivity, basal_map, friction, elem_counts, obs_weight, sign_bits, cluster_ids
):
    slots = blocks.shape[0]
    node_slots = connectivity.shape[1]
    node_count = obs_weight.shape[0]
    cell_count, group_size = sign_bits.shape
    tiles = lax.axis_size("tiles")
    groups = lax.axis_size("probes")
    pairs = slots * node_slots // LANES
    refs = pairs * LANES
    levels = (node_count + HALO) // RADIX
    padded_order = 2 * LANES
    window = cell_count + 2 * RIM

    vmem = pl.BlockSpec(memory_space=pltpu.VMEM)
    params = pltpu.CompilerParams(vmem_limit_bytes=VMEM_BYTES)
    shaped = jax.ShapeDtypeStruct

    hbm = pl.BlockSpec(memory_space=pltpu.HBM)
    smem = pl.BlockSpec(memory_space=pltpu.SMEM)

    def call(kernel, name, out_shape, operands, scratch=(), in_specs=None):
        in_specs = in_specs or [vmem] * len(operands)
        operands = [
            pltpu.with_memory_space_constraint(x, pltpu.HBM) if spec is hbm else x
            for x, spec in zip(operands, in_specs)
        ]
        return pl.pallas_call(
            kernel,
            out_shape=out_shape,
            in_specs=in_specs,
            out_specs=jax.tree.map(lambda _: vmem, out_shape),
            scratch_shapes=list(scratch),
            compiler_params=params,
            name=name,
        )(*operands)

    evens = range(0, tiles - 1, 2)
    odds = range(1, tiles - 1, 2)
    pairs_a = [(i, i + 1) for i in odds] + [(i + 1, i) for i in odds]
    pairs_b = [(i, i + 1) for i in evens] + [(i + 1, i) for i in evens]

    def swapped(a, b):
        return lax.ppermute(a, "tiles", pairs_a), lax.ppermute(b, "tiles", pairs_b)

    weight = obs_weight.T
    block, again = call(
        announce_kernel,
        "announce",
        [shaped((16, cell_count), F32)] * 2,
        [sign_bits.T, cluster_ids.reshape(1, cell_count), weight],
        [
            pltpu.VMEM((group_size, cell_count), jnp.int32),
            pltpu.VMEM((1, cell_count), jnp.int32),
            pltpu.VMEM((3, HALO), F32),
            pltpu.SemaphoreType.DMA((3,)),
        ],
        [hbm] * 3,
    )
    block_a, block_b = swapped(again, block)

    conn, cells, fr, loaded, node_hot, edge_hot, level_hot, cell_hot, spread, order = call(
        functools.partial(setup_kernel, levels),
        "setup",
        [
            shaped((pairs, LANES), jnp.int32),
            shaped((pairs, LANES), jnp.int32),
            shaped((slots, padded_order), F32),
            shaped(blocks.shape, BF16),
            shaped((RADIX, refs), BF16),
            shaped((EDGE_RADIX, refs), BF16),
            shaped((16 * (levels + 1), refs), BF16),
            shaped((LANES, refs), BF16),
            shaped((LANES, 2 * padded_order), BF16),
            shaped((2 * padded_order, 3 * LANES), BF16),
        ],
        [elem_counts, connectivity, basal_map, friction.transpose(2, 0, 1), blocks],
        [
            pltpu.VMEM(connectivity.shape, jnp.int32),
            pltpu.VMEM(basal_map.shape, jnp.int32),
            pltpu.VMEM((3, slots, node_slots), F32),
            pltpu.SemaphoreType.DMA((4,)),
        ],
        [smem] + [hbm] * 4,
    )
    factors, node_map, cell_map, spread_map, order_map = loaded, node_hot, cell_hot, spread, order

    edge = shaped((24, HALO), F32)
    message = shaped((24 * EDGE, EDGE_RADIX), BF16)
    rim = shaped((group_size, LANES), F32)
    whole = shaped((group_size, window), F32)
    field = shaped((group_size, cell_count), F32)
    everyone = ("tiles", "probes")

    carried = []
    factors = loaded
    squares = []
    samples = None
    for step in range(POWER + 1):
        last = step == POWER
        out_shape = [shaped((16 * pairs, 3 * LANES), BF16), edge, edge, message, message]
        out_shape += [rim] * (step > 0) + [field] * (step == 1)
        ordered, own_a, own_b, far, near, *extra = call(
            functools.partial(forward_kernel, step, tiles, levels),
            "forward",
            out_shape,
            [block, block_a, block_b, *carried]
            + [cells, fr, factors, node_map, level_hot, cell_hot, spread, order],
            [
                pltpu.VMEM((16 * pairs, 2 * padded_order), BF16),
                pltpu.VMEM((48, refs), BF16),
            ],
        )
        squares += extra[:1]
        if step == 1:
            samples = extra[1]
        new_a, new_b = swapped(far, near)
        inner = call(
            functools.partial(inner_kernel, levels),
            "inner",
            shaped((8 * pairs, 3 * LANES), F32),
            [ordered, weight, conn, node_hot, level_hot],
            [pltpu.VMEM((48 * (levels - 2), refs), BF16)],
        )
        operands = [block, block_a, block_b, own_a, own_b, new_a, new_b, inner, weight]
        operands += [conn, cells, fr, loaded, edge_hot, cell_map, spread_map, order_map]
        if last:
            operands += squares + [cluster_ids.reshape(1, cell_count)]
            packed = shaped((lax.axis_size(everyone), group_size, 2 * LANES), BF16)
            out_shape = [whole, packed]
        else:
            out_shape = [whole, rim, rim]
        basal, *messages = call(
            functools.partial(adjoint_kernel, last, tiles, levels),
            "adjoint",
            out_shape,
            operands,
            [
                pltpu.VMEM((16 * pairs, 2 * padded_order), BF16),
                pltpu.VMEM((8 * pairs, 3 * LANES), BF16),
                pltpu.VMEM((48, refs), BF16),
            ],
        )
        if not last:
            if step == 0:
                *messages, source, ids = lax.optimization_barrier((*messages, loaded, conn))
                shape = shaped(blocks.shape, BF16)
                factors = call(turn_blocks_kernel, "turn_blocks", shape, [source])
                shape = shaped((refs, RADIX), BF16)
                node_map = call(turn_nodes_kernel, "turn_nodes", shape, [ids])
            if step == POWER - 1:
                *messages, ids = lax.optimization_barrier((*messages, cells))
                cell_map, spread_map, order_map = call(
                    functools.partial(turn_cells_kernel, node_slots),
                    "turn_cells",
                    [
                        shaped((refs, LANES), BF16),
                        shaped((2 * padded_order, LANES), BF16),
                        shaped((3 * LANES, 2 * padded_order), BF16),
                    ],
                    [ids],
                )
                basal, cell_map = lax.optimization_barrier((basal, cell_map))
            carried = [basal, *swapped(*messages)]

    gathered = lax.all_to_all(messages[0], everyone, 0, 0)
    gathered = gathered.reshape(tiles, groups, *gathered.shape[1:])
    samples, refined, gram = call(
        functools.partial(gram_kernel, POWER % 2 == 1, tiles, groups),
        "gram",
        [field, field, shaped((tiles, group_size, groups * group_size), F32)],
        [gathered, basal, samples],
    )
    return (samples.T, refined.T, gram)


def solution(mesh):
    in_specs = (
        P("tiles", None, None),
        P("tiles", None),
        P("tiles", None),
        P("tiles", None, None),
        P("tiles"),
        P("tiles", None),
        P("tiles", "probes"),
        P("tiles"),
    )
    out_specs = (P("tiles", "probes"), P("tiles", "probes"), P(None, "probes", None))
    return jax.shard_map(shards, mesh=mesh, in_specs=in_specs, out_specs=out_specs, check_vma=False)
```

```python
import functools

import jax
import jax.numpy as jnp
from jax import lax
from jax.experimental import pallas as pl
from jax.experimental.pallas import tpu as pltpu
from jax.sharding import PartitionSpec as P

HALO = 512
POWER = 2
RIM = 64
LANES = 128
RADIX = 512
EDGE_RADIX = 256
EDGE = HALO // EDGE_RADIX
SHRINK = 2.0**-40
VMEM_BYTES = 16 * 1024 * 1024

F32 = jnp.float32
BF16 = jnp.bfloat16


def dot(a, b):
    return lax.dot_general(a, b, (((1,), (0,)), ((), ())), preferred_element_type=F32)


def dot_nt(a, b):
    return lax.dot_general(a, b, (((1,), (1,)), ((), ())), preferred_element_type=F32)


def product(turned):
    return dot if turned else dot_nt


def split(x):
    hi = x.astype(BF16)
    return hi, (x - hi.astype(F32)).astype(BF16)


def rows_iota(shape):
    return lax.broadcasted_iota(jnp.int32, shape, 0)


def lanes_iota(shape):
    return lax.broadcasted_iota(jnp.int32, shape, 1)


def hot(mask):
    return jnp.where(mask, F32(1), F32(0)).astype(BF16)


def hot16(a, b):
    return jnp.where(a == b, jnp.ones((), BF16), jnp.zeros((), BF16))


def lane_tiles(count, tile):
    return jnp.concatenate([tile(i * LANES) for i in range(count)], axis=1)


def spread_matrix(node_slots, padded_order, turned=False):
    pair, wide = 2 * node_slots, 2 * padded_order

    def start(at):
        return (at // node_slots) * padded_order + 3 * (at % node_slots)

    def near(gap):
        return hot((gap >= 0) & (gap < 3))

    if turned:
        return near(rows_iota((wide, pair)) - start(lanes_iota((1, pair))))
    gap = lanes_iota((pair, LANES)) - start(rows_iota((pair, LANES)))
    return lane_tiles(wide // LANES, lambda at: near(gap + at))


def order_matrix(node_slots, padded_order, turned=False):
    pair, wide = 2 * node_slots, 2 * padded_order

    def source(at):
        inner = at % pair
        return (inner // node_slots) * padded_order + 3 * (inner % node_slots) + at // pair

    if not turned:
        return hot(rows_iota((wide, 3 * pair)) == source(lanes_iota((1, 3 * pair))))
    gap = lanes_iota((3 * pair, LANES)) - source(rows_iota((3 * pair, LANES)))
    return lane_tiles(wide // LANES, lambda at: hot(gap + at == 0))


def colour_of(ids):
    return (ids % 2) == (rows_iota(ids.shape) % 2)


def by_side(tile, a, b):
    even = tile % 2 == 0
    return jnp.where(even, b, a), jnp.where(even, a, b)


def to_swaps(tile, for_next, for_previous):
    even = tile % 2 == 0
    return jnp.where(even, for_previous, for_next), jnp.where(even, for_next, for_previous)


def announce_kernel(signs_hbm, ids_hbm, weight_hbm, out_ref, again_ref, signs, ids, lead, sems):
    loads = [
        pltpu.make_async_copy(signs_hbm, signs, sems.at[0]),
        pltpu.make_async_copy(ids_hbm, ids, sems.at[1]),
        pltpu.make_async_copy(weight_hbm.at[:, pl.ds(0, HALO)], lead, sems.at[2]),
    ]
    for load in loads:
        load.start()
    for load in loads:
        load.wait()
    colours = jnp.broadcast_to(ids[...], signs.shape)
    probes = jnp.where(colour_of(colours), (2 * signs[...] - 1).astype(F32), F32(0))
    out_ref[:8, :] = probes
    out_ref[8:, :] = jnp.zeros_like(probes)
    half = HALO // 2
    out_ref[8:11, :] = lead[:, :half]
    out_ref[11:14, :] = lead[:, half:]
    again_ref[...] = out_ref[...]


def halves_of(conn):
    low = conn % RADIX
    halves = []
    for at in range(0, RADIX, EDGE_RADIX):
        inside = (low >= at) & (low < at + EDGE_RADIX)
        halves.append(jnp.where(inside, low - at, -1).astype(F32))
    return halves


def setup_kernel(
    levels,
    counts,
    conn_hbm,
    cell_hbm,
    friction_hbm,
    blocks_hbm,
    conn_ref,
    cell_ref,
    fr_ref,
    blocks_ref,
    node_hot_ref,
    edge_hot_ref,
    level_hot_ref,
    cell_hot_ref,
    spread_ref,
    order_ref,
    conn_in,
    cell_in,
    friction_in,
    sems,
):
    pairs = conn_ref.shape[0]
    slots, padded_order = fr_ref.shape
    node_slots = conn_in.shape[1]
    window = 3 * LANES

    loads = [
        pltpu.make_async_copy(source, target, sems.at[i])
        for i, (source, target) in enumerate(
            [
                (conn_hbm, conn_in),
                (cell_hbm, cell_in),
                (friction_hbm, friction_in),
                (blocks_hbm, blocks_ref),
            ]
        )
    ]
    for load in loads:
        load.start()

    spread_ref[...] = spread_matrix(node_slots, padded_order)
    order_ref[...] = order_matrix(node_slots, padded_order)

    def paired(ref):
        return jnp.concatenate(
            [ref[pl.ds(0, pairs, stride=2), :], ref[pl.ds(1, pairs, stride=2), :]], axis=1
        )

    for load in loads[:3]:
        load.wait()
    conn = paired(conn_in)
    conn_ref[...] = conn
    cells = paired(cell_in)
    cells = jnp.where(cells < RIM, cells + (window - RIM), cells - RIM)
    cell_ref[...] = cells

    shape = (node_slots, padded_order)
    total = jnp.zeros((slots, padded_order), F32)
    for c in range(3):
        place = hot(lanes_iota(shape) == 3 * rows_iota(shape) + c)
        rest = friction_in[c]
        for _ in range(3):
            part = rest.astype(BF16)
            total = total + dot(part, place)
            rest = rest - part.astype(F32)
    live = rows_iota(total.shape) < counts[0]
    fr_ref[...] = jnp.where(live, total, F32(0))

    rows = rows_iota((EDGE_RADIX, LANES)).astype(F32).astype(BF16)
    halves = halves_of(conn)
    which = (conn // RADIX).astype(F32)
    ends = jnp.where(rows_iota((16, LANES)) < 8, F32(0), F32(levels - 1)).astype(BF16)
    cell_low = (cells % LANES).astype(F32)
    for m in range(pairs):
        at = pl.ds(m * LANES, LANES)
        total = jnp.zeros((EDGE_RADIX, LANES), BF16)
        for i, half in enumerate(halves):
            row = jnp.broadcast_to(half[m : m + 1, :], (EDGE_RADIX, LANES)).astype(BF16)
            mine = hot16(rows, row)
            node_hot_ref[i * EDGE_RADIX : (i + 1) * EDGE_RADIX, at] = mine
            total = total + mine
        edge_hot_ref[:, at] = total
        row = jnp.broadcast_to(which[m : m + 1, :], (16, LANES)).astype(BF16)
        for level in range(levels):
            mine = hot16(row, jnp.full((16, LANES), level, BF16))
            level_hot_ref[16 * level : 16 * level + 16, at] = mine
        level_hot_ref[16 * levels : 16 * levels + 16, at] = hot16(row, ends)
        row = jnp.broadcast_to(cell_low[m : m + 1, :], (LANES, LANES)).astype(BF16)
        cell_hot_ref[:, at] = hot16(rows[:LANES], row)
    loads[3].wait()


def turn_nodes_kernel(first, conn_ref, node_turn_ref):
    columns = [half.T for half in halves_of(conn_ref[...])]
    lanes = lanes_iota((LANES, EDGE_RADIX)).astype(F32).astype(BF16)
    for m in range(node_turn_ref.shape[0] // LANES):
        for i, column in enumerate(columns):
            row = column[:, first + m : first + m + 1]
            row = jnp.broadcast_to(row, (LANES, LANES)).astype(BF16)
            row = jnp.concatenate([row] * (EDGE_RADIX // LANES), axis=1)
            at = pl.ds(i * EDGE_RADIX, EDGE_RADIX)
            node_turn_ref[m * LANES : (m + 1) * LANES, at] = hot16(lanes, row)


def turn_blocks_kernel(blocks, turned_ref):
    for slot in range(blocks.shape[0]):
        turned_ref[slot] = blocks[slot].T


def turn_cells_kernel(node_slots, cell_ref, cell_turn_ref, spread_turn_ref, order_turn_ref):
    padded_order = order_turn_ref.shape[1] // 2
    spread_turn_ref[...] = spread_matrix(node_slots, padded_order, True)
    order_turn_ref[...] = order_matrix(node_slots, padded_order, True)
    cells = (cell_ref[...] % LANES).astype(F32).T
    lanes = lanes_iota((LANES, LANES)).astype(F32).astype(BF16)
    for m in range(cell_ref.shape[0]):
        row = jnp.broadcast_to(cells[:, m : m + 1], (LANES, LANES)).astype(BF16)
        cell_turn_ref[m * LANES : (m + 1) * LANES, :] = hot16(lanes, row)


def spread_levels(v_ref, ordered, level_hot, levels, pairs):
    for m in range(pairs):
        at = pl.ds(m * LANES, LANES)
        values = [ordered[16 * m : 16 * m + 16, c * LANES : (c + 1) * LANES] for c in range(3)]
        for i, level in enumerate(levels):
            mask = level_hot[16 * level : 16 * level + 16, at]
            for c in range(3):
                row = 48 * i + 16 * c
                v_ref[row : row + 16, at] = values[c] * mask


def both_parts(x):
    hi = x.astype(BF16).astype(F32)
    return jnp.concatenate([hi, x - hi], axis=0).astype(BF16)


def clear_padding(ref, padded_order):
    for half in range(2):
        end = (half + 1) * padded_order
        ref[:, end - LANES : end] = jnp.zeros((ref.shape[0], LANES), BF16)


def forward_kernel(step, tiles, levels, *refs):
    block_ref, block_a, block_b, *refs = refs
    first = step == 0
    if not first:
        basal_ref, rim_a, rim_b, *refs = refs
    cell_ref, fr_ref, factors, level_hot, cell_hot, spread_ref, order_ref, *refs = refs
    if first:
        node_hot, *refs = refs
    else:
        node_turn, node_turn_rest, *refs = refs
    ordered_ref, a_ref, b_ref, far_ref, near_ref, *refs = refs
    if not first:
        squares_ref, *refs = refs
    if step == 1:
        field_ref, *refs = refs
    f_ref, v_ref = refs

    order = factors.shape[1]
    padded_order = f_ref.shape[1] // 2
    pairs = factors.shape[0] // 2
    tile = lax.axis_index("tiles")

    lane = lanes_iota((8, LANES))
    low = lane < RIM
    after, before = by_side(tile, block_a[:8, :], block_b[:8, :])
    starts = [
        block_ref[:8, :LANES],
        block_ref[:8, LANES:],
        jnp.where(low, after[:, :LANES], before[:, LANES:]),
    ]
    if first:
        parts = starts
    else:
        after, before = by_side(tile, rim_a[...], rim_b[...])
        parts = [basal_ref[:, i * LANES : (i + 1) * LANES] for i in range(3)]
        parts[0] = parts[0] + jnp.where(low, before, F32(0))
        parts[1] = parts[1] + jnp.where(low, F32(0), after)
        parts[2] = parts[2] + jnp.where(low, after, before)
        there = (low & (tile < tiles - 1)) | (~low & (tile > 0))
        parts[2] = jnp.where(there, parts[2], F32(0))
        kept = [(start != 0) if step % 2 == 0 else (start == 0) for start in starts]
        parts = [jnp.where(keep, part, F32(0)) for keep, part in zip(kept, parts)]
        if step == 1:
            field_ref[:, :LANES] = parts[0]
            field_ref[:, LANES:] = parts[1]
        squares_ref[...] = parts[0] * parts[0] + parts[1] * parts[1]
    window = jnp.concatenate(parts, axis=0)
    if step == 1:
        window = window * F32(SHRINK)

    cells = cell_ref[...]
    hi, lo = split(window)
    picked = dot(jnp.concatenate([hi, lo], axis=0), cell_hot[...])
    tops = []
    rests = []
    for m in range(pairs):
        part = picked[:, m * LANES : (m + 1) * LANES]
        which = cells[m : m + 1, :] // LANES
        for base, out in ((0, tops), (24, rests)):
            chosen = jnp.where(which == 0, part[base : base + 8], F32(0))
            for level in (1, 2):
                at = base + 8 * level
                chosen = jnp.where(which == level, part[at : at + 8], chosen)
            out.append(chosen)
    stacked = jnp.concatenate(tops + rests, axis=0).astype(BF16)
    spread = dot(stacked, spread_ref[...])
    half = 8 * pairs
    spread = spread[:half] + spread[half:]

    clear_padding(f_ref, padded_order)
    for m in range(pairs):
        for side in range(2):
            at = side * padded_order
            slot = 2 * m + side
            inputs = spread[8 * m : 8 * m + 8, at : at + order] * fr_ref[slot : slot + 1, :order]
            if first:
                out = product(step > 0)(inputs.astype(BF16), factors[slot])
            else:
                out = product(step > 0)(both_parts(inputs), factors[slot])
                out = out[:8] + out[8:]
            f_ref[16 * m : 16 * m + 16, at : at + order] = both_parts(out)

    ordered = dot(f_ref[...], order_ref[...])
    ordered_ref[...] = ordered.astype(BF16)
    for m in range(pairs):
        at = pl.ds(m * LANES, LANES)
        mask = level_hot[16 * levels : 16 * levels + 16, at]
        for c in range(3):
            value = ordered[16 * m : 16 * m + 8, c * LANES : (c + 1) * LANES]
            value = jnp.concatenate([value, value], axis=0).astype(BF16)
            v_ref[16 * c : 16 * c + 16, at] = value * mask
    if first:
        rim = dot_nt(v_ref[...], node_hot[...])
    else:
        half = node_turn.shape[0]
        rim = dot(v_ref[:, :half], node_turn[...]) + dot(v_ref[:, half:], node_turn_rest[...])
    lead = jnp.concatenate([rim[16 * c : 16 * c + 8] for c in range(3)], axis=0)
    spill = jnp.concatenate([rim[16 * c + 8 : 16 * c + 16] for c in range(3)], axis=0)
    for ref, message, value in zip((a_ref, b_ref), (far_ref, near_ref), to_swaps(tile, spill, lead)):
        ref[...] = value
        pieces = [value[:, i * EDGE_RADIX : (i + 1) * EDGE_RADIX] for i in range(EDGE)]
        message[...] = jnp.concatenate(pieces, axis=0).astype(BF16)


def inner_kernel(levels, ordered_ref, weight_ref, conn_ref, node_hot, level_hot, picked_ref, v_ref):
    pairs = conn_ref.shape[0]
    conn = conn_ref[...]
    inside = range(1, levels - 1)
    spread_levels(v_ref, ordered_ref, level_hot, inside, pairs)
    nodes = dot_nt(v_ref[...], node_hot[...])
    rows = []
    for i in range(3 * len(inside)):
        value = nodes[16 * i : 16 * i + 8] + nodes[16 * i + 8 : 16 * i + 16]
        at = inside[i // 3] * RADIX
        rows.append(value * weight_ref[i % 3 : i % 3 + 1, at : at + RADIX])
    weighted = jnp.concatenate(rows, axis=0).astype(BF16)
    step = 2
    for start in range(0, pairs, step):
        found = dot(weighted, node_hot[:, start * LANES : (start + step) * LANES])
        for i in range(step):
            m = start + i
            which = conn[m : m + 1, :] // RADIX
            part = found[:, i * LANES : (i + 1) * LANES]
            chosen = jnp.zeros((24, LANES), F32)
            for at, level in enumerate(inside):
                chosen = jnp.where(which == level, part[24 * at : 24 * at + 24], chosen)
            for c in range(3):
                picked_ref[8 * m : 8 * m + 8, c * LANES : (c + 1) * LANES] = chosen[8 * c : 8 * c + 8]


def adjoint_kernel(last, clusters, levels, *refs):
    block_ref, block_a, block_b, own_a, own_b, new_a, new_b, inner_ref, weight_ref, *refs = refs
    conn_ref, cell_ref, fr_ref, blocks, edge_hot, cell_map, spread_map, order_map, *refs = refs
    if last:
        squares_1, squares_2, ids_ref, *refs = refs
        basal_ref, out_ref, p_ref, n_ref, v_ref = refs
    else:
        basal_ref, a_ref, b_ref, p_ref, n_ref, v_ref = refs

    order = blocks.shape[1]
    padded_order = p_ref.shape[1] // 2
    pairs = blocks.shape[0] // 2
    tile = lax.axis_index("tiles")

    spill, lead = by_side(tile, own_a[...], own_b[...])
    new_spill, new_lead = by_side(tile, new_a[...].astype(F32), new_b[...].astype(F32))
    after, before = by_side(tile, block_a[...], block_b[...])
    rows = []
    for i in range(3 * EDGE):
        c, at = i % 3, (i // 3) * EDGE_RADIX
        value = lead[8 * c : 8 * c + 8, at : at + EDGE_RADIX] + new_lead[8 * i : 8 * i + 8]
        rows.append(value * weight_ref[c : c + 1, at : at + EDGE_RADIX])
    for i in range(3 * EDGE):
        c, at = i % 3, (i // 3) * EDGE_RADIX
        value = spill[8 * c : 8 * c + 8, at : at + EDGE_RADIX] + new_spill[8 * i : 8 * i + 8]
        rows.append(value * after[8 + i : 9 + i, :])
    weighted = jnp.concatenate(rows, axis=0).astype(BF16)

    conn = conn_ref[...]
    first = levels * RADIX // EDGE_RADIX - EDGE
    edges = [*range(EDGE), *range(first, first + EDGE)]
    width = 2
    for start in range(0, pairs, width):
        found = dot(weighted, edge_hot[:, start * LANES : (start + width) * LANES])
        values = [[] for _ in range(3)]
        for i in range(width):
            m = start + i
            which = conn[m : m + 1, :] // EDGE_RADIX
            part = found[:, i * LANES : (i + 1) * LANES]
            for c in range(3):
                value = inner_ref[8 * m : 8 * m + 8, c * LANES : (c + 1) * LANES]
                for at, level in enumerate(edges):
                    row = 24 * at + 8 * c
                    value = jnp.where(which == level, part[row : row + 8], value)
                values[c].append(value)
        for c in range(3):
            rows = jnp.concatenate(values[c], axis=0).astype(BF16)
            n_ref[8 * start : 8 * (start + width), c * LANES : (c + 1) * LANES] = rows
    natural = product(last)(n_ref[...], order_map[...])
    clear_padding(p_ref, padded_order)
    for m in range(pairs):
        for side in range(2):
            at = side * padded_order
            slot = 2 * m + side
            out = dot(natural[8 * m : 8 * m + 8, at : at + order].astype(BF16), blocks[slot])
            out = out * fr_ref[slot : slot + 1, :order]
            p_ref[16 * m : 16 * m + 16, at : at + order] = both_parts(out)

    partial = product(last)(p_ref[...], spread_map[...])
    cells = cell_ref[...]
    for m in range(pairs):
        which = cells[m : m + 1, :] // LANES
        value = partial[16 * m : 16 * m + 8, :] + partial[16 * m + 8 : 16 * m + 16, :]
        rows = jnp.concatenate([jnp.where(which == level, value, F32(0)) for level in range(3)], axis=0)
        hi = rows.astype(BF16).astype(F32)
        both = jnp.concatenate([hi, rows - hi], axis=0)
        v_ref[:, m * LANES : (m + 1) * LANES] = both.astype(BF16)
    basal = product(last)(v_ref[...], cell_map[...])
    basal = basal[:24] + basal[24:]
    parts = [basal[8 * i : 8 * i + 8] for i in range(3)]
    for i in range(3):
        basal_ref[:, i * LANES : (i + 1) * LANES] = parts[i]
    lane = lanes_iota((8, LANES))
    if not last:
        for_next = jnp.where(lane < RIM, parts[2], parts[1])
        for_previous = jnp.where(lane < RIM, parts[0], parts[2])
        a_ref[...], b_ref[...] = to_swaps(tile, for_next, for_previous)
        return

    starts = [
        block_ref[:1, :LANES],
        block_ref[:1, LANES:],
        jnp.where(lane[:1] < RIM, after[:1, :LANES], before[:1, LANES:]),
    ]
    packed = []
    for start, part in zip(starts, parts):
        even = start != 0
        rows = [jnp.where(even, part[r + 1 : r + 2], part[r : r + 1]) for r in range(0, 8, 2)]
        packed.append(jnp.concatenate(rows, axis=0))
    extra = jnp.zeros((8, LANES), F32)
    for i, ref in enumerate((squares_1, squares_2)):
        rest = jnp.sum(ref[...], axis=1, keepdims=True)
        for j in range(3):
            piece = rest.astype(BF16).astype(F32)
            extra = jnp.where(lane == 3 * i + j, piece, extra)
            rest = rest - piece
    moved = pltpu.roll(extra, 8, 1)
    rows = [extra[r : r + 1] + moved[r + 1 : r + 2] for r in range(0, 8, 2)]
    extra = jnp.concatenate(rows, axis=0)
    ids = ids_ref[...]
    for k in range(1, clusters):
        below = jnp.sum((ids < k).astype(F32), axis=1, keepdims=True)
        extra = jnp.where(lane[:4] == 16 + k, below, extra)
    top = jnp.concatenate([packed[0], packed[1]], axis=1)
    message = jnp.concatenate([top, jnp.concatenate([packed[2], extra], axis=1)], axis=0)
    message = message.astype(BF16)
    for t in range(out_ref.shape[0]):
        out_ref[t] = message


def gram_kernel(
    keep_same, tiles, groups, g_ref, own_ref, samples_in, samples_ref, field_ref, gram_ref
):
    samples_ref[...] = samples_in[...]
    tile = lax.axis_index("tiles")
    group = lax.axis_index("probes")
    clusters = gram_ref.shape[0]
    cell_count = tiles * 2 * LANES
    low = lanes_iota((8, LANES)) < RIM
    row = rows_iota((8, LANES))

    def twice(x):
        out = jnp.broadcast_to(x[:1], (8, LANES))
        for r in range(1, 4):
            out = jnp.where(row >= 2 * r, jnp.broadcast_to(x[r : r + 1], (8, LANES)), out)
        return out

    def piece_of(t, p, lower, at):
        part = g_ref[t, p].astype(F32)
        return part[4 * lower : 4 * lower + 4, at * LANES : (at + 1) * LANES]

    def factor_of(p):
        def add(t, acc):
            return acc + g_ref[t, p].astype(F32)[4:, LANES:]

        sums = lax.fori_loop(0, tiles, add, jnp.zeros((4, LANES), F32), unroll=tiles <= 8)
        sums = twice(sums)
        sums = jnp.where(row % 2 == 0, sums, pltpu.roll(sums, LANES - 8, 1))
        first = jnp.sum(sums[:, :3], axis=1, keepdims=True)
        second = jnp.sum(sums[:, 3:6], axis=1, keepdims=True)
        scale = jnp.sqrt(first / cell_count + F32(1e-06))
        size = jnp.sqrt(second / cell_count) * F32(1 / SHRINK) / scale
        return F32(1 / SHRINK) / (scale * jnp.sqrt(size * size + F32(1e-06)))

    def ids_of(t):
        starts = twice(piece_of(t, 0, 1, 1))
        cell = lanes_iota((8, 2 * LANES)).astype(F32)
        ids = jnp.zeros(cell.shape, jnp.int32)
        for k in range(1, clusters):
            ids = ids + (cell >= starts[:, 16 + k : 17 + k]).astype(jnp.int32)
        return [ids[:, :LANES], ids[:, LANES:]]

    def field(t, p, ids, own=None):
        before = piece_of(jnp.maximum(t - 1, 0), p, 1, 0)
        before = jnp.where(low[:4] & (t > 0), before, F32(0))
        after = piece_of(jnp.minimum(t + 1, tiles - 1), p, 1, 0)
        after = jnp.where(~low[:4] & (t < tiles - 1), after, F32(0))
        if own is None:
            parts = [twice(piece_of(t, p, 0, 0) + before), twice(piece_of(t, p, 0, 1) + after)]
        else:
            parts = [own[0] + twice(before), own[1] + twice(after)]
        return [
            jnp.where(colour_of(i) if keep_same else ~colour_of(i), part, F32(0))
            for i, part in zip(ids, parts)
        ]

    factors = [factor_of(p) for p in range(groups)]
    mine_factor = factors[0]
    for p in range(1, groups):
        mine_factor = jnp.where(group == p, factors[p], mine_factor)
    own = [own_ref[:, at * LANES : (at + 1) * LANES] for at in range(2)]
    own = field(tile, group, ids_of(tile), own)
    field_ref[:, :LANES] = own[0] * mine_factor
    field_ref[:, LANES:] = own[1] * mine_factor

    def add_tile(t, acc):
        ids = ids_of(t)
        every = [
            jnp.concatenate(field(t, p, ids), axis=1) * factors[p] for p in range(groups)
        ]
        mine = every[0]
        for p in range(1, groups):
            mine = jnp.where(group == p, every[p], mine)
        ids = jnp.concatenate(ids, axis=1)
        left = jnp.concatenate([jnp.where(ids == k, mine, F32(0)) for k in range(clusters)], axis=0)
        return acc + lax.dot_general(
            left,
            jnp.concatenate(every, axis=0),
            (((1,), (1,)), ((), ())),
            precision=lax.Precision.HIGHEST,
            preferred_element_type=F32,
        )

    acc = jnp.zeros((8 * clusters, 8 * groups), F32)
    acc = lax.fori_loop(0, tiles, add_tile, acc, unroll=tiles <= 8)
    gram_ref[...] = acc.reshape(gram_ref.shape)


def shards(
    blocks, connectivity, basal_map, friction, elem_counts, obs_weight, sign_bits, cluster_ids
):
    slots = blocks.shape[0]
    node_slots = connectivity.shape[1]
    node_count = obs_weight.shape[0]
    cell_count, group_size = sign_bits.shape
    tiles = lax.axis_size("tiles")
    groups = lax.axis_size("probes")
    pairs = slots * node_slots // LANES
    refs = pairs * LANES
    levels = (node_count + HALO) // RADIX
    padded_order = 2 * LANES
    window = cell_count + 2 * RIM

    vmem = pl.BlockSpec(memory_space=pltpu.VMEM)
    params = pltpu.CompilerParams(vmem_limit_bytes=VMEM_BYTES)
    shaped = jax.ShapeDtypeStruct

    hbm = pl.BlockSpec(memory_space=pltpu.HBM)
    smem = pl.BlockSpec(memory_space=pltpu.SMEM)

    def call(kernel, name, out_shape, operands, scratch=(), in_specs=None):
        in_specs = in_specs or [vmem] * len(operands)
        operands = [
            pltpu.with_memory_space_constraint(x, pltpu.HBM) if spec is hbm else x
            for x, spec in zip(operands, in_specs)
        ]
        return pl.pallas_call(
            kernel,
            out_shape=out_shape,
            in_specs=in_specs,
            out_specs=jax.tree.map(lambda _: vmem, out_shape),
            scratch_shapes=list(scratch),
            compiler_params=params,
            name=name,
        )(*operands)

    evens = range(0, tiles - 1, 2)
    odds = range(1, tiles - 1, 2)
    pairs_a = [(i, i + 1) for i in odds] + [(i + 1, i) for i in odds]
    pairs_b = [(i, i + 1) for i in evens] + [(i + 1, i) for i in evens]

    def swapped(a, b):
        return lax.ppermute(a, "tiles", pairs_a), lax.ppermute(b, "tiles", pairs_b)

    weight = obs_weight.T
    block, again = call(
        announce_kernel,
        "announce",
        [shaped((16, cell_count), F32)] * 2,
        [sign_bits.T, cluster_ids.reshape(1, cell_count), weight],
        [
            pltpu.VMEM((group_size, cell_count), jnp.int32),
            pltpu.VMEM((1, cell_count), jnp.int32),
            pltpu.VMEM((3, HALO), F32),
            pltpu.SemaphoreType.DMA((3,)),
        ],
        [hbm] * 3,
    )
    block_a, block_b = swapped(again, block)

    conn, cells, fr, loaded, node_hot, edge_hot, level_hot, cell_hot, spread, order = call(
        functools.partial(setup_kernel, levels),
        "setup",
        [
            shaped((pairs, LANES), jnp.int32),
            shaped((pairs, LANES), jnp.int32),
            shaped((slots, padded_order), F32),
            shaped(blocks.shape, BF16),
            shaped((RADIX, refs), BF16),
            shaped((EDGE_RADIX, refs), BF16),
            shaped((16 * (levels + 1), refs), BF16),
            shaped((LANES, refs), BF16),
            shaped((LANES, 2 * padded_order), BF16),
            shaped((2 * padded_order, 3 * LANES), BF16),
        ],
        [elem_counts, connectivity, basal_map, friction.transpose(2, 0, 1), blocks],
        [
            pltpu.VMEM(connectivity.shape, jnp.int32),
            pltpu.VMEM(basal_map.shape, jnp.int32),
            pltpu.VMEM((3, slots, node_slots), F32),
            pltpu.SemaphoreType.DMA((4,)),
        ],
        [smem] + [hbm] * 4,
    )
    factors, node_maps = loaded, [node_hot]
    cell_map, spread_map, order_map = cell_hot, spread, order

    edge = shaped((24, HALO), F32)
    message = shaped((24 * EDGE, EDGE_RADIX), BF16)
    rim = shaped((group_size, LANES), F32)
    whole = shaped((group_size, window), F32)
    field = shaped((group_size, cell_count), F32)
    everyone = ("tiles", "probes")

    def turned_nodes(first_pair, ids):
        return call(
            functools.partial(turn_nodes_kernel, first_pair),
            "turn_nodes",
            shaped((refs // 2, RADIX), BF16),
            [ids],
        )

    carried = []
    squares = []
    samples = None
    for step in range(POWER + 1):
        last = step == POWER
        out_shape = [shaped((16 * pairs, 3 * LANES), BF16), edge, edge, message, message]
        out_shape += [rim] * (step > 0) + [field] * (step == 1)
        ordered, own_a, own_b, far, near, *extra = call(
            functools.partial(forward_kernel, step, tiles, levels),
            "forward",
            out_shape,
            [block, block_a, block_b, *carried]
            + [cells, fr, factors, level_hot, cell_hot, spread, order, *node_maps],
            [
                pltpu.VMEM((16 * pairs, 2 * padded_order), BF16),
                pltpu.VMEM((48, refs), BF16),
            ],
        )
        squares += extra[:1]
        if step == 1:
            samples = extra[1]
        if step == 0:
            far, near, ids = lax.optimization_barrier((far, near, conn))
            node_maps = [turned_nodes(0, ids)]
        new_a, new_b = swapped(far, near)
        inner = call(
            functools.partial(inner_kernel, levels),
            "inner",
            shaped((8 * pairs, 3 * LANES), F32),
            [ordered, weight, conn, node_hot, level_hot],
            [pltpu.VMEM((48 * (levels - 2), refs), BF16)],
        )
        if step == 0:
            inner, node_maps[0] = lax.optimization_barrier((inner, node_maps[0]))
        operands = [block, block_a, block_b, own_a, own_b, new_a, new_b, inner, weight]
        operands += [conn, cells, fr, loaded, edge_hot, cell_map, spread_map, order_map]
        if last:
            operands += squares + [cluster_ids.reshape(1, cell_count)]
            packed = shaped((lax.axis_size(everyone), group_size, 2 * LANES), BF16)
            out_shape = [whole, packed]
        else:
            out_shape = [whole, rim, rim]
        basal, *messages = call(
            functools.partial(adjoint_kernel, last, tiles, levels),
            "adjoint",
            out_shape,
            operands,
            [
                pltpu.VMEM((16 * pairs, 2 * padded_order), BF16),
                pltpu.VMEM((8 * pairs, 3 * LANES), BF16),
                pltpu.VMEM((48, refs), BF16),
            ],
        )
        if not last:
            if step == 0:
                *messages, source, ids = lax.optimization_barrier((*messages, loaded, conn))
                shape = shaped(blocks.shape, BF16)
                factors = call(turn_blocks_kernel, "turn_blocks", shape, [source])
                node_maps.append(turned_nodes(pairs // 2, ids))
            if step == POWER - 1:
                *messages, ids = lax.optimization_barrier((*messages, cells))
                cell_map, spread_map, order_map = call(
                    functools.partial(turn_cells_kernel, node_slots),
                    "turn_cells",
                    [
                        shaped((refs, LANES), BF16),
                        shaped((2 * padded_order, LANES), BF16),
                        shaped((3 * LANES, 2 * padded_order), BF16),
                    ],
                    [ids],
                )
                basal, cell_map = lax.optimization_barrier((basal, cell_map))
            carried = [basal, *swapped(*messages)]

    gathered = lax.all_to_all(messages[0], everyone, 0, 0)
    gathered = gathered.reshape(tiles, groups, *gathered.shape[1:])
    samples, refined, gram = call(
        functools.partial(gram_kernel, POWER % 2 == 1, tiles, groups),
        "gram",
        [field, field, shaped((tiles, group_size, groups * group_size), F32)],
        [gathered, basal, samples],
    )
    return (samples.T, refined.T, gram)


def solution(mesh):
    in_specs = (
        P("tiles", None, None),
        P("tiles", None),
        P("tiles", None),
        P("tiles", None, None),
        P("tiles"),
        P("tiles", None),
        P("tiles", "probes"),
        P("tiles"),
    )
    out_specs = (P("tiles", "probes"), P("tiles", "probes"), P(None, "probes", None))
    return jax.shard_map(shards, mesh=mesh, in_specs=in_specs, out_specs=out_specs, check_vma=False)
```

```python
import functools

import jax
import jax.numpy as jnp
from jax import lax
from jax.experimental import pallas as pl
from jax.experimental.pallas import tpu as pltpu
from jax.sharding import PartitionSpec as P

HALO = 512
POWER = 2
RIM = 64
LANES = 128
RADIX = 512
EDGE_RADIX = 256
EDGE = HALO // EDGE_RADIX
SHRINK = 2.0**-40
VMEM_BYTES = 16 * 1024 * 1024

F32 = jnp.float32
BF16 = jnp.bfloat16


def dot(a, b):
    return lax.dot_general(a, b, (((1,), (0,)), ((), ())), preferred_element_type=F32)


def dot_nt(a, b):
    return lax.dot_general(a, b, (((1,), (1,)), ((), ())), preferred_element_type=F32)


def product(turned):
    return dot if turned else dot_nt


def split(x):
    hi = x.astype(BF16)
    return hi, (x - hi.astype(F32)).astype(BF16)


def rows_iota(shape):
    return lax.broadcasted_iota(jnp.int32, shape, 0)


def lanes_iota(shape):
    return lax.broadcasted_iota(jnp.int32, shape, 1)


def hot(mask):
    return jnp.where(mask, F32(1), F32(0)).astype(BF16)


def hot16(a, b):
    return jnp.where(a == b, jnp.ones((), BF16), jnp.zeros((), BF16))


def lane_tiles(count, tile):
    return jnp.concatenate([tile(i * LANES) for i in range(count)], axis=1)


def spread_matrix(node_slots, padded_order, turned=False):
    pair, wide = 2 * node_slots, 2 * padded_order

    def start(at):
        return (at // node_slots) * padded_order + 3 * (at % node_slots)

    def near(gap):
        return hot((gap >= 0) & (gap < 3))

    if turned:
        return near(rows_iota((wide, pair)) - start(lanes_iota((1, pair))))
    gap = lanes_iota((pair, LANES)) - start(rows_iota((pair, LANES)))
    return lane_tiles(wide // LANES, lambda at: near(gap + at))


def order_matrix(node_slots, padded_order, turned=False):
    pair, wide = 2 * node_slots, 2 * padded_order

    def source(at):
        inner = at % pair
        return (inner // node_slots) * padded_order + 3 * (inner % node_slots) + at // pair

    if not turned:
        return hot(rows_iota((wide, 3 * pair)) == source(lanes_iota((1, 3 * pair))))
    gap = lanes_iota((3 * pair, LANES)) - source(rows_iota((3 * pair, LANES)))
    return lane_tiles(wide // LANES, lambda at: hot(gap + at == 0))


def colour_of(ids):
    return (ids % 2) == (rows_iota(ids.shape) % 2)


def by_side(tile, a, b):
    even = tile % 2 == 0
    return jnp.where(even, b, a), jnp.where(even, a, b)


def to_swaps(tile, for_next, for_previous):
    even = tile % 2 == 0
    return jnp.where(even, for_previous, for_next), jnp.where(even, for_next, for_previous)


def announce_kernel(signs_hbm, ids_hbm, weight_hbm, out_ref, again_ref, signs, ids, lead, sems):
    loads = [
        pltpu.make_async_copy(signs_hbm, signs, sems.at[0]),
        pltpu.make_async_copy(ids_hbm, ids, sems.at[1]),
        pltpu.make_async_copy(weight_hbm.at[:, pl.ds(0, HALO)], lead, sems.at[2]),
    ]
    for load in loads:
        load.start()
    for load in loads:
        load.wait()
    colours = jnp.broadcast_to(ids[...], signs.shape)
    probes = jnp.where(colour_of(colours), (2 * signs[...] - 1).astype(F32), F32(0))
    out_ref[:8, :] = probes
    out_ref[8:, :] = jnp.zeros_like(probes)
    half = HALO // 2
    out_ref[8:11, :] = lead[:, :half]
    out_ref[11:14, :] = lead[:, half:]
    again_ref[...] = out_ref[...]


def halves_of(conn):
    low = conn % RADIX
    halves = []
    for at in range(0, RADIX, EDGE_RADIX):
        inside = (low >= at) & (low < at + EDGE_RADIX)
        halves.append(jnp.where(inside, low - at, -1).astype(F32))
    return halves


def setup_kernel(
    levels,
    counts,
    conn_hbm,
    cell_hbm,
    friction_hbm,
    blocks_hbm,
    conn_ref,
    cell_ref,
    fr_ref,
    blocks_ref,
    node_hot_ref,
    edge_hot_ref,
    level_hot_ref,
    cell_hot_ref,
    spread_ref,
    order_ref,
    conn_in,
    cell_in,
    friction_in,
    sems,
):
    pairs = conn_ref.shape[0]
    slots, padded_order = fr_ref.shape
    node_slots = conn_in.shape[1]
    window = 3 * LANES

    loads = [
        pltpu.make_async_copy(source, target, sems.at[i])
        for i, (source, target) in enumerate(
            [
                (conn_hbm, conn_in),
                (cell_hbm, cell_in),
                (friction_hbm, friction_in),
                (blocks_hbm, blocks_ref),
            ]
        )
    ]
    for load in loads:
        load.start()

    spread_ref[...] = spread_matrix(node_slots, padded_order)
    order_ref[...] = order_matrix(node_slots, padded_order)

    def paired(ref):
        return jnp.concatenate(
            [ref[pl.ds(0, pairs, stride=2), :], ref[pl.ds(1, pairs, stride=2), :]], axis=1
        )

    for load in loads[:3]:
        load.wait()
    conn = paired(conn_in)
    conn_ref[...] = conn
    cells = paired(cell_in)
    cells = jnp.where(cells < RIM, cells + (window - RIM), cells - RIM)
    cell_ref[...] = cells

    shape = (node_slots, padded_order)
    total = jnp.zeros((slots, padded_order), F32)
    for c in range(3):
        place = hot(lanes_iota(shape) == 3 * rows_iota(shape) + c)
        rest = friction_in[c]
        for _ in range(3):
            part = rest.astype(BF16)
            total = total + dot(part, place)
            rest = rest - part.astype(F32)
    live = rows_iota(total.shape) < counts[0]
    fr_ref[...] = jnp.where(live, total, F32(0))

    rows = rows_iota((EDGE_RADIX, LANES)).astype(F32).astype(BF16)
    halves = halves_of(conn)
    which = (conn // RADIX).astype(F32)
    ends = jnp.where(rows_iota((16, LANES)) < 8, F32(0), F32(levels - 1)).astype(BF16)
    cell_low = (cells % LANES).astype(F32)
    for m in range(pairs):
        at = pl.ds(m * LANES, LANES)
        total = jnp.zeros((EDGE_RADIX, LANES), BF16)
        for i, half in enumerate(halves):
            row = jnp.broadcast_to(half[m : m + 1, :], (EDGE_RADIX, LANES)).astype(BF16)
            mine = hot16(rows, row)
            node_hot_ref[i * EDGE_RADIX : (i + 1) * EDGE_RADIX, at] = mine
            total = total + mine
        edge_hot_ref[:, at] = total
        row = jnp.broadcast_to(which[m : m + 1, :], (16, LANES)).astype(BF16)
        for level in range(levels):
            mine = hot16(row, jnp.full((16, LANES), level, BF16))
            level_hot_ref[16 * level : 16 * level + 16, at] = mine
        level_hot_ref[16 * levels : 16 * levels + 16, at] = hot16(row, ends)
        row = jnp.broadcast_to(cell_low[m : m + 1, :], (LANES, LANES)).astype(BF16)
        cell_hot_ref[:, at] = hot16(rows[:LANES], row)
    loads[3].wait()


def turn_nodes_kernel(conn_ref, node_turn_ref):
    columns = [half.T for half in halves_of(conn_ref[...])]
    lanes = lanes_iota((LANES, EDGE_RADIX)).astype(F32).astype(BF16)
    for m in range(conn_ref.shape[0]):
        for i, column in enumerate(columns):
            row = jnp.broadcast_to(column[:, m : m + 1], (LANES, LANES)).astype(BF16)
            row = jnp.concatenate([row] * (EDGE_RADIX // LANES), axis=1)
            at = pl.ds(i * EDGE_RADIX, EDGE_RADIX)
            node_turn_ref[m * LANES : (m + 1) * LANES, at] = hot16(lanes, row)


def turn_blocks_kernel(blocks, turned_ref):
    for slot in range(blocks.shape[0]):
        turned_ref[slot] = blocks[slot].T


def turn_cells_kernel(node_slots, cell_ref, cell_turn_ref, spread_turn_ref, order_turn_ref):
    padded_order = order_turn_ref.shape[1] // 2
    spread_turn_ref[...] = spread_matrix(node_slots, padded_order, True)
    order_turn_ref[...] = order_matrix(node_slots, padded_order, True)
    cells = (cell_ref[...] % LANES).astype(F32).T
    lanes = lanes_iota((LANES, LANES)).astype(F32).astype(BF16)
    for m in range(cell_ref.shape[0]):
        row = jnp.broadcast_to(cells[:, m : m + 1], (LANES, LANES)).astype(BF16)
        cell_turn_ref[m * LANES : (m + 1) * LANES, :] = hot16(lanes, row)


def spread_levels(v_ref, ordered, level_hot, levels, pairs):
    for m in range(pairs):
        at = pl.ds(m * LANES, LANES)
        values = [ordered[16 * m : 16 * m + 16, c * LANES : (c + 1) * LANES] for c in range(3)]
        for i, level in enumerate(levels):
            mask = level_hot[16 * level : 16 * level + 16, at]
            for c in range(3):
                row = 48 * i + 16 * c
                v_ref[row : row + 16, at] = values[c] * mask


def both_parts(x):
    hi = x.astype(BF16).astype(F32)
    return jnp.concatenate([hi, x - hi], axis=0).astype(BF16)


def clear_padding(ref, padded_order):
    for half in range(2):
        end = (half + 1) * padded_order
        ref[:, end - LANES : end] = jnp.zeros((ref.shape[0], LANES), BF16)


def forward_kernel(step, tiles, levels, *refs):
    block_ref, block_a, block_b, *refs = refs
    first = step == 0
    if not first:
        basal_ref, rim_a, rim_b, *refs = refs
    cell_ref, fr_ref, factors, node_map, level_hot, cell_hot, spread_ref, order_ref, *refs = refs
    ordered_ref, a_ref, b_ref, far_ref, near_ref, *refs = refs
    if not first:
        squares_ref, *refs = refs
    if step == 1:
        field_ref, *refs = refs
    f_ref, v_ref = refs

    order = factors.shape[1]
    padded_order = f_ref.shape[1] // 2
    pairs = factors.shape[0] // 2
    tile = lax.axis_index("tiles")

    lane = lanes_iota((8, LANES))
    low = lane < RIM
    after, before = by_side(tile, block_a[:8, :], block_b[:8, :])
    starts = [
        block_ref[:8, :LANES],
        block_ref[:8, LANES:],
        jnp.where(low, after[:, :LANES], before[:, LANES:]),
    ]
    if first:
        parts = starts
    else:
        after, before = by_side(tile, rim_a[...], rim_b[...])
        parts = [basal_ref[:, i * LANES : (i + 1) * LANES] for i in range(3)]
        parts[0] = parts[0] + jnp.where(low, before, F32(0))
        parts[1] = parts[1] + jnp.where(low, F32(0), after)
        parts[2] = parts[2] + jnp.where(low, after, before)
        there = (low & (tile < tiles - 1)) | (~low & (tile > 0))
        parts[2] = jnp.where(there, parts[2], F32(0))
        kept = [(start != 0) if step % 2 == 0 else (start == 0) for start in starts]
        parts = [jnp.where(keep, part, F32(0)) for keep, part in zip(kept, parts)]
        if step == 1:
            field_ref[:, :LANES] = parts[0]
            field_ref[:, LANES:] = parts[1]
        squares_ref[...] = parts[0] * parts[0] + parts[1] * parts[1]
    window = jnp.concatenate(parts, axis=0)
    if step == 1:
        window = window * F32(SHRINK)

    cells = cell_ref[...]
    hi, lo = split(window)
    picked = dot(jnp.concatenate([hi, lo], axis=0), cell_hot[...])
    tops = []
    rests = []
    for m in range(pairs):
        part = picked[:, m * LANES : (m + 1) * LANES]
        which = cells[m : m + 1, :] // LANES
        for base, out in ((0, tops), (24, rests)):
            chosen = jnp.where(which == 0, part[base : base + 8], F32(0))
            for level in (1, 2):
                at = base + 8 * level
                chosen = jnp.where(which == level, part[at : at + 8], chosen)
            out.append(chosen)
    stacked = jnp.concatenate(tops + rests, axis=0).astype(BF16)
    spread = dot(stacked, spread_ref[...])
    half = 8 * pairs
    spread = spread[:half] + spread[half:]

    clear_padding(f_ref, padded_order)
    for m in range(pairs):
        for side in range(2):
            at = side * padded_order
            slot = 2 * m + side
            inputs = spread[8 * m : 8 * m + 8, at : at + order] * fr_ref[slot : slot + 1, :order]
            if first:
                out = product(step > 0)(inputs.astype(BF16), factors[slot])
            else:
                out = product(step > 0)(both_parts(inputs), factors[slot])
                out = out[:8] + out[8:]
            f_ref[16 * m : 16 * m + 16, at : at + order] = both_parts(out)

    ordered = dot(f_ref[...], order_ref[...])
    ordered_ref[...] = ordered.astype(BF16)
    for m in range(pairs):
        at = pl.ds(m * LANES, LANES)
        mask = level_hot[16 * levels : 16 * levels + 16, at]
        for c in range(3):
            value = ordered[16 * m : 16 * m + 8, c * LANES : (c + 1) * LANES]
            value = jnp.concatenate([value, value], axis=0).astype(BF16)
            v_ref[16 * c : 16 * c + 16, at] = value * mask
    rim = product(step > 0)(v_ref[...], node_map[...])
    lead = jnp.concatenate([rim[16 * c : 16 * c + 8] for c in range(3)], axis=0)
    spill = jnp.concatenate([rim[16 * c + 8 : 16 * c + 16] for c in range(3)], axis=0)
    for ref, message, value in zip((a_ref, b_ref), (far_ref, near_ref), to_swaps(tile, spill, lead)):
        ref[...] = value
        pieces = [value[:, i * EDGE_RADIX : (i + 1) * EDGE_RADIX] for i in range(EDGE)]
        message[...] = jnp.concatenate(pieces, axis=0).astype(BF16)


def inner_kernel(levels, ordered_ref, weight_ref, conn_ref, node_hot, level_hot, picked_ref, v_ref):
    pairs = conn_ref.shape[0]
    conn = conn_ref[...]
    inside = range(1, levels - 1)
    spread_levels(v_ref, ordered_ref, level_hot, inside, pairs)
    nodes = dot_nt(v_ref[...], node_hot[...])
    rows = []
    for i in range(3 * len(inside)):
        value = nodes[16 * i : 16 * i + 8] + nodes[16 * i + 8 : 16 * i + 16]
        at = inside[i // 3] * RADIX
        rows.append(value * weight_ref[i % 3 : i % 3 + 1, at : at + RADIX])
    weighted = jnp.concatenate(rows, axis=0).astype(BF16)
    step = 4
    for start in range(0, pairs, step):
        found = dot(weighted, node_hot[:, start * LANES : (start + step) * LANES])
        for i in range(step):
            m = start + i
            which = conn[m : m + 1, :] // RADIX
            part = found[:, i * LANES : (i + 1) * LANES]
            chosen = jnp.zeros((24, LANES), F32)
            for at, level in enumerate(inside):
                chosen = jnp.where(which == level, part[24 * at : 24 * at + 24], chosen)
            for c in range(3):
                picked_ref[8 * m : 8 * m + 8, c * LANES : (c + 1) * LANES] = chosen[8 * c : 8 * c + 8]


def adjoint_kernel(last, clusters, levels, *refs):
    block_ref, block_a, block_b, own_a, own_b, new_a, new_b, inner_ref, weight_ref, *refs = refs
    conn_ref, cell_ref, fr_ref, blocks, edge_hot, cell_map, spread_map, order_map, *refs = refs
    if last:
        squares_1, squares_2, ids_ref, *refs = refs
        basal_ref, out_ref, p_ref, n_ref, v_ref = refs
    else:
        basal_ref, a_ref, b_ref, p_ref, n_ref, v_ref = refs

    order = blocks.shape[1]
    padded_order = p_ref.shape[1] // 2
    pairs = blocks.shape[0] // 2
    tile = lax.axis_index("tiles")

    spill, lead = by_side(tile, own_a[...], own_b[...])
    new_spill, new_lead = by_side(tile, new_a[...].astype(F32), new_b[...].astype(F32))
    after, before = by_side(tile, block_a[...], block_b[...])
    rows = []
    for i in range(3 * EDGE):
        c, at = i % 3, (i // 3) * EDGE_RADIX
        value = lead[8 * c : 8 * c + 8, at : at + EDGE_RADIX] + new_lead[8 * i : 8 * i + 8]
        rows.append(value * weight_ref[c : c + 1, at : at + EDGE_RADIX])
    for i in range(3 * EDGE):
        c, at = i % 3, (i // 3) * EDGE_RADIX
        value = spill[8 * c : 8 * c + 8, at : at + EDGE_RADIX] + new_spill[8 * i : 8 * i + 8]
        rows.append(value * after[8 + i : 9 + i, :])
    weighted = jnp.concatenate(rows, axis=0).astype(BF16)

    conn = conn_ref[...]
    first = levels * RADIX // EDGE_RADIX - EDGE
    edges = [*range(EDGE), *range(first, first + EDGE)]
    width = 4
    for start in range(0, pairs, width):
        found = dot(weighted, edge_hot[:, start * LANES : (start + width) * LANES])
        values = [[] for _ in range(3)]
        for i in range(width):
            m = start + i
            which = conn[m : m + 1, :] // EDGE_RADIX
            part = found[:, i * LANES : (i + 1) * LANES]
            for c in range(3):
                value = inner_ref[8 * m : 8 * m + 8, c * LANES : (c + 1) * LANES]
                for at, level in enumerate(edges):
                    row = 24 * at + 8 * c
                    value = jnp.where(which == level, part[row : row + 8], value)
                values[c].append(value)
        for c in range(3):
            rows = jnp.concatenate(values[c], axis=0).astype(BF16)
            n_ref[8 * start : 8 * (start + width), c * LANES : (c + 1) * LANES] = rows
    natural = product(last)(n_ref[...], order_map[...])
    clear_padding(p_ref, padded_order)
    for m in range(pairs):
        for side in range(2):
            at = side * padded_order
            slot = 2 * m + side
            out = dot(natural[8 * m : 8 * m + 8, at : at + order].astype(BF16), blocks[slot])
            out = out * fr_ref[slot : slot + 1, :order]
            p_ref[16 * m : 16 * m + 16, at : at + order] = both_parts(out)

    partial = product(last)(p_ref[...], spread_map[...])
    cells = cell_ref[...]
    for m in range(pairs):
        which = cells[m : m + 1, :] // LANES
        value = partial[16 * m : 16 * m + 8, :] + partial[16 * m + 8 : 16 * m + 16, :]
        rows = jnp.concatenate([jnp.where(which == level, value, F32(0)) for level in range(3)], axis=0)
        hi = rows.astype(BF16).astype(F32)
        both = jnp.concatenate([hi, rows - hi], axis=0)
        v_ref[:, m * LANES : (m + 1) * LANES] = both.astype(BF16)
    basal = product(last)(v_ref[...], cell_map[...])
    basal = basal[:24] + basal[24:]
    parts = [basal[8 * i : 8 * i + 8] for i in range(3)]
    for i in range(3):
        basal_ref[:, i * LANES : (i + 1) * LANES] = parts[i]
    lane = lanes_iota((8, LANES))
    if not last:
        for_next = jnp.where(lane < RIM, parts[2], parts[1])
        for_previous = jnp.where(lane < RIM, parts[0], parts[2])
        a_ref[...], b_ref[...] = to_swaps(tile, for_next, for_previous)
        return

    starts = [
        block_ref[:1, :LANES],
        block_ref[:1, LANES:],
        jnp.where(lane[:1] < RIM, after[:1, :LANES], before[:1, LANES:]),
    ]
    packed = []
    for start, part in zip(starts, parts):
        even = start != 0
        rows = [jnp.where(even, part[r + 1 : r + 2], part[r : r + 1]) for r in range(0, 8, 2)]
        packed.append(jnp.concatenate(rows, axis=0))
    extra = jnp.zeros((8, LANES), F32)
    for i, ref in enumerate((squares_1, squares_2)):
        rest = jnp.sum(ref[...], axis=1, keepdims=True)
        for j in range(3):
            piece = rest.astype(BF16).astype(F32)
            extra = jnp.where(lane == 3 * i + j, piece, extra)
            rest = rest - piece
    moved = pltpu.roll(extra, 8, 1)
    rows = [extra[r : r + 1] + moved[r + 1 : r + 2] for r in range(0, 8, 2)]
    extra = jnp.concatenate(rows, axis=0)
    ids = ids_ref[...]
    for k in range(1, clusters):
        below = jnp.sum((ids < k).astype(F32), axis=1, keepdims=True)
        extra = jnp.where(lane[:4] == 16 + k, below, extra)
    top = jnp.concatenate([packed[0], packed[1]], axis=1)
    message = jnp.concatenate([top, jnp.concatenate([packed[2], extra], axis=1)], axis=0)
    message = message.astype(BF16)
    for t in range(out_ref.shape[0]):
        out_ref[t] = message


def gram_kernel(
    keep_same, tiles, groups, g_ref, own_ref, samples_in, samples_ref, field_ref, gram_ref
):
    samples_ref[...] = samples_in[...]
    tile = lax.axis_index("tiles")
    group = lax.axis_index("probes")
    clusters = gram_ref.shape[0]
    cell_count = tiles * 2 * LANES
    low = lanes_iota((8, LANES)) < RIM
    row = rows_iota((8, LANES))

    def twice(x):
        out = jnp.broadcast_to(x[:1], (8, LANES))
        for r in range(1, 4):
            out = jnp.where(row >= 2 * r, jnp.broadcast_to(x[r : r + 1], (8, LANES)), out)
        return out

    def piece_of(t, p, lower, at):
        part = g_ref[t, p].astype(F32)
        return part[4 * lower : 4 * lower + 4, at * LANES : (at + 1) * LANES]

    def factor_of(p):
        def add(t, acc):
            return acc + g_ref[t, p].astype(F32)[4:, LANES:]

        sums = lax.fori_loop(0, tiles, add, jnp.zeros((4, LANES), F32), unroll=tiles <= 8)
        sums = twice(sums)
        sums = jnp.where(row % 2 == 0, sums, pltpu.roll(sums, LANES - 8, 1))
        first = jnp.sum(sums[:, :3], axis=1, keepdims=True)
        second = jnp.sum(sums[:, 3:6], axis=1, keepdims=True)
        scale = jnp.sqrt(first / cell_count + F32(1e-06))
        size = jnp.sqrt(second / cell_count) * F32(1 / SHRINK) / scale
        return F32(1 / SHRINK) / (scale * jnp.sqrt(size * size + F32(1e-06)))

    def ids_of(t):
        starts = twice(piece_of(t, 0, 1, 1))
        cell = lanes_iota((8, 2 * LANES)).astype(F32)
        ids = jnp.zeros(cell.shape, jnp.int32)
        for k in range(1, clusters):
            ids = ids + (cell >= starts[:, 16 + k : 17 + k]).astype(jnp.int32)
        return [ids[:, :LANES], ids[:, LANES:]]

    def field(t, p, ids, own=None):
        before = piece_of(jnp.maximum(t - 1, 0), p, 1, 0)
        before = jnp.where(low[:4] & (t > 0), before, F32(0))
        after = piece_of(jnp.minimum(t + 1, tiles - 1), p, 1, 0)
        after = jnp.where(~low[:4] & (t < tiles - 1), after, F32(0))
        if own is None:
            parts = [twice(piece_of(t, p, 0, 0) + before), twice(piece_of(t, p, 0, 1) + after)]
        else:
            parts = [own[0] + twice(before), own[1] + twice(after)]
        return [
            jnp.where(colour_of(i) if keep_same else ~colour_of(i), part, F32(0))
            for i, part in zip(ids, parts)
        ]

    factors = [factor_of(p) for p in range(groups)]
    mine_factor = factors[0]
    for p in range(1, groups):
        mine_factor = jnp.where(group == p, factors[p], mine_factor)
    own = [own_ref[:, at * LANES : (at + 1) * LANES] for at in range(2)]
    own = field(tile, group, ids_of(tile), own)
    field_ref[:, :LANES] = own[0] * mine_factor
    field_ref[:, LANES:] = own[1] * mine_factor

    def add_tile(t, acc):
        ids = ids_of(t)
        every = [
            jnp.concatenate(field(t, p, ids), axis=1) * factors[p] for p in range(groups)
        ]
        mine = every[0]
        for p in range(1, groups):
            mine = jnp.where(group == p, every[p], mine)
        ids = jnp.concatenate(ids, axis=1)
        left = jnp.concatenate([jnp.where(ids == k, mine, F32(0)) for k in range(clusters)], axis=0)
        return acc + lax.dot_general(
            left,
            jnp.concatenate(every, axis=0),
            (((1,), (1,)), ((), ())),
            precision=lax.Precision.HIGHEST,
            preferred_element_type=F32,
        )

    acc = jnp.zeros((8 * clusters, 8 * groups), F32)
    acc = lax.fori_loop(0, tiles, add_tile, acc, unroll=tiles <= 8)
    gram_ref[...] = acc.reshape(gram_ref.shape)


def shards(
    blocks, connectivity, basal_map, friction, elem_counts, obs_weight, sign_bits, cluster_ids
):
    slots = blocks.shape[0]
    node_slots = connectivity.shape[1]
    node_count = obs_weight.shape[0]
    cell_count, group_size = sign_bits.shape
    tiles = lax.axis_size("tiles")
    groups = lax.axis_size("probes")
    pairs = slots * node_slots // LANES
    refs = pairs * LANES
    levels = (node_count + HALO) // RADIX
    padded_order = 2 * LANES
    window = cell_count + 2 * RIM

    vmem = pl.BlockSpec(memory_space=pltpu.VMEM)
    params = pltpu.CompilerParams(vmem_limit_bytes=VMEM_BYTES)
    shaped = jax.ShapeDtypeStruct

    hbm = pl.BlockSpec(memory_space=pltpu.HBM)
    smem = pl.BlockSpec(memory_space=pltpu.SMEM)

    def call(kernel, name, out_shape, operands, scratch=(), in_specs=None):
        in_specs = in_specs or [vmem] * len(operands)
        operands = [
            pltpu.with_memory_space_constraint(x, pltpu.HBM) if spec is hbm else x
            for x, spec in zip(operands, in_specs)
        ]
        return pl.pallas_call(
            kernel,
            out_shape=out_shape,
            in_specs=in_specs,
            out_specs=jax.tree.map(lambda _: vmem, out_shape),
            scratch_shapes=list(scratch),
            compiler_params=params,
            name=name,
        )(*operands)

    evens = range(0, tiles - 1, 2)
    odds = range(1, tiles - 1, 2)
    pairs_a = [(i, i + 1) for i in odds] + [(i + 1, i) for i in odds]
    pairs_b = [(i, i + 1) for i in evens] + [(i + 1, i) for i in evens]

    def swapped(a, b):
        return lax.ppermute(a, "tiles", pairs_a), lax.ppermute(b, "tiles", pairs_b)

    weight = obs_weight.T
    block, again = call(
        announce_kernel,
        "announce",
        [shaped((16, cell_count), F32)] * 2,
        [sign_bits.T, cluster_ids.reshape(1, cell_count), weight],
        [
            pltpu.VMEM((group_size, cell_count), jnp.int32),
            pltpu.VMEM((1, cell_count), jnp.int32),
            pltpu.VMEM((3, HALO), F32),
            pltpu.SemaphoreType.DMA((3,)),
        ],
        [hbm] * 3,
    )
    block_a, block_b = swapped(again, block)

    conn, cells, fr, loaded, node_hot, edge_hot, level_hot, cell_hot, spread, order = call(
        functools.partial(setup_kernel, levels),
        "setup",
        [
            shaped((pairs, LANES), jnp.int32),
            shaped((pairs, LANES), jnp.int32),
            shaped((slots, padded_order), F32),
            shaped(blocks.shape, BF16),
            shaped((RADIX, refs), BF16),
            shaped((EDGE_RADIX, refs), BF16),
            shaped((16 * (levels + 1), refs), BF16),
            shaped((LANES, refs), BF16),
            shaped((LANES, 2 * padded_order), BF16),
            shaped((2 * padded_order, 3 * LANES), BF16),
        ],
        [elem_counts, connectivity, basal_map, friction.transpose(2, 0, 1), blocks],
        [
            pltpu.VMEM(connectivity.shape, jnp.int32),
            pltpu.VMEM(basal_map.shape, jnp.int32),
            pltpu.VMEM((3, slots, node_slots), F32),
            pltpu.SemaphoreType.DMA((4,)),
        ],
        [smem] + [hbm] * 4,
    )
    factors, node_map, cell_map, spread_map, order_map = loaded, node_hot, cell_hot, spread, order

    edge = shaped((24, HALO), F32)
    message = shaped((24 * EDGE, EDGE_RADIX), BF16)
    rim = shaped((group_size, LANES), F32)
    whole = shaped((group_size, window), F32)
    field = shaped((group_size, cell_count), F32)
    everyone = ("tiles", "probes")

    carried = []
    factors = loaded
    squares = []
    samples = None
    for step in range(POWER + 1):
        last = step == POWER
        out_shape = [shaped((16 * pairs, 3 * LANES), BF16), edge, edge, message, message]
        out_shape += [rim] * (step > 0) + [field] * (step == 1)
        ordered, own_a, own_b, far, near, *extra = call(
            functools.partial(forward_kernel, step, tiles, levels),
            "forward",
            out_shape,
            [block, block_a, block_b, *carried]
            + [cells, fr, factors, node_map, level_hot, cell_hot, spread, order],
            [
                pltpu.VMEM((16 * pairs, 2 * padded_order), BF16),
                pltpu.VMEM((48, refs), BF16),
            ],
        )
        squares += extra[:1]
        if step == 1:
            samples = extra[1]
        new_a, new_b = swapped(far, near)
        inner = call(
            functools.partial(inner_kernel, levels),
            "inner",
            shaped((8 * pairs, 3 * LANES), F32),
            [ordered, weight, conn, node_hot, level_hot],
            [pltpu.VMEM((48 * (levels - 2), refs), BF16)],
        )
        operands = [block, block_a, block_b, own_a, own_b, new_a, new_b, inner, weight]
        operands += [conn, cells, fr, loaded, edge_hot, cell_map, spread_map, order_map]
        if last:
            operands += squares + [cluster_ids.reshape(1, cell_count)]
            packed = shaped((lax.axis_size(everyone), group_size, 2 * LANES), BF16)
            out_shape = [whole, packed]
        else:
            out_shape = [whole, rim, rim]
        basal, *messages = call(
            functools.partial(adjoint_kernel, last, tiles, levels),
            "adjoint",
            out_shape,
            operands,
            [
                pltpu.VMEM((16 * pairs, 2 * padded_order), BF16),
                pltpu.VMEM((8 * pairs, 3 * LANES), BF16),
                pltpu.VMEM((48, refs), BF16),
            ],
        )
        if not last:
            if step == 0:
                *messages, source, ids = lax.optimization_barrier((*messages, loaded, conn))
                shape = shaped(blocks.shape, BF16)
                factors = call(turn_blocks_kernel, "turn_blocks", shape, [source])
                shape = shaped((refs, RADIX), BF16)
                node_map = call(turn_nodes_kernel, "turn_nodes", shape, [ids])
            if step == POWER - 1:
                *messages, ids = lax.optimization_barrier((*messages, cells))
                cell_map, spread_map, order_map = call(
                    functools.partial(turn_cells_kernel, node_slots),
                    "turn_cells",
                    [
                        shaped((refs, LANES), BF16),
                        shaped((2 * padded_order, LANES), BF16),
                        shaped((3 * LANES, 2 * padded_order), BF16),
                    ],
                    [ids],
                )
                basal, cell_map = lax.optimization_barrier((basal, cell_map))
            carried = [basal, *swapped(*messages)]

    gathered = lax.all_to_all(messages[0], everyone, 0, 0)
    gathered = gathered.reshape(tiles, groups, *gathered.shape[1:])
    samples, refined, gram = call(
        functools.partial(gram_kernel, POWER % 2 == 1, tiles, groups),
        "gram",
        [field, field, shaped((tiles, group_size, groups * group_size), F32)],
        [gathered, basal, samples],
    )
    return (samples.T, refined.T, gram)


def solution(mesh):
    in_specs = (
        P("tiles", None, None),
        P("tiles", None),
        P("tiles", None),
        P("tiles", None, None),
        P("tiles"),
        P("tiles", None),
        P("tiles", "probes"),
        P("tiles"),
    )
    out_specs = (P("tiles", "probes"), P("tiles", "probes"), P(None, "probes", None))
    return jax.shard_map(shards, mesh=mesh, in_specs=in_specs, out_specs=out_specs, check_vma=False)
```
